32 devices in a mesh: expert: 16 (over z, y, x), tensor: 2 (over core).
Axes of the slice: x: 2, y: 2, z: 4, core: 2. Of those that a mesh axis runs over, the one named last changes fastest.
Arguments:
- tokens: bfloat16 [2048, 2048], P(('expert', 'tensor')), may hold values from -40 to 40
- cotangent: bfloat16 [2048, 2048], P(('expert', 'tensor')), may hold values from -32 to 32
- gain: float32 [2048], replicated, may hold values from 0.1 to 1.9
- expert_ids: int32 [2048, 8], P('expert'), may hold values from 0 to 31, all different within a row; in each aligned block of 128 rows (0 to 127, 128 to 255, ...) at most 48 rows name the same one
- gate_probs: float32 [2048, 8], P('expert'), may hold values from 0.05 to 0.3
- gate_up_weight: bfloat16 [32, 2048, 1536], P(('expert', 'tensor')), may hold values from -0.125 to 0.125
- down_weight: bfloat16 [32, 768, 2048], P(('expert', 'tensor')), may hold values from -0.21875 to 0.21875
Outputs:
- mixed: bfloat16 [2048, 2048], P(('expert', 'tensor'))
- token_grad: bfloat16 [2048, 2048], P(('expert', 'tensor'))
- prob_grad: float32 [2048, 8], P(('expert', 'tensor'))
- gain_grad: float32 [2048], replicated
- gate_up_grad: bfloat16 [32, 2048, 1536], P(('expert', 'tensor'))
- down_grad: bfloat16 [32, 768, 2048], P(('expert', 'tensor'))
The draws below stay inside these ranges and needn't reach their ends.
Inputs may be any that keep to these rules, and one draw needn't show every extreme that they name: `expert_ids`: in each aligned block of 128 rows, the tokens of one index of the expert axis, no expert is named by more than 48 rows.
All inputs are finite; a program needn't handle non-finite values.
Results may differ from the reference program's by a relative error of at most 0.009.
Values may be sent and summed in bfloat16 or wider, within the bound.
No kernel may reach another device: no remote copies, remote signals or barrier semaphores. Data moves between devices by JAX's collectives and lax.ppermute only.
A program may use at most 128 MiB of HBM per device.

```python
import math
import jax
import jax.numpy as jnp
import numpy as np
from jax import lax

D = 2048
FF = 768
TOP = 8
TOK_GRP = 128
EXPERTS = 32
UNIT_BLOCKS = 1
FF_DEV = 768
TOKENS = 2048
CAP = 48


def draw_tokens(key, part):
    first, second, third = jax.random.split(jax.random.fold_in(key, 11), 3)
    base_draw = jax.random.truncated_normal(first, -4.0, 4.0, (TOKENS, D), jnp.float32)
    row_scale = jnp.exp(jax.random.uniform(second, (TOKENS, 1), jnp.float32, 0.0, math.log(10.0))) / math.sqrt(10.0)
    column_scale = jnp.exp(jax.random.uniform(third, (1, D), jnp.float32, 0.0, math.log(10.0))) / math.sqrt(10.0)
    return (base_draw * row_scale * column_scale).astype(jnp.bfloat16)


def draw_cotangent(key, part):
    first, second = jax.random.split(jax.random.fold_in(key, 23), 2)
    position = jnp.arange(TOKENS, dtype=jnp.float32)[:, None] / TOKENS
    roughness = jnp.exp(jax.random.uniform(second, (TOKENS, 1), jnp.float32, 0.0, math.log(2.0)))
    base_draw = jax.random.truncated_normal(first, -4.0, 4.0, (TOKENS, D), jnp.float32)
    rising = 1.0 + 2.0 * position
    return (base_draw * rising * roughness).astype(jnp.bfloat16)


def block_levels(stream_key, extent, cuts, least, top_value):
    factor_of, own = 1.0, jax.random.fold_in(stream_key, 6)
    for dim, blocks in cuts:
        heights = jnp.exp(jax.random.uniform(jax.random.fold_in(own, dim), (blocks,), jnp.float32, least / len(cuts), top_value / len(cuts)))
        factor_of = factor_of * jnp.repeat(heights, extent[dim] // blocks).reshape([-1 if axis == dim else 1 for axis in range(len(extent))])
    return factor_of


def shared_out(own_key, own, number, rows, count, top, limit, lean):
    sequence = jax.random.permutation(own_key, count)
    packed, common = load_shares(count, rows * top, limit, lean, True), load_shares(count, rows * top, limit, lean, False)
    places = jnp.arange(count)

    def named(lengths, rotation):
        used = int((lengths > 0).sum())
        fixed = max(1, used // 4)
        passed = fixed + (places - fixed + rotation * (used - fixed)) % max(1, count - fixed)
        return jnp.zeros((count,), jnp.int32).at[sequence[jnp.where(places < fixed, places, passed)]].set(jnp.asarray(lengths, jnp.int32))

    lengths = jnp.where(number % 4 == 0, named(packed, number // 4), named(common, number - number // 4 - 1))
    mixed = jax.random.permutation(jax.random.fold_in(own, 3), count)
    donor, receiver = mixed[0:count // 2 * 2:2], mixed[1:count // 2 * 2:2]
    slack = jnp.minimum(lengths[donor] - 1, limit - lengths[receiver]) // 2
    slack = jnp.where((donor == sequence[0]) | (receiver == sequence[0]) | (lengths[receiver] == 0), 0, jnp.maximum(slack, 0))
    passed = jax.random.randint(jax.random.fold_in(own, 4), (count // 2,), 0, 1 << 20) % (slack + 1)
    lengths = lengths.at[donor].add(-passed).at[receiver].add(passed)
    labels = jnp.searchsorted(jnp.cumsum(lengths), jnp.arange(rows * top), side="right").astype(jnp.int32)
    listing = labels.reshape(top, rows).T
    listing = listing[jax.random.permutation(jax.random.fold_in(own, 1), rows)]
    rotation = jax.random.randint(jax.random.fold_in(own, 2), (rows, 1), 0, top)
    return jnp.take_along_axis(listing, (jnp.arange(top)[None, :] + rotation) % top, axis=1)


def load_shares(count, total, reach, lean, full):
    weights = [(1 << 20) // math.isqrt(standing ** lean) + 1 for standing in range(1, count + 1)]
    largest = reach if full else min(reach, max(-(-total // count), total * weights[0] // sum(weights)))
    least = 1 if total - largest >= count - 1 else 0
    holding, rest = [largest] + [least] * (count - 1), total - largest - least * (count - 1)
    while rest > 0:
        free = [i for i in range(1, count) if holding[i] < largest] or [i for i in range(1, count) if holding[i] < reach]
        mass, left = sum([weights[i] for i in free]), rest
        for i in free:
            extra = min(reach - holding[i], max(1, left * weights[i] // mass), rest)
            holding[i] = holding[i] + extra
            rest = rest - extra
    return np.array(holding)


def gaussian(own_key, dims, scale, limit, cuts=(), kind=jnp.bfloat16):
    result = scale * jax.random.normal(own_key, dims, jnp.float32)
    if cuts:
        result = result * block_levels(own_key, dims, cuts, -0.22, 0.18)
    return jnp.clip(result, -limit, limit).astype(kind)


def setup_inputs(seed: int = 0) -> dict:
    streams_of = jax.random.split(jax.random.key(seed), 8)
    tokens = draw_tokens(jax.random.fold_in(streams_of[7], 71), 0)
    cotangent = draw_cotangent(jax.random.fold_in(streams_of[7], 71), 0)
    gain = jnp.clip(1.0 + 0.18 * jax.random.normal(streams_of[2], (D,), jnp.float32), 0.1, 1.9)
    expert_ids_keys = jax.random.split(jax.random.fold_in(streams_of[3], 1), TOKENS // TOK_GRP)
    expert_ids_turns = jax.random.permutation(jax.random.fold_in(streams_of[3], 3), TOKENS // TOK_GRP)
    expert_ids = jax.vmap(lambda own, number: shared_out(jax.random.fold_in(streams_of[3], 2), own, number, TOK_GRP, EXPERTS, TOP, CAP, 2))(expert_ids_keys, expert_ids_turns).reshape((TOKENS, TOP))
    gate_probs = jnp.clip(0.05 + 0.25 * jax.random.uniform(streams_of[4], (TOKENS, TOP), jnp.float32) ** block_levels(streams_of[4], (TOKENS, TOP), ((0, 16),), -0.2, 0.2), 0.05, 0.3)
    gate_up_weight = gaussian(streams_of[5], (EXPERTS * UNIT_BLOCKS, D, 2 * FF_DEV), D ** -0.5, 0.125, ((0, 32),))
    down_weight = gaussian(streams_of[6], (EXPERTS * UNIT_BLOCKS, FF_DEV, D), FF ** -0.5, 0.21875, ((0, 32),))
    return {"tokens": tokens, "cotangent": cotangent, "gain": gain, "expert_ids": expert_ids, "gate_probs": gate_probs, "gate_up_weight": gate_up_weight, "down_weight": down_weight}


def expert_forward(rows, gate_up, down_proj):
    projected = jnp.dot(rows, gate_up, preferred_element_type=jnp.float32)
    half_width = down_proj.shape[0]
    gate_pre = projected[:, :half_width]
    up_pre = projected[:, half_width:]
    sigmoid_gate = jax.nn.sigmoid(gate_pre)
    hidden = (gate_pre * sigmoid_gate * up_pre).astype(jnp.bfloat16)
    block_out = jnp.dot(hidden, down_proj, preferred_element_type=jnp.float32).astype(jnp.bfloat16)
    return (gate_pre, up_pre, sigmoid_gate, hidden, block_out)

def expert_backward(rows, slot_grads, gate_up, down_proj, gate_pre, up_pre, sigmoid_gate, hidden):
    hidden_grad = lax.dot_general(slot_grads, down_proj, (((1,), (1,)), ((), ())), preferred_element_type=jnp.float32)
    gate_grad = (hidden_grad * up_pre * sigmoid_gate * (1.0 + gate_pre * (1.0 - sigmoid_gate))).astype(jnp.bfloat16)
    up_grad = (hidden_grad * gate_pre * sigmoid_gate).astype(jnp.bfloat16)
    joined_grad = jnp.concatenate([gate_grad, up_grad], axis=1)
    down_part = lax.dot_general(hidden, slot_grads, (((0,), (0,)), ((), ())), preferred_element_type=jnp.float32).astype(jnp.bfloat16)
    gate_up_part = lax.dot_general(rows, joined_grad, (((0,), (0,)), ((), ())), preferred_element_type=jnp.float32).astype(jnp.bfloat16)
    input_grad = lax.dot_general(joined_grad, gate_up, (((1,), (1,)), ((), ())), preferred_element_type=jnp.float32).astype(jnp.bfloat16)
    return (input_grad, gate_up_part, down_part)

def reference(tokens, cotangent, gain, expert_ids, gate_probs, gate_up_weight, down_weight):
    values = tokens.astype(jnp.float32)
    inv_rms = lax.rsqrt(lax.optimization_barrier(jnp.mean(values * values, axis=1, keepdims=True)) + 1e-06)
    scaled = values * inv_rms
    normed = (scaled * gain[None, :]).astype(jnp.bfloat16)
    cot_values = cotangent.astype(jnp.float32)
    groups = TOKENS // TOK_GRP
    slots = groups * CAP
    row_ids = jnp.arange(TOKENS, dtype=jnp.int32)
    group_of = row_ids // TOK_GRP
    top_ids = jnp.arange(TOP, dtype=jnp.int32)
    normed_pad = jnp.concatenate([normed, jnp.zeros((1, D), jnp.bfloat16)], axis=0)
    cot_pad = jnp.concatenate([cot_values, jnp.zeros((1, D), jnp.float32)], axis=0)

    def per_expert(carry, expert):
        out_acc, grad_acc, prob_acc = carry
        matches = expert_ids == expert
        chosen = jnp.any(matches, axis=1)
        prob_of = lax.optimization_barrier(jnp.sum(jnp.where(matches, gate_probs, 0.0), axis=1))
        slot_of = lax.optimization_barrier(jnp.sum(jnp.where(matches, top_ids[None, :], 0), axis=1)).astype(jnp.int32)
        counts = chosen.astype(jnp.int32).reshape(groups, TOK_GRP)
        rank_in = (jnp.cumsum(counts, axis=1) - counts).reshape(TOKENS).astype(jnp.int32)
        target = jnp.where(chosen, group_of * CAP + rank_in, slots).astype(jnp.int32)
        table = jnp.full((slots + 1,), TOKENS, jnp.int32).at[target].set(row_ids)[:slots]
        rows = normed_pad[table]
        slot_cot = cot_pad[table]
        slot_prob = jnp.concatenate([prob_of, jnp.zeros((1,), prob_of.dtype)])[table]
        slot_index = jnp.concatenate([slot_of, jnp.zeros((1,), jnp.int32)])[table]
        slot_grads = (slot_prob[:, None] * slot_cot).astype(jnp.bfloat16)
        out_sum = jnp.zeros((slots, D), jnp.float32)
        input_sum = jnp.zeros((slots, D), jnp.float32)
        gate_up_parts = []
        down_parts = []
        for block_index in range(UNIT_BLOCKS):
            weight_row = (expert * UNIT_BLOCKS + block_index).astype(jnp.int32)
            gate_up = lax.dynamic_index_in_dim(gate_up_weight, weight_row, 0, keepdims=False)
            down_proj = lax.dynamic_index_in_dim(down_weight, weight_row, 0, keepdims=False)
            gate_pre, up_pre, sigmoid_gate, hidden, block_out = expert_forward(rows, gate_up, down_proj)
            input_grad, gate_up_part, down_part = expert_backward(rows, slot_grads, gate_up, down_proj, gate_pre, up_pre, sigmoid_gate, hidden)
            out_sum = out_sum + block_out.astype(jnp.float32)
            input_sum = input_sum + input_grad.astype(jnp.float32)
            gate_up_parts.append(gate_up_part)
            down_parts.append(down_part)
        out_acc = out_acc.at[table].add(slot_prob[:, None] * out_sum)
        grad_acc = grad_acc.at[table].add(input_sum)
        prob_acc = prob_acc.at[table * TOP + slot_index].add(lax.optimization_barrier(jnp.sum(slot_cot * out_sum, axis=1)))
        return ((out_acc, grad_acc, prob_acc), (jnp.stack(gate_up_parts), jnp.stack(down_parts)))
    init = (jnp.zeros((TOKENS + 1, D), jnp.float32), jnp.zeros((TOKENS + 1, D), jnp.float32), jnp.zeros(((TOKENS + 1) * TOP,), jnp.float32))
    finals, stacked = lax.scan(per_expert, init, jnp.arange(EXPERTS, dtype=jnp.int32))
    out_acc, grad_acc, prob_acc = finals
    gate_up_all, down_all = stacked
    mixed = (values + out_acc[:TOKENS]).astype(jnp.bfloat16)
    normed_grad = grad_acc[:TOKENS]
    gain_grad = lax.optimization_barrier(jnp.sum(normed_grad * scaled, axis=0))
    gain_side = normed_grad * gain[None, :]
    token_grad = (cot_values + inv_rms * (gain_side - scaled * lax.optimization_barrier(jnp.mean(gain_side * scaled, axis=1, keepdims=True)))).astype(jnp.bfloat16)
    prob_grad = prob_acc[:TOKENS * TOP].reshape(TOKENS, TOP)
    gate_up_grad = gate_up_all.reshape(EXPERTS * UNIT_BLOCKS, D, 2 * FF_DEV)
    down_grad = down_all.reshape(EXPERTS * UNIT_BLOCKS, FF_DEV, D)
    return (mixed, token_grad, prob_grad, gain_grad, gate_up_grad, down_grad)
```

```python
import functools

import jax
import jax.numpy as jnp
from jax import lax
from jax.experimental import pallas as pl
from jax.experimental.pallas import tpu as pltpu
from jax.sharding import PartitionSpec as P

TOP = 8
EXP_DEV = 2
VMEM_LIMIT = 48 * 1024 * 1024


def normalize(rows):
    values = rows.astype(jnp.float32)
    inv_rms = lax.rsqrt(jnp.mean(values * values, axis=1, keepdims=True) + 1e-06)
    return (values * inv_rms, inv_rms)


def expert_forward(rows, gate_up, down_proj):
    projected = jnp.dot(rows, gate_up, preferred_element_type=jnp.float32)
    half_width = down_proj.shape[0]
    gate_pre = projected[:, :half_width]
    up_pre = projected[:, half_width:]
    sigmoid_gate = jax.nn.sigmoid(gate_pre)
    hidden = (gate_pre * sigmoid_gate * up_pre).astype(jnp.bfloat16)
    block_out = jnp.dot(hidden, down_proj, preferred_element_type=jnp.float32).astype(jnp.bfloat16)
    return (gate_pre, up_pre, sigmoid_gate, hidden, block_out)


def expert_backward(rows, slot_grads, gate_up, down_proj, gate_pre, up_pre, sigmoid_gate, hidden):
    hidden_grad = lax.dot_general(
        slot_grads, down_proj, (((1,), (1,)), ((), ())), preferred_element_type=jnp.float32
    )
    gate_grad = (
        hidden_grad * up_pre * sigmoid_gate * (1.0 + gate_pre * (1.0 - sigmoid_gate))
    ).astype(jnp.bfloat16)
    up_grad = (hidden_grad * gate_pre * sigmoid_gate).astype(jnp.bfloat16)
    joined_grad = jnp.concatenate([gate_grad, up_grad], axis=1)
    down_part = lax.dot_general(
        hidden, slot_grads, (((0,), (0,)), ((), ())), preferred_element_type=jnp.float32
    ).astype(jnp.bfloat16)
    gate_up_part = lax.dot_general(
        rows, joined_grad, (((0,), (0,)), ((), ())), preferred_element_type=jnp.float32
    ).astype(jnp.bfloat16)
    input_grad = lax.dot_general(
        joined_grad, gate_up, (((1,), (1,)), ((), ())), preferred_element_type=jnp.float32
    ).astype(jnp.bfloat16)
    return (input_grad, gate_up_part, down_part)


def routed_shards(tokens, cotangent, gain, expert_ids, gate_probs, gate_up_weight, down_weight):
    tensor_size = lax.axis_size("tensor")
    expert_size = lax.axis_size("expert")
    my_rank = lax.axis_index("tensor")
    blocks_each = tensor_size // EXP_DEV
    my_type = my_rank // blocks_each
    group_rows = expert_ids.shape[0]
    features = tokens.shape[1]
    capacity = 3 * group_rows * TOP // (2 * EXP_DEV * expert_size)
    highest = lax.Precision.HIGHEST
    scaled_own, inv_own = normalize(tokens)
    carried = (scaled_own * gain[None, :]).astype(jnp.bfloat16)
    group_first, group_grads = (
        lax.all_gather(carried, "tensor", axis=0, tiled=True),
        lax.all_gather(cotangent, "tensor", axis=0, tiled=True),
    )
    targets = jnp.arange(expert_size, dtype=jnp.int32) * EXP_DEV + my_type
    matches = expert_ids[:, :, None] == targets[None, None, :]
    chosen = jnp.any(matches, axis=1)
    weight_of = jnp.sum(jnp.where(matches, gate_probs[:, :, None], 0.0), axis=1)
    slot_of = jnp.sum(
        jnp.where(matches, jnp.arange(TOP, dtype=jnp.int32)[None, :, None], 0), axis=1
    )
    row_ids = jnp.arange(group_rows, dtype=jnp.int32)
    earlier = (row_ids[None, :] < row_ids[:, None]).astype(jnp.bfloat16)
    rank_in = jnp.dot(
        earlier, chosen.astype(jnp.bfloat16), preferred_element_type=jnp.float32
    ).astype(jnp.int32)
    placed = chosen.T[:, None, :] & (
        rank_in.T[:, None, :] == jnp.arange(capacity, dtype=jnp.int32)[None, :, None]
    )
    source = jnp.sum(jnp.where(placed, row_ids[None, None, :], 0), axis=2)
    filled = jnp.any(placed, axis=2)
    slot_prob = jnp.sum(jnp.where(placed, weight_of.T[:, None, :], 0.0), axis=2)
    slot_index = jnp.sum(jnp.where(placed, slot_of.T[:, None, :], 0), axis=2)
    sent_rows = jnp.where(
        filled[:, :, None], jnp.take(group_first, source, axis=0), jnp.zeros((), jnp.bfloat16)
    )
    sent_grads = (
        slot_prob[:, :, None] * jnp.take(group_grads, source, axis=0).astype(jnp.float32)
    ).astype(jnp.bfloat16)
    gate_up = gate_up_weight[0]
    down_proj = down_weight[0]
    arrived_rows, arrived_grads = (
        lax.all_to_all(sent_rows, "expert", split_axis=0, concat_axis=0, tiled=True),
        lax.all_to_all(sent_grads, "expert", split_axis=0, concat_axis=0, tiled=True),
    )
    rows = arrived_rows.reshape(-1, features)
    slot_grads = arrived_grads.reshape(-1, features)
    gate_pre, up_pre, sigmoid_gate, hidden, block_out = expert_forward(rows, gate_up, down_proj)
    out_slots = block_out.reshape(expert_size, capacity, features)
    input_grad, gate_up_part, down_part = expert_backward(
        rows, slot_grads, gate_up, down_proj, gate_pre, up_pre, sigmoid_gate, hidden
    )
    input_slots = input_grad.reshape(expert_size, capacity, features)
    out_back, input_back = (
        lax.all_to_all(out_slots, "expert", split_axis=0, concat_axis=0, tiled=True),
        lax.all_to_all(input_slots, "expert", split_axis=0, concat_axis=0, tiled=True),
    )
    out_flat = out_back.reshape(-1, features)
    input_flat = input_back.reshape(-1, features)
    used_source = source.reshape(-1)
    used_filled = filled.reshape(-1)
    used_prob = slot_prob.reshape(-1)
    used_index = slot_index.reshape(-1)
    cot_slots = jnp.take(group_grads, used_source, axis=0)
    prob_values = jnp.einsum("sd,sd->s", cot_slots, out_flat, preferred_element_type=jnp.float32)
    hit = (row_ids[:, None] == used_source[None, :]) & used_filled[None, :]
    input_part = jnp.dot(hit.astype(jnp.bfloat16), input_flat, preferred_element_type=jnp.float32)
    weighting = jnp.where(hit, used_prob[None, :], 0.0)
    out_part = jnp.dot(
        weighting,
        out_flat.astype(jnp.float32),
        precision=highest,
        preferred_element_type=jnp.float32,
    )
    prob_columns = jnp.where(
        used_index[:, None] == jnp.arange(TOP, dtype=jnp.int32)[None, :], prob_values[:, None], 0.0
    )
    prob_part = jnp.dot(
        hit.astype(jnp.float32), prob_columns, precision=highest, preferred_element_type=jnp.float32
    )
    out_sum, normed_grad, prob_grad = (
        lax.psum_scatter(out_part, "tensor", scatter_dimension=0, tiled=True),
        lax.psum_scatter(input_part, "tensor", scatter_dimension=0, tiled=True),
        lax.psum_scatter(prob_part, "tensor", scatter_dimension=0, tiled=True),
    )
    mixed = (tokens.astype(jnp.float32) + out_sum).astype(jnp.bfloat16)
    gain_side = normed_grad * gain[None, :]
    token_grad = (
        cotangent.astype(jnp.float32)
        + inv_own
        * (gain_side - scaled_own * jnp.mean(gain_side * scaled_own, axis=1, keepdims=True))
    ).astype(jnp.bfloat16)
    gain_grad = lax.psum(jnp.sum(normed_grad * scaled_own, axis=0), ("expert", "tensor"))
    return (mixed, token_grad, prob_grad, gain_grad, gate_up_part[None], down_part[None])


BOTH = ("expert", "tensor")


def flip_first(expert, core):
    return expert ^ (2 if core == 0 else 1)


def flip_second(expert, core):
    return expert ^ (1 if core == 0 else 2)


def send(array, expert_size, place):
    pairs = []
    for expert in range(expert_size):
        for core in range(2):
            to_expert, to_core = place(expert, core)
            pairs.append((expert * 2 + core, to_expert * 2 + to_core))
    return lax.ppermute(array, BOTH, pairs)


def send_first(array, expert_size):
    return send(array, expert_size, lambda e, c: (flip_first(e, c), c))


def send_second(array, expert_size):
    return send(array, expert_size, lambda e, c: (flip_second(e, c), c))


def send_core(array, expert_size):
    return send(array, expert_size, lambda e, c: (e, 1 - c))


def send_along(array, expert_size, step):
    return send(array, expert_size, lambda e, c: ((e + 4 * step) % expert_size, c))


def gather_rows(own, expert_size):
    gathered = []
    for step in range(expert_size // 4):
        block = own if step == 0 else send_along(own, expert_size, -step)
        pair = jnp.stack([block, send_second(block, expert_size)])
        quad = jnp.concatenate([pair, send_first(pair, expert_size)])
        gathered.append((quad, send_core(quad, expert_size)))
    return gathered


def add_half(left, right):
    return (left.astype(jnp.float32) + right.astype(jnp.float32)).astype(jnp.bfloat16)


def scatter_sum(parts, expert_size):
    total = None
    for step in list(range(1, expert_size // 4)) + [0]:
        mine, other = parts[step]
        quad = add_half(mine, send_core(other, expert_size))
        pair = add_half(quad[:2], send_first(quad[2:], expert_size))
        block = add_half(pair[0], send_second(pair[1], expert_size))
        if step:
            block = send_along(block, expert_size, step)
        total = block.astype(jnp.float32) if total is None else total + block.astype(jnp.float32)
    return total


def swapped(index):
    return (index % 2) * 2 + index // 2


def select_norm_kernel(pick_ref, mine_ref, other_ref, gain_ref, normed_ref, scaled_ref):
    half = mine_ref.shape[1]
    rows = jnp.dot(pick_ref[0][:, :half], mine_ref[0], preferred_element_type=jnp.float32)
    rows += jnp.dot(pick_ref[0][:, half:], other_ref[0], preferred_element_type=jnp.float32)
    inv_rms = lax.rsqrt(jnp.mean(rows * rows, axis=1, keepdims=True) + 1e-06)
    scaled = rows * inv_rms
    scaled_ref[0] = scaled.astype(jnp.bfloat16)
    normed_ref[0] = (scaled * gain_ref[...]).astype(jnp.bfloat16)


def select_grad_kernel(pick_ref, mine_ref, other_ref, prob_ref, cot_ref, grad_ref):
    half = mine_ref.shape[1]
    rows = jnp.dot(pick_ref[0][:, :half], mine_ref[0], preferred_element_type=jnp.float32)
    rows += jnp.dot(pick_ref[0][:, half:], other_ref[0], preferred_element_type=jnp.float32)
    cot_ref[0] = rows.astype(jnp.bfloat16)
    grad_ref[0] = (rows * prob_ref[0]).astype(jnp.bfloat16)


def select(kernel, pick, mine, other, extra, extra_spec):
    _, capacity, group_rows = pick.shape
    half, features = mine.shape[1:]
    out = jax.ShapeDtypeStruct((4, capacity, features), jnp.bfloat16)
    return pl.pallas_call(
        kernel,
        grid=(4,),
        in_specs=[
            pl.BlockSpec((1, capacity, group_rows), lambda i: (i, 0, 0)),
            pl.BlockSpec((1, half, features), lambda i: (i, 0, 0)),
            pl.BlockSpec((1, half, features), lambda i: (swapped(i), 0, 0)),
            extra_spec,
        ],
        out_specs=[pl.BlockSpec((1, capacity, features), lambda i: (i, 0, 0))] * 2,
        out_shape=[out, out],
        compiler_params=pltpu.CompilerParams(vmem_limit_bytes=VMEM_LIMIT),
        cost_estimate=pl.CostEstimate(
            flops=8 * capacity * group_rows * features,
            bytes_accessed=16 * half * features + 16 * capacity * features,
            transcendentals=0,
        ),
    )(pick, mine, other, extra)


def expand_kernel(pick_ref, rows_ref, prob_ref, mine_ref, other_ref):
    half = mine_ref.shape[1]
    rows = (rows_ref[0].astype(jnp.float32) * prob_ref[0]).astype(jnp.bfloat16)
    pick = pick_ref[0]
    for columns, out_ref in ((pick[:, :half], mine_ref), (pick[:, half:], other_ref)):
        out_ref[0] = lax.dot_general(
            columns, rows, (((0,), (0,)), ((), ())), preferred_element_type=jnp.float32
        ).astype(jnp.bfloat16)


def expand(pick, rows, prob):
    _, capacity, group_rows = pick.shape
    half, features = group_rows // 2, rows.shape[2]
    out = jax.ShapeDtypeStruct((4, half, features), jnp.bfloat16)
    return pl.pallas_call(
        expand_kernel,
        grid=(4,),
        in_specs=[
            pl.BlockSpec((1, capacity, group_rows), lambda i: (i, 0, 0)),
            pl.BlockSpec((1, capacity, features), lambda i: (i, 0, 0)),
            pl.BlockSpec((1, capacity, 1), lambda i: (i, 0, 0)),
        ],
        out_specs=[
            pl.BlockSpec((1, half, features), lambda i: (i, 0, 0)),
            pl.BlockSpec((1, half, features), lambda i: (swapped(i), 0, 0)),
        ],
        out_shape=[out, out],
        compiler_params=pltpu.CompilerParams(vmem_limit_bytes=VMEM_LIMIT),
        cost_estimate=pl.CostEstimate(
            flops=8 * capacity * group_rows * features,
            bytes_accessed=16 * half * features + 8 * capacity * features,
            transcendentals=0,
        ),
    )(pick, rows, prob)


def broadcast_shards(tokens, cotangent, gain, expert_ids, gate_probs, gate_up_weight, down_weight):
    expert_size = lax.axis_size("expert")
    steps = expert_size // 4
    expert, core = lax.axis_index("expert"), lax.axis_index("tensor")
    my_expert = expert * EXP_DEV + core
    group_rows = expert_ids.shape[0]
    half = group_rows // 2
    features = tokens.shape[1]
    capacity = 3 * group_rows * TOP // (2 * EXP_DEV * expert_size)
    gate_up, down_proj = gate_up_weight[0], down_weight[0]

    tables = jnp.concatenate([expert_ids.T.astype(jnp.float32), gate_probs.T])
    tables = lax.all_gather(tables, "expert", axis=0)
    token_blocks = gather_rows(tokens, expert_size)
    cot_blocks = gather_rows(cotangent, expert_size)

    plane = expert % 4
    step_ids, firsts, seconds = (
        jnp.arange(steps)[:, None, None], jnp.arange(2)[None, :, None], jnp.arange(2)[None, None, :]
    )
    bits = jnp.where(core == 0, firsts * 2 + seconds, seconds * 2 + firsts)
    group = (((expert // 4 + step_ids) % steps) * 4 + (plane ^ bits)).reshape(-1)
    all_groups = jnp.arange(expert_size)
    far = (all_groups % 4) ^ plane
    place = ((all_groups // 4 - expert // 4) % steps) * 4 + jnp.where(core == 0, far, swapped(far))

    near = jnp.take(tables, group, axis=0)
    near = jnp.where(core == 0, near, jnp.roll(near, half, axis=2))
    matches = near[:, :TOP] == my_expert.astype(jnp.float32)
    chosen = jnp.any(matches, axis=1)
    weight_of = jnp.sum(jnp.where(matches, near[:, TOP:], 0.0), axis=1)
    row_ids = jnp.arange(group_rows, dtype=jnp.int32)
    earlier = (row_ids[:, None] < row_ids[None, :]).astype(jnp.bfloat16)
    rank_in = jnp.dot(chosen.astype(jnp.bfloat16), earlier, preferred_element_type=jnp.float32)
    placed = chosen[:, None, :] & (
        rank_in.astype(jnp.int32)[:, None, :] == jnp.arange(capacity, dtype=jnp.int32)[None, :, None]
    )
    pick = placed.astype(jnp.bfloat16)
    slot_prob = jnp.sum(jnp.where(placed, weight_of[:, None, :], 0.0), axis=2, keepdims=True)

    def part(array, step):
        return array[step * 4:(step + 1) * 4]

    normed_rows, scaled_rows, cot_rows, slot_grads = [], [], [], []
    for step in range(steps):
        mine, other = token_blocks[step]
        one, two = select(
            select_norm_kernel, part(pick, step), mine, other, gain[None, :],
            pl.BlockSpec((1, features), lambda i: (0, 0)),
        )
        normed_rows.append(one)
        scaled_rows.append(two)
    for step in range(steps):
        mine, other = cot_blocks[step]
        one, two = select(
            select_grad_kernel, part(pick, step), mine, other, part(slot_prob, step),
            pl.BlockSpec((1, capacity, 1), lambda i: (i, 0, 0)),
        )
        cot_rows.append(one)
        slot_grads.append(two)
    rows = jnp.concatenate(normed_rows).reshape(-1, features)
    gate_pre, up_pre, sigmoid_gate, hidden, block_out = expert_forward(rows, gate_up, down_proj)
    out_slots = block_out.reshape(expert_size, capacity, features)
    out_parts = [
        expand(part(pick, step), part(out_slots, step), part(slot_prob, step)) for step in range(steps)
    ]
    out_sum = scatter_sum(out_parts, expert_size)

    grads = jnp.concatenate(slot_grads).reshape(-1, features)
    input_grad, gate_up_part, down_part = expert_backward(
        rows, grads, gate_up, down_proj, gate_pre, up_pre, sigmoid_gate, hidden
    )
    input_slots = input_grad.reshape(expert_size, capacity, features)
    ones = jnp.ones_like(slot_prob)
    input_parts = [
        expand(part(pick, step), part(input_slots, step), part(ones, step)) for step in range(steps)
    ]

    scaled = jnp.concatenate(scaled_rows)
    gain_term = jnp.sum(input_slots.astype(jnp.float32) * scaled.astype(jnp.float32), axis=(0, 1))
    cots = jnp.concatenate(cot_rows)
    prob_value = jnp.sum(cots.astype(jnp.float32) * out_slots.astype(jnp.float32), axis=2)
    prob_rows = jnp.sum(jnp.where(placed, prob_value[:, :, None], 0.0), axis=1)
    prob_rows = jnp.where(core == 0, prob_rows, jnp.roll(prob_rows, half, axis=1))
    prob_rows = jnp.take(prob_rows, place, axis=0).reshape(-1)
    terms = jnp.concatenate([prob_rows, gain_term]).reshape(-1, 128)
    terms = lax.all_gather(terms, BOTH, axis=0)
    terms = terms.reshape(terms.shape[0], -1)

    normed_grad = scatter_sum(input_parts, expert_size)

    gain_grad = jnp.sum(terms[:, expert_size * group_rows:], axis=0)
    own_values = lax.dynamic_slice_in_dim(terms, expert * group_rows + core * half, half, axis=1)
    own_ids = lax.dynamic_slice_in_dim(expert_ids, core * half, half, axis=0)
    named = own_ids.T[None, :, :] == jnp.arange(terms.shape[0], dtype=jnp.int32)[:, None, None]
    prob_grad = jnp.sum(jnp.where(named, own_values[:, None, :], 0.0), axis=0).T

    scaled_own, inv_own = normalize(tokens)
    mixed = (tokens.astype(jnp.float32) + out_sum).astype(jnp.bfloat16)
    gain_side = normed_grad * gain[None, :]
    token_grad = (
        cotangent.astype(jnp.float32)
        + inv_own
        * (gain_side - scaled_own * jnp.mean(gain_side * scaled_own, axis=1, keepdims=True))
    ).astype(jnp.bfloat16)
    return (mixed, token_grad, prob_grad, gain_grad, gate_up_part[None], down_part[None])


def solution(mesh):
    in_specs = (
        P(("expert", "tensor"), None),
        P(("expert", "tensor"), None),
        P(),
        P("expert", None),
        P("expert", None),
        P(("expert", "tensor"), None, None),
        P(("expert", "tensor"), None, None),
    )
    out_specs = (
        P(("expert", "tensor"), None),
        P(("expert", "tensor"), None),
        P(("expert", "tensor"), None),
        P(),
        P(("expert", "tensor"), None, None),
        P(("expert", "tensor"), None, None),
    )
    expert_size, tensor_size = mesh.shape["expert"], mesh.shape["tensor"]
    few = tensor_size == EXP_DEV and expert_size % 4 == 0 and expert_size <= 4 * TOP
    shards = broadcast_shards if few else routed_shards
    return jax.shard_map(shards, mesh=mesh, in_specs=in_specs, out_specs=out_specs, check_vma=False)
```

```python
import functools

import jax
import jax.numpy as jnp
from jax import lax
from jax.experimental import pallas as pl
from jax.experimental.pallas import tpu as pltpu
from jax.sharding import PartitionSpec as P

TOP = 8
EXP_DEV = 2
VMEM_LIMIT = 48 * 1024 * 1024


def normalize(rows):
    values = rows.astype(jnp.float32)
    inv_rms = lax.rsqrt(jnp.mean(values * values, axis=1, keepdims=True) + 1e-06)
    return (values * inv_rms, inv_rms)


def expert_forward(rows, gate_up, down_proj):
    projected = jnp.dot(rows, gate_up, preferred_element_type=jnp.float32)
    half_width = down_proj.shape[0]
    gate_pre = projected[:, :half_width]
    up_pre = projected[:, half_width:]
    sigmoid_gate = jax.nn.sigmoid(gate_pre)
    hidden = (gate_pre * sigmoid_gate * up_pre).astype(jnp.bfloat16)
    block_out = jnp.dot(hidden, down_proj, preferred_element_type=jnp.float32).astype(jnp.bfloat16)
    return (gate_pre, up_pre, sigmoid_gate, hidden, block_out)


def times_transposed(left, right):
    return lax.dot_general(left, right, (((1,), (1,)), ((), ())), preferred_element_type=jnp.float32)


def outer_sum(left, right):
    product = lax.dot_general(left, right, (((0,), (0,)), ((), ())), preferred_element_type=jnp.float32)
    return product.astype(jnp.bfloat16)


def backward_inner(slot_grads, down_proj, gate_pre, up_pre, sigmoid_gate):
    hidden_grad = times_transposed(slot_grads, down_proj)
    gate_grad = (
        hidden_grad * up_pre * sigmoid_gate * (1.0 + gate_pre * (1.0 - sigmoid_gate))
    ).astype(jnp.bfloat16)
    up_grad = (hidden_grad * gate_pre * sigmoid_gate).astype(jnp.bfloat16)
    return jnp.concatenate([gate_grad, up_grad], axis=1)


def expert_backward(rows, slot_grads, gate_up, down_proj, gate_pre, up_pre, sigmoid_gate, hidden):
    joined_grad = backward_inner(slot_grads, down_proj, gate_pre, up_pre, sigmoid_gate)
    input_grad = times_transposed(joined_grad, gate_up).astype(jnp.bfloat16)
    return (input_grad, outer_sum(rows, joined_grad), outer_sum(hidden, slot_grads))


def routed_shards(tokens, cotangent, gain, expert_ids, gate_probs, gate_up_weight, down_weight):
    tensor_size = lax.axis_size("tensor")
    expert_size = lax.axis_size("expert")
    my_rank = lax.axis_index("tensor")
    blocks_each = tensor_size // EXP_DEV
    my_type = my_rank // blocks_each
    group_rows = expert_ids.shape[0]
    features = tokens.shape[1]
    capacity = 3 * group_rows * TOP // (2 * EXP_DEV * expert_size)
    highest = lax.Precision.HIGHEST
    scaled_own, inv_own = normalize(tokens)
    carried = (scaled_own * gain[None, :]).astype(jnp.bfloat16)
    group_first, group_grads = (
        lax.all_gather(carried, "tensor", axis=0, tiled=True),
        lax.all_gather(cotangent, "tensor", axis=0, tiled=True),
    )
    targets = jnp.arange(expert_size, dtype=jnp.int32) * EXP_DEV + my_type
    matches = expert_ids[:, :, None] == targets[None, None, :]
    chosen = jnp.any(matches, axis=1)
    weight_of = jnp.sum(jnp.where(matches, gate_probs[:, :, None], 0.0), axis=1)
    slot_of = jnp.sum(
        jnp.where(matches, jnp.arange(TOP, dtype=jnp.int32)[None, :, None], 0), axis=1
    )
    row_ids = jnp.arange(group_rows, dtype=jnp.int32)
    earlier = (row_ids[None, :] < row_ids[:, None]).astype(jnp.bfloat16)
    rank_in = jnp.dot(
        earlier, chosen.astype(jnp.bfloat16), preferred_element_type=jnp.float32
    ).astype(jnp.int32)
    placed = chosen.T[:, None, :] & (
        rank_in.T[:, None, :] == jnp.arange(capacity, dtype=jnp.int32)[None, :, None]
    )
    source = jnp.sum(jnp.where(placed, row_ids[None, None, :], 0), axis=2)
    filled = jnp.any(placed, axis=2)
    slot_prob = jnp.sum(jnp.where(placed, weight_of.T[:, None, :], 0.0), axis=2)
    slot_index = jnp.sum(jnp.where(placed, slot_of.T[:, None, :], 0), axis=2)
    sent_rows = jnp.where(
        filled[:, :, None], jnp.take(group_first, source, axis=0), jnp.zeros((), jnp.bfloat16)
    )
    sent_grads = (
        slot_prob[:, :, None] * jnp.take(group_grads, source, axis=0).astype(jnp.float32)
    ).astype(jnp.bfloat16)
    gate_up = gate_up_weight[0]
    down_proj = down_weight[0]
    arrived_rows, arrived_grads = (
        lax.all_to_all(sent_rows, "expert", split_axis=0, concat_axis=0, tiled=True),
        lax.all_to_all(sent_grads, "expert", split_axis=0, concat_axis=0, tiled=True),
    )
    rows = arrived_rows.reshape(-1, features)
    slot_grads = arrived_grads.reshape(-1, features)
    gate_pre, up_pre, sigmoid_gate, hidden, block_out = expert_forward(rows, gate_up, down_proj)
    out_slots = block_out.reshape(expert_size, capacity, features)
    input_grad, gate_up_part, down_part = expert_backward(
        rows, slot_grads, gate_up, down_proj, gate_pre, up_pre, sigmoid_gate, hidden
    )
    input_slots = input_grad.reshape(expert_size, capacity, features)
    out_back, input_back = (
        lax.all_to_all(out_slots, "expert", split_axis=0, concat_axis=0, tiled=True),
        lax.all_to_all(input_slots, "expert", split_axis=0, concat_axis=0, tiled=True),
    )
    out_flat = out_back.reshape(-1, features)
    input_flat = input_back.reshape(-1, features)
    used_source = source.reshape(-1)
    used_filled = filled.reshape(-1)
    used_prob = slot_prob.reshape(-1)
    used_index = slot_index.reshape(-1)
    cot_slots = jnp.take(group_grads, used_source, axis=0)
    prob_values = jnp.einsum("sd,sd->s", cot_slots, out_flat, preferred_element_type=jnp.float32)
    hit = (row_ids[:, None] == used_source[None, :]) & used_filled[None, :]
    input_part = jnp.dot(hit.astype(jnp.bfloat16), input_flat, preferred_element_type=jnp.float32)
    weighting = jnp.where(hit, used_prob[None, :], 0.0)
    out_part = jnp.dot(
        weighting,
        out_flat.astype(jnp.float32),
        precision=highest,
        preferred_element_type=jnp.float32,
    )
    prob_columns = jnp.where(
        used_index[:, None] == jnp.arange(TOP, dtype=jnp.int32)[None, :], prob_values[:, None], 0.0
    )
    prob_part = jnp.dot(
        hit.astype(jnp.float32), prob_columns, precision=highest, preferred_element_type=jnp.float32
    )
    out_sum, normed_grad, prob_grad = (
        lax.psum_scatter(out_part, "tensor", scatter_dimension=0, tiled=True),
        lax.psum_scatter(input_part, "tensor", scatter_dimension=0, tiled=True),
        lax.psum_scatter(prob_part, "tensor", scatter_dimension=0, tiled=True),
    )
    mixed = (tokens.astype(jnp.float32) + out_sum).astype(jnp.bfloat16)
    gain_side = normed_grad * gain[None, :]
    token_grad = (
        cotangent.astype(jnp.float32)
        + inv_own
        * (gain_side - scaled_own * jnp.mean(gain_side * scaled_own, axis=1, keepdims=True))
    ).astype(jnp.bfloat16)
    gain_grad = lax.psum(jnp.sum(normed_grad * scaled_own, axis=0), ("expert", "tensor"))
    return (mixed, token_grad, prob_grad, gain_grad, gate_up_part[None], down_part[None])


BOTH = ("expert", "tensor")


def flip_first(expert, core):
    return expert ^ (2 if core == 0 else 1)


def flip_second(expert, core):
    return expert ^ (1 if core == 0 else 2)


def send(array, place):
    pairs = []
    for expert in range(lax.axis_size("expert")):
        for core in range(2):
            to_expert, to_core = place(expert, core)
            pairs.append((expert * 2 + core, to_expert * 2 + to_core))
    return lax.ppermute(array, BOTH, pairs)


def send_first(array):
    return send(array, lambda e, c: (flip_first(e, c), c))


def send_second(array):
    return send(array, lambda e, c: (flip_second(e, c), c))


def send_bit(array, bit):
    return send(array, lambda e, c: (e ^ bit, c))


def send_core(array):
    return send(array, lambda e, c: (e, 1 - c))


def send_along(array, step):
    size = lax.axis_size("expert")
    return send(array, lambda e, c: ((e + 4 * step) % size, c))


def after(array, *others):
    return lax.optimization_barrier((array,) + others)[0]


def gather_plane(block):
    pair = jnp.concatenate([block, send_second(block)])
    quad = jnp.concatenate([pair, send_first(pair)])
    return quad, send_core(quad)


def add_half(left, right):
    return (left.astype(jnp.float32) + right.astype(jnp.float32)).astype(jnp.bfloat16)


def fold(array, sender):
    half = array.shape[0] // 2
    return add_half(array[:half], sender(array[half:]))


def gather_tables(table):
    steps = lax.axis_size("expert") // 4
    planes = jnp.stack([table] + [send_along(table, -step) for step in range(1, steps)])
    pair = jnp.stack([planes, send_second(planes)])
    return jnp.stack([pair, send_first(pair)])


def far_first(array):
    far = array[:, :, 1:].reshape((-1,) + array.shape[3:])
    return jnp.concatenate([far, array[:, :, 0].reshape((-1,) + array.shape[3:])])


def from_far_first(array, steps):
    far = array[:4 * (steps - 1)].reshape((2, 2, steps - 1) + array.shape[1:])
    return jnp.concatenate([array[4 * (steps - 1):].reshape((2, 2, 1) + array.shape[1:]), far], axis=2)


def swapped(index, count):
    bits = index // count
    return ((bits % 2) * 2 + bits // 2) * count + index % count


def chosen_rows(pick_ref, mine_ref, other_ref):
    half = mine_ref.shape[1]
    rows = jnp.dot(pick_ref[0][:, :half], mine_ref[0], preferred_element_type=jnp.float32)
    return rows + jnp.dot(pick_ref[0][:, half:], other_ref[0], preferred_element_type=jnp.float32)


def select_norm_kernel(pick_ref, mine_ref, other_ref, gain_ref, *refs):
    normed_ref = refs[-1]
    rows = chosen_rows(pick_ref, mine_ref, other_ref)
    inv_rms = lax.rsqrt(jnp.mean(rows * rows, axis=1, keepdims=True) + 1e-06)
    normed_ref[0] = (rows * inv_rms * gain_ref[...]).astype(jnp.bfloat16)


def select_grad_kernel(pick_ref, mine_ref, other_ref, prob_ref, *refs):
    cot_ref, grad_ref = refs[-2:]
    rows = chosen_rows(pick_ref, mine_ref, other_ref)
    cot_ref[0] = rows.astype(jnp.bfloat16)
    grad_ref[0] = (rows * prob_ref[0]).astype(jnp.bfloat16)


def select(kernel, outputs, pick, blocks, extra, count, arrays, which, first_group, held):
    groups, capacity, group_rows = pick.shape
    mine, other = blocks
    half, features = mine.shape[1:]
    out = jax.ShapeDtypeStruct((groups, capacity, features), jnp.bfloat16)

    def group_spec(*shape):
        return pl.BlockSpec((1,) + shape, lambda i: (first_group + i, 0, 0))

    if extra.ndim == 2:
        extra_spec = pl.BlockSpec(extra.shape, lambda i: (0, 0))
    else:
        extra_spec = group_spec(capacity, 1)
    return pl.pallas_call(
        kernel,
        grid=(4 * count,),
        in_specs=[
            group_spec(capacity, group_rows),
            pl.BlockSpec((1, half, features), lambda i: (i * arrays + which, 0, 0)),
            pl.BlockSpec((1, half, features), lambda i: (swapped(i, count) * arrays + which, 0, 0)),
            extra_spec,
        ] + [pl.BlockSpec(memory_space=pl.ANY)] * len(held),
        out_specs=[group_spec(capacity, features)] * outputs,
        out_shape=[out] * outputs,
        input_output_aliases={4 + n: n for n in range(len(held))},
        compiler_params=pltpu.CompilerParams(vmem_limit_bytes=VMEM_LIMIT),
        cost_estimate=pl.CostEstimate(
            flops=8 * count * capacity * group_rows * features,
            bytes_accessed=16 * count * half * features + 8 * outputs * count * capacity * features,
            transcendentals=0,
        ),
    )(pick, mine, other, extra, *held)


def expand_kernel(weighted, pick_ref, prob_ref, *refs):
    sources, (mine_ref, other_ref) = refs[:-2], refs[-2:]
    half = mine_ref.shape[1]
    pick = pick_ref[0]
    for place, (source_ref, by_prob) in enumerate(zip(sources, weighted)):
        rows = source_ref[0]
        if by_prob:
            rows = (rows.astype(jnp.float32) * prob_ref[0]).astype(jnp.bfloat16)
        for columns, out_ref in ((pick[:, :half], mine_ref), (pick[:, half:], other_ref)):
            out_ref[place] = lax.dot_general(
                columns, rows, (((0,), (0,)), ((), ())), preferred_element_type=jnp.float32
            ).astype(jnp.bfloat16)


def expand(pick, prob, slots, weighted, count, first_group):
    _, capacity, group_rows = pick.shape
    half, features, arrays = group_rows // 2, slots[0].shape[2], len(slots)
    out = jax.ShapeDtypeStruct((4 * count * arrays, half, features), jnp.bfloat16)

    def group_spec(*shape):
        return pl.BlockSpec((1,) + shape, lambda i: (first_group + i, 0, 0))

    return pl.pallas_call(
        functools.partial(expand_kernel, weighted),
        grid=(4 * count,),
        in_specs=[group_spec(capacity, group_rows), group_spec(capacity, 1)]
        + [group_spec(capacity, features)] * arrays,
        out_specs=[
            pl.BlockSpec((arrays, half, features), lambda i: (i, 0, 0)),
            pl.BlockSpec((arrays, half, features), lambda i: (swapped(i, count), 0, 0)),
        ],
        out_shape=[out, out],
        compiler_params=pltpu.CompilerParams(vmem_limit_bytes=VMEM_LIMIT),
        cost_estimate=pl.CostEstimate(
            flops=8 * arrays * count * capacity * group_rows * features,
            bytes_accessed=8 * arrays * count * features * (group_rows + capacity),
            transcendentals=0,
        ),
    )(pick, prob, *slots)


def home_terms(columns, gain_term):
    steps, top, rows = columns.shape[2:]
    half = rows // 2
    gain_rows = gain_term.reshape(-1, 128)
    count = gain_rows.shape[0]

    def exchange(part, gains, sender):
        got = sender(jnp.concatenate([part.reshape(-1, 128), gains]))
        return got[:-count].reshape(part.shape), got[-count:]

    got, gains = exchange(columns[..., half:], gain_rows, send_core)
    columns, gain_rows = columns[..., :half] + got, gain_rows + gains
    for bit in (2, 1):
        got, gains = exchange(columns[1], gain_rows, functools.partial(send_bit, bit=bit))
        columns, gain_rows = columns[0] + got, gain_rows + gains
    total, all_gains = columns[0], [gain_rows]
    for step in range(1, steps):
        got, gains = exchange(columns[step], gain_rows, functools.partial(send_along, step=step))
        total = total + got
        all_gains.append(gains)
    order = (lax.axis_index("expert") // 4 - jnp.arange(steps)) % steps
    gains = jnp.take(jnp.stack(all_gains), order, axis=0)
    gain_sum = gains[0]
    for step in range(1, steps):
        gain_sum = gain_sum + gains[step]
    return total, gain_sum.reshape(-1)


def broadcast_shards(tokens, cotangent, gain, expert_ids, gate_probs, gate_up_weight, down_weight):
    expert_size = lax.axis_size("expert")
    steps = expert_size // 4
    far = 4 * (steps - 1)
    expert, core = lax.axis_index("expert"), lax.axis_index("tensor")
    my_expert = expert * EXP_DEV + core
    group_rows = expert_ids.shape[0]
    half = group_rows // 2
    features = tokens.shape[1]
    capacity = 3 * group_rows * TOP // (2 * EXP_DEV * expert_size)
    gate_up, down_proj = gate_up_weight[0], down_weight[0]

    tables = gather_tables(jnp.concatenate([expert_ids.T.astype(jnp.float32), gate_probs.T]))
    near_blocks = gather_plane(jnp.stack([tokens, cotangent]))
    token_far = jnp.stack([send_along(tokens, -step) for step in range(1, steps)])
    far_tokens = gather_plane(token_far)
    late_cot = after(cotangent, token_far)
    far_cots = gather_plane(
        after(jnp.stack([send_along(late_cot, -step) for step in range(1, steps)]), far_tokens[0])
    )

    tables = far_first(tables)
    tables = jnp.where(core == 0, tables, jnp.roll(tables, half, axis=2))
    matches = tables[:, :TOP] == my_expert.astype(jnp.float32)
    chosen = jnp.any(matches, axis=1)
    weight_of = jnp.sum(jnp.where(matches, tables[:, TOP:], 0.0), axis=1)
    row_ids = jnp.arange(group_rows, dtype=jnp.int32)
    earlier = (row_ids[:, None] < row_ids[None, :]).astype(jnp.bfloat16)
    rank_in = jnp.dot(chosen.astype(jnp.bfloat16), earlier, preferred_element_type=jnp.float32)
    placed = chosen[:, None, :] & (
        rank_in.astype(jnp.int32)[:, None, :] == jnp.arange(capacity, dtype=jnp.int32)[None, :, None]
    )
    pick = placed.astype(jnp.bfloat16)
    slot_prob = jnp.sum(jnp.where(placed, weight_of[:, None, :], 0.0), axis=2, keepdims=True)

    held = select(select_norm_kernel, 1, pick, near_blocks, gain[None, :], 1, 2, 0, far, ())
    rows, = select(
        select_norm_kernel, 1, pick, far_tokens, gain[None, :], steps - 1, 1, 0, 0, tuple(held)
    )
    held = select(select_grad_kernel, 2, pick, near_blocks, slot_prob, 1, 2, 1, far, ())
    rows = rows.reshape(-1, features)
    gate_pre, up_pre, sigmoid_gate, hidden, block_out = expert_forward(rows, gate_up, down_proj)
    out_slots = block_out.reshape(expert_size, capacity, features)
    out_mine, out_other = expand(pick, slot_prob, (out_slots,), (True,), steps - 1, 0)

    cots, grads = select(
        select_grad_kernel, 2, pick, far_cots, slot_prob, steps - 1, 1, 0, 0, tuple(held)
    )
    grads = after(grads.reshape(-1, features), out_other)
    joined_grad = backward_inner(grads, down_proj, gate_pre, up_pre, sigmoid_gate)
    out_quad = add_half(out_mine, send_core(out_other))
    input_grad = times_transposed(after(joined_grad, out_quad), gate_up).astype(jnp.bfloat16)
    input_slots = input_grad.reshape(expert_size, capacity, features)
    in_mine, in_other = expand(pick, slot_prob, (input_slots,), (False,), steps - 1, 0)
    out_pair = fold(out_quad, send_first)
    near_mine, near_other = expand(
        pick, slot_prob, (out_slots, after(input_slots, in_other, out_pair)), (True, False), 1, far
    )
    in_quad = add_half(in_mine, send_core(in_other))
    down_part = outer_sum(after(hidden, near_other, in_quad), grads)
    near_quad = add_half(near_mine, send_core(near_other))
    out_far = fold(out_pair, send_second)
    gate_up_part = outer_sum(after(rows, in_quad, near_quad, out_far), joined_grad)

    out_far = [send_along(out_far[step - 1], step) for step in range(1, steps)]
    in_far = fold(fold(in_quad, send_first), send_second)
    in_far = [send_along(in_far[step - 1], step) for step in range(1, steps)]
    near_sum = fold(fold(near_quad, send_first), send_second).astype(jnp.float32)
    out_sum = near_sum[0] + sum(block.astype(jnp.float32) for block in out_far)
    normed_grad = near_sum[1] + sum(block.astype(jnp.float32) for block in in_far)

    gain_term = jnp.sum(input_grad.astype(jnp.float32) * rows.astype(jnp.float32), axis=0) / gain
    prob_value = jnp.sum(cots.astype(jnp.float32) * out_slots.astype(jnp.float32), axis=2)
    prob_rows = jnp.sum(jnp.where(placed, prob_value[:, :, None], 0.0), axis=1)
    columns = from_far_first(jnp.where(matches, prob_rows[:, None, :], 0.0), steps)
    columns = jnp.where(core == 0, columns, jnp.swapaxes(columns, 0, 1))
    prob_sum, gain_grad = home_terms(after(columns, near_quad), after(gain_term, near_quad))

    scaled_own, inv_own = normalize(tokens)
    mixed = (tokens.astype(jnp.float32) + out_sum).astype(jnp.bfloat16)
    gain_side = normed_grad * gain[None, :]
    token_grad = (
        cotangent.astype(jnp.float32)
        + inv_own
        * (gain_side - scaled_own * jnp.mean(gain_side * scaled_own, axis=1, keepdims=True))
    ).astype(jnp.bfloat16)
    return (mixed, token_grad, prob_sum.T, gain_grad, gate_up_part[None], down_part[None])


def solution(mesh):
    in_specs = (
        P(("expert", "tensor"), None),
        P(("expert", "tensor"), None),
        P(),
        P("expert", None),
        P("expert", None),
        P(("expert", "tensor"), None, None),
        P(("expert", "tensor"), None, None),
    )
    out_specs = (
        P(("expert", "tensor"), None),
        P(("expert", "tensor"), None),
        P(("expert", "tensor"), None),
        P(),
        P(("expert", "tensor"), None, None),
        P(("expert", "tensor"), None, None),
    )
    expert_size, tensor_size = mesh.shape["expert"], mesh.shape["tensor"]
    few = tensor_size == EXP_DEV and expert_size % 4 == 0 and expert_size <= 4 * TOP
    shards = broadcast_shards if few else routed_shards
    return jax.shard_map(shards, mesh=mesh, in_specs=in_specs, out_specs=out_specs, check_vma=False)
```

```python
import functools

import jax
import jax.numpy as jnp
from jax import lax
from jax.experimental import pallas as pl
from jax.experimental.pallas import tpu as pltpu
from jax.sharding import PartitionSpec as P

TOP = 8
EXP_DEV = 2
VMEM_LIMIT = 48 * 1024 * 1024


def normalize(rows):
    values = rows.astype(jnp.float32)
    inv_rms = lax.rsqrt(jnp.mean(values * values, axis=1, keepdims=True) + 1e-06)
    return (values * inv_rms, inv_rms)


def expert_forward(rows, gate_up, down_proj):
    projected = jnp.dot(rows, gate_up, preferred_element_type=jnp.float32)
    half_width = down_proj.shape[0]
    gate_pre = projected[:, :half_width]
    up_pre = projected[:, half_width:]
    sigmoid_gate = jax.nn.sigmoid(gate_pre)
    hidden = (gate_pre * sigmoid_gate * up_pre).astype(jnp.bfloat16)
    block_out = jnp.dot(hidden, down_proj, preferred_element_type=jnp.float32).astype(jnp.bfloat16)
    return (gate_pre, up_pre, sigmoid_gate, hidden, block_out)


def times_transposed(left, right):
    return lax.dot_general(left, right, (((1,), (1,)), ((), ())), preferred_element_type=jnp.float32)


def outer_sum(left, right):
    product = lax.dot_general(left, right, (((0,), (0,)), ((), ())), preferred_element_type=jnp.float32)
    return product.astype(jnp.bfloat16)


def backward_inner(slot_grads, down_proj, gate_pre, up_pre, sigmoid_gate):
    hidden_grad = times_transposed(slot_grads, down_proj)
    gate_grad = (
        hidden_grad * up_pre * sigmoid_gate * (1.0 + gate_pre * (1.0 - sigmoid_gate))
    ).astype(jnp.bfloat16)
    up_grad = (hidden_grad * gate_pre * sigmoid_gate).astype(jnp.bfloat16)
    return jnp.concatenate([gate_grad, up_grad], axis=1)


def expert_backward(rows, slot_grads, gate_up, down_proj, gate_pre, up_pre, sigmoid_gate, hidden):
    joined_grad = backward_inner(slot_grads, down_proj, gate_pre, up_pre, sigmoid_gate)
    input_grad = times_transposed(joined_grad, gate_up).astype(jnp.bfloat16)
    return (input_grad, outer_sum(rows, joined_grad), outer_sum(hidden, slot_grads))


def routed_shards(tokens, cotangent, gain, expert_ids, gate_probs, gate_up_weight, down_weight):
    tensor_size = lax.axis_size("tensor")
    expert_size = lax.axis_size("expert")
    my_rank = lax.axis_index("tensor")
    blocks_each = tensor_size // EXP_DEV
    my_type = my_rank // blocks_each
    group_rows = expert_ids.shape[0]
    features = tokens.shape[1]
    capacity = 3 * group_rows * TOP // (2 * EXP_DEV * expert_size)
    highest = lax.Precision.HIGHEST
    scaled_own, inv_own = normalize(tokens)
    carried = (scaled_own * gain[None, :]).astype(jnp.bfloat16)
    group_first, group_grads = (
        lax.all_gather(carried, "tensor", axis=0, tiled=True),
        lax.all_gather(cotangent, "tensor", axis=0, tiled=True),
    )
    targets = jnp.arange(expert_size, dtype=jnp.int32) * EXP_DEV + my_type
    matches = expert_ids[:, :, None] == targets[None, None, :]
    chosen = jnp.any(matches, axis=1)
    weight_of = jnp.sum(jnp.where(matches, gate_probs[:, :, None], 0.0), axis=1)
    slot_of = jnp.sum(
        jnp.where(matches, jnp.arange(TOP, dtype=jnp.int32)[None, :, None], 0), axis=1
    )
    row_ids = jnp.arange(group_rows, dtype=jnp.int32)
    earlier = (row_ids[None, :] < row_ids[:, None]).astype(jnp.bfloat16)
    rank_in = jnp.dot(
        earlier, chosen.astype(jnp.bfloat16), preferred_element_type=jnp.float32
    ).astype(jnp.int32)
    placed = chosen.T[:, None, :] & (
        rank_in.T[:, None, :] == jnp.arange(capacity, dtype=jnp.int32)[None, :, None]
    )
    source = jnp.sum(jnp.where(placed, row_ids[None, None, :], 0), axis=2)
    filled = jnp.any(placed, axis=2)
    slot_prob = jnp.sum(jnp.where(placed, weight_of.T[:, None, :], 0.0), axis=2)
    slot_index = jnp.sum(jnp.where(placed, slot_of.T[:, None, :], 0), axis=2)
    sent_rows = jnp.where(
        filled[:, :, None], jnp.take(group_first, source, axis=0), jnp.zeros((), jnp.bfloat16)
    )
    sent_grads = (
        slot_prob[:, :, None] * jnp.take(group_grads, source, axis=0).astype(jnp.float32)
    ).astype(jnp.bfloat16)
    gate_up = gate_up_weight[0]
    down_proj = down_weight[0]
    arrived_rows, arrived_grads = (
        lax.all_to_all(sent_rows, "expert", split_axis=0, concat_axis=0, tiled=True),
        lax.all_to_all(sent_grads, "expert", split_axis=0, concat_axis=0, tiled=True),
    )
    rows = arrived_rows.reshape(-1, features)
    slot_grads = arrived_grads.reshape(-1, features)
    gate_pre, up_pre, sigmoid_gate, hidden, block_out = expert_forward(rows, gate_up, down_proj)
    out_slots = block_out.reshape(expert_size, capacity, features)
    input_grad, gate_up_part, down_part = expert_backward(
        rows, slot_grads, gate_up, down_proj, gate_pre, up_pre, sigmoid_gate, hidden
    )
    input_slots = input_grad.reshape(expert_size, capacity, features)
    out_back, input_back = (
        lax.all_to_all(out_slots, "expert", split_axis=0, concat_axis=0, tiled=True),
        lax.all_to_all(input_slots, "expert", split_axis=0, concat_axis=0, tiled=True),
    )
    out_flat = out_back.reshape(-1, features)
    input_flat = input_back.reshape(-1, features)
    used_source = source.reshape(-1)
    used_filled = filled.reshape(-1)
    used_prob = slot_prob.reshape(-1)
    used_index = slot_index.reshape(-1)
    cot_slots = jnp.take(group_grads, used_source, axis=0)
    prob_values = jnp.einsum("sd,sd->s", cot_slots, out_flat, preferred_element_type=jnp.float32)
    hit = (row_ids[:, None] == used_source[None, :]) & used_filled[None, :]
    input_part = jnp.dot(hit.astype(jnp.bfloat16), input_flat, preferred_element_type=jnp.float32)
    weighting = jnp.where(hit, used_prob[None, :], 0.0)
    out_part = jnp.dot(
        weighting,
        out_flat.astype(jnp.float32),
        precision=highest,
        preferred_element_type=jnp.float32,
    )
    prob_columns = jnp.where(
        used_index[:, None] == jnp.arange(TOP, dtype=jnp.int32)[None, :], prob_values[:, None], 0.0
    )
    prob_part = jnp.dot(
        hit.astype(jnp.float32), prob_columns, precision=highest, preferred_element_type=jnp.float32
    )
    out_sum, normed_grad, prob_grad = (
        lax.psum_scatter(out_part, "tensor", scatter_dimension=0, tiled=True),
        lax.psum_scatter(input_part, "tensor", scatter_dimension=0, tiled=True),
        lax.psum_scatter(prob_part, "tensor", scatter_dimension=0, tiled=True),
    )
    mixed = (tokens.astype(jnp.float32) + out_sum).astype(jnp.bfloat16)
    gain_side = normed_grad * gain[None, :]
    token_grad = (
        cotangent.astype(jnp.float32)
        + inv_own
        * (gain_side - scaled_own * jnp.mean(gain_side * scaled_own, axis=1, keepdims=True))
    ).astype(jnp.bfloat16)
    gain_grad = lax.psum(jnp.sum(normed_grad * scaled_own, axis=0), ("expert", "tensor"))
    return (mixed, token_grad, prob_grad, gain_grad, gate_up_part[None], down_part[None])


BOTH = ("expert", "tensor")


def flip_first(expert, core):
    return expert ^ (2 if core == 0 else 1)


def flip_second(expert, core):
    return expert ^ (1 if core == 0 else 2)


def send(array, place):
    pairs = []
    for expert in range(lax.axis_size("expert")):
        for core in range(2):
            to_expert, to_core = place(expert, core)
            pairs.append((expert * 2 + core, to_expert * 2 + to_core))
    return lax.ppermute(array, BOTH, pairs)


def send_first(array):
    return send(array, lambda e, c: (flip_first(e, c), c))


def send_second(array):
    return send(array, lambda e, c: (flip_second(e, c), c))


def send_bit(array, bit):
    return send(array, lambda e, c: (e ^ bit, c))


def send_core(array):
    return send(array, lambda e, c: (e, 1 - c))


def send_along(array, step):
    size = lax.axis_size("expert")
    return send(array, lambda e, c: ((e + 4 * step) % size, c))


def after(array, *others):
    return lax.optimization_barrier((array,) + others)[0]


def together(*arrays):
    return lax.optimization_barrier(arrays)


def add_up(*terms):
    return sum(term.astype(jnp.float32) for term in terms)


def narrow(value):
    return value.astype(jnp.bfloat16)


def gather_tables(table):
    steps = lax.axis_size("expert") // 4
    planes = jnp.stack([table] + [send_along(table, -step) for step in range(1, steps)])
    pair = jnp.stack([planes, send_second(planes)])
    last = send_first(pair)
    return jnp.stack([pair, last]), last


def far_first(array):
    far = array[:, :, 1:].reshape((-1,) + array.shape[3:])
    return jnp.concatenate([far, array[:, :, 0].reshape((-1,) + array.shape[3:])])


def from_far_first(array, steps):
    far = array[:4 * (steps - 1)].reshape((2, 2, steps - 1) + array.shape[1:])
    return jnp.concatenate([array[4 * (steps - 1):].reshape((2, 2, 1) + array.shape[1:]), far], axis=2)


def swapped(index):
    return (index % 2) * 2 + index // 2


def chosen_rows(pick, mine, other):
    half = mine.shape[0]
    rows = jnp.dot(pick[:, :half], mine, preferred_element_type=jnp.float32)
    return rows + jnp.dot(pick[:, half:], other, preferred_element_type=jnp.float32)


def select_kernel(kinds, count, *refs):
    pick_ref, prob_ref, gain_ref, pieces = refs[0], refs[1], refs[2], refs[3:7]
    outputs = refs[len(refs) - sum(1 if kind == "norm" else 2 for kind in kinds):]

    def work(mine_ref, other_ref):
        for group in range(count):
            places = iter(outputs)
            for number, kind in enumerate(kinds):
                block = group * len(kinds) + number
                rows = chosen_rows(pick_ref[group], mine_ref[block], other_ref[block])
                if kind == "norm":
                    inv_rms = lax.rsqrt(jnp.mean(rows * rows, axis=1, keepdims=True) + 1e-06)
                    next(places)[group] = (rows * inv_rms * gain_ref[...]).astype(jnp.bfloat16)
                else:
                    next(places)[group] = rows.astype(jnp.bfloat16)
                    next(places)[group] = (rows * prob_ref[group]).astype(jnp.bfloat16)

    for first in range(2):
        for second in range(2):
            pl.when(pl.program_id(0) == first * 2 + second)(
                functools.partial(work, pieces[first], pieces[2 + second])
            )


def select(kinds, pick, prob, gain, pieces, count, first_group, held):
    groups, capacity, group_rows = pick.shape
    blocks = count * len(kinds)
    half, features = pieces[0].shape[1:]
    outputs = sum(1 if kind == "norm" else 2 for kind in kinds)
    out = jax.ShapeDtypeStruct((groups, capacity, features), jnp.bfloat16)
    first_block = first_group // count

    def group_spec(*shape):
        return pl.BlockSpec((count,) + shape, lambda i: (first_block + i, 0, 0))

    def piece_spec(place):
        return pl.BlockSpec((blocks, half, features), lambda i: (place(i), 0, 0))

    return pl.pallas_call(
        functools.partial(select_kernel, kinds, count),
        grid=(4,),
        in_specs=[
            group_spec(capacity, group_rows),
            group_spec(capacity, 1),
            pl.BlockSpec((1, features), lambda i: (0, 0)),
            piece_spec(lambda i: jnp.minimum(i, 1)),
            piece_spec(lambda i: jnp.maximum(i - 2, 0)),
            piece_spec(lambda i: i // 2),
            piece_spec(lambda i: jnp.maximum(i - 2, 0)),
        ] + [pl.BlockSpec(memory_space=pl.ANY)] * len(held),
        out_specs=[group_spec(capacity, features)] * outputs,
        out_shape=[out] * outputs,
        input_output_aliases={7 + n: n for n in range(len(held))},
        compiler_params=pltpu.CompilerParams(vmem_limit_bytes=VMEM_LIMIT),
        cost_estimate=pl.CostEstimate(
            flops=8 * blocks * capacity * group_rows * features,
            bytes_accessed=16 * blocks * half * features + 8 * outputs * count * capacity * features,
            transcendentals=0,
        ),
    )(pick, prob, gain, *pieces, *held)


def expand_kernel(weighted, count, pick_ref, prob_ref, *refs):
    sources, (mine_ref, other_ref) = refs[:-2], refs[-2:]
    half = mine_ref.shape[1]
    for group in range(count):
        pick = pick_ref[group]
        for number, (source_ref, by_prob) in enumerate(zip(sources, weighted)):
            rows = source_ref[group]
            if by_prob:
                rows = (rows.astype(jnp.float32) * prob_ref[group]).astype(jnp.bfloat16)
            for columns, out_ref in ((pick[:, :half], mine_ref), (pick[:, half:], other_ref)):
                out_ref[group * len(sources) + number] = lax.dot_general(
                    columns, rows, (((0,), (0,)), ((), ())), preferred_element_type=jnp.float32
                ).astype(jnp.bfloat16)


def expand(pick, prob, slots, weighted, count, first_group):
    _, capacity, group_rows = pick.shape
    half, features, arrays = group_rows // 2, slots[0].shape[2], len(slots)
    out = jax.ShapeDtypeStruct((4 * count * arrays, half, features), jnp.bfloat16)
    first_block = first_group // count

    def group_spec(*shape):
        return pl.BlockSpec((count,) + shape, lambda i: (first_block + i, 0, 0))

    return pl.pallas_call(
        functools.partial(expand_kernel, weighted, count),
        grid=(4,),
        in_specs=[group_spec(capacity, group_rows), group_spec(capacity, 1)]
        + [group_spec(capacity, features)] * arrays,
        out_specs=[
            pl.BlockSpec((count * arrays, half, features), lambda i: (i, 0, 0)),
            pl.BlockSpec((count * arrays, half, features), lambda i: (swapped(i), 0, 0)),
        ],
        out_shape=[out, out],
        compiler_params=pltpu.CompilerParams(vmem_limit_bytes=VMEM_LIMIT),
        cost_estimate=pl.CostEstimate(
            flops=8 * arrays * count * capacity * group_rows * features,
            bytes_accessed=8 * arrays * count * features * (group_rows + capacity),
            transcendentals=0,
        ),
    )(pick, prob, *slots)


def home_terms(columns, gain_term):
    steps, top, rows = columns.shape[2:]
    half = rows // 2
    gain_rows = gain_term.reshape(-1, 128)
    count = gain_rows.shape[0]

    def exchange(part, gains, sender):
        got = sender(jnp.concatenate([part.reshape(-1, 128), gains]))
        return got[:-count].reshape(part.shape), got[-count:]

    got, gains = exchange(columns[..., half:], gain_rows, send_core)
    columns, gain_rows = columns[..., :half] + got, gain_rows + gains
    for bit in (2, 1):
        got, gains = exchange(columns[1], gain_rows, functools.partial(send_bit, bit=bit))
        columns, gain_rows = columns[0] + got, gain_rows + gains
    total, all_gains = columns[0], [gain_rows]
    for step in range(1, steps):
        got, gains = exchange(columns[step], gain_rows, functools.partial(send_along, step=step))
        total = total + got
        all_gains.append(gains)
    order = (lax.axis_index("expert") // 4 - jnp.arange(steps)) % steps
    gains = jnp.take(jnp.stack(all_gains), order, axis=0)
    gain_sum = gains[0]
    for step in range(1, steps):
        gain_sum = gain_sum + gains[step]
    return total, gain_sum.reshape(-1)


def broadcast_shards(tokens, cotangent, gain, expert_ids, gate_probs, gate_up_weight, down_weight):
    expert_size = lax.axis_size("expert")
    steps = expert_size // 4
    far = 4 * (steps - 1)
    expert, core = lax.axis_index("expert"), lax.axis_index("tensor")
    my_expert = expert * EXP_DEV + core
    group_rows = expert_ids.shape[0]
    half = group_rows // 2
    features = tokens.shape[1]
    capacity = 3 * group_rows * TOP // (2 * EXP_DEV * expert_size)
    gate_up, down_proj = gate_up_weight[0], down_weight[0]

    near_own = jnp.stack([tokens, cotangent])
    near_pair = jnp.concatenate([near_own, send_second(near_own)])
    near_far_pair = send_first(near_pair)
    tables, tables_last = gather_tables(
        jnp.concatenate([expert_ids.T.astype(jnp.float32), gate_probs.T])
    )
    token_far = jnp.stack([send_along(tokens, -step) for step in range(1, steps)])
    token_far = after(token_far, tables_last)
    late_cot = after(cotangent, token_far)
    cot_steps = [send_along(late_cot, -step) for step in range(1, steps)]
    token_second = after(send_second(token_far), near_far_pair, cot_steps[0])
    token_pair = jnp.concatenate([token_far, token_second])
    token_far_pair = after(send_first(token_pair), *cot_steps)
    near_pieces = (near_pair, near_far_pair, send_core(near_pair), send_core(near_far_pair))
    cot_far = after(jnp.stack(cot_steps), token_far_pair)
    cot_second = send_second(cot_far)
    token_pieces = (
        token_pair, token_far_pair, send_core(token_pair), after(send_core(token_far_pair), cot_second)
    )
    cot_pair = jnp.concatenate([cot_far, cot_second])
    cot_far_pair = send_first(cot_pair)
    cot_pieces = (cot_pair, cot_far_pair, send_core(cot_pair), send_core(cot_far_pair))

    tables = far_first(tables)
    tables = jnp.where(core == 0, tables, jnp.roll(tables, half, axis=2))
    matches = tables[:, :TOP] == my_expert.astype(jnp.float32)
    chosen = jnp.any(matches, axis=1)
    weight_of = jnp.sum(jnp.where(matches, tables[:, TOP:], 0.0), axis=1)
    row_ids = jnp.arange(group_rows, dtype=jnp.int32)
    earlier = (row_ids[:, None] < row_ids[None, :]).astype(jnp.bfloat16)
    rank_in = jnp.dot(chosen.astype(jnp.bfloat16), earlier, preferred_element_type=jnp.float32)
    placed = chosen[:, None, :] & (
        rank_in.astype(jnp.int32)[:, None, :] == jnp.arange(capacity, dtype=jnp.int32)[None, :, None]
    )
    pick = placed.astype(jnp.bfloat16)
    slot_prob = jnp.sum(jnp.where(placed, weight_of[:, None, :], 0.0), axis=2, keepdims=True)

    gain_row = gain[None, :]
    rows, cots, grads = select(("norm", "grad"), pick, slot_prob, gain_row, near_pieces, 1, far, ())
    rows, = select(("norm",), pick, slot_prob, gain_row, token_pieces, steps - 1, 0, (rows,))
    rows = rows.reshape(-1, features)
    gate_pre, up_pre, sigmoid_gate, hidden, block_out = expert_forward(rows, gate_up, down_proj)
    out_slots = block_out.reshape(expert_size, capacity, features)
    out_mine, out_other = expand(pick, slot_prob, (out_slots,), (True,), steps - 1, 0)

    half_far, one_far = 2 * (steps - 1), steps - 1
    out_core = send_core(out_other)
    out_upper = narrow(add_up(out_mine[half_far:], out_core[half_far:]))
    out_first = send_first(out_upper)
    cots, grads = select(
        ("grad",), after(pick, out_upper), slot_prob, gain_row, cot_pieces, steps - 1, 0, (cots, grads)
    )
    grads = grads.reshape(-1, features)
    joined_grad = backward_inner(grads, down_proj, gate_pre, up_pre, sigmoid_gate)
    input_grad = times_transposed(joined_grad, gate_up).astype(jnp.bfloat16)
    input_slots = input_grad.reshape(expert_size, capacity, features)
    in_mine, in_other = expand(pick, slot_prob, (input_slots,), (False,), steps - 1, 0)
    in_core = send_core(in_other)
    out_middle = narrow(
        add_up(out_mine[one_far:half_far], out_core[one_far:half_far], after(out_first, in_other)[one_far:])
    )
    out_second = send_second(out_middle)
    near_mine, near_other = expand(
        pick, slot_prob, (out_slots, after(input_slots, in_other)), (True, False), 1, far
    )
    near_core = send_core(near_other)
    in_upper = narrow(add_up(in_mine[half_far:], after(in_core, out_middle, near_other)[half_far:]))
    in_first = send_first(in_upper)
    down_part = outer_sum(after(hidden, in_upper), grads)
    gain_term = jnp.sum(input_grad.astype(jnp.float32) * rows.astype(jnp.float32), axis=0) / gain
    prob_value = jnp.sum(cots.astype(jnp.float32) * out_slots.astype(jnp.float32), axis=2)
    prob_rows = jnp.sum(jnp.where(placed, prob_value[:, :, None], 0.0), axis=1)
    columns = from_far_first(jnp.where(matches, prob_rows[:, None, :], 0.0), steps)
    columns = jnp.where(core == 0, columns, jnp.swapaxes(columns, 0, 1))
    prob_sum, gain_grad = home_terms(after(columns, in_upper), after(gain_term, in_upper))

    def own_plane(mine, core_part, first_part, second_part, count):
        return add_up(mine[:count], core_part[:count], first_part[:count], second_part[:count])

    out_second, down_part = together(out_second, down_part)
    out_planes = narrow(own_plane(out_mine, out_core, out_first, out_second, one_far))
    out_far = [send_along(out_planes[step - 1], step) for step in range(1, steps)]
    in_first, near_core, prob_sum, gain_grad = together(
        in_first, near_core, prob_sum, gain_grad, *out_far[:2]
    )[:4]
    in_middle = narrow(
        add_up(in_mine[one_far:half_far], in_core[one_far:half_far], in_first[one_far:])
    )
    in_second = send_second(in_middle)
    in_planes = narrow(own_plane(in_mine, in_core, in_first, after(in_second, *out_far), one_far))
    in_far = [send_along(in_planes[step - 1], step) for step in range(1, steps)]
    gate_up_part = outer_sum(after(rows, in_far[0]), joined_grad)
    near_upper = narrow(add_up(near_mine[4:], after(near_core, in_planes)[4:]))
    near_first = send_first(near_upper)
    near_middle = narrow(add_up(near_mine[2:4], near_core[2:4], near_first[2:]))
    near_second = send_second(near_middle)
    near_sum = own_plane(near_mine, near_core, near_first, near_second, 2)
    out_sum = near_sum[0] + add_up(*out_far)
    normed_grad = near_sum[1] + add_up(*in_far)

    scaled_own, inv_own = normalize(tokens)
    mixed = (tokens.astype(jnp.float32) + out_sum).astype(jnp.bfloat16)
    gain_side = normed_grad * gain[None, :]
    token_grad = (
        cotangent.astype(jnp.float32)
        + inv_own
        * (gain_side - scaled_own * jnp.mean(gain_side * scaled_own, axis=1, keepdims=True))
    ).astype(jnp.bfloat16)
    return (mixed, token_grad, prob_sum.T, gain_grad, gate_up_part[None], down_part[None])


def solution(mesh):
    in_specs = (
        P(("expert", "tensor"), None),
        P(("expert", "tensor"), None),
        P(),
        P("expert", None),
        P("expert", None),
        P(("expert", "tensor"), None, None),
        P(("expert", "tensor"), None, None),
    )
    out_specs = (
        P(("expert", "tensor"), None),
        P(("expert", "tensor"), None),
        P(("expert", "tensor"), None),
        P(),
        P(("expert", "tensor"), None, None),
        P(("expert", "tensor"), None, None),
    )
    expert_size, tensor_size = mesh.shape["expert"], mesh.shape["tensor"]
    few = tensor_size == EXP_DEV and expert_size % 4 == 0 and expert_size <= 4 * TOP
    shards = broadcast_shards if few else routed_shards
    return jax.shard_map(shards, mesh=mesh, in_specs=in_specs, out_specs=out_specs, check_vma=False)
```

```python
import functools

import jax
import jax.numpy as jnp
from jax import lax
from jax.experimental import pallas as pl
from jax.experimental.pallas import tpu as pltpu
from jax.sharding import PartitionSpec as P

TOP = 8
EXP_DEV = 2
SMALL_VMEM = 24 * 1024 * 1024
LARGE_VMEM = 48 * 1024 * 1024
LITTLE = pl.CostEstimate(flops=1000000, bytes_accessed=100000, transcendentals=0)


def normalize(rows):
    values = rows.astype(jnp.float32)
    inv_rms = lax.rsqrt(jnp.mean(values * values, axis=1, keepdims=True) + 1e-06)
    return (values * inv_rms, inv_rms)


def expert_forward(rows, gate_up, down_proj):
    projected = jnp.dot(rows, gate_up, preferred_element_type=jnp.float32)
    half_width = down_proj.shape[0]
    gate_pre = projected[:, :half_width]
    up_pre = projected[:, half_width:]
    sigmoid_gate = jax.nn.sigmoid(gate_pre)
    hidden = (gate_pre * sigmoid_gate * up_pre).astype(jnp.bfloat16)
    block_out = jnp.dot(hidden, down_proj, preferred_element_type=jnp.float32).astype(jnp.bfloat16)
    return (gate_pre, up_pre, sigmoid_gate, hidden, block_out)


def times_transposed(left, right):
    return lax.dot_general(left, right, (((1,), (1,)), ((), ())), preferred_element_type=jnp.float32)


def outer_sum(left, right):
    product = lax.dot_general(left, right, (((0,), (0,)), ((), ())), preferred_element_type=jnp.float32)
    return product.astype(jnp.bfloat16)


def backward_inner(slot_grads, down_proj, gate_pre, up_pre, sigmoid_gate):
    hidden_grad = times_transposed(slot_grads, down_proj)
    gate_grad = (
        hidden_grad * up_pre * sigmoid_gate * (1.0 + gate_pre * (1.0 - sigmoid_gate))
    ).astype(jnp.bfloat16)
    up_grad = (hidden_grad * gate_pre * sigmoid_gate).astype(jnp.bfloat16)
    return jnp.concatenate([gate_grad, up_grad], axis=1)


def expert_backward(rows, slot_grads, gate_up, down_proj, gate_pre, up_pre, sigmoid_gate, hidden):
    joined_grad = backward_inner(slot_grads, down_proj, gate_pre, up_pre, sigmoid_gate)
    input_grad = times_transposed(joined_grad, gate_up).astype(jnp.bfloat16)
    return (input_grad, outer_sum(rows, joined_grad), outer_sum(hidden, slot_grads))


def routed_shards(tokens, cotangent, gain, expert_ids, gate_probs, gate_up_weight, down_weight):
    tensor_size = lax.axis_size("tensor")
    expert_size = lax.axis_size("expert")
    my_rank = lax.axis_index("tensor")
    blocks_each = tensor_size // EXP_DEV
    my_type = my_rank // blocks_each
    group_rows = expert_ids.shape[0]
    features = tokens.shape[1]
    capacity = 3 * group_rows * TOP // (2 * EXP_DEV * expert_size)
    highest = lax.Precision.HIGHEST
    scaled_own, inv_own = normalize(tokens)
    carried = (scaled_own * gain[None, :]).astype(jnp.bfloat16)
    group_first, group_grads = (
        lax.all_gather(carried, "tensor", axis=0, tiled=True),
        lax.all_gather(cotangent, "tensor", axis=0, tiled=True),
    )
    targets = jnp.arange(expert_size, dtype=jnp.int32) * EXP_DEV + my_type
    matches = expert_ids[:, :, None] == targets[None, None, :]
    chosen = jnp.any(matches, axis=1)
    weight_of = jnp.sum(jnp.where(matches, gate_probs[:, :, None], 0.0), axis=1)
    slot_of = jnp.sum(
        jnp.where(matches, jnp.arange(TOP, dtype=jnp.int32)[None, :, None], 0), axis=1
    )
    row_ids = jnp.arange(group_rows, dtype=jnp.int32)
    earlier = (row_ids[None, :] < row_ids[:, None]).astype(jnp.bfloat16)
    rank_in = jnp.dot(
        earlier, chosen.astype(jnp.bfloat16), preferred_element_type=jnp.float32
    ).astype(jnp.int32)
    placed = chosen.T[:, None, :] & (
        rank_in.T[:, None, :] == jnp.arange(capacity, dtype=jnp.int32)[None, :, None]
    )
    source = jnp.sum(jnp.where(placed, row_ids[None, None, :], 0), axis=2)
    filled = jnp.any(placed, axis=2)
    slot_prob = jnp.sum(jnp.where(placed, weight_of.T[:, None, :], 0.0), axis=2)
    slot_index = jnp.sum(jnp.where(placed, slot_of.T[:, None, :], 0), axis=2)
    sent_rows = jnp.where(
        filled[:, :, None], jnp.take(group_first, source, axis=0), jnp.zeros((), jnp.bfloat16)
    )
    sent_grads = (
        slot_prob[:, :, None] * jnp.take(group_grads, source, axis=0).astype(jnp.float32)
    ).astype(jnp.bfloat16)
    gate_up = gate_up_weight[0]
    down_proj = down_weight[0]
    arrived_rows, arrived_grads = (
        lax.all_to_all(sent_rows, "expert", split_axis=0, concat_axis=0, tiled=True),
        lax.all_to_all(sent_grads, "expert", split_axis=0, concat_axis=0, tiled=True),
    )
    rows = arrived_rows.reshape(-1, features)
    slot_grads = arrived_grads.reshape(-1, features)
    gate_pre, up_pre, sigmoid_gate, hidden, block_out = expert_forward(rows, gate_up, down_proj)
    out_slots = block_out.reshape(expert_size, capacity, features)
    input_grad, gate_up_part, down_part = expert_backward(
        rows, slot_grads, gate_up, down_proj, gate_pre, up_pre, sigmoid_gate, hidden
    )
    input_slots = input_grad.reshape(expert_size, capacity, features)
    out_back, input_back = (
        lax.all_to_all(out_slots, "expert", split_axis=0, concat_axis=0, tiled=True),
        lax.all_to_all(input_slots, "expert", split_axis=0, concat_axis=0, tiled=True),
    )
    out_flat = out_back.reshape(-1, features)
    input_flat = input_back.reshape(-1, features)
    used_source = source.reshape(-1)
    used_filled = filled.reshape(-1)
    used_prob = slot_prob.reshape(-1)
    used_index = slot_index.reshape(-1)
    cot_slots = jnp.take(group_grads, used_source, axis=0)
    prob_values = jnp.einsum("sd,sd->s", cot_slots, out_flat, preferred_element_type=jnp.float32)
    hit = (row_ids[:, None] == used_source[None, :]) & used_filled[None, :]
    input_part = jnp.dot(hit.astype(jnp.bfloat16), input_flat, preferred_element_type=jnp.float32)
    weighting = jnp.where(hit, used_prob[None, :], 0.0)
    out_part = jnp.dot(
        weighting,
        out_flat.astype(jnp.float32),
        precision=highest,
        preferred_element_type=jnp.float32,
    )
    prob_columns = jnp.where(
        used_index[:, None] == jnp.arange(TOP, dtype=jnp.int32)[None, :], prob_values[:, None], 0.0
    )
    prob_part = jnp.dot(
        hit.astype(jnp.float32), prob_columns, precision=highest, preferred_element_type=jnp.float32
    )
    out_sum, normed_grad, prob_grad = (
        lax.psum_scatter(out_part, "tensor", scatter_dimension=0, tiled=True),
        lax.psum_scatter(input_part, "tensor", scatter_dimension=0, tiled=True),
        lax.psum_scatter(prob_part, "tensor", scatter_dimension=0, tiled=True),
    )
    mixed = (tokens.astype(jnp.float32) + out_sum).astype(jnp.bfloat16)
    gain_side = normed_grad * gain[None, :]
    token_grad = (
        cotangent.astype(jnp.float32)
        + inv_own
        * (gain_side - scaled_own * jnp.mean(gain_side * scaled_own, axis=1, keepdims=True))
    ).astype(jnp.bfloat16)
    gain_grad = lax.psum(jnp.sum(normed_grad * scaled_own, axis=0), ("expert", "tensor"))
    return (mixed, token_grad, prob_grad, gain_grad, gate_up_part[None], down_part[None])


BOTH = ("expert", "tensor")


def flip_first(expert, core):
    return expert ^ (2 if core == 0 else 1)


def flip_second(expert, core):
    return expert ^ (1 if core == 0 else 2)


def send(array, place):
    pairs = []
    for expert in range(lax.axis_size("expert")):
        for core in range(2):
            to_expert, to_core = place(expert, core)
            pairs.append((expert * 2 + core, to_expert * 2 + to_core))
    return lax.ppermute(array, BOTH, pairs)


def send_first(array):
    return send(array, lambda e, c: (flip_first(e, c), c))


def send_second(array):
    return send(array, lambda e, c: (flip_second(e, c), c))


def send_bit(array, bit):
    return send(array, lambda e, c: (e ^ bit, c))


def send_core(array):
    return send(array, lambda e, c: (e, 1 - c))


def send_along(array, step):
    size = lax.axis_size("expert")
    return send(array, lambda e, c: ((e + 4 * step) % size, c))


def after(array, *others):
    return lax.optimization_barrier((array,) + others)[0]


def together(*arrays):
    return lax.optimization_barrier(arrays)


def add_up(*terms):
    return sum(term.astype(jnp.float32) for term in terms)


def narrow(value):
    return value.astype(jnp.bfloat16)


def gather_tables(table):
    steps = lax.axis_size("expert") // 4
    planes = jnp.stack([table] + [send_along(table, -step) for step in range(1, steps)])
    pair = jnp.stack([planes, send_second(planes)])
    return jnp.stack([pair, send_first(pair)])


def far_first(array):
    far = array[:, :, 1:].reshape((-1,) + array.shape[3:])
    return jnp.concatenate([far, array[:, :, 0].reshape((-1,) + array.shape[3:])])


def from_far_first(array, steps):
    far = array[:4 * (steps - 1)].reshape((2, 2, steps - 1) + array.shape[1:])
    return jnp.concatenate([array[4 * (steps - 1):].reshape((2, 2, 1) + array.shape[1:]), far], axis=2)


def swapped(index):
    return (index % 2) * 2 + index // 2


def chosen_rows(pick, mine, other):
    return jnp.dot(pick, jnp.concatenate([mine, other]), preferred_element_type=jnp.float32)


def norm_kernel(count, pick_ref, *refs):
    pieces, gain_ref, normed_ref = refs[:4], refs[4], refs[-1]

    def work(mine_ref, other_ref):
        for group in range(count):
            rows = chosen_rows(pick_ref[group], mine_ref[group], other_ref[group])
            inv_rms = lax.rsqrt(jnp.mean(rows * rows, axis=1, keepdims=True) + 1e-06)
            normed_ref[group] = (rows * inv_rms * gain_ref[...]).astype(jnp.bfloat16)

    by_place(work, pieces)


def grad_kernel(count, pick_ref, *refs):
    pieces, prob_ref, out_ref, (grad_ref, value_ref) = refs[:4], refs[4], refs[5], refs[-2:]

    def work(mine_ref, other_ref):
        for group in range(count):
            rows = chosen_rows(pick_ref[group], mine_ref[group], other_ref[group])
            grad_ref[group] = (rows * prob_ref[group]).astype(jnp.bfloat16)
            value_ref[group] = jnp.sum(rows * out_ref[group].astype(jnp.float32), axis=1, keepdims=True)

    by_place(work, pieces)


def by_place(work, pieces):
    for first in range(2):
        for second in range(2):
            pl.when(pl.program_id(0) == first * 2 + second)(
                functools.partial(work, pieces[first], pieces[2 + second])
            )


def group_spec(count, first_group, *shape):
    first_block = first_group // count
    return pl.BlockSpec((count,) + shape, lambda i: (first_block + i, 0, 0))


def select(kernel, pick, pieces, extras, extra_specs, out_shapes, count, arrays, which, first_group, held):
    _, capacity, group_rows = pick.shape
    half, features = pieces[0].shape[1:]

    def piece_spec(place):
        return pl.BlockSpec((count, half, features), lambda i: (place(i) * arrays + which, 0, 0))

    return pl.pallas_call(
        functools.partial(kernel, count),
        grid=(4,),
        in_specs=[
            group_spec(count, first_group, capacity, group_rows),
            piece_spec(lambda i: jnp.minimum(i, 1)),
            piece_spec(lambda i: jnp.maximum(i - 2, 0)),
            piece_spec(lambda i: i // 2),
            piece_spec(lambda i: jnp.maximum(i - 2, 0)),
        ] + extra_specs + [pl.BlockSpec(memory_space=pl.ANY)] * len(held),
        out_specs=[group_spec(count, first_group, *out.shape[1:]) for out in out_shapes],
        out_shape=out_shapes,
        input_output_aliases={5 + len(extras) + n: n for n in range(len(held))},
        compiler_params=pltpu.CompilerParams(vmem_limit_bytes=SMALL_VMEM),
        cost_estimate=LITTLE,
    )(pick, *pieces, *extras, *held)


def select_normed(pick, gain, pieces, count, arrays, first_group, held):
    groups, capacity, _ = pick.shape
    features = pieces[0].shape[2]
    return select(
        norm_kernel, pick, pieces, [gain], [pl.BlockSpec((1, features), lambda i: (0, 0))],
        [jax.ShapeDtypeStruct((groups, capacity, features), jnp.bfloat16)],
        count, arrays, 0, first_group, held,
    )


def select_grads(pick, prob, out_slots, pieces, count, arrays, which, first_group, held):
    groups, capacity, _ = pick.shape
    features = pieces[0].shape[2]
    return select(
        grad_kernel, pick, pieces, [prob, out_slots],
        [group_spec(count, first_group, capacity, 1), group_spec(count, first_group, capacity, features)],
        [
            jax.ShapeDtypeStruct((groups, capacity, features), jnp.bfloat16),
            jax.ShapeDtypeStruct((groups, capacity, 1), jnp.float32),
        ],
        count, arrays, which, first_group, held,
    )


def expand_kernel(weighted, count, back_ref, prob_ref, *refs):
    sources, (mine_ref, other_ref) = refs[:-2], refs[-2:]
    half = mine_ref.shape[1]
    for group in range(count):
        for number, (source_ref, by_prob) in enumerate(zip(sources, weighted)):
            rows = source_ref[group]
            if by_prob:
                rows = (rows.astype(jnp.float32) * prob_ref[group]).astype(jnp.bfloat16)
            spread = jnp.dot(back_ref[group], rows, preferred_element_type=jnp.float32)
            place = group * len(sources) + number
            mine_ref[place] = spread[:half].astype(jnp.bfloat16)
            other_ref[place] = spread[half:].astype(jnp.bfloat16)


def expand(back, prob, slots, weighted, count, first_group):
    _, group_rows, capacity = back.shape
    half, features, arrays = group_rows // 2, slots[0].shape[2], len(slots)
    out = jax.ShapeDtypeStruct((4 * count * arrays, half, features), jnp.bfloat16)
    return pl.pallas_call(
        functools.partial(expand_kernel, weighted, count),
        grid=(4,),
        in_specs=[
            group_spec(count, first_group, group_rows, capacity),
            group_spec(count, first_group, capacity, 1),
        ] + [group_spec(count, first_group, capacity, features)] * arrays,
        out_specs=[
            pl.BlockSpec((count * arrays, half, features), lambda i: (i, 0, 0)),
            pl.BlockSpec((count * arrays, half, features), lambda i: (swapped(i), 0, 0)),
        ],
        out_shape=[out, out],
        compiler_params=pltpu.CompilerParams(vmem_limit_bytes=SMALL_VMEM),
        cost_estimate=LITTLE,
    )(back, prob, *slots)


def forward_kernel(rows_ref, gate_up_ref, down_ref, projected_ref, hidden_ref, out_ref):
    projected = jnp.dot(rows_ref[...], gate_up_ref[0], preferred_element_type=jnp.float32)
    projected_ref[...] = projected
    half_width = hidden_ref.shape[1]
    gate_pre, up_pre = projected[:, :half_width], projected[:, half_width:]
    hidden = (gate_pre * jax.nn.sigmoid(gate_pre) * up_pre).astype(jnp.bfloat16)
    hidden_ref[...] = hidden
    out_ref[...] = jnp.dot(hidden, down_ref[0], preferred_element_type=jnp.float32).astype(jnp.bfloat16)


def backward_kernel(
    grads_ref, projected_ref, rows_ref, gate_up_ref, down_ref, joined_ref, input_ref, gain_ref
):
    half_width = projected_ref.shape[1] // 2
    hidden_grad = times_transposed(grads_ref[...], down_ref[0])
    gate_pre, up_pre = projected_ref[:, :half_width], projected_ref[:, half_width:]
    sigmoid_gate = jax.nn.sigmoid(gate_pre)
    common = hidden_grad * sigmoid_gate
    joined_ref[:, :half_width] = (
        common * up_pre * (1.0 + gate_pre * (1.0 - sigmoid_gate))
    ).astype(jnp.bfloat16)
    joined_ref[:, half_width:] = (common * gate_pre).astype(jnp.bfloat16)
    input_grad = times_transposed(joined_ref[...], gate_up_ref[0]).astype(jnp.bfloat16)
    input_ref[...] = input_grad

    @pl.when(pl.program_id(0) == 0)
    def _():
        gain_ref[...] = jnp.zeros_like(gain_ref)

    terms = input_grad.astype(jnp.float32) * rows_ref[...].astype(jnp.float32)
    gain_ref[...] += jnp.sum(terms, axis=0, keepdims=True)


def by_rows(kernel, inputs, weights, outputs, sums):
    block = inputs[0].shape[0] // 2

    def row_spec(array):
        return pl.BlockSpec((block,) + array.shape[1:], lambda i: (i, 0))

    def whole_spec(array):
        return pl.BlockSpec(array.shape, lambda i: (0,) * array.ndim)

    return pl.pallas_call(
        kernel,
        grid=(2,),
        in_specs=[row_spec(array) for array in inputs] + [whole_spec(array) for array in weights],
        out_specs=[row_spec(array) for array in outputs] + [whole_spec(array) for array in sums],
        out_shape=outputs + sums,
        compiler_params=pltpu.CompilerParams(vmem_limit_bytes=LARGE_VMEM),
        cost_estimate=LITTLE,
    )(*inputs, *weights)


def pack(columns, gains):
    return jnp.concatenate([columns.reshape(-1, 128), gains])


def unpack_add(columns, gains, got):
    count = gains.shape[0]
    return columns + got[:-count].reshape(columns.shape), gains + got[-count:]


def planes_in_order(gains):
    steps = len(gains)
    order = (lax.axis_index("expert") // 4 - jnp.arange(steps)) % steps
    ordered = jnp.take(jnp.stack(gains), order, axis=0)
    return functools.reduce(jnp.add, [ordered[step] for step in range(steps)]).reshape(-1)


def broadcast_shards(tokens, cotangent, gain, expert_ids, gate_probs, gate_up_weight, down_weight):
    expert_size = lax.axis_size("expert")
    steps = expert_size // 4
    far = 4 * (steps - 1)
    expert, core = lax.axis_index("expert"), lax.axis_index("tensor")
    my_expert = expert * EXP_DEV + core
    group_rows = expert_ids.shape[0]
    half = group_rows // 2
    features = tokens.shape[1]
    capacity = 3 * group_rows * TOP // (2 * EXP_DEV * expert_size)
    near_own = jnp.stack([tokens, cotangent])
    near_pair = jnp.concatenate([near_own, send_second(near_own)])
    near_far_pair = send_first(near_pair)
    token_far = jnp.stack([send_along(tokens, -step) for step in range(1, steps)])
    tables = gather_tables(
        after(jnp.concatenate([expert_ids.T.astype(jnp.float32), gate_probs.T]), token_far)
    )
    late_cot = after(cotangent, token_far)
    cot_steps = [send_along(late_cot, -step) for step in range(1, steps)]
    token_second = after(send_second(token_far), near_far_pair, cot_steps[0])
    token_pair = jnp.concatenate([token_far, token_second])
    token_far_pair = after(send_first(token_pair), *cot_steps)
    near_pieces = (near_pair, near_far_pair, send_core(near_pair), send_core(near_far_pair))
    cot_far = after(jnp.stack(cot_steps), token_far_pair)
    cot_second = send_second(cot_far)
    token_pieces = (
        token_pair, token_far_pair, send_core(token_pair), after(send_core(token_far_pair), cot_second)
    )
    cot_pair = jnp.concatenate([cot_far, cot_second])
    cot_far_pair = send_first(cot_pair)

    tables = far_first(tables)
    tables = jnp.where(core == 0, tables, jnp.roll(tables, half, axis=2))
    matches = tables[:, :TOP] == my_expert.astype(jnp.float32)
    chosen = jnp.any(matches, axis=1)
    weight_of = jnp.sum(jnp.where(matches, tables[:, TOP:], 0.0), axis=1)
    row_ids = jnp.arange(group_rows, dtype=jnp.int32)
    earlier = (row_ids[:, None] < row_ids[None, :]).astype(jnp.bfloat16)
    rank_in = jnp.dot(chosen.astype(jnp.bfloat16), earlier, preferred_element_type=jnp.float32)
    placed = chosen[:, None, :] & (
        rank_in.astype(jnp.int32)[:, None, :] == jnp.arange(capacity, dtype=jnp.int32)[None, :, None]
    )
    pick = placed.astype(jnp.bfloat16)
    back = jnp.swapaxes(pick, 1, 2)
    slot_prob = jnp.sum(jnp.where(placed, weight_of[:, None, :], 0.0), axis=2, keepdims=True)

    gain_row = gain[None, :]
    rows = select_normed(pick, gain_row, near_pieces, 1, 2, far, ())
    rows, = select_normed(pick, gain_row, token_pieces, steps - 1, 1, 0, tuple(rows))
    rows = rows.reshape(-1, features)
    slots, width = rows.shape[0], down_weight.shape[1]
    projected, hidden, block_out = by_rows(
        forward_kernel, [rows], [gate_up_weight, down_weight],
        [
            jax.ShapeDtypeStruct((slots, 2 * width), jnp.float32),
            jax.ShapeDtypeStruct((slots, width), jnp.bfloat16),
            jax.ShapeDtypeStruct((slots, features), jnp.bfloat16),
        ], [],
    )
    block_out, cot_far_pair = together(block_out, cot_far_pair)
    cot_pieces = (cot_pair, cot_far_pair, send_core(cot_pair), send_core(cot_far_pair))
    out_slots = block_out.reshape(expert_size, capacity, features)
    out_mine, out_other = expand(back, slot_prob, (out_slots,), (True,), steps - 1, 0)

    half_far, one_far = 2 * (steps - 1), steps - 1
    out_core = send_core(out_other)
    out_upper = narrow(add_up(out_mine[half_far:], out_core[half_far:]))
    out_first = send_first(out_upper)
    held = select_grads(
        after(pick, out_other), slot_prob, out_slots, near_pieces, 1, 2, 1, far, ()
    )
    grads, prob_value = select_grads(
        after(pick, out_upper), slot_prob, out_slots, cot_pieces, steps - 1, 1, 0, 0, tuple(held)
    )
    grads = grads.reshape(-1, features)
    joined_grad, input_grad, gain_term = by_rows(
        backward_kernel, [grads, projected, rows], [gate_up_weight, down_weight],
        [
            jax.ShapeDtypeStruct((slots, 2 * width), jnp.bfloat16),
            jax.ShapeDtypeStruct((slots, features), jnp.bfloat16),
        ],
        [jax.ShapeDtypeStruct((1, features), jnp.float32)],
    )
    input_grad, out_first = together(input_grad, out_first)
    input_slots = input_grad.reshape(expert_size, capacity, features)
    in_mine, in_other = expand(back, slot_prob, (input_slots,), (False,), steps - 1, 0)
    in_core = send_core(in_other)
    out_middle = narrow(
        add_up(out_mine[one_far:half_far], out_core[one_far:half_far], after(out_first, in_other)[one_far:])
    )
    out_second = send_second(out_middle)
    near_mine, near_other = expand(
        back, after(slot_prob, in_other), (out_slots, input_slots), (True, False), 1, far
    )
    near_core = send_core(near_other)
    in_upper = narrow(add_up(in_mine[half_far:], after(in_core, out_middle, near_other)[half_far:]))
    in_first = send_first(in_upper)
    gains = (gain_term[0] / gain).reshape(-1, 128)
    prob_rows = jnp.sum(jnp.where(placed, prob_value, 0.0), axis=1)
    columns = from_far_first(jnp.where(matches, prob_rows[:, None, :], 0.0), steps)
    columns = jnp.where(core == 0, columns, jnp.swapaxes(columns, 0, 1))
    got = send_core(after(pack(columns[..., half:], gains), in_upper))
    down_part = outer_sum(after(hidden, in_upper), grads)

    def own_plane(mine, core_part, first_part, second_part, count):
        return add_up(mine[:count], core_part[:count], first_part[:count], second_part[:count])

    out_second, down_part, got = together(out_second, down_part, got)
    columns, gains = unpack_add(columns[..., :half], gains, got)
    got = send_bit(pack(columns[1], gains), 2)
    out_planes = narrow(own_plane(out_mine, out_core, out_first, out_second, one_far))
    out_far = [send_along(out_planes[step - 1], step) for step in range(1, steps)]
    gate_up_part = outer_sum(after(rows, out_planes), joined_grad)
    in_first, near_core, gate_up_part, got = together(
        in_first, near_core, gate_up_part, got, *out_far[:2]
    )[:4]
    columns, gains = unpack_add(columns[0], gains, got)
    in_middle = narrow(
        add_up(in_mine[one_far:half_far], in_core[one_far:half_far], in_first[one_far:])
    )
    in_second = send_second(in_middle)
    got = send_bit(pack(columns[1], gains), 1)
    in_second, got = together(in_second, got, *out_far)[:2]
    columns, gains = unpack_add(columns[0], gains, got)
    in_planes = narrow(own_plane(in_mine, in_core, in_first, in_second, one_far))
    messages = [send_along(pack(columns[step], gains), step) for step in range(1, steps)]
    in_far = [send_along(in_planes[step - 1], step) for step in range(1, steps)]
    near_upper = narrow(add_up(near_mine[4:], after(near_core, in_planes)[4:]))
    near_first = send_first(near_upper)
    near_middle = narrow(add_up(near_mine[2:4], near_core[2:4], near_first[2:]))
    near_second = send_second(near_middle)
    near_sum = own_plane(near_mine, near_core, near_first, near_second, 2)
    out_sum = near_sum[0] + add_up(*out_far)
    normed_grad = near_sum[1] + add_up(*in_far)

    prob_sum, all_gains = columns[0], [gains]
    for message in messages:
        prob_sum = prob_sum + message[:-gains.shape[0]].reshape(prob_sum.shape)
        all_gains.append(message[-gains.shape[0]:])
    gain_grad = planes_in_order(all_gains)

    scaled_own, inv_own = normalize(tokens)
    mixed = (tokens.astype(jnp.float32) + out_sum).astype(jnp.bfloat16)
    gain_side = normed_grad * gain[None, :]
    token_grad = (
        cotangent.astype(jnp.float32)
        + inv_own
        * (gain_side - scaled_own * jnp.mean(gain_side * scaled_own, axis=1, keepdims=True))
    ).astype(jnp.bfloat16)
    return (mixed, token_grad, prob_sum.T, gain_grad, gate_up_part[None], down_part[None])


def solution(mesh):
    in_specs = (
        P(("expert", "tensor"), None),
        P(("expert", "tensor"), None),
        P(),
        P("expert", None),
        P("expert", None),
        P(("expert", "tensor"), None, None),
        P(("expert", "tensor"), None, None),
    )
    out_specs = (
        P(("expert", "tensor"), None),
        P(("expert", "tensor"), None),
        P(("expert", "tensor"), None),
        P(),
        P(("expert", "tensor"), None, None),
        P(("expert", "tensor"), None, None),
    )
    expert_size, tensor_size = mesh.shape["expert"], mesh.shape["tensor"]
    few = tensor_size == EXP_DEV and expert_size % 4 == 0 and expert_size <= 4 * TOP
    shards = broadcast_shards if few else routed_shards
    return jax.shard_map(shards, mesh=mesh, in_specs=in_specs, out_specs=out_specs, check_vma=False)
```

```python
import functools

import jax
import jax.numpy as jnp
from jax import lax
from jax.experimental import pallas as pl
from jax.experimental.pallas import tpu as pltpu
from jax.sharding import PartitionSpec as P

TOP = 8
EXP_DEV = 2
SMALL_VMEM = 24 * 1024 * 1024
LARGE_VMEM = 48 * 1024 * 1024
LITTLE = pl.CostEstimate(flops=1000000, bytes_accessed=100000, transcendentals=0)


def normalize(rows):
    values = rows.astype(jnp.float32)
    inv_rms = lax.rsqrt(jnp.mean(values * values, axis=1, keepdims=True) + 1e-06)
    return (values * inv_rms, inv_rms)


def expert_forward(rows, gate_up, down_proj):
    projected = jnp.dot(rows, gate_up, preferred_element_type=jnp.float32)
    half_width = down_proj.shape[0]
    gate_pre = projected[:, :half_width]
    up_pre = projected[:, half_width:]
    sigmoid_gate = jax.nn.sigmoid(gate_pre)
    hidden = (gate_pre * sigmoid_gate * up_pre).astype(jnp.bfloat16)
    block_out = jnp.dot(hidden, down_proj, preferred_element_type=jnp.float32).astype(jnp.bfloat16)
    return (gate_pre, up_pre, sigmoid_gate, hidden, block_out)


def times_transposed(left, right):
    return lax.dot_general(left, right, (((1,), (1,)), ((), ())), preferred_element_type=jnp.float32)


def outer_sum(left, right):
    product = lax.dot_general(left, right, (((0,), (0,)), ((), ())), preferred_element_type=jnp.float32)
    return product.astype(jnp.bfloat16)


def backward_inner(slot_grads, down_proj, gate_pre, up_pre, sigmoid_gate):
    hidden_grad = times_transposed(slot_grads, down_proj)
    gate_grad = (
        hidden_grad * up_pre * sigmoid_gate * (1.0 + gate_pre * (1.0 - sigmoid_gate))
    ).astype(jnp.bfloat16)
    up_grad = (hidden_grad * gate_pre * sigmoid_gate).astype(jnp.bfloat16)
    return jnp.concatenate([gate_grad, up_grad], axis=1)


def expert_backward(rows, slot_grads, gate_up, down_proj, gate_pre, up_pre, sigmoid_gate, hidden):
    joined_grad = backward_inner(slot_grads, down_proj, gate_pre, up_pre, sigmoid_gate)
    input_grad = times_transposed(joined_grad, gate_up).astype(jnp.bfloat16)
    return (input_grad, outer_sum(rows, joined_grad), outer_sum(hidden, slot_grads))


def routed_shards(tokens, cotangent, gain, expert_ids, gate_probs, gate_up_weight, down_weight):
    tensor_size = lax.axis_size("tensor")
    expert_size = lax.axis_size("expert")
    my_rank = lax.axis_index("tensor")
    blocks_each = tensor_size // EXP_DEV
    my_type = my_rank // blocks_each
    group_rows = expert_ids.shape[0]
    features = tokens.shape[1]
    capacity = 3 * group_rows * TOP // (2 * EXP_DEV * expert_size)
    highest = lax.Precision.HIGHEST
    scaled_own, inv_own = normalize(tokens)
    carried = (scaled_own * gain[None, :]).astype(jnp.bfloat16)
    group_first, group_grads = (
        lax.all_gather(carried, "tensor", axis=0, tiled=True),
        lax.all_gather(cotangent, "tensor", axis=0, tiled=True),
    )
    targets = jnp.arange(expert_size, dtype=jnp.int32) * EXP_DEV + my_type
    matches = expert_ids[:, :, None] == targets[None, None, :]
    chosen = jnp.any(matches, axis=1)
    weight_of = jnp.sum(jnp.where(matches, gate_probs[:, :, None], 0.0), axis=1)
    slot_of = jnp.sum(
        jnp.where(matches, jnp.arange(TOP, dtype=jnp.int32)[None, :, None], 0), axis=1
    )
    row_ids = jnp.arange(group_rows, dtype=jnp.int32)
    earlier = (row_ids[None, :] < row_ids[:, None]).astype(jnp.bfloat16)
    rank_in = jnp.dot(
        earlier, chosen.astype(jnp.bfloat16), preferred_element_type=jnp.float32
    ).astype(jnp.int32)
    placed = chosen.T[:, None, :] & (
        rank_in.T[:, None, :] == jnp.arange(capacity, dtype=jnp.int32)[None, :, None]
    )
    source = jnp.sum(jnp.where(placed, row_ids[None, None, :], 0), axis=2)
    filled = jnp.any(placed, axis=2)
    slot_prob = jnp.sum(jnp.where(placed, weight_of.T[:, None, :], 0.0), axis=2)
    slot_index = jnp.sum(jnp.where(placed, slot_of.T[:, None, :], 0), axis=2)
    sent_rows = jnp.where(
        filled[:, :, None], jnp.take(group_first, source, axis=0), jnp.zeros((), jnp.bfloat16)
    )
    sent_grads = (
        slot_prob[:, :, None] * jnp.take(group_grads, source, axis=0).astype(jnp.float32)
    ).astype(jnp.bfloat16)
    gate_up = gate_up_weight[0]
    down_proj = down_weight[0]
    arrived_rows, arrived_grads = (
        lax.all_to_all(sent_rows, "expert", split_axis=0, concat_axis=0, tiled=True),
        lax.all_to_all(sent_grads, "expert", split_axis=0, concat_axis=0, tiled=True),
    )
    rows = arrived_rows.reshape(-1, features)
    slot_grads = arrived_grads.reshape(-1, features)
    gate_pre, up_pre, sigmoid_gate, hidden, block_out = expert_forward(rows, gate_up, down_proj)
    out_slots = block_out.reshape(expert_size, capacity, features)
    input_grad, gate_up_part, down_part = expert_backward(
        rows, slot_grads, gate_up, down_proj, gate_pre, up_pre, sigmoid_gate, hidden
    )
    input_slots = input_grad.reshape(expert_size, capacity, features)
    out_back, input_back = (
        lax.all_to_all(out_slots, "expert", split_axis=0, concat_axis=0, tiled=True),
        lax.all_to_all(input_slots, "expert", split_axis=0, concat_axis=0, tiled=True),
    )
    out_flat = out_back.reshape(-1, features)
    input_flat = input_back.reshape(-1, features)
    used_source = source.reshape(-1)
    used_filled = filled.reshape(-1)
    used_prob = slot_prob.reshape(-1)
    used_index = slot_index.reshape(-1)
    cot_slots = jnp.take(group_grads, used_source, axis=0)
    prob_values = jnp.einsum("sd,sd->s", cot_slots, out_flat, preferred_element_type=jnp.float32)
    hit = (row_ids[:, None] == used_source[None, :]) & used_filled[None, :]
    input_part = jnp.dot(hit.astype(jnp.bfloat16), input_flat, preferred_element_type=jnp.float32)
    weighting = jnp.where(hit, used_prob[None, :], 0.0)
    out_part = jnp.dot(
        weighting,
        out_flat.astype(jnp.float32),
        precision=highest,
        preferred_element_type=jnp.float32,
    )
    prob_columns = jnp.where(
        used_index[:, None] == jnp.arange(TOP, dtype=jnp.int32)[None, :], prob_values[:, None], 0.0
    )
    prob_part = jnp.dot(
        hit.astype(jnp.float32), prob_columns, precision=highest, preferred_element_type=jnp.float32
    )
    out_sum, normed_grad, prob_grad = (
        lax.psum_scatter(out_part, "tensor", scatter_dimension=0, tiled=True),
        lax.psum_scatter(input_part, "tensor", scatter_dimension=0, tiled=True),
        lax.psum_scatter(prob_part, "tensor", scatter_dimension=0, tiled=True),
    )
    mixed = (tokens.astype(jnp.float32) + out_sum).astype(jnp.bfloat16)
    gain_side = normed_grad * gain[None, :]
    token_grad = (
        cotangent.astype(jnp.float32)
        + inv_own
        * (gain_side - scaled_own * jnp.mean(gain_side * scaled_own, axis=1, keepdims=True))
    ).astype(jnp.bfloat16)
    gain_grad = lax.psum(jnp.sum(normed_grad * scaled_own, axis=0), ("expert", "tensor"))
    return (mixed, token_grad, prob_grad, gain_grad, gate_up_part[None], down_part[None])


BOTH = ("expert", "tensor")


def flip_first(expert, core):
    return expert ^ (2 if core == 0 else 1)


def flip_second(expert, core):
    return expert ^ (1 if core == 0 else 2)


def send(array, place):
    pairs = []
    for expert in range(lax.axis_size("expert")):
        for core in range(2):
            to_expert, to_core = place(expert, core)
            pairs.append((expert * 2 + core, to_expert * 2 + to_core))
    return lax.ppermute(array, BOTH, pairs)


def send_first(array):
    return send(array, lambda e, c: (flip_first(e, c), c))


def send_second(array):
    return send(array, lambda e, c: (flip_second(e, c), c))


def send_bit(array, bit):
    return send(array, lambda e, c: (e ^ bit, c))


def send_core(array):
    return send(array, lambda e, c: (e, 1 - c))


def send_along(array, step):
    size = lax.axis_size("expert")
    return send(array, lambda e, c: ((e + 4 * step) % size, c))


def after(array, *others):
    return lax.optimization_barrier((array,) + others)[0]


def together(*arrays):
    return lax.optimization_barrier(arrays)


def add_up(*terms):
    return sum(term.astype(jnp.float32) for term in terms)


def narrow(value):
    return value.astype(jnp.bfloat16)


def plane_tables(table):
    pair = jnp.stack([table, send_second(table)])
    return jnp.stack([pair, send_first(pair)])


def far_first(array):
    far = array[:, :, 1:].reshape((-1,) + array.shape[3:])
    return jnp.concatenate([far, array[:, :, 0].reshape((-1,) + array.shape[3:])])


def from_far_first(array, steps):
    far = array[:4 * (steps - 1)].reshape((2, 2, steps - 1) + array.shape[1:])
    return jnp.concatenate([array[4 * (steps - 1):].reshape((2, 2, 1) + array.shape[1:]), far], axis=2)


def chosen_rows(pick, mine, other):
    return jnp.dot(pick, jnp.concatenate([mine, other]), preferred_element_type=jnp.float32)


def norm_kernel(count, pick_ref, *refs):
    pieces, gain_ref, normed_ref = refs[:4], refs[4], refs[-1]

    def work(mine_ref, other_ref):
        for group in range(count):
            rows = chosen_rows(pick_ref[group], mine_ref[group], other_ref[group])
            inv_rms = lax.rsqrt(jnp.mean(rows * rows, axis=1, keepdims=True) + 1e-06)
            normed_ref[group] = (rows * inv_rms * gain_ref[...]).astype(jnp.bfloat16)

    by_place(work, pieces)


def grad_kernel(count, pick_ref, *refs):
    pieces, prob_ref, out_ref, (grad_ref, value_ref) = refs[:4], refs[4], refs[5], refs[-2:]

    def work(mine_ref, other_ref):
        for group in range(count):
            rows = chosen_rows(pick_ref[group], mine_ref[group], other_ref[group])
            grad_ref[group] = (rows * prob_ref[group]).astype(jnp.bfloat16)
            value_ref[group] = jnp.sum(rows * out_ref[group].astype(jnp.float32), axis=1, keepdims=True)

    by_place(work, pieces)


def by_place(work, pieces):
    for first in range(2):
        for second in range(2):
            pl.when(pl.program_id(0) == first * 2 + second)(
                functools.partial(work, pieces[first], pieces[2 + second])
            )


def group_spec(count, first_group, *shape):
    first_block = first_group // count
    return pl.BlockSpec((count,) + shape, lambda i: (first_block + i, 0, 0))


def select(kernel, pick, pieces, extras, extra_specs, out_shapes, count, arrays, which, first_group, held):
    _, capacity, group_rows = pick.shape
    half, features = pieces[0].shape[1:]

    def piece_spec(place):
        return pl.BlockSpec((count, half, features), lambda i: (place(i) * arrays + which, 0, 0))

    return pl.pallas_call(
        functools.partial(kernel, count),
        grid=(4,),
        in_specs=[
            group_spec(count, first_group, capacity, group_rows),
            piece_spec(lambda i: jnp.minimum(i, 1)),
            piece_spec(lambda i: jnp.maximum(i - 2, 0)),
            piece_spec(lambda i: i // 2),
            piece_spec(lambda i: jnp.maximum(i - 2, 0)),
        ] + extra_specs + [pl.BlockSpec(memory_space=pl.ANY)] * len(held),
        out_specs=[group_spec(count, first_group, *out.shape[1:]) for out in out_shapes],
        out_shape=out_shapes,
        input_output_aliases={5 + len(extras) + n: n for n in range(len(held))},
        compiler_params=pltpu.CompilerParams(vmem_limit_bytes=SMALL_VMEM),
        cost_estimate=LITTLE,
    )(pick, *pieces, *extras, *held)


def select_normed(pick, gain, pieces, count, arrays, first_group, held):
    groups, capacity, _ = pick.shape
    features = pieces[0].shape[2]
    return select(
        norm_kernel, pick, pieces, [gain], [pl.BlockSpec((1, features), lambda i: (0, 0))],
        [jax.ShapeDtypeStruct((groups, capacity, features), jnp.bfloat16)],
        count, arrays, 0, first_group, held,
    )


def select_grads(pick, prob, out_slots, pieces, count, arrays, which, first_group, held):
    groups, capacity, _ = pick.shape
    features = pieces[0].shape[2]
    return select(
        grad_kernel, pick, pieces, [prob, out_slots],
        [group_spec(count, first_group, capacity, 1), group_spec(count, first_group, capacity, features)],
        [
            jax.ShapeDtypeStruct((groups, capacity, features), jnp.bfloat16),
            jax.ShapeDtypeStruct((groups, capacity, 1), jnp.float32),
        ],
        count, arrays, which, first_group, held,
    )


def expand_kernel(weighted, count, back_ref, prob_ref, *refs):
    sources, (mine_ref, low_ref, high_ref) = refs[:-3], refs[-3:]
    half = mine_ref.shape[1]
    for group in range(count):
        for number, (source_ref, by_prob) in enumerate(zip(sources, weighted)):
            rows = source_ref[group]
            if by_prob:
                rows = (rows.astype(jnp.float32) * prob_ref[group]).astype(jnp.bfloat16)
            spread = jnp.dot(back_ref[group], rows, preferred_element_type=jnp.float32)
            place = group * len(sources) + number
            mine_ref[place] = spread[:half].astype(jnp.bfloat16)
            for second, out_ref in ((0, low_ref), (1, high_ref)):
                @pl.when(lax.rem(pl.program_id(0), 2) == second)
                def _(out_ref=out_ref, place=place, spread=spread):
                    out_ref[place] = spread[half:].astype(jnp.bfloat16)


def expand(back, prob, slots, weighted, count, first_group):
    _, group_rows, capacity = back.shape
    half, features, arrays = group_rows // 2, slots[0].shape[2], len(slots)
    blocks = count * arrays
    piece = jax.ShapeDtypeStruct((2 * blocks, half, features), jnp.bfloat16)
    return pl.pallas_call(
        functools.partial(expand_kernel, weighted, count),
        grid=(4,),
        in_specs=[
            group_spec(count, first_group, group_rows, capacity),
            group_spec(count, first_group, capacity, 1),
        ] + [group_spec(count, first_group, capacity, features)] * arrays,
        out_specs=[pl.BlockSpec((blocks, half, features), lambda i: (i, 0, 0))]
        + [pl.BlockSpec((blocks, half, features), lambda i: (i // 2, 0, 0))] * 2,
        out_shape=[jax.ShapeDtypeStruct((4 * blocks, half, features), jnp.bfloat16), piece, piece],
        compiler_params=pltpu.CompilerParams(vmem_limit_bytes=SMALL_VMEM),
        cost_estimate=LITTLE,
    )(back, prob, *slots)


def forward_kernel(units, rows_ref, gate_ref, up_ref, down_ref, gate_pre_ref, up_pre_ref, hidden_ref, out_ref):
    step = pl.program_id(0)
    block = gate_pre_ref.shape[1]

    @pl.when(step < units)
    def _():
        gate_pre = jnp.dot(rows_ref[...], gate_ref[0], preferred_element_type=jnp.float32)
        up_pre = jnp.dot(rows_ref[...], up_ref[0], preferred_element_type=jnp.float32)
        gate_pre_ref[...] = gate_pre
        up_pre_ref[...] = up_pre
        columns = pl.ds(pl.multiple_of(step * block, block), block)
        hidden_ref[:, columns] = (gate_pre * jax.nn.sigmoid(gate_pre) * up_pre).astype(jnp.bfloat16)

    @pl.when(step >= units)
    def _():
        out_ref[...] = jnp.dot(
            hidden_ref[...], down_ref[0], preferred_element_type=jnp.float32
        ).astype(jnp.bfloat16)


def forward(rows, gate_up_weight, down_weight):
    slots, features = rows.shape
    width = down_weight.shape[1]
    block, units, wide = 256, width // 256, features // 2
    early = lambda i: jnp.minimum(i, units - 1)
    late = lambda i: jnp.maximum(i - units, 0)
    return pl.pallas_call(
        functools.partial(forward_kernel, units),
        grid=(units + 2,),
        in_specs=[
            pl.BlockSpec((slots, features), lambda i: (0, 0)),
            pl.BlockSpec((1, features, block), lambda i: (0, 0, early(i))),
            pl.BlockSpec((1, features, block), lambda i: (0, 0, units + early(i))),
            pl.BlockSpec((1, width, wide), lambda i: (0, 0, late(i))),
        ],
        out_specs=[
            pl.BlockSpec((slots, block), lambda i: (0, early(i))),
            pl.BlockSpec((slots, block), lambda i: (0, early(i))),
            pl.BlockSpec((slots, width), lambda i: (0, 0)),
            pl.BlockSpec((slots, wide), lambda i: (0, late(i))),
        ],
        out_shape=[
            jax.ShapeDtypeStruct((slots, width), jnp.float32),
            jax.ShapeDtypeStruct((slots, width), jnp.float32),
            jax.ShapeDtypeStruct((slots, width), jnp.bfloat16),
            jax.ShapeDtypeStruct((slots, features), jnp.bfloat16),
        ],
        compiler_params=pltpu.CompilerParams(vmem_limit_bytes=LARGE_VMEM),
        cost_estimate=LITTLE,
    )(rows, gate_up_weight, gate_up_weight, down_weight)


def backward_kernel(
    units, grads_ref, gate_pre_ref, up_pre_ref, down_ref, gate_up_ref, rows_ref, joined_ref, input_ref, gain_ref
):
    step = pl.program_id(0)
    block = gate_pre_ref.shape[1]

    @pl.when(step < units)
    def _():
        gate_pre, up_pre = gate_pre_ref[...], up_pre_ref[...]
        sigmoid_gate = jax.nn.sigmoid(gate_pre)
        common = times_transposed(grads_ref[...], down_ref[0]) * sigmoid_gate
        gate_grad = common * up_pre * (1.0 + gate_pre * (1.0 - sigmoid_gate))
        start = pl.multiple_of(step * block, block)
        joined_ref[:, pl.ds(start, block)] = gate_grad.astype(jnp.bfloat16)
        joined_ref[:, pl.ds(units * block + start, block)] = (common * gate_pre).astype(jnp.bfloat16)

    @pl.when(step >= units)
    def _():
        input_grad = times_transposed(joined_ref[...], gate_up_ref[0]).astype(jnp.bfloat16)
        input_ref[...] = input_grad
        terms = input_grad.astype(jnp.float32) * rows_ref[...].astype(jnp.float32)
        gain_ref[...] = jnp.sum(terms, axis=0, keepdims=True)


def backward(grads, gate_pre, up_pre, rows, gate_up_weight, down_weight):
    slots, features = rows.shape
    width = down_weight.shape[1]
    block, units, wide = 256, width // 256, features // 4
    early = lambda i: jnp.minimum(i, units - 1)
    late = lambda i: jnp.maximum(i - units, 0)
    return pl.pallas_call(
        functools.partial(backward_kernel, units),
        grid=(units + 4,),
        in_specs=[
            pl.BlockSpec((slots, features), lambda i: (0, 0)),
            pl.BlockSpec((slots, block), lambda i: (0, early(i))),
            pl.BlockSpec((slots, block), lambda i: (0, early(i))),
            pl.BlockSpec((1, block, features), lambda i: (0, early(i), 0)),
            pl.BlockSpec((1, wide, 2 * width), lambda i: (0, late(i), 0)),
            pl.BlockSpec((slots, wide), lambda i: (0, late(i))),
        ],
        out_specs=[
            pl.BlockSpec((slots, 2 * width), lambda i: (0, 0)),
            pl.BlockSpec((slots, wide), lambda i: (0, late(i))),
            pl.BlockSpec((1, wide), lambda i: (0, late(i))),
        ],
        out_shape=[
            jax.ShapeDtypeStruct((slots, 2 * width), jnp.bfloat16),
            jax.ShapeDtypeStruct((slots, features), jnp.bfloat16),
            jax.ShapeDtypeStruct((1, features), jnp.float32),
        ],
        compiler_params=pltpu.CompilerParams(vmem_limit_bytes=LARGE_VMEM),
        cost_estimate=LITTLE,
    )(grads, gate_pre, up_pre, down_weight, gate_up_weight, rows)


def pack(columns, gains):
    return jnp.concatenate([columns.reshape(-1, 128), gains])


def unpack_add(columns, gains, got):
    count = gains.shape[0]
    return columns + got[:-count].reshape(columns.shape), gains + got[-count:]


def planes_in_order(gains):
    steps = len(gains)
    order = (lax.axis_index("expert") // 4 - jnp.arange(steps)) % steps
    ordered = jnp.take(jnp.stack(gains), order, axis=0)
    return functools.reduce(jnp.add, [ordered[step] for step in range(steps)]).reshape(-1)


def broadcast_shards(tokens, cotangent, gain, expert_ids, gate_probs, gate_up_weight, down_weight):
    expert_size = lax.axis_size("expert")
    steps = expert_size // 4
    far = 4 * (steps - 1)
    expert, core = lax.axis_index("expert"), lax.axis_index("tensor")
    my_expert = expert * EXP_DEV + core
    group_rows = expert_ids.shape[0]
    half = group_rows // 2
    features = tokens.shape[1]
    capacity = 3 * group_rows * TOP // (2 * EXP_DEV * expert_size)
    near_own = jnp.stack([tokens, cotangent])
    near_pair = jnp.concatenate([near_own, send_second(near_own)])
    near_far_pair = send_first(near_pair)
    tables = plane_tables(
        after(jnp.concatenate([expert_ids.T.astype(jnp.float32), gate_probs.T]), near_pair)
    )
    token_far = jnp.stack([send_along(tokens, -step) for step in range(1, steps)])
    late_tables = after(tables, token_far)
    far_tables = [send_along(late_tables, -step) for step in range(1, steps)]
    late_cot = after(cotangent, token_far)
    cot_steps = [send_along(late_cot, -step) for step in range(1, steps)]
    token_second = after(send_second(token_far), near_far_pair, cot_steps[0], *far_tables)
    token_pair = jnp.concatenate([token_far, token_second])
    token_far_pair = after(send_first(token_pair), *cot_steps)
    near_pieces = (near_pair, near_far_pair, send_core(near_pair), send_core(near_far_pair))
    cot_far = after(jnp.stack(cot_steps), token_far_pair)
    cot_second = send_second(cot_far)
    token_pieces = (
        token_pair, token_far_pair, send_core(token_pair), after(send_core(token_far_pair), cot_second)
    )
    cot_pair = jnp.concatenate([cot_far, cot_second])
    cot_far_pair = send_first(cot_pair)

    tables = far_first(jnp.stack([tables] + far_tables, axis=2))
    tables = jnp.where(core == 0, tables, jnp.roll(tables, half, axis=2))
    matches = tables[:, :TOP] == my_expert.astype(jnp.float32)
    chosen = jnp.any(matches, axis=1)
    weight_of = jnp.sum(jnp.where(matches, tables[:, TOP:], 0.0), axis=1)
    row_ids = jnp.arange(group_rows, dtype=jnp.int32)
    earlier = (row_ids[:, None] < row_ids[None, :]).astype(jnp.bfloat16)
    rank_in = jnp.dot(chosen.astype(jnp.bfloat16), earlier, preferred_element_type=jnp.float32)
    placed = chosen[:, None, :] & (
        rank_in.astype(jnp.int32)[:, None, :] == jnp.arange(capacity, dtype=jnp.int32)[None, :, None]
    )
    pick = placed.astype(jnp.bfloat16)
    back = jnp.swapaxes(pick, 1, 2)
    slot_prob = jnp.sum(jnp.where(placed, weight_of[:, None, :], 0.0), axis=2, keepdims=True)

    gain_row = gain[None, :]
    rows = select_normed(pick, gain_row, near_pieces, 1, 2, far, ())
    rows, = select_normed(pick, gain_row, token_pieces, steps - 1, 1, 0, tuple(rows))
    rows = rows.reshape(-1, features)
    gate_pre, up_pre, hidden, block_out = forward(rows, gate_up_weight, down_weight)
    block_out, cot_far_pair = together(block_out, cot_far_pair)
    cot_pieces = (cot_pair, cot_far_pair, send_core(cot_pair), send_core(cot_far_pair))
    out_slots = block_out.reshape(expert_size, capacity, features)
    out_mine, out_low, out_high = expand(back, slot_prob, (out_slots,), (True,), steps - 1, 0)

    half_far, one_far = 2 * (steps - 1), steps - 1
    out_core_high = send_core(out_high)
    out_core = send_core(out_low)
    out_upper = narrow(add_up(out_mine[half_far:], out_core_high))
    out_first = send_first(out_upper)
    held = select_grads(
        after(pick, out_high), slot_prob, out_slots, near_pieces, 1, 2, 1, far, ()
    )
    grads, prob_value = select_grads(
        after(pick, out_upper), slot_prob, out_slots, cot_pieces, steps - 1, 1, 0, 0, tuple(held)
    )
    grads = grads.reshape(-1, features)
    joined_grad, input_grad, gain_term = backward(
        grads, gate_pre, up_pre, rows, gate_up_weight, down_weight
    )
    input_grad, out_first = together(input_grad, out_first)
    input_slots = input_grad.reshape(expert_size, capacity, features)
    in_mine, in_low, in_high = expand(back, slot_prob, (input_slots,), (False,), steps - 1, 0)
    in_core_high = send_core(in_high)
    in_core = send_core(in_low)
    out_middle = narrow(
        add_up(out_mine[one_far:half_far], out_core[one_far:half_far], after(out_first, in_high)[one_far:])
    )
    out_second = send_second(out_middle)
    near_mine, near_low, near_high = expand(
        back, after(slot_prob, in_high), (out_slots, input_slots), (True, False), 1, far
    )
    near_core_high = send_core(near_high)
    near_core = send_core(near_low)
    in_upper = narrow(add_up(in_mine[half_far:], after(in_core_high, out_middle, near_high)))
    in_first = send_first(in_upper)
    gains = (gain_term[0] / gain).reshape(-1, 128)
    prob_rows = jnp.sum(jnp.where(placed, prob_value, 0.0), axis=1)
    columns = from_far_first(jnp.where(matches, prob_rows[:, None, :], 0.0), steps)
    columns = jnp.where(core == 0, columns, jnp.swapaxes(columns, 0, 1))
    got = send_core(after(pack(columns[..., half:], gains), in_upper))
    down_part = outer_sum(after(hidden, in_upper), grads)

    def own_plane(mine, core_part, first_part, second_part, count):
        return add_up(mine[:count], core_part[:count], first_part[:count], second_part[:count])

    out_second, down_part, got = together(out_second, down_part, got)
    columns, gains = unpack_add(columns[..., :half], gains, got)
    got = send_bit(pack(columns[1], gains), 2)
    out_planes = narrow(own_plane(out_mine, out_core, out_first, out_second, one_far))
    out_far = [send_along(out_planes[step - 1], step) for step in range(1, steps)]
    gate_up_part = outer_sum(after(rows, out_planes), joined_grad)
    in_first, near_core, gate_up_part, got = together(
        in_first, near_core, gate_up_part, got, out_far[len(out_far) // 2]
    )[:4]
    columns, gains = unpack_add(columns[0], gains, got)
    in_middle = narrow(
        add_up(in_mine[one_far:half_far], in_core[one_far:half_far], in_first[one_far:])
    )
    in_second = send_second(in_middle)
    got = send_bit(pack(columns[1], gains), 1)
    in_second, got = together(in_second, got, *out_far)[:2]
    columns, gains = unpack_add(columns[0], gains, got)
    in_planes = narrow(own_plane(in_mine, in_core, in_first, in_second, one_far))
    messages = [send_along(pack(columns[step], gains), step) for step in range(1, steps)]
    in_far = [send_along(in_planes[step - 1], step) for step in range(1, steps)]
    near_upper = narrow(add_up(near_mine[4:], after(near_core_high, in_planes)))
    near_first = send_first(near_upper)
    near_middle = narrow(add_up(near_mine[2:4], near_core[2:4], near_first[2:]))
    near_second = send_second(near_middle)
    near_sum = own_plane(near_mine, near_core, near_first, near_second, 2)
    out_sum = near_sum[0] + add_up(*out_far)
    normed_grad = near_sum[1] + add_up(*in_far)

    prob_sum, all_gains = columns[0], [gains]
    for message in messages:
        prob_sum = prob_sum + message[:-gains.shape[0]].reshape(prob_sum.shape)
        all_gains.append(message[-gains.shape[0]:])
    gain_grad = planes_in_order(all_gains)

    scaled_own, inv_own = normalize(tokens)
    mixed = (tokens.astype(jnp.float32) + out_sum).astype(jnp.bfloat16)
    gain_side = normed_grad * gain[None, :]
    token_grad = (
        cotangent.astype(jnp.float32)
        + inv_own
        * (gain_side - scaled_own * jnp.mean(gain_side * scaled_own, axis=1, keepdims=True))
    ).astype(jnp.bfloat16)
    return (mixed, token_grad, prob_sum.T, gain_grad, gate_up_part[None], down_part[None])


def solution(mesh):
    in_specs = (
        P(("expert", "tensor"), None),
        P(("expert", "tensor"), None),
        P(),
        P("expert", None),
        P("expert", None),
        P(("expert", "tensor"), None, None),
        P(("expert", "tensor"), None, None),
    )
    out_specs = (
        P(("expert", "tensor"), None),
        P(("expert", "tensor"), None),
        P(("expert", "tensor"), None),
        P(),
        P(("expert", "tensor"), None, None),
        P(("expert", "tensor"), None, None),
    )
    expert_size, tensor_size = mesh.shape["expert"], mesh.shape["tensor"]
    few = tensor_size == EXP_DEV and expert_size % 4 == 0 and expert_size <= 4 * TOP
    shards = broadcast_shards if few else routed_shards
    return jax.shard_map(shards, mesh=mesh, in_specs=in_specs, out_specs=out_specs, check_vma=False)
```

```python
import functools

import jax
import jax.numpy as jnp
from jax import lax
from jax.experimental import pallas as pl
from jax.experimental.pallas import tpu as pltpu
from jax.sharding import PartitionSpec as P

TOP = 8
EXP_DEV = 2
VMEM_LIMIT = 63 * 1024 * 1024
LITTLE = pl.CostEstimate(flops=1000000, bytes_accessed=100000, transcendentals=0)


def normalize(rows):
    values = rows.astype(jnp.float32)
    inv_rms = lax.rsqrt(jnp.mean(values * values, axis=1, keepdims=True) + 1e-06)
    return (values * inv_rms, inv_rms)


def expert_forward(rows, gate_up, down_proj):
    projected = jnp.dot(rows, gate_up, preferred_element_type=jnp.float32)
    half_width = down_proj.shape[0]
    gate_pre = projected[:, :half_width]
    up_pre = projected[:, half_width:]
    sigmoid_gate = jax.nn.sigmoid(gate_pre)
    hidden = (gate_pre * sigmoid_gate * up_pre).astype(jnp.bfloat16)
    block_out = jnp.dot(hidden, down_proj, preferred_element_type=jnp.float32).astype(jnp.bfloat16)
    return (gate_pre, up_pre, sigmoid_gate, hidden, block_out)


def times_transposed(left, right):
    return lax.dot_general(left, right, (((1,), (1,)), ((), ())), preferred_element_type=jnp.float32)


def outer_sum(left, right):
    product = lax.dot_general(left, right, (((0,), (0,)), ((), ())), preferred_element_type=jnp.float32)
    return product.astype(jnp.bfloat16)


def backward_inner(slot_grads, down_proj, gate_pre, up_pre, sigmoid_gate):
    hidden_grad = times_transposed(slot_grads, down_proj)
    gate_grad = (
        hidden_grad * up_pre * sigmoid_gate * (1.0 + gate_pre * (1.0 - sigmoid_gate))
    ).astype(jnp.bfloat16)
    up_grad = (hidden_grad * gate_pre * sigmoid_gate).astype(jnp.bfloat16)
    return jnp.concatenate([gate_grad, up_grad], axis=1)


def expert_backward(rows, slot_grads, gate_up, down_proj, gate_pre, up_pre, sigmoid_gate, hidden):
    joined_grad = backward_inner(slot_grads, down_proj, gate_pre, up_pre, sigmoid_gate)
    input_grad = times_transposed(joined_grad, gate_up).astype(jnp.bfloat16)
    return (input_grad, outer_sum(rows, joined_grad), outer_sum(hidden, slot_grads))


def routed_shards(tokens, cotangent, gain, expert_ids, gate_probs, gate_up_weight, down_weight):
    tensor_size = lax.axis_size("tensor")
    expert_size = lax.axis_size("expert")
    my_rank = lax.axis_index("tensor")
    blocks_each = tensor_size // EXP_DEV
    my_type = my_rank // blocks_each
    group_rows = expert_ids.shape[0]
    features = tokens.shape[1]
    capacity = 3 * group_rows * TOP // (2 * EXP_DEV * expert_size)
    highest = lax.Precision.HIGHEST
    scaled_own, inv_own = normalize(tokens)
    carried = (scaled_own * gain[None, :]).astype(jnp.bfloat16)
    group_first, group_grads = (
        lax.all_gather(carried, "tensor", axis=0, tiled=True),
        lax.all_gather(cotangent, "tensor", axis=0, tiled=True),
    )
    targets = jnp.arange(expert_size, dtype=jnp.int32) * EXP_DEV + my_type
    matches = expert_ids[:, :, None] == targets[None, None, :]
    chosen = jnp.any(matches, axis=1)
    weight_of = jnp.sum(jnp.where(matches, gate_probs[:, :, None], 0.0), axis=1)
    slot_of = jnp.sum(
        jnp.where(matches, jnp.arange(TOP, dtype=jnp.int32)[None, :, None], 0), axis=1
    )
    row_ids = jnp.arange(group_rows, dtype=jnp.int32)
    earlier = (row_ids[None, :] < row_ids[:, None]).astype(jnp.bfloat16)
    rank_in = jnp.dot(
        earlier, chosen.astype(jnp.bfloat16), preferred_element_type=jnp.float32
    ).astype(jnp.int32)
    placed = chosen.T[:, None, :] & (
        rank_in.T[:, None, :] == jnp.arange(capacity, dtype=jnp.int32)[None, :, None]
    )
    source = jnp.sum(jnp.where(placed, row_ids[None, None, :], 0), axis=2)
    filled = jnp.any(placed, axis=2)
    slot_prob = jnp.sum(jnp.where(placed, weight_of.T[:, None, :], 0.0), axis=2)
    slot_index = jnp.sum(jnp.where(placed, slot_of.T[:, None, :], 0), axis=2)
    sent_rows = jnp.where(
        filled[:, :, None], jnp.take(group_first, source, axis=0), jnp.zeros((), jnp.bfloat16)
    )
    sent_grads = (
        slot_prob[:, :, None] * jnp.take(group_grads, source, axis=0).astype(jnp.float32)
    ).astype(jnp.bfloat16)
    gate_up = gate_up_weight[0]
    down_proj = down_weight[0]
    arrived_rows, arrived_grads = (
        lax.all_to_all(sent_rows, "expert", split_axis=0, concat_axis=0, tiled=True),
        lax.all_to_all(sent_grads, "expert", split_axis=0, concat_axis=0, tiled=True),
    )
    rows = arrived_rows.reshape(-1, features)
    slot_grads = arrived_grads.reshape(-1, features)
    gate_pre, up_pre, sigmoid_gate, hidden, block_out = expert_forward(rows, gate_up, down_proj)
    out_slots = block_out.reshape(expert_size, capacity, features)
    input_grad, gate_up_part, down_part = expert_backward(
        rows, slot_grads, gate_up, down_proj, gate_pre, up_pre, sigmoid_gate, hidden
    )
    input_slots = input_grad.reshape(expert_size, capacity, features)
    out_back, input_back = (
        lax.all_to_all(out_slots, "expert", split_axis=0, concat_axis=0, tiled=True),
        lax.all_to_all(input_slots, "expert", split_axis=0, concat_axis=0, tiled=True),
    )
    out_flat = out_back.reshape(-1, features)
    input_flat = input_back.reshape(-1, features)
    used_source = source.reshape(-1)
    used_filled = filled.reshape(-1)
    used_prob = slot_prob.reshape(-1)
    used_index = slot_index.reshape(-1)
    cot_slots = jnp.take(group_grads, used_source, axis=0)
    prob_values = jnp.einsum("sd,sd->s", cot_slots, out_flat, preferred_element_type=jnp.float32)
    hit = (row_ids[:, None] == used_source[None, :]) & used_filled[None, :]
    input_part = jnp.dot(hit.astype(jnp.bfloat16), input_flat, preferred_element_type=jnp.float32)
    weighting = jnp.where(hit, used_prob[None, :], 0.0)
    out_part = jnp.dot(
        weighting,
        out_flat.astype(jnp.float32),
        precision=highest,
        preferred_element_type=jnp.float32,
    )
    prob_columns = jnp.where(
        used_index[:, None] == jnp.arange(TOP, dtype=jnp.int32)[None, :], prob_values[:, None], 0.0
    )
    prob_part = jnp.dot(
        hit.astype(jnp.float32), prob_columns, precision=highest, preferred_element_type=jnp.float32
    )
    out_sum, normed_grad, prob_grad = (
        lax.psum_scatter(out_part, "tensor", scatter_dimension=0, tiled=True),
        lax.psum_scatter(input_part, "tensor", scatter_dimension=0, tiled=True),
        lax.psum_scatter(prob_part, "tensor", scatter_dimension=0, tiled=True),
    )
    mixed = (tokens.astype(jnp.float32) + out_sum).astype(jnp.bfloat16)
    gain_side = normed_grad * gain[None, :]
    token_grad = (
        cotangent.astype(jnp.float32)
        + inv_own
        * (gain_side - scaled_own * jnp.mean(gain_side * scaled_own, axis=1, keepdims=True))
    ).astype(jnp.bfloat16)
    gain_grad = lax.psum(jnp.sum(normed_grad * scaled_own, axis=0), ("expert", "tensor"))
    return (mixed, token_grad, prob_grad, gain_grad, gate_up_part[None], down_part[None])


BOTH = ("expert", "tensor")


def flip_first(expert, core):
    return expert ^ (2 if core == 0 else 1)


def flip_second(expert, core):
    return expert ^ (1 if core == 0 else 2)


def send(array, place):
    pairs = []
    for expert in range(lax.axis_size("expert")):
        for core in range(2):
            to_expert, to_core = place(expert, core)
            pairs.append((expert * 2 + core, to_expert * 2 + to_core))
    return lax.ppermute(array, BOTH, pairs)


def send_first(array):
    return send(array, lambda e, c: (flip_first(e, c), c))


def send_second(array):
    return send(array, lambda e, c: (flip_second(e, c), c))


def send_bit(array, bit):
    return send(array, lambda e, c: (e ^ bit, c))


def send_core(array):
    return send(array, lambda e, c: (e, 1 - c))


def send_along(array, step):
    size = lax.axis_size("expert")
    return send(array, lambda e, c: ((e + 4 * step) % size, c))


def after(array, *others):
    return lax.optimization_barrier((array,) + others)[0]


def together(*arrays):
    return lax.optimization_barrier(arrays)


def add_up(*terms):
    return sum(term.astype(jnp.float32) for term in terms)


def narrow(value):
    return value.astype(jnp.bfloat16)


def plane_tables(table):
    pair = jnp.stack([table, send_second(table)])
    return jnp.stack([pair, send_first(pair)])


def far_first(array):
    far = array[:, :, 1:].reshape((-1,) + array.shape[3:])
    return jnp.concatenate([far, array[:, :, 0].reshape((-1,) + array.shape[3:])])


def from_far_first(array, steps):
    far = array[:4 * (steps - 1)].reshape((2, 2, steps - 1) + array.shape[1:])
    return jnp.concatenate([array[4 * (steps - 1):].reshape((2, 2, 1) + array.shape[1:]), far], axis=2)


def chosen_rows(pick, mine, other):
    return jnp.dot(pick, jnp.concatenate([mine, other]), preferred_element_type=jnp.float32)


def norm_kernel(count, pick_ref, *refs):
    pieces, gain_ref, normed_ref = refs[:4], refs[4], refs[-1]

    def work(mine_ref, other_ref):
        for group in range(count):
            rows = chosen_rows(pick_ref[group], mine_ref[group], other_ref[group])
            inv_rms = lax.rsqrt(jnp.mean(rows * rows, axis=1, keepdims=True) + 1e-06)
            normed_ref[group] = (rows * inv_rms * gain_ref[...]).astype(jnp.bfloat16)

    by_place(work, pieces)


def grad_kernel(count, pick_ref, *refs):
    pieces, prob_ref, out_ref, (grad_ref, value_ref) = refs[:4], refs[4], refs[5], refs[-2:]

    def work(mine_ref, other_ref):
        for group in range(count):
            rows = chosen_rows(pick_ref[group], mine_ref[group], other_ref[group])
            grad_ref[group] = (rows * prob_ref[group]).astype(jnp.bfloat16)
            value_ref[group] = jnp.sum(rows * out_ref[group].astype(jnp.float32), axis=1, keepdims=True)

    by_place(work, pieces)


def by_place(work, pieces):
    for first in range(2):
        for second in range(2):
            pl.when(pl.program_id(0) == first * 2 + second)(
                functools.partial(work, pieces[first], pieces[2 + second])
            )


def group_spec(count, first_group, *shape):
    first_block = first_group // count
    return pl.BlockSpec((count,) + shape, lambda i: (first_block + i, 0, 0))


def select(kernel, pick, pieces, extras, extra_specs, out_shapes, count, arrays, which, first_group, held):
    _, capacity, group_rows = pick.shape
    half, features = pieces[0].shape[1:]

    def piece_spec(place):
        return pl.BlockSpec((count, half, features), lambda i: (place(i) * arrays + which, 0, 0))

    return pl.pallas_call(
        functools.partial(kernel, count),
        grid=(4,),
        in_specs=[
            group_spec(count, first_group, capacity, group_rows),
            piece_spec(lambda i: jnp.minimum(i, 1)),
            piece_spec(lambda i: jnp.maximum(i - 2, 0)),
            piece_spec(lambda i: i // 2),
            piece_spec(lambda i: jnp.maximum(i - 2, 0)),
        ] + extra_specs + [pl.BlockSpec(memory_space=pl.ANY)] * len(held),
        out_specs=[group_spec(count, first_group, *out.shape[1:]) for out in out_shapes],
        out_shape=out_shapes,
        input_output_aliases={5 + len(extras) + n: n for n in range(len(held))},
        compiler_params=pltpu.CompilerParams(vmem_limit_bytes=VMEM_LIMIT),
        cost_estimate=LITTLE,
    )(pick, *pieces, *extras, *held)


def select_normed(pick, gain, pieces, count, arrays, first_group, held):
    groups, capacity, _ = pick.shape
    features = pieces[0].shape[2]
    return select(
        norm_kernel, pick, pieces, [gain], [pl.BlockSpec((1, features), lambda i: (0, 0))],
        [jax.ShapeDtypeStruct((groups, capacity, features), jnp.bfloat16)],
        count, arrays, 0, first_group, held,
    )


def select_grads(pick, prob, out_slots, pieces, count, arrays, which, first_group, held):
    groups, capacity, _ = pick.shape
    features = pieces[0].shape[2]
    return select(
        grad_kernel, pick, pieces, [prob, out_slots],
        [group_spec(count, first_group, capacity, 1), group_spec(count, first_group, capacity, features)],
        [
            jax.ShapeDtypeStruct((groups, capacity, features), jnp.bfloat16),
            jax.ShapeDtypeStruct((groups, capacity, 1), jnp.float32),
        ],
        count, arrays, which, first_group, held,
    )


def expand_kernel(weighted, count, back_ref, prob_ref, *refs):
    sources, (mine_ref, low_ref, high_ref) = refs[:-3], refs[-3:]
    half = mine_ref.shape[1]
    for group in range(count):
        for number, (source_ref, by_prob) in enumerate(zip(sources, weighted)):
            rows = source_ref[group]
            if by_prob:
                rows = (rows.astype(jnp.float32) * prob_ref[group]).astype(jnp.bfloat16)
            spread = jnp.dot(back_ref[group], rows, preferred_element_type=jnp.float32)
            place = group * len(sources) + number
            mine_ref[place] = spread[:half].astype(jnp.bfloat16)
            for second, out_ref in ((0, low_ref), (1, high_ref)):
                @pl.when(lax.rem(pl.program_id(0), 2) == second)
                def _(out_ref=out_ref, place=place, spread=spread):
                    out_ref[place] = spread[half:].astype(jnp.bfloat16)


def expand(back, prob, slots, weighted, count, first_group):
    _, group_rows, capacity = back.shape
    half, features, arrays = group_rows // 2, slots[0].shape[2], len(slots)
    blocks = count * arrays
    piece = jax.ShapeDtypeStruct((2 * blocks, half, features), jnp.bfloat16)
    return pl.pallas_call(
        functools.partial(expand_kernel, weighted, count),
        grid=(4,),
        in_specs=[
            group_spec(count, first_group, group_rows, capacity),
            group_spec(count, first_group, capacity, 1),
        ] + [group_spec(count, first_group, capacity, features)] * arrays,
        out_specs=[pl.BlockSpec((blocks, half, features), lambda i: (i, 0, 0))]
        + [pl.BlockSpec((blocks, half, features), lambda i: (i // 2, 0, 0))] * 2,
        out_shape=[jax.ShapeDtypeStruct((4 * blocks, half, features), jnp.bfloat16), piece, piece],
        compiler_params=pltpu.CompilerParams(vmem_limit_bytes=VMEM_LIMIT),
        cost_estimate=LITTLE,
    )(back, prob, *slots)


def forward_kernel(rows_ref, gate_up_ref, down_ref, gate_pre_ref, up_pre_ref, hidden_ref, out_ref):
    projected = jnp.dot(rows_ref[...], gate_up_ref[0], preferred_element_type=jnp.float32)
    half_width = hidden_ref.shape[1]
    gate_pre, up_pre = projected[:, :half_width], projected[:, half_width:]
    gate_pre_ref[...] = gate_pre
    up_pre_ref[...] = up_pre
    hidden = (gate_pre * jax.nn.sigmoid(gate_pre) * up_pre).astype(jnp.bfloat16)
    hidden_ref[...] = hidden
    out_ref[...] = jnp.dot(hidden, down_ref[0], preferred_element_type=jnp.float32).astype(jnp.bfloat16)


def forward(rows, gate_up_weight, down_weight):
    slots, features = rows.shape
    width = down_weight.shape[1]
    block = slots // 2

    def row_spec(columns):
        return pl.BlockSpec((block, columns), lambda i: (i, 0))

    return pl.pallas_call(
        forward_kernel,
        grid=(2,),
        in_specs=[
            row_spec(features),
            pl.BlockSpec((1, features, 2 * width), lambda i: (0, 0, 0)),
            pl.BlockSpec((1, width, features), lambda i: (0, 0, 0)),
        ],
        out_specs=[row_spec(width), row_spec(width), row_spec(width), row_spec(features)],
        out_shape=[
            jax.ShapeDtypeStruct((slots, width), jnp.float32),
            jax.ShapeDtypeStruct((slots, width), jnp.float32),
            jax.ShapeDtypeStruct((slots, width), jnp.bfloat16),
            jax.ShapeDtypeStruct((slots, features), jnp.bfloat16),
        ],
        compiler_params=pltpu.CompilerParams(vmem_limit_bytes=VMEM_LIMIT),
        cost_estimate=LITTLE,
    )(rows, gate_up_weight, down_weight)


def backward_kernel(
    units, grads_ref, gate_pre_ref, up_pre_ref, down_ref, gate_up_ref, rows_ref, joined_ref, input_ref, gain_ref
):
    step = pl.program_id(0)
    block = gate_pre_ref.shape[1]

    @pl.when(step < units)
    def _():
        gate_pre, up_pre = gate_pre_ref[...], up_pre_ref[...]
        sigmoid_gate = jax.nn.sigmoid(gate_pre)
        common = times_transposed(grads_ref[...], down_ref[0]) * sigmoid_gate
        gate_grad = common * up_pre * (1.0 + gate_pre * (1.0 - sigmoid_gate))
        start = pl.multiple_of(step * block, block)
        joined_ref[:, pl.ds(start, block)] = gate_grad.astype(jnp.bfloat16)
        joined_ref[:, pl.ds(units * block + start, block)] = (common * gate_pre).astype(jnp.bfloat16)

    @pl.when(step >= units)
    def _():
        input_grad = times_transposed(joined_ref[...], gate_up_ref[0]).astype(jnp.bfloat16)
        input_ref[...] = input_grad
        terms = input_grad.astype(jnp.float32) * rows_ref[...].astype(jnp.float32)
        gain_ref[...] = jnp.sum(terms, axis=0, keepdims=True)


def backward(grads, gate_pre, up_pre, rows, gate_up_weight, down_weight):
    slots, features = rows.shape
    width = down_weight.shape[1]
    block, units, wide = 256, width // 256, features // 4
    early = lambda i: jnp.minimum(i, units - 1)
    late = lambda i: jnp.maximum(i - units, 0)
    return pl.pallas_call(
        functools.partial(backward_kernel, units),
        grid=(units + 4,),
        in_specs=[
            pl.BlockSpec((slots, features), lambda i: (0, 0)),
            pl.BlockSpec((slots, block), lambda i: (0, early(i))),
            pl.BlockSpec((slots, block), lambda i: (0, early(i))),
            pl.BlockSpec((1, block, features), lambda i: (0, early(i), 0)),
            pl.BlockSpec((1, wide, 2 * width), lambda i: (0, late(i), 0)),
            pl.BlockSpec((slots, wide), lambda i: (0, late(i))),
        ],
        out_specs=[
            pl.BlockSpec((slots, 2 * width), lambda i: (0, 0)),
            pl.BlockSpec((slots, wide), lambda i: (0, late(i))),
            pl.BlockSpec((1, wide), lambda i: (0, late(i))),
        ],
        out_shape=[
            jax.ShapeDtypeStruct((slots, 2 * width), jnp.bfloat16),
            jax.ShapeDtypeStruct((slots, features), jnp.bfloat16),
            jax.ShapeDtypeStruct((1, features), jnp.float32),
        ],
        compiler_params=pltpu.CompilerParams(vmem_limit_bytes=VMEM_LIMIT),
        cost_estimate=LITTLE,
    )(grads, gate_pre, up_pre, down_weight, gate_up_weight, rows)


def pack(columns, gains):
    return jnp.concatenate([columns.reshape(-1, 128), gains])


def unpack_add(columns, gains, got):
    count = gains.shape[0]
    return columns + got[:-count].reshape(columns.shape), gains + got[-count:]


def planes_in_order(gains):
    steps = len(gains)
    order = (lax.axis_index("expert") // 4 - jnp.arange(steps)) % steps
    ordered = jnp.take(jnp.stack(gains), order, axis=0)
    return functools.reduce(jnp.add, [ordered[step] for step in range(steps)]).reshape(-1)


def broadcast_shards(tokens, cotangent, gain, expert_ids, gate_probs, gate_up_weight, down_weight):
    expert_size = lax.axis_size("expert")
    steps = expert_size // 4
    far = 4 * (steps - 1)
    expert, core = lax.axis_index("expert"), lax.axis_index("tensor")
    my_expert = expert * EXP_DEV + core
    group_rows = expert_ids.shape[0]
    half = group_rows // 2
    features = tokens.shape[1]
    capacity = 3 * group_rows * TOP // (2 * EXP_DEV * expert_size)
    near_own = jnp.stack([tokens, cotangent])
    near_pair = jnp.concatenate([near_own, send_second(near_own)])
    near_far_pair = send_first(near_pair)
    tables = plane_tables(
        after(jnp.concatenate([expert_ids.T.astype(jnp.float32), gate_probs.T]), near_pair)
    )
    token_far = after(jnp.stack([send_along(tokens, -step) for step in range(1, steps)]), tables)
    late_tables = after(tables, token_far)
    far_tables = [send_along(late_tables, -step) for step in range(1, steps)]
    late_cot = after(cotangent, token_far)
    cot_steps = [send_along(late_cot, -step) for step in range(1, steps)]
    token_second = after(send_second(token_far), near_far_pair, cot_steps[0], *far_tables)
    token_pair = jnp.concatenate([token_far, token_second])
    tables = far_first(jnp.stack([tables] + far_tables, axis=2))
    tables = jnp.where(core == 0, tables, jnp.roll(tables, half, axis=2))
    matches = tables[:, :TOP] == my_expert.astype(jnp.float32)
    chosen = jnp.any(matches, axis=1)
    weight_of = jnp.sum(jnp.where(matches, tables[:, TOP:], 0.0), axis=1)
    row_ids = jnp.arange(group_rows, dtype=jnp.int32)
    earlier = (row_ids[:, None] < row_ids[None, :]).astype(jnp.bfloat16)
    rank_in = jnp.dot(chosen.astype(jnp.bfloat16), earlier, preferred_element_type=jnp.float32)
    placed = chosen[:, None, :] & (
        rank_in.astype(jnp.int32)[:, None, :] == jnp.arange(capacity, dtype=jnp.int32)[None, :, None]
    )
    pick = placed.astype(jnp.bfloat16)
    back = jnp.swapaxes(pick, 1, 2)
    slot_prob = jnp.sum(jnp.where(placed, weight_of[:, None, :], 0.0), axis=2, keepdims=True)

    gain_row = gain[None, :]
    near_pieces = (near_pair, near_far_pair, send_core(near_pair), send_core(near_far_pair))
    rows, = select_normed(pick, gain_row, near_pieces, 1, 2, far, ())
    token_far_pair, rows = together(send_first(token_pair), rows, *cot_steps)[:2]
    cot_far = after(jnp.stack(cot_steps), token_far_pair)
    cot_second = send_second(cot_far)
    token_pieces = (
        token_pair, token_far_pair, send_core(token_pair), after(send_core(token_far_pair), cot_second)
    )
    cot_pair = jnp.concatenate([cot_far, cot_second])
    cot_far_pair = send_first(cot_pair)

    rows, = select_normed(pick, gain_row, token_pieces, steps - 1, 1, 0, (rows,))
    rows = rows.reshape(-1, features)
    gate_pre, up_pre, hidden, block_out = forward(rows, gate_up_weight, down_weight)
    block_out, cot_far_pair = together(block_out, cot_far_pair)
    cot_pieces = (cot_pair, cot_far_pair, send_core(cot_pair), send_core(cot_far_pair))
    out_slots = block_out.reshape(expert_size, capacity, features)
    out_mine, out_low, out_high = expand(back, slot_prob, (out_slots,), (True,), steps - 1, 0)

    half_far, one_far = 2 * (steps - 1), steps - 1
    out_core_high = send_core(out_high)
    out_core = send_core(out_low)
    out_upper = narrow(add_up(out_mine[half_far:], out_core_high))
    out_first = send_first(out_upper)
    held = select_grads(
        after(pick, out_high), slot_prob, out_slots, near_pieces, 1, 2, 1, far, ()
    )
    grads, prob_value = select_grads(
        after(pick, out_upper), slot_prob, out_slots, cot_pieces, steps - 1, 1, 0, 0, tuple(held)
    )
    grads = grads.reshape(-1, features)
    joined_grad, input_grad, gain_term = backward(
        grads, gate_pre, up_pre, rows, gate_up_weight, down_weight
    )
    input_grad, out_first = together(input_grad, out_first)
    input_slots = input_grad.reshape(expert_size, capacity, features)
    in_mine, in_low, in_high = expand(back, slot_prob, (input_slots,), (False,), steps - 1, 0)
    in_core_high = send_core(in_high)
    in_core = send_core(in_low)
    out_middle = narrow(
        add_up(out_mine[one_far:half_far], out_core[one_far:half_far], after(out_first, in_high)[one_far:])
    )
    out_second = send_second(out_middle)
    near_mine, near_low, near_high = expand(
        back, after(slot_prob, in_high), (out_slots, input_slots), (True, False), 1, far
    )
    near_core_high = send_core(near_high)
    near_core = send_core(near_low)
    in_upper = narrow(add_up(in_mine[half_far:], after(in_core_high, out_middle, near_high)))
    in_first = send_first(in_upper)
    gains = (gain_term[0] / gain).reshape(-1, 128)
    prob_rows = jnp.sum(jnp.where(placed, prob_value, 0.0), axis=1)
    columns = from_far_first(jnp.where(matches, prob_rows[:, None, :], 0.0), steps)
    columns = jnp.where(core == 0, columns, jnp.swapaxes(columns, 0, 1))
    got = send_core(after(pack(columns[..., half:], gains), in_upper))
    down_part = outer_sum(after(hidden, in_upper), grads)

    def own_plane(mine, core_part, first_part, second_part, count):
        return add_up(mine[:count], core_part[:count], first_part[:count], second_part[:count])

    out_second, down_part, got = together(out_second, down_part, got)
    columns, gains = unpack_add(columns[..., :half], gains, got)
    got = send_bit(pack(columns[1], gains), 2)
    out_planes = narrow(own_plane(out_mine, out_core, out_first, out_second, one_far))
    out_far = [send_along(out_planes[step - 1], step) for step in range(1, steps)]
    gate_up_part = outer_sum(after(rows, out_planes), joined_grad)
    in_first, near_core, gate_up_part, got = together(
        in_first, near_core, gate_up_part, got, out_far[len(out_far) // 2]
    )[:4]
    columns, gains = unpack_add(columns[0], gains, got)
    in_middle = narrow(
        add_up(in_mine[one_far:half_far], in_core[one_far:half_far], in_first[one_far:])
    )
    in_second = send_second(in_middle)
    got = send_bit(pack(columns[1], gains), 1)
    in_second, got = together(in_second, got, *out_far)[:2]
    columns, gains = unpack_add(columns[0], gains, got)
    in_planes = narrow(own_plane(in_mine, in_core, in_first, in_second, one_far))
    messages = [send_along(pack(columns[step], gains), step) for step in range(1, steps)]
    in_far = [send_along(in_planes[step - 1], step) for step in range(1, steps)]
    near_upper = narrow(add_up(near_mine[4:], after(near_core_high, in_planes)))
    near_first = send_first(near_upper)
    near_middle = narrow(add_up(near_mine[2:4], near_core[2:4], near_first[2:]))
    near_second = send_second(near_middle)
    near_sum = own_plane(near_mine, near_core, near_first, near_second, 2)
    out_sum = near_sum[0] + add_up(*out_far)
    normed_grad = near_sum[1] + add_up(*in_far)

    prob_sum, all_gains = columns[0], [gains]
    for message in messages:
        prob_sum = prob_sum + message[:-gains.shape[0]].reshape(prob_sum.shape)
        all_gains.append(message[-gains.shape[0]:])
    gain_grad = planes_in_order(all_gains)

    scaled_own, inv_own = normalize(tokens)
    mixed = (tokens.astype(jnp.float32) + out_sum).astype(jnp.bfloat16)
    gain_side = normed_grad * gain[None, :]
    token_grad = (
        cotangent.astype(jnp.float32)
        + inv_own
        * (gain_side - scaled_own * jnp.mean(gain_side * scaled_own, axis=1, keepdims=True))
    ).astype(jnp.bfloat16)
    return (mixed, token_grad, prob_sum.T, gain_grad, gate_up_part[None], down_part[None])


def solution(mesh):
    in_specs = (
        P(("expert", "tensor"), None),
        P(("expert", "tensor"), None),
        P(),
        P("expert", None),
        P("expert", None),
        P(("expert", "tensor"), None, None),
        P(("expert", "tensor"), None, None),
    )
    out_specs = (
        P(("expert", "tensor"), None),
        P(("expert", "tensor"), None),
        P(("expert", "tensor"), None),
        P(),
        P(("expert", "tensor"), None, None),
        P(("expert", "tensor"), None, None),
    )
    expert_size, tensor_size = mesh.shape["expert"], mesh.shape["tensor"]
    few = tensor_size == EXP_DEV and expert_size % 4 == 0 and expert_size <= 4 * TOP
    shards = broadcast_shards if few else routed_shards
    return jax.shard_map(shards, mesh=mesh, in_specs=in_specs, out_specs=out_specs, check_vma=False)
```

```python
import functools

import jax
import jax.numpy as jnp
from jax import lax
from jax.experimental import pallas as pl
from jax.experimental.pallas import tpu as pltpu
from jax.sharding import PartitionSpec as P

TOP = 8
EXP_DEV = 2
VMEM_LIMIT = 63 * 1024 * 1024
LITTLE = pl.CostEstimate(flops=1000000, bytes_accessed=100000, transcendentals=0)


def normalize(rows):
    values = rows.astype(jnp.float32)
    inv_rms = lax.rsqrt(jnp.mean(values * values, axis=1, keepdims=True) + 1e-06)
    return (values * inv_rms, inv_rms)


def expert_forward(rows, gate_up, down_proj):
    projected = jnp.dot(rows, gate_up, preferred_element_type=jnp.float32)
    half_width = down_proj.shape[0]
    gate_pre = projected[:, :half_width]
    up_pre = projected[:, half_width:]
    sigmoid_gate = jax.nn.sigmoid(gate_pre)
    hidden = (gate_pre * sigmoid_gate * up_pre).astype(jnp.bfloat16)
    block_out = jnp.dot(hidden, down_proj, preferred_element_type=jnp.float32).astype(jnp.bfloat16)
    return (gate_pre, up_pre, sigmoid_gate, hidden, block_out)


def times_transposed(left, right):
    return lax.dot_general(left, right, (((1,), (1,)), ((), ())), preferred_element_type=jnp.float32)


def outer_sum(left, right):
    product = lax.dot_general(left, right, (((0,), (0,)), ((), ())), preferred_element_type=jnp.float32)
    return product.astype(jnp.bfloat16)


def backward_inner(slot_grads, down_proj, gate_pre, up_pre, sigmoid_gate):
    hidden_grad = times_transposed(slot_grads, down_proj)
    gate_grad = (
        hidden_grad * up_pre * sigmoid_gate * (1.0 + gate_pre * (1.0 - sigmoid_gate))
    ).astype(jnp.bfloat16)
    up_grad = (hidden_grad * gate_pre * sigmoid_gate).astype(jnp.bfloat16)
    return jnp.concatenate([gate_grad, up_grad], axis=1)


def expert_backward(rows, slot_grads, gate_up, down_proj, gate_pre, up_pre, sigmoid_gate, hidden):
    joined_grad = backward_inner(slot_grads, down_proj, gate_pre, up_pre, sigmoid_gate)
    input_grad = times_transposed(joined_grad, gate_up).astype(jnp.bfloat16)
    return (input_grad, outer_sum(rows, joined_grad), outer_sum(hidden, slot_grads))


def routed_shards(tokens, cotangent, gain, expert_ids, gate_probs, gate_up_weight, down_weight):
    tensor_size = lax.axis_size("tensor")
    expert_size = lax.axis_size("expert")
    my_rank = lax.axis_index("tensor")
    blocks_each = tensor_size // EXP_DEV
    my_type = my_rank // blocks_each
    group_rows = expert_ids.shape[0]
    features = tokens.shape[1]
    capacity = 3 * group_rows * TOP // (2 * EXP_DEV * expert_size)
    highest = lax.Precision.HIGHEST
    scaled_own, inv_own = normalize(tokens)
    carried = (scaled_own * gain[None, :]).astype(jnp.bfloat16)
    group_first, group_grads = (
        lax.all_gather(carried, "tensor", axis=0, tiled=True),
        lax.all_gather(cotangent, "tensor", axis=0, tiled=True),
    )
    targets = jnp.arange(expert_size, dtype=jnp.int32) * EXP_DEV + my_type
    matches = expert_ids[:, :, None] == targets[None, None, :]
    chosen = jnp.any(matches, axis=1)
    weight_of = jnp.sum(jnp.where(matches, gate_probs[:, :, None], 0.0), axis=1)
    slot_of = jnp.sum(
        jnp.where(matches, jnp.arange(TOP, dtype=jnp.int32)[None, :, None], 0), axis=1
    )
    row_ids = jnp.arange(group_rows, dtype=jnp.int32)
    earlier = (row_ids[None, :] < row_ids[:, None]).astype(jnp.bfloat16)
    rank_in = jnp.dot(
        earlier, chosen.astype(jnp.bfloat16), preferred_element_type=jnp.float32
    ).astype(jnp.int32)
    placed = chosen.T[:, None, :] & (
        rank_in.T[:, None, :] == jnp.arange(capacity, dtype=jnp.int32)[None, :, None]
    )
    source = jnp.sum(jnp.where(placed, row_ids[None, None, :], 0), axis=2)
    filled = jnp.any(placed, axis=2)
    slot_prob = jnp.sum(jnp.where(placed, weight_of.T[:, None, :], 0.0), axis=2)
    slot_index = jnp.sum(jnp.where(placed, slot_of.T[:, None, :], 0), axis=2)
    sent_rows = jnp.where(
        filled[:, :, None], jnp.take(group_first, source, axis=0), jnp.zeros((), jnp.bfloat16)
    )
    sent_grads = (
        slot_prob[:, :, None] * jnp.take(group_grads, source, axis=0).astype(jnp.float32)
    ).astype(jnp.bfloat16)
    gate_up = gate_up_weight[0]
    down_proj = down_weight[0]
    arrived_rows, arrived_grads = (
        lax.all_to_all(sent_rows, "expert", split_axis=0, concat_axis=0, tiled=True),
        lax.all_to_all(sent_grads, "expert", split_axis=0, concat_axis=0, tiled=True),
    )
    rows = arrived_rows.reshape(-1, features)
    slot_grads = arrived_grads.reshape(-1, features)
    gate_pre, up_pre, sigmoid_gate, hidden, block_out = expert_forward(rows, gate_up, down_proj)
    out_slots = block_out.reshape(expert_size, capacity, features)
    input_grad, gate_up_part, down_part = expert_backward(
        rows, slot_grads, gate_up, down_proj, gate_pre, up_pre, sigmoid_gate, hidden
    )
    input_slots = input_grad.reshape(expert_size, capacity, features)
    out_back, input_back = (
        lax.all_to_all(out_slots, "expert", split_axis=0, concat_axis=0, tiled=True),
        lax.all_to_all(input_slots, "expert", split_axis=0, concat_axis=0, tiled=True),
    )
    out_flat = out_back.reshape(-1, features)
    input_flat = input_back.reshape(-1, features)
    used_source = source.reshape(-1)
    used_filled = filled.reshape(-1)
    used_prob = slot_prob.reshape(-1)
    used_index = slot_index.reshape(-1)
    cot_slots = jnp.take(group_grads, used_source, axis=0)
    prob_values = jnp.einsum("sd,sd->s", cot_slots, out_flat, preferred_element_type=jnp.float32)
    hit = (row_ids[:, None] == used_source[None, :]) & used_filled[None, :]
    input_part = jnp.dot(hit.astype(jnp.bfloat16), input_flat, preferred_element_type=jnp.float32)
    weighting = jnp.where(hit, used_prob[None, :], 0.0)
    out_part = jnp.dot(
        weighting,
        out_flat.astype(jnp.float32),
        precision=highest,
        preferred_element_type=jnp.float32,
    )
    prob_columns = jnp.where(
        used_index[:, None] == jnp.arange(TOP, dtype=jnp.int32)[None, :], prob_values[:, None], 0.0
    )
    prob_part = jnp.dot(
        hit.astype(jnp.float32), prob_columns, precision=highest, preferred_element_type=jnp.float32
    )
    out_sum, normed_grad, prob_grad = (
        lax.psum_scatter(out_part, "tensor", scatter_dimension=0, tiled=True),
        lax.psum_scatter(input_part, "tensor", scatter_dimension=0, tiled=True),
        lax.psum_scatter(prob_part, "tensor", scatter_dimension=0, tiled=True),
    )
    mixed = (tokens.astype(jnp.float32) + out_sum).astype(jnp.bfloat16)
    gain_side = normed_grad * gain[None, :]
    token_grad = (
        cotangent.astype(jnp.float32)
        + inv_own
        * (gain_side - scaled_own * jnp.mean(gain_side * scaled_own, axis=1, keepdims=True))
    ).astype(jnp.bfloat16)
    gain_grad = lax.psum(jnp.sum(normed_grad * scaled_own, axis=0), ("expert", "tensor"))
    return (mixed, token_grad, prob_grad, gain_grad, gate_up_part[None], down_part[None])


BOTH = ("expert", "tensor")


def flip_first(expert, core):
    return expert ^ (2 if core == 0 else 1)


def flip_second(expert, core):
    return expert ^ (1 if core == 0 else 2)


def send(array, place):
    pairs = []
    for expert in range(lax.axis_size("expert")):
        for core in range(2):
            to_expert, to_core = place(expert, core)
            pairs.append((expert * 2 + core, to_expert * 2 + to_core))
    return lax.ppermute(array, BOTH, pairs)


def send_first(array):
    return send(array, lambda e, c: (flip_first(e, c), c))


def send_second(array):
    return send(array, lambda e, c: (flip_second(e, c), c))


def send_bit(array, bit):
    return send(array, lambda e, c: (e ^ bit, c))


def send_core(array):
    return send(array, lambda e, c: (e, 1 - c))


def send_along(array, step):
    size = lax.axis_size("expert")
    return send(array, lambda e, c: ((e + 4 * step) % size, c))


def after(array, *others):
    return lax.optimization_barrier((array,) + others)[0]


def together(*arrays):
    return lax.optimization_barrier(arrays)


def add_up(*terms):
    return sum(term.astype(jnp.float32) for term in terms)


def narrow(value):
    return value.astype(jnp.bfloat16)


def plane_tables(table):
    pair = jnp.stack([table, send_second(table)])
    return jnp.stack([pair, send_first(pair)])


def far_first(array):
    far = array[:, :, 1:].reshape((-1,) + array.shape[3:])
    return jnp.concatenate([far, array[:, :, 0].reshape((-1,) + array.shape[3:])])


def from_far_first(array, steps):
    far = array[:4 * (steps - 1)].reshape((2, 2, steps - 1) + array.shape[1:])
    return jnp.concatenate([array[4 * (steps - 1):].reshape((2, 2, 1) + array.shape[1:]), far], axis=2)


def start(source, target, semaphore):
    copy = pltpu.make_async_copy(source, target, semaphore)
    copy.start()
    return copy


def select_kernel(count, arrays, which, first_group, grads, pick_ref, scale_ref, *refs):
    pieces, refs = refs[:4], refs[4:]
    if grads:
        out_slots, (_, grad_ref, value_ref, loaded, made, loads, stores, outs, out_loads) = refs[0], refs[-9:]
    else:
        grad_ref, loaded, made, loads, stores = refs[-5:]
    half = pieces[0].shape[1]
    copies, written = [], []
    for group in range(4 * count):
        place, inner = divmod(group, count)
        first, second = divmod(place, 2)
        mine = pieces[first].at[(second * count + inner) * arrays + which]
        other = pieces[2 + second].at[(first * count + inner) * arrays + which]
        both = [
            start(mine, loaded.at[group, pl.ds(0, half)], loads.at[group, 0]),
            start(other, loaded.at[group, pl.ds(half, half)], loads.at[group, 1]),
        ]
        if grads:
            both.append(start(out_slots.at[first_group + group], outs.at[group], out_loads.at[group]))
        copies.append(both)
    for group in range(4 * count):
        for copy in copies[group]:
            copy.wait()
        rows = jnp.dot(pick_ref[first_group + group], loaded[group], preferred_element_type=jnp.float32)
        if grads:
            made[group] = (rows * scale_ref[first_group + group]).astype(jnp.bfloat16)
            value_ref[group] = jnp.sum(rows * outs[group].astype(jnp.float32), axis=1, keepdims=True)
        else:
            inv_rms = lax.rsqrt(jnp.mean(rows * rows, axis=1, keepdims=True) + 1e-06)
            made[group] = (rows * inv_rms * scale_ref[...]).astype(jnp.bfloat16)
        written.append(start(made.at[group], grad_ref.at[first_group + group], stores.at[group]))
    for copy in written:
        copy.wait()


def select(pick, scale, pieces, count, arrays, which, first_group, held=None, out_slots=None):
    groups, capacity, group_rows = pick.shape
    features = pieces[0].shape[2]
    many, grads = 4 * count, out_slots is not None
    anywhere, whole = pl.BlockSpec(memory_space=pl.ANY), pl.BlockSpec(memory_space=pltpu.VMEM)
    operands = [pick, scale, *pieces] + ([out_slots] if grads else []) + ([] if held is None else [held])
    out_shape = [jax.ShapeDtypeStruct((groups, capacity, features), jnp.bfloat16)]
    scratch = [
        pltpu.VMEM((many, group_rows, features), jnp.bfloat16),
        pltpu.VMEM((many, capacity, features), jnp.bfloat16),
        pltpu.SemaphoreType.DMA((many, 2)),
        pltpu.SemaphoreType.DMA((many,)),
    ]
    if grads:
        out_shape.append(jax.ShapeDtypeStruct((many, capacity, 1), jnp.float32))
        scratch += [
            pltpu.VMEM((many, capacity, features), jnp.bfloat16), pltpu.SemaphoreType.DMA((many,)),
        ]
    kernel = functools.partial(select_kernel, count, arrays, which, first_group, grads)
    if grads and held is None:
        inner = kernel
        kernel = lambda *refs: inner(*refs[:7], None, *refs[7:])
    return pl.pallas_call(
        kernel,
        in_specs=[whole, whole] + [anywhere] * (len(operands) - 2),
        out_specs=[anywhere] + [whole] * (len(out_shape) - 1),
        out_shape=out_shape,
        scratch_shapes=scratch,
        input_output_aliases={} if held is None else {len(operands) - 1: 0},
        compiler_params=pltpu.CompilerParams(vmem_limit_bytes=VMEM_LIMIT),
        cost_estimate=LITTLE,
    )(*operands)


def expand_kernel(weighted, count, first_group, back_ref, prob_ref, *refs):
    arrays = len(weighted)
    sources, mine_ref, pieces = refs[:arrays], refs[arrays], refs[arrays + 1:arrays + 3]
    loaded, spread, loads, stores = refs[arrays + 3:]
    half = mine_ref.shape[1]
    copies, written = [], []
    for group in range(4 * count):
        for number, source in enumerate(sources):
            place = group * arrays + number
            copies.append(start(source.at[first_group + group], loaded.at[place], loads.at[place]))
    for group in range(4 * count):
        outer, inner = divmod(group, count)
        first, second = divmod(outer, 2)
        for number, by_prob in enumerate(weighted):
            place = group * arrays + number
            copies[place].wait()
            rows = loaded[place]
            if by_prob:
                rows = (rows.astype(jnp.float32) * prob_ref[first_group + group]).astype(jnp.bfloat16)
            spread[place] = jnp.dot(
                back_ref[first_group + group], rows, preferred_element_type=jnp.float32
            ).astype(jnp.bfloat16)
            target = pieces[second].at[(first * count + inner) * arrays + number]
            written += [
                start(spread.at[place, pl.ds(half, half)], target, stores.at[place, 0]),
                start(spread.at[place, pl.ds(0, half)], mine_ref.at[place], stores.at[place, 1]),
            ]
    for copy in written:
        copy.wait()


def expand(back, prob, slots, weighted, count, first_group):
    _, group_rows, capacity = back.shape
    half, features, arrays = group_rows // 2, slots[0].shape[2], len(slots)
    blocks = 4 * count * arrays
    anywhere, whole = pl.BlockSpec(memory_space=pl.ANY), pl.BlockSpec(memory_space=pltpu.VMEM)
    piece = jax.ShapeDtypeStruct((blocks // 2, half, features), jnp.bfloat16)
    return pl.pallas_call(
        functools.partial(expand_kernel, weighted, count, first_group),
        in_specs=[whole, whole] + [anywhere] * arrays,
        out_specs=[anywhere] * 3,
        out_shape=[jax.ShapeDtypeStruct((blocks, half, features), jnp.bfloat16), piece, piece],
        scratch_shapes=[
            pltpu.VMEM((blocks, capacity, features), jnp.bfloat16),
            pltpu.VMEM((blocks, group_rows, features), jnp.bfloat16),
            pltpu.SemaphoreType.DMA((blocks,)),
            pltpu.SemaphoreType.DMA((blocks, 2)),
        ],
        compiler_params=pltpu.CompilerParams(vmem_limit_bytes=VMEM_LIMIT),
        cost_estimate=LITTLE,
    )(back, prob, *slots)


def forward_kernel(rows_ref, gate_up_ref, down_ref, gate_pre_ref, up_pre_ref, hidden_ref, out_ref):
    projected = jnp.dot(rows_ref[...], gate_up_ref[0], preferred_element_type=jnp.float32)
    half_width = hidden_ref.shape[1]
    gate_pre, up_pre = projected[:, :half_width], projected[:, half_width:]
    gate_pre_ref[...] = gate_pre
    up_pre_ref[...] = up_pre
    hidden = (gate_pre * jax.nn.sigmoid(gate_pre) * up_pre).astype(jnp.bfloat16)
    hidden_ref[...] = hidden
    out_ref[...] = jnp.dot(hidden, down_ref[0], preferred_element_type=jnp.float32).astype(jnp.bfloat16)


def forward(rows, gate_up_weight, down_weight):
    slots, features = rows.shape
    width = down_weight.shape[1]
    block = slots // 2

    def row_spec(columns):
        return pl.BlockSpec((block, columns), lambda i: (i, 0))

    return pl.pallas_call(
        forward_kernel,
        grid=(2,),
        in_specs=[
            row_spec(features),
            pl.BlockSpec((1, features, 2 * width), lambda i: (0, 0, 0)),
            pl.BlockSpec((1, width, features), lambda i: (0, 0, 0)),
        ],
        out_specs=[row_spec(width), row_spec(width), row_spec(width), row_spec(features)],
        out_shape=[
            jax.ShapeDtypeStruct((slots, width), jnp.float32),
            jax.ShapeDtypeStruct((slots, width), jnp.float32),
            jax.ShapeDtypeStruct((slots, width), jnp.bfloat16),
            jax.ShapeDtypeStruct((slots, features), jnp.bfloat16),
        ],
        compiler_params=pltpu.CompilerParams(vmem_limit_bytes=VMEM_LIMIT),
        cost_estimate=LITTLE,
    )(rows, gate_up_weight, down_weight)


def backward_kernel(
    units, grads_ref, gate_pre_ref, up_pre_ref, down_ref, gate_up_ref, rows_ref, joined_ref, input_ref, gain_ref
):
    step = pl.program_id(0)
    block = gate_pre_ref.shape[1]

    @pl.when(step < units)
    def _():
        gate_pre, up_pre = gate_pre_ref[...], up_pre_ref[...]
        sigmoid_gate = jax.nn.sigmoid(gate_pre)
        common = times_transposed(grads_ref[...], down_ref[0]) * sigmoid_gate
        gate_grad = common * up_pre * (1.0 + gate_pre * (1.0 - sigmoid_gate))
        start = pl.multiple_of(step * block, block)
        joined_ref[:, pl.ds(start, block)] = gate_grad.astype(jnp.bfloat16)
        joined_ref[:, pl.ds(units * block + start, block)] = (common * gate_pre).astype(jnp.bfloat16)

    @pl.when(step >= units)
    def _():
        input_grad = times_transposed(joined_ref[...], gate_up_ref[0]).astype(jnp.bfloat16)
        input_ref[...] = input_grad
        terms = input_grad.astype(jnp.float32) * rows_ref[...].astype(jnp.float32)
        gain_ref[...] = jnp.sum(terms, axis=0, keepdims=True)


def backward(grads, gate_pre, up_pre, rows, gate_up_weight, down_weight):
    slots, features = rows.shape
    width = down_weight.shape[1]
    block, units, wide = 256, width // 256, features // 4
    early = lambda i: jnp.minimum(i, units - 1)
    late = lambda i: jnp.maximum(i - units, 0)
    return pl.pallas_call(
        functools.partial(backward_kernel, units),
        grid=(units + 4,),
        in_specs=[
            pl.BlockSpec((slots, features), lambda i: (0, 0)),
            pl.BlockSpec((slots, block), lambda i: (0, early(i))),
            pl.BlockSpec((slots, block), lambda i: (0, early(i))),
            pl.BlockSpec((1, block, features), lambda i: (0, early(i), 0)),
            pl.BlockSpec((1, wide, 2 * width), lambda i: (0, late(i), 0)),
            pl.BlockSpec((slots, wide), lambda i: (0, late(i))),
        ],
        out_specs=[
            pl.BlockSpec((slots, 2 * width), lambda i: (0, 0)),
            pl.BlockSpec((slots, wide), lambda i: (0, late(i))),
            pl.BlockSpec((1, wide), lambda i: (0, late(i))),
        ],
        out_shape=[
            jax.ShapeDtypeStruct((slots, 2 * width), jnp.bfloat16),
            jax.ShapeDtypeStruct((slots, features), jnp.bfloat16),
            jax.ShapeDtypeStruct((1, features), jnp.float32),
        ],
        compiler_params=pltpu.CompilerParams(vmem_limit_bytes=VMEM_LIMIT),
        cost_estimate=LITTLE,
    )(grads, gate_pre, up_pre, down_weight, gate_up_weight, rows)


def pack(columns, gains):
    return jnp.concatenate([columns.reshape(-1, 128), gains])


def unpack_add(columns, gains, got):
    count = gains.shape[0]
    return columns + got[:-count].reshape(columns.shape), gains + got[-count:]


def planes_in_order(gains):
    steps = len(gains)
    order = (lax.axis_index("expert") // 4 - jnp.arange(steps)) % steps
    ordered = jnp.take(jnp.stack(gains), order, axis=0)
    return functools.reduce(jnp.add, [ordered[step] for step in range(steps)]).reshape(-1)


def broadcast_shards(tokens, cotangent, gain, expert_ids, gate_probs, gate_up_weight, down_weight):
    expert_size = lax.axis_size("expert")
    steps = expert_size // 4
    far = 4 * (steps - 1)
    expert, core = lax.axis_index("expert"), lax.axis_index("tensor")
    my_expert = expert * EXP_DEV + core
    group_rows = expert_ids.shape[0]
    half = group_rows // 2
    features = tokens.shape[1]
    capacity = 3 * group_rows * TOP // (2 * EXP_DEV * expert_size)
    near_own = jnp.stack([tokens, cotangent])
    near_pair = jnp.concatenate([near_own, send_second(near_own)])
    near_far_pair = send_first(near_pair)
    tables = plane_tables(
        after(jnp.concatenate([expert_ids.T.astype(jnp.float32), gate_probs.T]), near_pair)
    )
    token_far = after(jnp.stack([send_along(tokens, -step) for step in range(1, steps)]), tables)
    late_tables = after(tables, token_far)
    far_tables = [send_along(late_tables, -step) for step in range(1, steps)]
    late_cot = after(cotangent, token_far)
    cot_steps = [send_along(late_cot, -step) for step in range(1, steps)]
    token_second = after(send_second(token_far), near_far_pair, cot_steps[len(cot_steps) // 2], *far_tables)
    token_pair = jnp.concatenate([token_far, token_second])
    tables = far_first(jnp.stack([tables] + far_tables, axis=2))
    tables = jnp.where(core == 0, tables, jnp.roll(tables, half, axis=2))
    matches = tables[:, :TOP] == my_expert.astype(jnp.float32)
    chosen = jnp.any(matches, axis=1)
    weight_of = jnp.sum(jnp.where(matches, tables[:, TOP:], 0.0), axis=1)
    row_ids = jnp.arange(group_rows, dtype=jnp.int32)
    earlier = (row_ids[:, None] < row_ids[None, :]).astype(jnp.bfloat16)
    rank_in = jnp.dot(chosen.astype(jnp.bfloat16), earlier, preferred_element_type=jnp.float32)
    placed = chosen[:, None, :] & (
        rank_in.astype(jnp.int32)[:, None, :] == jnp.arange(capacity, dtype=jnp.int32)[None, :, None]
    )
    pick = placed.astype(jnp.bfloat16)
    back = jnp.swapaxes(pick, 1, 2)
    slot_prob = jnp.sum(jnp.where(placed, weight_of[:, None, :], 0.0), axis=2, keepdims=True)

    gain_row = gain[None, :]
    near_pieces = (near_pair, near_far_pair, send_core(near_pair), send_core(near_far_pair))
    rows, = select(pick, gain_row, near_pieces, 1, 2, 0, far)
    token_far_pair, rows = together(send_first(token_pair), rows, *cot_steps)[:2]
    cot_far = after(jnp.stack(cot_steps), token_far_pair)
    cot_second = send_second(cot_far)
    token_pieces = (
        token_pair, token_far_pair, send_core(token_pair), after(send_core(token_far_pair), cot_second)
    )
    cot_pair = jnp.concatenate([cot_far, cot_second])
    cot_far_pair = send_first(cot_pair)

    rows, = select(pick, gain_row, token_pieces, steps - 1, 1, 0, 0, rows)
    rows = rows.reshape(-1, features)
    gate_pre, up_pre, hidden, block_out = forward(rows, gate_up_weight, down_weight)
    block_out, cot_far_pair = together(block_out, cot_far_pair)
    cot_pieces = (cot_pair, cot_far_pair, send_core(cot_pair), send_core(cot_far_pair))
    out_slots = block_out.reshape(expert_size, capacity, features)
    out_mine, out_low, out_high = expand(back, slot_prob, (out_slots,), (True,), steps - 1, 0)

    half_far, one_far = 2 * (steps - 1), steps - 1
    grads, near_value = select(
        after(pick, out_high), slot_prob, near_pieces, 1, 2, 1, far, None, out_slots
    )
    out_core_high, grads = together(send_core(out_high), grads)
    out_core = send_core(out_low)
    out_upper = narrow(add_up(out_mine[half_far:], out_core_high))
    out_first = send_first(out_upper)
    grads, prob_value = select(
        after(pick, out_upper), slot_prob, cot_pieces, steps - 1, 1, 0, 0, grads, out_slots
    )
    prob_value = jnp.concatenate([prob_value, near_value])
    grads = grads.reshape(-1, features)
    joined_grad, input_grad, gain_term = backward(
        grads, gate_pre, up_pre, rows, gate_up_weight, down_weight
    )
    input_grad, out_first = together(input_grad, out_first)
    input_slots = input_grad.reshape(expert_size, capacity, features)
    out_middle = narrow(
        add_up(out_mine[one_far:half_far], out_core[one_far:half_far], out_first[one_far:])
    )
    out_second = send_second(out_middle)
    in_mine, in_low, in_high = expand(back, after(slot_prob, out_middle), (input_slots,), (False,), steps - 1, 0)
    in_core_high = send_core(in_high)
    in_core = send_core(in_low)
    near_mine, near_low, near_high = expand(
        back, after(slot_prob, in_high), (out_slots, input_slots), (True, False), 1, far
    )
    near_core_high = send_core(near_high)
    near_core = send_core(near_low)
    in_upper = narrow(add_up(in_mine[half_far:], after(in_core_high, out_middle, near_high)))
    in_first = send_first(in_upper)
    gains = (gain_term[0] / gain).reshape(-1, 128)
    prob_rows = jnp.sum(jnp.where(placed, prob_value, 0.0), axis=1)
    columns = from_far_first(jnp.where(matches, prob_rows[:, None, :], 0.0), steps)
    columns = jnp.where(core == 0, columns, jnp.swapaxes(columns, 0, 1))
    got = send_core(after(pack(columns[..., half:], gains), in_upper))
    down_part = outer_sum(after(hidden, in_upper), grads)

    def own_plane(mine, core_part, first_part, second_part, count):
        return add_up(mine[:count], core_part[:count], first_part[:count], second_part[:count])

    out_second, down_part, got = together(out_second, down_part, got)
    columns, gains = unpack_add(columns[..., :half], gains, got)
    got = send_bit(pack(columns[1], gains), 2)
    out_planes = narrow(own_plane(out_mine, out_core, out_first, out_second, one_far))
    out_far = [send_along(out_planes[step - 1], step) for step in range(1, steps)]
    gate_up_part = outer_sum(after(rows, out_planes), joined_grad)
    in_first, near_core, gate_up_part, got = together(
        in_first, near_core, gate_up_part, got, out_far[len(out_far) // 2]
    )[:4]
    columns, gains = unpack_add(columns[0], gains, got)
    in_middle = narrow(
        add_up(in_mine[one_far:half_far], in_core[one_far:half_far], in_first[one_far:])
    )
    in_second = send_second(in_middle)
    got = send_bit(pack(columns[1], gains), 1)
    in_second, got = together(in_second, got, *out_far)[:2]
    columns, gains = unpack_add(columns[0], gains, got)
    in_planes = narrow(own_plane(in_mine, in_core, in_first, in_second, one_far))
    messages = [send_along(pack(columns[step], gains), step) for step in range(1, steps)]
    in_far = [send_along(in_planes[step - 1], step) for step in range(1, steps)]
    near_upper = narrow(add_up(near_mine[4:], after(near_core_high, in_planes)))
    near_first = send_first(near_upper)
    near_middle = narrow(add_up(near_mine[2:4], near_core[2:4], near_first[2:]))
    near_second = send_second(near_middle)
    near_sum = own_plane(near_mine, near_core, near_first, near_second, 2)
    out_sum = near_sum[0] + add_up(*out_far)
    normed_grad = near_sum[1] + add_up(*in_far)

    prob_sum, all_gains = columns[0], [gains]
    for message in messages:
        prob_sum = prob_sum + message[:-gains.shape[0]].reshape(prob_sum.shape)
        all_gains.append(message[-gains.shape[0]:])
    gain_grad = planes_in_order(all_gains)

    scaled_own, inv_own = normalize(tokens)
    mixed = (tokens.astype(jnp.float32) + out_sum).astype(jnp.bfloat16)
    gain_side = normed_grad * gain[None, :]
    token_grad = (
        cotangent.astype(jnp.float32)
        + inv_own
        * (gain_side - scaled_own * jnp.mean(gain_side * scaled_own, axis=1, keepdims=True))
    ).astype(jnp.bfloat16)
    return (mixed, token_grad, prob_sum.T, gain_grad, gate_up_part[None], down_part[None])


def solution(mesh):
    in_specs = (
        P(("expert", "tensor"), None),
        P(("expert", "tensor"), None),
        P(),
        P("expert", None),
        P("expert", None),
        P(("expert", "tensor"), None, None),
        P(("expert", "tensor"), None, None),
    )
    out_specs = (
        P(("expert", "tensor"), None),
        P(("expert", "tensor"), None),
        P(("expert", "tensor"), None),
        P(),
        P(("expert", "tensor"), None, None),
        P(("expert", "tensor"), None, None),
    )
    expert_size, tensor_size = mesh.shape["expert"], mesh.shape["tensor"]
    few = tensor_size == EXP_DEV and expert_size % 4 == 0 and expert_size <= 4 * TOP
    shards = broadcast_shards if few else routed_shards
    return jax.shard_map(shards, mesh=mesh, in_specs=in_specs, out_specs=out_specs, check_vma=False)
```

```python
import functools

import jax
import jax.numpy as jnp
from jax import lax
from jax.experimental import pallas as pl
from jax.experimental.pallas import tpu as pltpu
from jax.sharding import PartitionSpec as P

TOP = 8
EXP_DEV = 2
VMEM_LIMIT = 63 * 1024 * 1024
LITTLE = pl.CostEstimate(flops=1000000, bytes_accessed=100000, transcendentals=0)


def normalize(rows):
    values = rows.astype(jnp.float32)
    inv_rms = lax.rsqrt(jnp.mean(values * values, axis=1, keepdims=True) + 1e-06)
    return (values * inv_rms, inv_rms)


def expert_forward(rows, gate_up, down_proj):
    projected = jnp.dot(rows, gate_up, preferred_element_type=jnp.float32)
    half_width = down_proj.shape[0]
    gate_pre = projected[:, :half_width]
    up_pre = projected[:, half_width:]
    sigmoid_gate = jax.nn.sigmoid(gate_pre)
    hidden = (gate_pre * sigmoid_gate * up_pre).astype(jnp.bfloat16)
    block_out = jnp.dot(hidden, down_proj, preferred_element_type=jnp.float32).astype(jnp.bfloat16)
    return (gate_pre, up_pre, sigmoid_gate, hidden, block_out)


def times_transposed(left, right):
    return lax.dot_general(left, right, (((1,), (1,)), ((), ())), preferred_element_type=jnp.float32)


def outer_sum(left, right):
    product = lax.dot_general(left, right, (((0,), (0,)), ((), ())), preferred_element_type=jnp.float32)
    return product.astype(jnp.bfloat16)


def backward_inner(slot_grads, down_proj, gate_pre, up_pre, sigmoid_gate):
    hidden_grad = times_transposed(slot_grads, down_proj)
    gate_grad = (
        hidden_grad * up_pre * sigmoid_gate * (1.0 + gate_pre * (1.0 - sigmoid_gate))
    ).astype(jnp.bfloat16)
    up_grad = (hidden_grad * gate_pre * sigmoid_gate).astype(jnp.bfloat16)
    return jnp.concatenate([gate_grad, up_grad], axis=1)


def expert_backward(rows, slot_grads, gate_up, down_proj, gate_pre, up_pre, sigmoid_gate, hidden):
    joined_grad = backward_inner(slot_grads, down_proj, gate_pre, up_pre, sigmoid_gate)
    input_grad = times_transposed(joined_grad, gate_up).astype(jnp.bfloat16)
    return (input_grad, outer_sum(rows, joined_grad), outer_sum(hidden, slot_grads))


def routed_shards(tokens, cotangent, gain, expert_ids, gate_probs, gate_up_weight, down_weight):
    tensor_size = lax.axis_size("tensor")
    expert_size = lax.axis_size("expert")
    my_rank = lax.axis_index("tensor")
    blocks_each = tensor_size // EXP_DEV
    my_type = my_rank // blocks_each
    group_rows = expert_ids.shape[0]
    features = tokens.shape[1]
    capacity = 3 * group_rows * TOP // (2 * EXP_DEV * expert_size)
    highest = lax.Precision.HIGHEST
    scaled_own, inv_own = normalize(tokens)
    carried = (scaled_own * gain[None, :]).astype(jnp.bfloat16)
    group_first, group_grads = (
        lax.all_gather(carried, "tensor", axis=0, tiled=True),
        lax.all_gather(cotangent, "tensor", axis=0, tiled=True),
    )
    targets = jnp.arange(expert_size, dtype=jnp.int32) * EXP_DEV + my_type
    matches = expert_ids[:, :, None] == targets[None, None, :]
    chosen = jnp.any(matches, axis=1)
    weight_of = jnp.sum(jnp.where(matches, gate_probs[:, :, None], 0.0), axis=1)
    slot_of = jnp.sum(
        jnp.where(matches, jnp.arange(TOP, dtype=jnp.int32)[None, :, None], 0), axis=1
    )
    row_ids = jnp.arange(group_rows, dtype=jnp.int32)
    earlier = (row_ids[None, :] < row_ids[:, None]).astype(jnp.bfloat16)
    rank_in = jnp.dot(
        earlier, chosen.astype(jnp.bfloat16), preferred_element_type=jnp.float32
    ).astype(jnp.int32)
    placed = chosen.T[:, None, :] & (
        rank_in.T[:, None, :] == jnp.arange(capacity, dtype=jnp.int32)[None, :, None]
    )
    source = jnp.sum(jnp.where(placed, row_ids[None, None, :], 0), axis=2)
    filled = jnp.any(placed, axis=2)
    slot_prob = jnp.sum(jnp.where(placed, weight_of.T[:, None, :], 0.0), axis=2)
    slot_index = jnp.sum(jnp.where(placed, slot_of.T[:, None, :], 0), axis=2)
    sent_rows = jnp.where(
        filled[:, :, None], jnp.take(group_first, source, axis=0), jnp.zeros((), jnp.bfloat16)
    )
    sent_grads = (
        slot_prob[:, :, None] * jnp.take(group_grads, source, axis=0).astype(jnp.float32)
    ).astype(jnp.bfloat16)
    gate_up = gate_up_weight[0]
    down_proj = down_weight[0]
    arrived_rows, arrived_grads = (
        lax.all_to_all(sent_rows, "expert", split_axis=0, concat_axis=0, tiled=True),
        lax.all_to_all(sent_grads, "expert", split_axis=0, concat_axis=0, tiled=True),
    )
    rows = arrived_rows.reshape(-1, features)
    slot_grads = arrived_grads.reshape(-1, features)
    gate_pre, up_pre, sigmoid_gate, hidden, block_out = expert_forward(rows, gate_up, down_proj)
    out_slots = block_out.reshape(expert_size, capacity, features)
    input_grad, gate_up_part, down_part = expert_backward(
        rows, slot_grads, gate_up, down_proj, gate_pre, up_pre, sigmoid_gate, hidden
    )
    input_slots = input_grad.reshape(expert_size, capacity, features)
    out_back, input_back = (
        lax.all_to_all(out_slots, "expert", split_axis=0, concat_axis=0, tiled=True),
        lax.all_to_all(input_slots, "expert", split_axis=0, concat_axis=0, tiled=True),
    )
    out_flat = out_back.reshape(-1, features)
    input_flat = input_back.reshape(-1, features)
    used_source = source.reshape(-1)
    used_filled = filled.reshape(-1)
    used_prob = slot_prob.reshape(-1)
    used_index = slot_index.reshape(-1)
    cot_slots = jnp.take(group_grads, used_source, axis=0)
    prob_values = jnp.einsum("sd,sd->s", cot_slots, out_flat, preferred_element_type=jnp.float32)
    hit = (row_ids[:, None] == used_source[None, :]) & used_filled[None, :]
    input_part = jnp.dot(hit.astype(jnp.bfloat16), input_flat, preferred_element_type=jnp.float32)
    weighting = jnp.where(hit, used_prob[None, :], 0.0)
    out_part = jnp.dot(
        weighting,
        out_flat.astype(jnp.float32),
        precision=highest,
        preferred_element_type=jnp.float32,
    )
    prob_columns = jnp.where(
        used_index[:, None] == jnp.arange(TOP, dtype=jnp.int32)[None, :], prob_values[:, None], 0.0
    )
    prob_part = jnp.dot(
        hit.astype(jnp.float32), prob_columns, precision=highest, preferred_element_type=jnp.float32
    )
    out_sum, normed_grad, prob_grad = (
        lax.psum_scatter(out_part, "tensor", scatter_dimension=0, tiled=True),
        lax.psum_scatter(input_part, "tensor", scatter_dimension=0, tiled=True),
        lax.psum_scatter(prob_part, "tensor", scatter_dimension=0, tiled=True),
    )
    mixed = (tokens.astype(jnp.float32) + out_sum).astype(jnp.bfloat16)
    gain_side = normed_grad * gain[None, :]
    token_grad = (
        cotangent.astype(jnp.float32)
        + inv_own
        * (gain_side - scaled_own * jnp.mean(gain_side * scaled_own, axis=1, keepdims=True))
    ).astype(jnp.bfloat16)
    gain_grad = lax.psum(jnp.sum(normed_grad * scaled_own, axis=0), ("expert", "tensor"))
    return (mixed, token_grad, prob_grad, gain_grad, gate_up_part[None], down_part[None])


BOTH = ("expert", "tensor")


def flip_first(expert, core):
    return expert ^ (2 if core == 0 else 1)


def flip_second(expert, core):
    return expert ^ (1 if core == 0 else 2)


def send(array, place):
    pairs = []
    for expert in range(lax.axis_size("expert")):
        for core in range(2):
            to_expert, to_core = place(expert, core)
            pairs.append((expert * 2 + core, to_expert * 2 + to_core))
    return lax.ppermute(array, BOTH, pairs)


def send_first(array):
    return send(array, lambda e, c: (flip_first(e, c), c))


def send_second(array):
    return send(array, lambda e, c: (flip_second(e, c), c))


def send_bit(array, bit):
    return send(array, lambda e, c: (e ^ bit, c))


def send_core(array):
    return send(array, lambda e, c: (e, 1 - c))


def send_along(array, step):
    size = lax.axis_size("expert")
    return send(array, lambda e, c: ((e + 4 * step) % size, c))


def after(array, *others):
    return lax.optimization_barrier((array,) + others)[0]


def together(*arrays):
    return lax.optimization_barrier(arrays)


def add_up(*terms):
    return sum(term.astype(jnp.float32) for term in terms)


def narrow(value):
    return value.astype(jnp.bfloat16)


def plane_tables(table):
    pair = jnp.stack([table, send_second(table)])
    return jnp.stack([pair, send_first(pair)])


def far_first(array):
    far = array[:, :, 1:].reshape((-1,) + array.shape[3:])
    return jnp.concatenate([far, array[:, :, 0].reshape((-1,) + array.shape[3:])])


def from_far_first(array, steps):
    far = array[:4 * (steps - 1)].reshape((2, 2, steps - 1) + array.shape[1:])
    return jnp.concatenate([array[4 * (steps - 1):].reshape((2, 2, 1) + array.shape[1:]), far], axis=2)


def start(source, target, semaphore):
    copy = pltpu.make_async_copy(source, target, semaphore)
    copy.start()
    return copy


def chosen_rows(pick, mine, other):
    return jnp.dot(pick, jnp.concatenate([mine, other]), preferred_element_type=jnp.float32)


def norm_kernel(count, pick_ref, *refs):
    pieces, gain_ref, normed_ref = refs[:4], refs[4], refs[-1]

    def work(mine_ref, other_ref):
        for group in range(count):
            rows = chosen_rows(pick_ref[group], mine_ref[group], other_ref[group])
            inv_rms = lax.rsqrt(jnp.mean(rows * rows, axis=1, keepdims=True) + 1e-06)
            normed_ref[group] = (rows * inv_rms * gain_ref[...]).astype(jnp.bfloat16)

    by_place(work, pieces)


def grad_kernel(count, pick_ref, *refs):
    pieces, prob_ref, out_ref, (grad_ref, value_ref) = refs[:4], refs[4], refs[5], refs[-2:]

    def work(mine_ref, other_ref):
        for group in range(count):
            rows = chosen_rows(pick_ref[group], mine_ref[group], other_ref[group])
            grad_ref[group] = (rows * prob_ref[group]).astype(jnp.bfloat16)
            value_ref[group] = jnp.sum(rows * out_ref[group].astype(jnp.float32), axis=1, keepdims=True)

    by_place(work, pieces)


def by_place(work, pieces):
    for first in range(2):
        for second in range(2):
            pl.when(pl.program_id(0) == first * 2 + second)(
                functools.partial(work, pieces[first], pieces[2 + second])
            )


def group_spec(count, first_group, *shape):
    first_block = first_group // count
    return pl.BlockSpec((count,) + shape, lambda i: (first_block + i, 0, 0))


def select(kernel, pick, pieces, extras, extra_specs, out_shapes, count, arrays, which, first_group, held):
    _, capacity, group_rows = pick.shape
    half, features = pieces[0].shape[1:]

    def piece_spec(place):
        return pl.BlockSpec((count, half, features), lambda i: (place(i) * arrays + which, 0, 0))

    return pl.pallas_call(
        functools.partial(kernel, count),
        grid=(4,),
        in_specs=[
            group_spec(count, first_group, capacity, group_rows),
            piece_spec(lambda i: jnp.minimum(i, 1)),
            piece_spec(lambda i: jnp.maximum(i - 2, 0)),
            piece_spec(lambda i: i // 2),
            piece_spec(lambda i: jnp.maximum(i - 2, 0)),
        ] + extra_specs + [pl.BlockSpec(memory_space=pl.ANY)] * len(held),
        out_specs=[group_spec(count, first_group, *out.shape[1:]) for out in out_shapes],
        out_shape=out_shapes,
        input_output_aliases={5 + len(extras) + n: n for n in range(len(held))},
        compiler_params=pltpu.CompilerParams(vmem_limit_bytes=VMEM_LIMIT),
        cost_estimate=LITTLE,
    )(pick, *pieces, *extras, *held)


def select_normed(pick, gain, pieces, count, arrays, first_group, held):
    groups, capacity, _ = pick.shape
    features = pieces[0].shape[2]
    return select(
        norm_kernel, pick, pieces, [gain], [pl.BlockSpec((1, features), lambda i: (0, 0))],
        [jax.ShapeDtypeStruct((groups, capacity, features), jnp.bfloat16)],
        count, arrays, 0, first_group, held,
    )


def select_grads(pick, prob, out_slots, pieces, count, arrays, which, first_group, held):
    groups, capacity, _ = pick.shape
    features = pieces[0].shape[2]
    return select(
        grad_kernel, pick, pieces, [prob, out_slots],
        [group_spec(count, first_group, capacity, 1), group_spec(count, first_group, capacity, features)],
        [
            jax.ShapeDtypeStruct((groups, capacity, features), jnp.bfloat16),
            jax.ShapeDtypeStruct((groups, capacity, 1), jnp.float32),
        ],
        count, arrays, which, first_group, held,
    )


def expand_kernel(weighted, count, first_group, back_ref, prob_ref, *refs):
    arrays = len(weighted)
    sources, mine_ref, pieces = refs[:arrays], refs[arrays], refs[arrays + 1:arrays + 3]
    loaded, spread, loads, stores = refs[arrays + 3:]
    half = mine_ref.shape[1]
    copies, written = [], []
    for group in range(4 * count):
        for number, source in enumerate(sources):
            place = group * arrays + number
            copies.append(start(source.at[first_group + group], loaded.at[place], loads.at[place]))
    for group in range(4 * count):
        outer, inner = divmod(group, count)
        first, second = divmod(outer, 2)
        for number, by_prob in enumerate(weighted):
            place = group * arrays + number
            copies[place].wait()
            rows = loaded[place]
            if by_prob:
                rows = (rows.astype(jnp.float32) * prob_ref[first_group + group]).astype(jnp.bfloat16)
            spread[place] = jnp.dot(
                back_ref[first_group + group], rows, preferred_element_type=jnp.float32
            ).astype(jnp.bfloat16)
            target = pieces[second].at[(first * count + inner) * arrays + number]
            written += [
                start(spread.at[place, pl.ds(half, half)], target, stores.at[place, 0]),
                start(spread.at[place, pl.ds(0, half)], mine_ref.at[place], stores.at[place, 1]),
            ]
    for copy in written:
        copy.wait()


def expand(back, prob, slots, weighted, count, first_group):
    _, group_rows, capacity = back.shape
    half, features, arrays = group_rows // 2, slots[0].shape[2], len(slots)
    blocks = 4 * count * arrays
    anywhere, whole = pl.BlockSpec(memory_space=pl.ANY), pl.BlockSpec(memory_space=pltpu.VMEM)
    piece = jax.ShapeDtypeStruct((blocks // 2, half, features), jnp.bfloat16)
    return pl.pallas_call(
        functools.partial(expand_kernel, weighted, count, first_group),
        in_specs=[whole, whole] + [anywhere] * arrays,
        out_specs=[anywhere] * 3,
        out_shape=[jax.ShapeDtypeStruct((blocks, half, features), jnp.bfloat16), piece, piece],
        scratch_shapes=[
            pltpu.VMEM((blocks, capacity, features), jnp.bfloat16),
            pltpu.VMEM((blocks, group_rows, features), jnp.bfloat16),
            pltpu.SemaphoreType.DMA((blocks,)),
            pltpu.SemaphoreType.DMA((blocks, 2)),
        ],
        compiler_params=pltpu.CompilerParams(vmem_limit_bytes=VMEM_LIMIT),
        cost_estimate=LITTLE,
    )(back, prob, *slots)


def forward_kernel(rows_ref, gate_up_ref, down_ref, gate_pre_ref, up_pre_ref, hidden_ref, out_ref):
    projected = jnp.dot(rows_ref[...], gate_up_ref[0], preferred_element_type=jnp.float32)
    half_width = hidden_ref.shape[1]
    gate_pre, up_pre = projected[:, :half_width], projected[:, half_width:]
    gate_pre_ref[...] = gate_pre
    up_pre_ref[...] = up_pre
    hidden = (gate_pre * jax.nn.sigmoid(gate_pre) * up_pre).astype(jnp.bfloat16)
    hidden_ref[...] = hidden
    out_ref[...] = jnp.dot(hidden, down_ref[0], preferred_element_type=jnp.float32).astype(jnp.bfloat16)


def forward(rows, gate_up_weight, down_weight):
    slots, features = rows.shape
    width = down_weight.shape[1]
    block = slots // 2

    def row_spec(columns):
        return pl.BlockSpec((block, columns), lambda i: (i, 0))

    return pl.pallas_call(
        forward_kernel,
        grid=(2,),
        in_specs=[
            row_spec(features),
            pl.BlockSpec((1, features, 2 * width), lambda i: (0, 0, 0)),
            pl.BlockSpec((1, width, features), lambda i: (0, 0, 0)),
        ],
        out_specs=[row_spec(width), row_spec(width), row_spec(width), row_spec(features)],
        out_shape=[
            jax.ShapeDtypeStruct((slots, width), jnp.float32),
            jax.ShapeDtypeStruct((slots, width), jnp.float32),
            jax.ShapeDtypeStruct((slots, width), jnp.bfloat16),
            jax.ShapeDtypeStruct((slots, features), jnp.bfloat16),
        ],
        compiler_params=pltpu.CompilerParams(vmem_limit_bytes=VMEM_LIMIT),
        cost_estimate=LITTLE,
    )(rows, gate_up_weight, down_weight)


def backward_kernel(
    units, grads_ref, gate_pre_ref, up_pre_ref, down_ref, gate_up_ref, rows_ref, joined_ref, input_ref, gain_ref
):
    step = pl.program_id(0)
    block = gate_pre_ref.shape[1]

    @pl.when(step < units)
    def _():
        gate_pre, up_pre = gate_pre_ref[...], up_pre_ref[...]
        sigmoid_gate = jax.nn.sigmoid(gate_pre)
        common = times_transposed(grads_ref[...], down_ref[0]) * sigmoid_gate
        gate_grad = common * up_pre * (1.0 + gate_pre * (1.0 - sigmoid_gate))
        start = pl.multiple_of(step * block, block)
        joined_ref[:, pl.ds(start, block)] = gate_grad.astype(jnp.bfloat16)
        joined_ref[:, pl.ds(units * block + start, block)] = (common * gate_pre).astype(jnp.bfloat16)

    @pl.when(step >= units)
    def _():
        input_grad = times_transposed(joined_ref[...], gate_up_ref[0]).astype(jnp.bfloat16)
        input_ref[...] = input_grad
        terms = input_grad.astype(jnp.float32) * rows_ref[...].astype(jnp.float32)
        gain_ref[...] = jnp.sum(terms, axis=0, keepdims=True)


def backward(grads, gate_pre, up_pre, rows, gate_up_weight, down_weight):
    slots, features = rows.shape
    width = down_weight.shape[1]
    block, units, wide = 256, width // 256, features // 4
    early = lambda i: jnp.minimum(i, units - 1)
    late = lambda i: jnp.maximum(i - units, 0)
    return pl.pallas_call(
        functools.partial(backward_kernel, units),
        grid=(units + 4,),
        in_specs=[
            pl.BlockSpec((slots, features), lambda i: (0, 0)),
            pl.BlockSpec((slots, block), lambda i: (0, early(i))),
            pl.BlockSpec((slots, block), lambda i: (0, early(i))),
            pl.BlockSpec((1, block, features), lambda i: (0, early(i), 0)),
            pl.BlockSpec((1, wide, 2 * width), lambda i: (0, late(i), 0)),
            pl.BlockSpec((slots, wide), lambda i: (0, late(i))),
        ],
        out_specs=[
            pl.BlockSpec((slots, 2 * width), lambda i: (0, 0)),
            pl.BlockSpec((slots, wide), lambda i: (0, late(i))),
            pl.BlockSpec((1, wide), lambda i: (0, late(i))),
        ],
        out_shape=[
            jax.ShapeDtypeStruct((slots, 2 * width), jnp.bfloat16),
            jax.ShapeDtypeStruct((slots, features), jnp.bfloat16),
            jax.ShapeDtypeStruct((1, features), jnp.float32),
        ],
        compiler_params=pltpu.CompilerParams(vmem_limit_bytes=VMEM_LIMIT),
        cost_estimate=LITTLE,
    )(grads, gate_pre, up_pre, down_weight, gate_up_weight, rows)


def pack(columns, gains):
    return jnp.concatenate([columns.reshape(-1, 128), gains])


def unpack_add(columns, gains, got):
    count = gains.shape[0]
    return columns + got[:-count].reshape(columns.shape), gains + got[-count:]


def planes_in_order(gains):
    steps = len(gains)
    order = (lax.axis_index("expert") // 4 - jnp.arange(steps)) % steps
    ordered = jnp.take(jnp.stack(gains), order, axis=0)
    return functools.reduce(jnp.add, [ordered[step] for step in range(steps)]).reshape(-1)


def broadcast_shards(tokens, cotangent, gain, expert_ids, gate_probs, gate_up_weight, down_weight):
    expert_size = lax.axis_size("expert")
    steps = expert_size // 4
    far = 4 * (steps - 1)
    expert, core = lax.axis_index("expert"), lax.axis_index("tensor")
    my_expert = expert * EXP_DEV + core
    group_rows = expert_ids.shape[0]
    half = group_rows // 2
    features = tokens.shape[1]
    capacity = 3 * group_rows * TOP // (2 * EXP_DEV * expert_size)
    near_own = jnp.stack([tokens, cotangent])
    near_pair = jnp.concatenate([near_own, send_second(near_own)])
    near_far_pair = send_first(near_pair)
    tables = plane_tables(
        after(jnp.concatenate([expert_ids.T.astype(jnp.float32), gate_probs.T]), near_pair)
    )
    token_far = after(jnp.stack([send_along(tokens, -step) for step in range(1, steps)]), tables)
    late_tables = after(tables, token_far)
    far_tables = [send_along(late_tables, -step) for step in range(1, steps)]
    late_cot = after(cotangent, token_far)
    cot_steps = [send_along(late_cot, -step) for step in range(1, steps)]
    token_second = after(send_second(token_far), near_far_pair, cot_steps[len(cot_steps) // 2], *far_tables)
    token_pair = jnp.concatenate([token_far, token_second])
    tables = far_first(jnp.stack([tables] + far_tables, axis=2))
    tables = jnp.where(core == 0, tables, jnp.roll(tables, half, axis=2))
    matches = tables[:, :TOP] == my_expert.astype(jnp.float32)
    chosen = jnp.any(matches, axis=1)
    weight_of = jnp.sum(jnp.where(matches, tables[:, TOP:], 0.0), axis=1)
    row_ids = jnp.arange(group_rows, dtype=jnp.int32)
    earlier = (row_ids[:, None] < row_ids[None, :]).astype(jnp.bfloat16)
    rank_in = jnp.dot(chosen.astype(jnp.bfloat16), earlier, preferred_element_type=jnp.float32)
    placed = chosen[:, None, :] & (
        rank_in.astype(jnp.int32)[:, None, :] == jnp.arange(capacity, dtype=jnp.int32)[None, :, None]
    )
    pick = placed.astype(jnp.bfloat16)
    back = jnp.swapaxes(pick, 1, 2)
    slot_prob = jnp.sum(jnp.where(placed, weight_of[:, None, :], 0.0), axis=2, keepdims=True)

    gain_row = gain[None, :]
    near_pieces = (near_pair, near_far_pair, send_core(near_pair), send_core(near_far_pair))
    rows, = select_normed(pick, gain_row, near_pieces, 1, 2, far, ())
    cot_steps = together(*cot_steps, rows)
    rows, cot_far = cot_steps[-1], jnp.stack(cot_steps[:-1])
    token_far_pair, cot_far = together(send_first(token_pair), cot_far)
    cot_second = send_second(cot_far)
    token_pieces = (token_pair, token_far_pair, send_core(token_pair), send_core(token_far_pair))
    rows, = select_normed(pick, gain_row, token_pieces, steps - 1, 1, 0, (rows,))
    rows, cot_second = together(rows, cot_second)
    cot_pair = jnp.concatenate([cot_far, cot_second])
    cot_far_pair = send_first(cot_pair)

    rows = rows.reshape(-1, features)
    gate_pre, up_pre, hidden, block_out = forward(rows, gate_up_weight, down_weight)
    block_out, cot_far_pair = together(block_out, cot_far_pair)
    cot_pieces = (cot_pair, cot_far_pair, send_core(cot_pair), send_core(cot_far_pair))
    out_slots = block_out.reshape(expert_size, capacity, features)
    out_mine, out_low, out_high = expand(back, slot_prob, (out_slots,), (True,), steps - 1, 0)

    half_far, one_far = 2 * (steps - 1), steps - 1
    own_mine, own_low, own_high = expand(
        back, after(slot_prob, out_high), (out_slots,), (True,), 1, far
    )
    own_core_high = send_core(own_high)
    own_core = send_core(own_low)
    held = select_grads(
        after(pick, out_high), slot_prob, out_slots, near_pieces, 1, 2, 1, far, ()
    )
    out_core_high = after(send_core(out_high), own_high, held[1])
    out_core = send_core(out_low)
    out_upper = narrow(add_up(out_mine[half_far:], out_core_high))
    out_first = send_first(out_upper)
    own_upper = narrow(add_up(own_mine[2:], after(own_core_high, out_upper)))
    own_first = send_first(own_upper)
    grads, prob_value = select_grads(
        after(pick, own_upper), slot_prob, out_slots, cot_pieces, steps - 1, 1, 0, 0, tuple(held)
    )
    grads = grads.reshape(-1, features)
    joined_grad, input_grad, gain_term = backward(
        grads, gate_pre, up_pre, rows, gate_up_weight, down_weight
    )
    input_grad, out_first, own_first = together(input_grad, out_first, own_first)
    input_slots = input_grad.reshape(expert_size, capacity, features)
    out_middle = narrow(
        add_up(out_mine[one_far:half_far], out_core[one_far:half_far], out_first[one_far:])
    )
    out_second = send_second(out_middle)
    in_mine, in_low, in_high = expand(back, after(slot_prob, out_middle), (input_slots,), (False,), steps - 1, 0)
    own_middle = narrow(add_up(own_mine[1:2], own_core[1:], own_first[1:]))
    own_second = send_second(own_middle)
    in_high, out_second, own_second = together(in_high, out_second, own_second)
    in_core_high = send_core(in_high)
    in_core = send_core(in_low)
    def own_plane(mine, core_part, first_part, second_part, count):
        return add_up(mine[:count], core_part[:count], first_part[:count], second_part[:count])

    out_planes = narrow(own_plane(out_mine, out_core, out_first, out_second, one_far))
    out_far = [send_along(out_planes[step - 1], step) for step in range(1, steps)]
    near_mine, near_low, near_high = expand(
        back, after(slot_prob, in_high), (input_slots,), (False,), 1, far
    )
    near_core_high = send_core(near_high)
    near_core = send_core(near_low)
    in_upper = narrow(add_up(in_mine[half_far:], after(in_core_high, out_middle, near_high)))
    in_first = send_first(in_upper)
    gains = (gain_term[0] / gain).reshape(-1, 128)
    prob_rows = jnp.sum(jnp.where(placed, prob_value, 0.0), axis=1)
    columns = from_far_first(jnp.where(matches, prob_rows[:, None, :], 0.0), steps)
    columns = jnp.where(core == 0, columns, jnp.swapaxes(columns, 0, 1))
    got = send_core(after(pack(columns[..., half:], gains), in_upper))
    down_part = outer_sum(after(hidden, in_upper), grads)

    down_part, got = together(down_part, got)
    columns, gains = unpack_add(columns[..., :half], gains, got)
    got = send_bit(pack(columns[1], gains), 2)
    gate_up_part = outer_sum(after(rows, in_upper), joined_grad)
    in_first, near_core, gate_up_part, got = together(
        in_first, near_core, gate_up_part, got, *out_far
    )[:4]
    columns, gains = unpack_add(columns[0], gains, got)
    in_middle = narrow(
        add_up(in_mine[one_far:half_far], in_core[one_far:half_far], in_first[one_far:])
    )
    in_second = send_second(in_middle)
    got = send_bit(pack(columns[1], gains), 1)
    in_second, got = together(in_second, got)
    columns, gains = unpack_add(columns[0], gains, got)
    in_planes = narrow(own_plane(in_mine, in_core, in_first, in_second, one_far))
    messages = [send_along(pack(columns[step], gains), step) for step in range(1, steps)]
    in_far = [send_along(in_planes[step - 1], step) for step in range(1, steps)]
    near_upper = narrow(add_up(near_mine[2:], after(near_core_high, in_planes)))
    near_first = send_first(near_upper)
    near_middle = narrow(add_up(near_mine[1:2], near_core[1:], near_first[1:]))
    near_second = send_second(near_middle)
    out_sum = own_plane(own_mine, own_core, own_first, own_second, 1)[0] + add_up(*out_far)
    normed_grad = own_plane(near_mine, near_core, near_first, near_second, 1)[0] + add_up(*in_far)

    prob_sum, all_gains = columns[0], [gains]
    for message in messages:
        prob_sum = prob_sum + message[:-gains.shape[0]].reshape(prob_sum.shape)
        all_gains.append(message[-gains.shape[0]:])
    gain_grad = planes_in_order(all_gains)

    scaled_own, inv_own = normalize(tokens)
    mixed = (tokens.astype(jnp.float32) + out_sum).astype(jnp.bfloat16)
    gain_side = normed_grad * gain[None, :]
    token_grad = (
        cotangent.astype(jnp.float32)
        + inv_own
        * (gain_side - scaled_own * jnp.mean(gain_side * scaled_own, axis=1, keepdims=True))
    ).astype(jnp.bfloat16)
    return (mixed, token_grad, prob_sum.T, gain_grad, gate_up_part[None], down_part[None])


def solution(mesh):
    in_specs = (
        P(("expert", "tensor"), None),
        P(("expert", "tensor"), None),
        P(),
        P("expert", None),
        P("expert", None),
        P(("expert", "tensor"), None, None),
        P(("expert", "tensor"), None, None),
    )
    out_specs = (
        P(("expert", "tensor"), None),
        P(("expert", "tensor"), None),
        P(("expert", "tensor"), None),
        P(),
        P(("expert", "tensor"), None, None),
        P(("expert", "tensor"), None, None),
    )
    expert_size, tensor_size = mesh.shape["expert"], mesh.shape["tensor"]
    few = tensor_size == EXP_DEV and expert_size % 4 == 0 and expert_size <= 4 * TOP
    shards = broadcast_shards if few else routed_shards
    return jax.shard_map(shards, mesh=mesh, in_specs=in_specs, out_specs=out_specs, check_vma=False)
```

```python
import functools

import jax
import jax.numpy as jnp
from jax import lax
from jax.experimental import pallas as pl
from jax.experimental.pallas import tpu as pltpu
from jax.sharding import PartitionSpec as P

TOP = 8
EXP_DEV = 2
VMEM_LIMIT = 63 * 1024 * 1024
LITTLE = pl.CostEstimate(flops=1000000, bytes_accessed=100000, transcendentals=0)


def normalize(rows):
    values = rows.astype(jnp.float32)
    inv_rms = lax.rsqrt(jnp.mean(values * values, axis=1, keepdims=True) + 1e-06)
    return (values * inv_rms, inv_rms)


def expert_forward(rows, gate_up, down_proj):
    projected = jnp.dot(rows, gate_up, preferred_element_type=jnp.float32)
    half_width = down_proj.shape[0]
    gate_pre = projected[:, :half_width]
    up_pre = projected[:, half_width:]
    sigmoid_gate = jax.nn.sigmoid(gate_pre)
    hidden = (gate_pre * sigmoid_gate * up_pre).astype(jnp.bfloat16)
    block_out = jnp.dot(hidden, down_proj, preferred_element_type=jnp.float32).astype(jnp.bfloat16)
    return (gate_pre, up_pre, sigmoid_gate, hidden, block_out)


def times_transposed(left, right):
    return lax.dot_general(left, right, (((1,), (1,)), ((), ())), preferred_element_type=jnp.float32)


def outer_sum(left, right):
    product = lax.dot_general(left, right, (((0,), (0,)), ((), ())), preferred_element_type=jnp.float32)
    return product.astype(jnp.bfloat16)


def backward_inner(slot_grads, down_proj, gate_pre, up_pre, sigmoid_gate):
    hidden_grad = times_transposed(slot_grads, down_proj)
    gate_grad = (
        hidden_grad * up_pre * sigmoid_gate * (1.0 + gate_pre * (1.0 - sigmoid_gate))
    ).astype(jnp.bfloat16)
    up_grad = (hidden_grad * gate_pre * sigmoid_gate).astype(jnp.bfloat16)
    return jnp.concatenate([gate_grad, up_grad], axis=1)


def expert_backward(rows, slot_grads, gate_up, down_proj, gate_pre, up_pre, sigmoid_gate, hidden):
    joined_grad = backward_inner(slot_grads, down_proj, gate_pre, up_pre, sigmoid_gate)
    input_grad = times_transposed(joined_grad, gate_up).astype(jnp.bfloat16)
    return (input_grad, outer_sum(rows, joined_grad), outer_sum(hidden, slot_grads))


def routed_shards(tokens, cotangent, gain, expert_ids, gate_probs, gate_up_weight, down_weight):
    tensor_size = lax.axis_size("tensor")
    expert_size = lax.axis_size("expert")
    my_rank = lax.axis_index("tensor")
    blocks_each = tensor_size // EXP_DEV
    my_type = my_rank // blocks_each
    group_rows = expert_ids.shape[0]
    features = tokens.shape[1]
    capacity = 3 * group_rows * TOP // (2 * EXP_DEV * expert_size)
    highest = lax.Precision.HIGHEST
    scaled_own, inv_own = normalize(tokens)
    carried = (scaled_own * gain[None, :]).astype(jnp.bfloat16)
    group_first, group_grads = (
        lax.all_gather(carried, "tensor", axis=0, tiled=True),
        lax.all_gather(cotangent, "tensor", axis=0, tiled=True),
    )
    targets = jnp.arange(expert_size, dtype=jnp.int32) * EXP_DEV + my_type
    matches = expert_ids[:, :, None] == targets[None, None, :]
    chosen = jnp.any(matches, axis=1)
    weight_of = jnp.sum(jnp.where(matches, gate_probs[:, :, None], 0.0), axis=1)
    slot_of = jnp.sum(
        jnp.where(matches, jnp.arange(TOP, dtype=jnp.int32)[None, :, None], 0), axis=1
    )
    row_ids = jnp.arange(group_rows, dtype=jnp.int32)
    earlier = (row_ids[None, :] < row_ids[:, None]).astype(jnp.bfloat16)
    rank_in = jnp.dot(
        earlier, chosen.astype(jnp.bfloat16), preferred_element_type=jnp.float32
    ).astype(jnp.int32)
    placed = chosen.T[:, None, :] & (
        rank_in.T[:, None, :] == jnp.arange(capacity, dtype=jnp.int32)[None, :, None]
    )
    source = jnp.sum(jnp.where(placed, row_ids[None, None, :], 0), axis=2)
    filled = jnp.any(placed, axis=2)
    slot_prob = jnp.sum(jnp.where(placed, weight_of.T[:, None, :], 0.0), axis=2)
    slot_index = jnp.sum(jnp.where(placed, slot_of.T[:, None, :], 0), axis=2)
    sent_rows = jnp.where(
        filled[:, :, None], jnp.take(group_first, source, axis=0), jnp.zeros((), jnp.bfloat16)
    )
    sent_grads = (
        slot_prob[:, :, None] * jnp.take(group_grads, source, axis=0).astype(jnp.float32)
    ).astype(jnp.bfloat16)
    gate_up = gate_up_weight[0]
    down_proj = down_weight[0]
    arrived_rows, arrived_grads = (
        lax.all_to_all(sent_rows, "expert", split_axis=0, concat_axis=0, tiled=True),
        lax.all_to_all(sent_grads, "expert", split_axis=0, concat_axis=0, tiled=True),
    )
    rows = arrived_rows.reshape(-1, features)
    slot_grads = arrived_grads.reshape(-1, features)
    gate_pre, up_pre, sigmoid_gate, hidden, block_out = expert_forward(rows, gate_up, down_proj)
    out_slots = block_out.reshape(expert_size, capacity, features)
    input_grad, gate_up_part, down_part = expert_backward(
        rows, slot_grads, gate_up, down_proj, gate_pre, up_pre, sigmoid_gate, hidden
    )
    input_slots = input_grad.reshape(expert_size, capacity, features)
    out_back, input_back = (
        lax.all_to_all(out_slots, "expert", split_axis=0, concat_axis=0, tiled=True),
        lax.all_to_all(input_slots, "expert", split_axis=0, concat_axis=0, tiled=True),
    )
    out_flat = out_back.reshape(-1, features)
    input_flat = input_back.reshape(-1, features)
    used_source = source.reshape(-1)
    used_filled = filled.reshape(-1)
    used_prob = slot_prob.reshape(-1)
    used_index = slot_index.reshape(-1)
    cot_slots = jnp.take(group_grads, used_source, axis=0)
    prob_values = jnp.einsum("sd,sd->s", cot_slots, out_flat, preferred_element_type=jnp.float32)
    hit = (row_ids[:, None] == used_source[None, :]) & used_filled[None, :]
    input_part = jnp.dot(hit.astype(jnp.bfloat16), input_flat, preferred_element_type=jnp.float32)
    weighting = jnp.where(hit, used_prob[None, :], 0.0)
    out_part = jnp.dot(
        weighting,
        out_flat.astype(jnp.float32),
        precision=highest,
        preferred_element_type=jnp.float32,
    )
    prob_columns = jnp.where(
        used_index[:, None] == jnp.arange(TOP, dtype=jnp.int32)[None, :], prob_values[:, None], 0.0
    )
    prob_part = jnp.dot(
        hit.astype(jnp.float32), prob_columns, precision=highest, preferred_element_type=jnp.float32
    )
    out_sum, normed_grad, prob_grad = (
        lax.psum_scatter(out_part, "tensor", scatter_dimension=0, tiled=True),
        lax.psum_scatter(input_part, "tensor", scatter_dimension=0, tiled=True),
        lax.psum_scatter(prob_part, "tensor", scatter_dimension=0, tiled=True),
    )
    mixed = (tokens.astype(jnp.float32) + out_sum).astype(jnp.bfloat16)
    gain_side = normed_grad * gain[None, :]
    token_grad = (
        cotangent.astype(jnp.float32)
        + inv_own
        * (gain_side - scaled_own * jnp.mean(gain_side * scaled_own, axis=1, keepdims=True))
    ).astype(jnp.bfloat16)
    gain_grad = lax.psum(jnp.sum(normed_grad * scaled_own, axis=0), ("expert", "tensor"))
    return (mixed, token_grad, prob_grad, gain_grad, gate_up_part[None], down_part[None])


BOTH = ("expert", "tensor")


def flip_first(expert, core):
    return expert ^ (2 if core == 0 else 1)


def flip_second(expert, core):
    return expert ^ (1 if core == 0 else 2)


def send(array, place):
    pairs = []
    for expert in range(lax.axis_size("expert")):
        for core in range(2):
            to_expert, to_core = place(expert, core)
            pairs.append((expert * 2 + core, to_expert * 2 + to_core))
    return lax.ppermute(array, BOTH, pairs)


def send_first(array):
    return send(array, lambda e, c: (flip_first(e, c), c))


def send_second(array):
    return send(array, lambda e, c: (flip_second(e, c), c))


def send_bit(array, bit):
    return send(array, lambda e, c: (e ^ bit, c))


def send_core(array):
    return send(array, lambda e, c: (e, 1 - c))


def send_along(array, step):
    size = lax.axis_size("expert")
    return send(array, lambda e, c: ((e + 4 * step) % size, c))


def after(array, *others):
    return lax.optimization_barrier((array,) + others)[0]


def together(*arrays):
    return lax.optimization_barrier(arrays)


def add_up(*terms):
    return sum(term.astype(jnp.float32) for term in terms)


def narrow(value):
    return value.astype(jnp.bfloat16)


def plane_tables(table):
    pair = jnp.stack([table, send_second(table)])
    return jnp.stack([pair, send_first(pair)])


def far_first(array):
    far = array[:, :, 1:].reshape((-1,) + array.shape[3:])
    return jnp.concatenate([far, array[:, :, 0].reshape((-1,) + array.shape[3:])])


def from_far_first(array, steps):
    far = array[:4 * (steps - 1)].reshape((2, 2, steps - 1) + array.shape[1:])
    return jnp.concatenate([array[4 * (steps - 1):].reshape((2, 2, 1) + array.shape[1:]), far], axis=2)


def start(source, target, semaphore):
    copy = pltpu.make_async_copy(source, target, semaphore)
    copy.start()
    return copy


def chosen_rows(pick, mine, other):
    return jnp.dot(pick, jnp.concatenate([mine, other]), preferred_element_type=jnp.float32)


def norm_kernel(count, pick_ref, *refs):
    pieces, gain_ref, normed_ref = refs[:4], refs[4], refs[-1]

    def work(mine_ref, other_ref):
        for group in range(count):
            rows = chosen_rows(pick_ref[group], mine_ref[group], other_ref[group])
            inv_rms = lax.rsqrt(jnp.mean(rows * rows, axis=1, keepdims=True) + 1e-06)
            normed_ref[group] = (rows * inv_rms * gain_ref[...]).astype(jnp.bfloat16)

    by_place(work, pieces)


def grad_kernel(count, pick_ref, *refs):
    pieces, prob_ref, out_ref, (grad_ref, value_ref) = refs[:4], refs[4], refs[5], refs[-2:]

    def work(mine_ref, other_ref):
        for group in range(count):
            rows = chosen_rows(pick_ref[group], mine_ref[group], other_ref[group])
            grad_ref[group] = (rows * prob_ref[group]).astype(jnp.bfloat16)
            value_ref[group] = jnp.sum(rows * out_ref[group].astype(jnp.float32), axis=1, keepdims=True)

    by_place(work, pieces)


def by_place(work, pieces):
    for first in range(2):
        for second in range(2):
            pl.when(pl.program_id(0) == first * 2 + second)(
                functools.partial(work, pieces[first], pieces[2 + second])
            )


def group_spec(count, first_group, *shape):
    first_block = first_group // count
    return pl.BlockSpec((count,) + shape, lambda i: (first_block + i, 0, 0))


def select(kernel, pick, pieces, extras, extra_specs, out_shapes, count, arrays, which, first_group, held):
    _, capacity, group_rows = pick.shape
    half, features = pieces[0].shape[1:]

    def piece_spec(place):
        return pl.BlockSpec((count, half, features), lambda i: (place(i) * arrays + which, 0, 0))

    return pl.pallas_call(
        functools.partial(kernel, count),
        grid=(4,),
        in_specs=[
            group_spec(count, first_group, capacity, group_rows),
            piece_spec(lambda i: jnp.minimum(i, 1)),
            piece_spec(lambda i: jnp.maximum(i - 2, 0)),
            piece_spec(lambda i: i // 2),
            piece_spec(lambda i: jnp.maximum(i - 2, 0)),
        ] + extra_specs + [pl.BlockSpec(memory_space=pl.ANY)] * len(held),
        out_specs=[group_spec(count, first_group, *out.shape[1:]) for out in out_shapes],
        out_shape=out_shapes,
        input_output_aliases={5 + len(extras) + n: n for n in range(len(held))},
        compiler_params=pltpu.CompilerParams(vmem_limit_bytes=VMEM_LIMIT),
        cost_estimate=LITTLE,
    )(pick, *pieces, *extras, *held)


def select_normed(pick, gain, pieces, count, arrays, first_group, held):
    groups, capacity, _ = pick.shape
    features = pieces[0].shape[2]
    return select(
        norm_kernel, pick, pieces, [gain], [pl.BlockSpec((1, features), lambda i: (0, 0))],
        [jax.ShapeDtypeStruct((groups, capacity, features), jnp.bfloat16)],
        count, arrays, 0, first_group, held,
    )


def select_grads(pick, prob, out_slots, pieces, count, arrays, which, first_group, held):
    groups, capacity, _ = pick.shape
    features = pieces[0].shape[2]
    return select(
        grad_kernel, pick, pieces, [prob, out_slots],
        [group_spec(count, first_group, capacity, 1), group_spec(count, first_group, capacity, features)],
        [
            jax.ShapeDtypeStruct((groups, capacity, features), jnp.bfloat16),
            jax.ShapeDtypeStruct((groups, capacity, 1), jnp.float32),
        ],
        count, arrays, which, first_group, held,
    )


def expand_kernel(weighted, count, first_group, back_ref, prob_ref, *refs):
    arrays = len(weighted)
    sources, mine_ref, pieces = refs[:arrays], refs[arrays], refs[arrays + 1:arrays + 3]
    loaded, spread, loads, stores = refs[arrays + 3:]
    half = mine_ref.shape[1]
    copies, written = [], []
    for group in range(4 * count):
        for number, source in enumerate(sources):
            place = group * arrays + number
            copies.append(start(source.at[first_group + group], loaded.at[place], loads.at[place]))
    for group in range(4 * count):
        outer, inner = divmod(group, count)
        first, second = divmod(outer, 2)
        for number, by_prob in enumerate(weighted):
            place = group * arrays + number
            copies[place].wait()
            rows = loaded[place]
            if by_prob:
                rows = (rows.astype(jnp.float32) * prob_ref[first_group + group]).astype(jnp.bfloat16)
            spread[place] = jnp.dot(
                back_ref[first_group + group], rows, preferred_element_type=jnp.float32
            ).astype(jnp.bfloat16)
            target = pieces[second].at[(first * count + inner) * arrays + number]
            written += [
                start(spread.at[place, pl.ds(half, half)], target, stores.at[place, 0]),
                start(spread.at[place, pl.ds(0, half)], mine_ref.at[place], stores.at[place, 1]),
            ]
    for copy in written:
        copy.wait()


def expand(back, prob, slots, weighted, count, first_group):
    _, group_rows, capacity = back.shape
    half, features, arrays = group_rows // 2, slots[0].shape[2], len(slots)
    blocks = 4 * count * arrays
    anywhere, whole = pl.BlockSpec(memory_space=pl.ANY), pl.BlockSpec(memory_space=pltpu.VMEM)
    piece = jax.ShapeDtypeStruct((blocks // 2, half, features), jnp.bfloat16)
    return pl.pallas_call(
        functools.partial(expand_kernel, weighted, count, first_group),
        in_specs=[whole, whole] + [anywhere] * arrays,
        out_specs=[anywhere] * 3,
        out_shape=[jax.ShapeDtypeStruct((blocks, half, features), jnp.bfloat16), piece, piece],
        scratch_shapes=[
            pltpu.VMEM((blocks, capacity, features), jnp.bfloat16),
            pltpu.VMEM((blocks, group_rows, features), jnp.bfloat16),
            pltpu.SemaphoreType.DMA((blocks,)),
            pltpu.SemaphoreType.DMA((blocks, 2)),
        ],
        compiler_params=pltpu.CompilerParams(vmem_limit_bytes=VMEM_LIMIT),
        cost_estimate=LITTLE,
    )(back, prob, *slots)


def forward_kernel(rows_ref, gate_up_ref, down_ref, gate_pre_ref, up_pre_ref, hidden_ref, out_ref):
    projected = jnp.dot(rows_ref[...], gate_up_ref[0], preferred_element_type=jnp.float32)
    half_width = hidden_ref.shape[1]
    gate_pre, up_pre = projected[:, :half_width], projected[:, half_width:]
    gate_pre_ref[...] = gate_pre
    up_pre_ref[...] = up_pre
    hidden = (gate_pre * jax.nn.sigmoid(gate_pre) * up_pre).astype(jnp.bfloat16)
    hidden_ref[...] = hidden
    out_ref[...] = jnp.dot(hidden, down_ref[0], preferred_element_type=jnp.float32).astype(jnp.bfloat16)


def forward(rows, gate_up_weight, down_weight):
    slots, features = rows.shape
    width = down_weight.shape[1]
    block = slots // 2

    def row_spec(columns):
        return pl.BlockSpec((block, columns), lambda i: (i, 0))

    return pl.pallas_call(
        forward_kernel,
        grid=(2,),
        in_specs=[
            row_spec(features),
            pl.BlockSpec((1, features, 2 * width), lambda i: (0, 0, 0)),
            pl.BlockSpec((1, width, features), lambda i: (0, 0, 0)),
        ],
        out_specs=[row_spec(width), row_spec(width), row_spec(width), row_spec(features)],
        out_shape=[
            jax.ShapeDtypeStruct((slots, width), jnp.float32),
            jax.ShapeDtypeStruct((slots, width), jnp.float32),
            jax.ShapeDtypeStruct((slots, width), jnp.bfloat16),
            jax.ShapeDtypeStruct((slots, features), jnp.bfloat16),
        ],
        compiler_params=pltpu.CompilerParams(vmem_limit_bytes=VMEM_LIMIT),
        cost_estimate=LITTLE,
    )(rows, gate_up_weight, down_weight)


def inner_kernel(units, grads_ref, gate_pre_ref, up_pre_ref, down_ref, joined_ref):
    step = pl.program_id(0)
    block = gate_pre_ref.shape[1]
    gate_pre, up_pre = gate_pre_ref[...], up_pre_ref[...]
    sigmoid_gate = jax.nn.sigmoid(gate_pre)
    common = times_transposed(grads_ref[...], down_ref[0]) * sigmoid_gate
    gate_grad = common * up_pre * (1.0 + gate_pre * (1.0 - sigmoid_gate))
    start = pl.multiple_of(step * block, block)
    joined_ref[:, pl.ds(start, block)] = gate_grad.astype(jnp.bfloat16)
    joined_ref[:, pl.ds(units * block + start, block)] = (common * gate_pre).astype(jnp.bfloat16)


def backward_hidden(grads, gate_pre, up_pre, down_weight):
    slots, features = grads.shape
    width = down_weight.shape[1]
    block, units = 256, width // 256
    return pl.pallas_call(
        functools.partial(inner_kernel, units),
        grid=(units,),
        in_specs=[
            pl.BlockSpec((slots, features), lambda i: (0, 0)),
            pl.BlockSpec((slots, block), lambda i: (0, i)),
            pl.BlockSpec((slots, block), lambda i: (0, i)),
            pl.BlockSpec((1, block, features), lambda i: (0, i, 0)),
        ],
        out_specs=pl.BlockSpec((slots, 2 * width), lambda i: (0, 0)),
        out_shape=jax.ShapeDtypeStruct((slots, 2 * width), jnp.bfloat16),
        compiler_params=pltpu.CompilerParams(vmem_limit_bytes=VMEM_LIMIT),
        cost_estimate=LITTLE,
    )(grads, gate_pre, up_pre, down_weight)


def input_kernel(joined_ref, gate_up_ref, rows_ref, *refs):
    input_ref, gain_ref = refs[-2:]
    input_grad = times_transposed(joined_ref[...], gate_up_ref[0]).astype(jnp.bfloat16)
    input_ref[...] = input_grad
    terms = input_grad.astype(jnp.float32) * rows_ref[...].astype(jnp.float32)
    gain_ref[...] = jnp.sum(terms, axis=0, keepdims=True)


def backward_input(joined_grad, gate_up_weight, rows, part, held):
    slots, features = rows.shape
    width = joined_grad.shape[1]
    wide = features // 4
    first = 2 * part
    return pl.pallas_call(
        input_kernel,
        grid=(2,),
        in_specs=[
            pl.BlockSpec((slots, width), lambda i: (0, 0)),
            pl.BlockSpec((1, wide, width), lambda i: (0, first + i, 0)),
            pl.BlockSpec((slots, wide), lambda i: (0, first + i)),
        ] + [pl.BlockSpec(memory_space=pl.ANY)] * len(held),
        out_specs=[
            pl.BlockSpec((slots, wide), lambda i: (0, first + i)),
            pl.BlockSpec((1, wide), lambda i: (0, i)),
        ],
        out_shape=[
            jax.ShapeDtypeStruct((slots, features), jnp.bfloat16),
            jax.ShapeDtypeStruct((1, features // 2), jnp.float32),
        ],
        input_output_aliases={3 + n: n for n in range(len(held))},
        compiler_params=pltpu.CompilerParams(vmem_limit_bytes=VMEM_LIMIT),
        cost_estimate=LITTLE,
    )(joined_grad, gate_up_weight, rows, *held)


def pack(columns, gains):
    return jnp.concatenate([columns.reshape(-1, 128), gains])


def unpack_add(columns, gains, got):
    count = gains.shape[0]
    return columns + got[:-count].reshape(columns.shape), gains + got[-count:]


def planes_in_order(gains):
    steps = len(gains)
    order = (lax.axis_index("expert") // 4 - jnp.arange(steps)) % steps
    ordered = jnp.take(jnp.stack(gains), order, axis=0)
    return functools.reduce(jnp.add, [ordered[step] for step in range(steps)]).reshape(-1)


def broadcast_shards(tokens, cotangent, gain, expert_ids, gate_probs, gate_up_weight, down_weight):
    expert_size = lax.axis_size("expert")
    steps = expert_size // 4
    far = 4 * (steps - 1)
    expert, core = lax.axis_index("expert"), lax.axis_index("tensor")
    my_expert = expert * EXP_DEV + core
    group_rows = expert_ids.shape[0]
    half = group_rows // 2
    features = tokens.shape[1]
    capacity = 3 * group_rows * TOP // (2 * EXP_DEV * expert_size)
    near_own = jnp.stack([tokens, cotangent])
    near_pair = jnp.concatenate([near_own, send_second(near_own)])
    near_far_pair = send_first(near_pair)
    tables = plane_tables(
        after(jnp.concatenate([expert_ids.T.astype(jnp.float32), gate_probs.T]), near_pair)
    )
    token_far = after(jnp.stack([send_along(tokens, -step) for step in range(1, steps)]), tables)
    late_tables = after(tables, token_far)
    far_tables = [send_along(late_tables, -step) for step in range(1, steps)]
    late_cot = after(cotangent, token_far)
    cot_steps = [send_along(late_cot, -step) for step in range(1, steps)]
    token_second = after(send_second(token_far), near_far_pair, cot_steps[len(cot_steps) // 2], *far_tables)
    token_pair = jnp.concatenate([token_far, token_second])
    tables = far_first(jnp.stack([tables] + far_tables, axis=2))
    tables = jnp.where(core == 0, tables, jnp.roll(tables, half, axis=2))
    matches = tables[:, :TOP] == my_expert.astype(jnp.float32)
    chosen = jnp.any(matches, axis=1)
    weight_of = jnp.sum(jnp.where(matches, tables[:, TOP:], 0.0), axis=1)
    row_ids = jnp.arange(group_rows, dtype=jnp.int32)
    earlier = (row_ids[:, None] < row_ids[None, :]).astype(jnp.bfloat16)
    rank_in = jnp.dot(chosen.astype(jnp.bfloat16), earlier, preferred_element_type=jnp.float32)
    placed = chosen[:, None, :] & (
        rank_in.astype(jnp.int32)[:, None, :] == jnp.arange(capacity, dtype=jnp.int32)[None, :, None]
    )
    pick = placed.astype(jnp.bfloat16)
    back = jnp.swapaxes(pick, 1, 2)
    slot_prob = jnp.sum(jnp.where(placed, weight_of[:, None, :], 0.0), axis=2, keepdims=True)

    gain_row = gain[None, :]
    near_pieces = (near_pair, near_far_pair, send_core(near_pair), send_core(near_far_pair))
    rows, = select_normed(pick, gain_row, near_pieces, 1, 2, far, ())
    cot_steps = together(*cot_steps, rows)
    rows, cot_far = cot_steps[-1], jnp.stack(cot_steps[:-1])
    token_far_pair, cot_far = together(send_first(token_pair), cot_far)
    cot_second = send_second(cot_far)
    token_pieces = (token_pair, token_far_pair, send_core(token_pair), send_core(token_far_pair))
    rows, = select_normed(pick, gain_row, token_pieces, steps - 1, 1, 0, (rows,))
    rows, cot_second = together(rows, cot_second)
    cot_pair = jnp.concatenate([cot_far, cot_second])
    cot_far_pair = send_first(cot_pair)

    rows = rows.reshape(-1, features)
    gate_pre, up_pre, hidden, block_out = forward(rows, gate_up_weight, down_weight)
    out_slots = block_out.reshape(expert_size, capacity, features)
    out_mine, out_low, out_high = expand(back, slot_prob, (out_slots,), (True,), steps - 1, 0)
    out_high, cot_far_pair = together(out_high, cot_far_pair)
    cot_pieces = (cot_pair, cot_far_pair, send_core(cot_pair), send_core(cot_far_pair))

    half_far, one_far = 2 * (steps - 1), steps - 1
    held = select_grads(
        after(pick, out_high), slot_prob, out_slots, near_pieces, 1, 2, 1, far, ()
    )
    out_core_high = after(send_core(out_high), held[1])
    out_core = send_core(out_low)
    out_upper = narrow(add_up(out_mine[half_far:], out_core_high))
    out_first = send_first(out_upper)
    grads, prob_value = select_grads(
        after(pick, out_upper), slot_prob, out_slots, cot_pieces, steps - 1, 1, 0, 0, tuple(held)
    )
    grads = grads.reshape(-1, features)
    joined_grad = backward_hidden(grads, gate_pre, up_pre, down_weight)
    input_grad, gain_low = backward_input(joined_grad, gate_up_weight, rows, 0, ())
    out_first, gain_low = together(out_first, gain_low)
    out_middle = narrow(
        add_up(out_mine[one_far:half_far], out_core[one_far:half_far], out_first[one_far:])
    )
    out_second = send_second(out_middle)
    input_grad, gain_high = backward_input(
        joined_grad, gate_up_weight, after(rows, out_middle), 1, (input_grad,)
    )
    gain_term = jnp.concatenate([gain_low[0], gain_high[0]])
    input_slots = input_grad.reshape(expert_size, capacity, features)
    in_mine, in_low, in_high = expand(back, slot_prob, (input_slots,), (False,), steps - 1, 0)
    in_high, out_second = together(in_high, out_second)
    in_core_high = send_core(in_high)
    in_core = send_core(in_low)

    def own_plane(mine, core_part, first_part, second_part, count):
        return add_up(mine[:count], core_part[:count], first_part[:count], second_part[:count])

    out_planes = narrow(own_plane(out_mine, out_core, out_first, out_second, one_far))
    out_far = [send_along(out_planes[step - 1], step) for step in range(1, steps)]
    in_upper = narrow(add_up(in_mine[half_far:], after(in_core_high, out_planes)))
    in_first = send_first(in_upper)
    near_mine, near_low, near_high = expand(
        back, after(slot_prob, in_upper), (out_slots, input_slots), (True, False), 1, far
    )
    near_core_high = send_core(near_high)
    near_core = send_core(near_low)
    gains = (gain_term / gain).reshape(-1, 128)
    prob_rows = jnp.sum(jnp.where(placed, prob_value, 0.0), axis=1)
    columns = from_far_first(jnp.where(matches, prob_rows[:, None, :], 0.0), steps)
    columns = jnp.where(core == 0, columns, jnp.swapaxes(columns, 0, 1))
    got = send_core(after(pack(columns[..., half:], gains), in_upper))
    down_part = outer_sum(after(hidden, in_upper), grads)

    middle = len(out_far) // 2
    down_part, got, out_far[middle] = together(down_part, got, out_far[middle])
    columns, gains = unpack_add(columns[..., :half], gains, got)
    got = send_bit(pack(columns[1], gains), 2)
    gate_up_part = outer_sum(after(rows, near_high, down_part), joined_grad)
    gate_up_part, got = together(gate_up_part, got)
    columns, gains = unpack_add(columns[0], gains, got)
    got = send_bit(pack(columns[1], gains), 1)
    in_first, near_core, got = together(in_first, near_core, got, *out_far)[:3]
    columns, gains = unpack_add(columns[0], gains, got)
    in_middle = narrow(
        add_up(in_mine[one_far:half_far], in_core[one_far:half_far], in_first[one_far:])
    )
    in_second = send_second(in_middle)
    messages = [send_along(pack(columns[step], gains), step) for step in range(1, steps)]
    in_second, *messages = together(in_second, *messages)
    in_planes = narrow(own_plane(in_mine, in_core, in_first, in_second, one_far))
    in_far = [send_along(in_planes[step - 1], step) for step in range(1, steps)]
    near_upper = narrow(add_up(near_mine[4:], after(near_core_high, in_planes)))
    near_first = send_first(near_upper)
    near_middle = narrow(add_up(near_mine[2:4], near_core[2:], near_first[2:]))
    near_second = send_second(near_middle)
    near_sum = own_plane(near_mine, near_core, near_first, near_second, 2)
    out_sum = near_sum[0] + add_up(*out_far)
    normed_grad = near_sum[1] + add_up(*in_far)

    prob_sum, all_gains = columns[0], [gains]
    for message in messages:
        prob_sum = prob_sum + message[:-gains.shape[0]].reshape(prob_sum.shape)
        all_gains.append(message[-gains.shape[0]:])
    gain_grad = planes_in_order(all_gains)

    scaled_own, inv_own = normalize(tokens)
    mixed = (tokens.astype(jnp.float32) + out_sum).astype(jnp.bfloat16)
    gain_side = normed_grad * gain[None, :]
    token_grad = (
        cotangent.astype(jnp.float32)
        + inv_own
        * (gain_side - scaled_own * jnp.mean(gain_side * scaled_own, axis=1, keepdims=True))
    ).astype(jnp.bfloat16)
    return (mixed, token_grad, prob_sum.T, gain_grad, gate_up_part[None], down_part[None])


def solution(mesh):
    in_specs = (
        P(("expert", "tensor"), None),
        P(("expert", "tensor"), None),
        P(),
        P("expert", None),
        P("expert", None),
        P(("expert", "tensor"), None, None),
        P(("expert", "tensor"), None, None),
    )
    out_specs = (
        P(("expert", "tensor"), None),
        P(("expert", "tensor"), None),
        P(("expert", "tensor"), None),
        P(),
        P(("expert", "tensor"), None, None),
        P(("expert", "tensor"), None, None),
    )
    expert_size, tensor_size = mesh.shape["expert"], mesh.shape["tensor"]
    few = tensor_size == EXP_DEV and expert_size % 4 == 0 and expert_size <= 4 * TOP
    shards = broadcast_shards if few else routed_shards
    return jax.shard_map(shards, mesh=mesh, in_specs=in_specs, out_specs=out_specs, check_vma=False)
```

```python
import functools

import jax
import jax.numpy as jnp
from jax import lax
from jax.experimental import pallas as pl
from jax.experimental.pallas import tpu as pltpu
from jax.sharding import PartitionSpec as P

TOP = 8
EXP_DEV = 2
VMEM_LIMIT = 63 * 1024 * 1024
LITTLE = pl.CostEstimate(flops=1000000, bytes_accessed=100000, transcendentals=0)


def normalize(rows):
    values = rows.astype(jnp.float32)
    inv_rms = lax.rsqrt(jnp.mean(values * values, axis=1, keepdims=True) + 1e-06)
    return (values * inv_rms, inv_rms)


def expert_forward(rows, gate_up, down_proj):
    projected = jnp.dot(rows, gate_up, preferred_element_type=jnp.float32)
    half_width = down_proj.shape[0]
    gate_pre = projected[:, :half_width]
    up_pre = projected[:, half_width:]
    sigmoid_gate = jax.nn.sigmoid(gate_pre)
    hidden = (gate_pre * sigmoid_gate * up_pre).astype(jnp.bfloat16)
    block_out = jnp.dot(hidden, down_proj, preferred_element_type=jnp.float32).astype(jnp.bfloat16)
    return (gate_pre, up_pre, sigmoid_gate, hidden, block_out)


def times_transposed(left, right):
    return lax.dot_general(left, right, (((1,), (1,)), ((), ())), preferred_element_type=jnp.float32)


def outer_sum(left, right):
    product = lax.dot_general(left, right, (((0,), (0,)), ((), ())), preferred_element_type=jnp.float32)
    return product.astype(jnp.bfloat16)


def backward_inner(slot_grads, down_proj, gate_pre, up_pre, sigmoid_gate):
    hidden_grad = times_transposed(slot_grads, down_proj)
    gate_grad = (
        hidden_grad * up_pre * sigmoid_gate * (1.0 + gate_pre * (1.0 - sigmoid_gate))
    ).astype(jnp.bfloat16)
    up_grad = (hidden_grad * gate_pre * sigmoid_gate).astype(jnp.bfloat16)
    return jnp.concatenate([gate_grad, up_grad], axis=1)


def expert_backward(rows, slot_grads, gate_up, down_proj, gate_pre, up_pre, sigmoid_gate, hidden):
    joined_grad = backward_inner(slot_grads, down_proj, gate_pre, up_pre, sigmoid_gate)
    input_grad = times_transposed(joined_grad, gate_up).astype(jnp.bfloat16)
    return (input_grad, outer_sum(rows, joined_grad), outer_sum(hidden, slot_grads))


def routed_shards(tokens, cotangent, gain, expert_ids, gate_probs, gate_up_weight, down_weight):
    tensor_size = lax.axis_size("tensor")
    expert_size = lax.axis_size("expert")
    my_rank = lax.axis_index("tensor")
    blocks_each = tensor_size // EXP_DEV
    my_type = my_rank // blocks_each
    group_rows = expert_ids.shape[0]
    features = tokens.shape[1]
    capacity = 3 * group_rows * TOP // (2 * EXP_DEV * expert_size)
    highest = lax.Precision.HIGHEST
    scaled_own, inv_own = normalize(tokens)
    carried = (scaled_own * gain[None, :]).astype(jnp.bfloat16)
    group_first, group_grads = (
        lax.all_gather(carried, "tensor", axis=0, tiled=True),
        lax.all_gather(cotangent, "tensor", axis=0, tiled=True),
    )
    targets = jnp.arange(expert_size, dtype=jnp.int32) * EXP_DEV + my_type
    matches = expert_ids[:, :, None] == targets[None, None, :]
    chosen = jnp.any(matches, axis=1)
    weight_of = jnp.sum(jnp.where(matches, gate_probs[:, :, None], 0.0), axis=1)
    slot_of = jnp.sum(
        jnp.where(matches, jnp.arange(TOP, dtype=jnp.int32)[None, :, None], 0), axis=1
    )
    row_ids = jnp.arange(group_rows, dtype=jnp.int32)
    earlier = (row_ids[None, :] < row_ids[:, None]).astype(jnp.bfloat16)
    rank_in = jnp.dot(
        earlier, chosen.astype(jnp.bfloat16), preferred_element_type=jnp.float32
    ).astype(jnp.int32)
    placed = chosen.T[:, None, :] & (
        rank_in.T[:, None, :] == jnp.arange(capacity, dtype=jnp.int32)[None, :, None]
    )
    source = jnp.sum(jnp.where(placed, row_ids[None, None, :], 0), axis=2)
    filled = jnp.any(placed, axis=2)
    slot_prob = jnp.sum(jnp.where(placed, weight_of.T[:, None, :], 0.0), axis=2)
    slot_index = jnp.sum(jnp.where(placed, slot_of.T[:, None, :], 0), axis=2)
    sent_rows = jnp.where(
        filled[:, :, None], jnp.take(group_first, source, axis=0), jnp.zeros((), jnp.bfloat16)
    )
    sent_grads = (
        slot_prob[:, :, None] * jnp.take(group_grads, source, axis=0).astype(jnp.float32)
    ).astype(jnp.bfloat16)
    gate_up = gate_up_weight[0]
    down_proj = down_weight[0]
    arrived_rows, arrived_grads = (
        lax.all_to_all(sent_rows, "expert", split_axis=0, concat_axis=0, tiled=True),
        lax.all_to_all(sent_grads, "expert", split_axis=0, concat_axis=0, tiled=True),
    )
    rows = arrived_rows.reshape(-1, features)
    slot_grads = arrived_grads.reshape(-1, features)
    gate_pre, up_pre, sigmoid_gate, hidden, block_out = expert_forward(rows, gate_up, down_proj)
    out_slots = block_out.reshape(expert_size, capacity, features)
    input_grad, gate_up_part, down_part = expert_backward(
        rows, slot_grads, gate_up, down_proj, gate_pre, up_pre, sigmoid_gate, hidden
    )
    input_slots = input_grad.reshape(expert_size, capacity, features)
    out_back, input_back = (
        lax.all_to_all(out_slots, "expert", split_axis=0, concat_axis=0, tiled=True),
        lax.all_to_all(input_slots, "expert", split_axis=0, concat_axis=0, tiled=True),
    )
    out_flat = out_back.reshape(-1, features)
    input_flat = input_back.reshape(-1, features)
    used_source = source.reshape(-1)
    used_filled = filled.reshape(-1)
    used_prob = slot_prob.reshape(-1)
    used_index = slot_index.reshape(-1)
    cot_slots = jnp.take(group_grads, used_source, axis=0)
    prob_values = jnp.einsum("sd,sd->s", cot_slots, out_flat, preferred_element_type=jnp.float32)
    hit = (row_ids[:, None] == used_source[None, :]) & used_filled[None, :]
    input_part = jnp.dot(hit.astype(jnp.bfloat16), input_flat, preferred_element_type=jnp.float32)
    weighting = jnp.where(hit, used_prob[None, :], 0.0)
    out_part = jnp.dot(
        weighting,
        out_flat.astype(jnp.float32),
        precision=highest,
        preferred_element_type=jnp.float32,
    )
    prob_columns = jnp.where(
        used_index[:, None] == jnp.arange(TOP, dtype=jnp.int32)[None, :], prob_values[:, None], 0.0
    )
    prob_part = jnp.dot(
        hit.astype(jnp.float32), prob_columns, precision=highest, preferred_element_type=jnp.float32
    )
    out_sum, normed_grad, prob_grad = (
        lax.psum_scatter(out_part, "tensor", scatter_dimension=0, tiled=True),
        lax.psum_scatter(input_part, "tensor", scatter_dimension=0, tiled=True),
        lax.psum_scatter(prob_part, "tensor", scatter_dimension=0, tiled=True),
    )
    mixed = (tokens.astype(jnp.float32) + out_sum).astype(jnp.bfloat16)
    gain_side = normed_grad * gain[None, :]
    token_grad = (
        cotangent.astype(jnp.float32)
        + inv_own
        * (gain_side - scaled_own * jnp.mean(gain_side * scaled_own, axis=1, keepdims=True))
    ).astype(jnp.bfloat16)
    gain_grad = lax.psum(jnp.sum(normed_grad * scaled_own, axis=0), ("expert", "tensor"))
    return (mixed, token_grad, prob_grad, gain_grad, gate_up_part[None], down_part[None])


BOTH = ("expert", "tensor")


def flip_first(expert, core):
    return expert ^ (2 if core == 0 else 1)


def flip_second(expert, core):
    return expert ^ (1 if core == 0 else 2)


def send(array, place):
    pairs = []
    for expert in range(lax.axis_size("expert")):
        for core in range(2):
            to_expert, to_core = place(expert, core)
            pairs.append((expert * 2 + core, to_expert * 2 + to_core))
    return lax.ppermute(array, BOTH, pairs)


def send_first(array):
    return send(array, lambda e, c: (flip_first(e, c), c))


def send_second(array):
    return send(array, lambda e, c: (flip_second(e, c), c))


def send_bit(array, bit):
    return send(array, lambda e, c: (e ^ bit, c))


def send_core(array):
    return send(array, lambda e, c: (e, 1 - c))


def send_along(array, step):
    size = lax.axis_size("expert")
    return send(array, lambda e, c: ((e + 4 * step) % size, c))


def after(array, *others):
    return lax.optimization_barrier((array,) + others)[0]


def together(*arrays):
    return lax.optimization_barrier(arrays)


def add_up(*terms):
    return sum(term.astype(jnp.float32) for term in terms)


def narrow(value):
    return value.astype(jnp.bfloat16)


def plane_tables(table):
    pair = jnp.stack([table, send_second(table)])
    return jnp.stack([pair, send_first(pair)])


def far_first(array):
    far = array[:, :, 1:].reshape((-1,) + array.shape[3:])
    return jnp.concatenate([far, array[:, :, 0].reshape((-1,) + array.shape[3:])])


def from_far_first(array, steps):
    far = array[:4 * (steps - 1)].reshape((2, 2, steps - 1) + array.shape[1:])
    return jnp.concatenate([array[4 * (steps - 1):].reshape((2, 2, 1) + array.shape[1:]), far], axis=2)


def start(source, target, semaphore):
    copy = pltpu.make_async_copy(source, target, semaphore)
    copy.start()
    return copy


def chosen_rows(pick, mine, other):
    return jnp.dot(pick, jnp.concatenate([mine, other]), preferred_element_type=jnp.float32)


def norm_kernel(count, pick_ref, *refs):
    pieces, gain_ref, normed_ref = refs[:4], refs[4], refs[-1]

    def work(mine_ref, other_ref):
        for group in range(count):
            rows = chosen_rows(pick_ref[group], mine_ref[group], other_ref[group])
            inv_rms = lax.rsqrt(jnp.mean(rows * rows, axis=1, keepdims=True) + 1e-06)
            normed_ref[group] = (rows * inv_rms * gain_ref[...]).astype(jnp.bfloat16)

    by_place(work, pieces)


def grad_kernel(count, pick_ref, *refs):
    pieces, prob_ref, out_ref, (grad_ref, value_ref) = refs[:4], refs[4], refs[5], refs[-2:]

    def work(mine_ref, other_ref):
        for group in range(count):
            rows = chosen_rows(pick_ref[group], mine_ref[group], other_ref[group])
            grad_ref[group] = (rows * prob_ref[group]).astype(jnp.bfloat16)
            value_ref[group] = jnp.sum(rows * out_ref[group].astype(jnp.float32), axis=1, keepdims=True)

    by_place(work, pieces)


def by_place(work, pieces):
    for first in range(2):
        for second in range(2):
            pl.when(pl.program_id(0) == first * 2 + second)(
                functools.partial(work, pieces[first], pieces[2 + second])
            )


def group_spec(count, first_group, *shape):
    first_block = first_group // count
    return pl.BlockSpec((count,) + shape, lambda i: (first_block + i, 0, 0))


def select(kernel, pick, pieces, extras, extra_specs, out_shapes, count, arrays, which, first_group, held):
    _, capacity, group_rows = pick.shape
    half, features = pieces[0].shape[1:]

    def piece_spec(place):
        return pl.BlockSpec((count, half, features), lambda i: (place(i) * arrays + which, 0, 0))

    return pl.pallas_call(
        functools.partial(kernel, count),
        grid=(4,),
        in_specs=[
            group_spec(count, first_group, capacity, group_rows),
            piece_spec(lambda i: jnp.minimum(i, 1)),
            piece_spec(lambda i: jnp.maximum(i - 2, 0)),
            piece_spec(lambda i: i // 2),
            piece_spec(lambda i: jnp.maximum(i - 2, 0)),
        ] + extra_specs + [pl.BlockSpec(memory_space=pl.ANY)] * len(held),
        out_specs=[group_spec(count, first_group, *out.shape[1:]) for out in out_shapes],
        out_shape=out_shapes,
        input_output_aliases={5 + len(extras) + n: n for n in range(len(held))},
        compiler_params=pltpu.CompilerParams(vmem_limit_bytes=VMEM_LIMIT),
        cost_estimate=LITTLE,
    )(pick, *pieces, *extras, *held)


def select_normed(pick, gain, pieces, count, arrays, first_group, held):
    groups, capacity, _ = pick.shape
    features = pieces[0].shape[2]
    return select(
        norm_kernel, pick, pieces, [gain], [pl.BlockSpec((1, features), lambda i: (0, 0))],
        [jax.ShapeDtypeStruct((groups, capacity, features), jnp.bfloat16)],
        count, arrays, 0, first_group, held,
    )


def select_grads(pick, prob, out_slots, pieces, count, arrays, which, first_group, held):
    groups, capacity, _ = pick.shape
    features = pieces[0].shape[2]
    return select(
        grad_kernel, pick, pieces, [prob, out_slots],
        [group_spec(count, first_group, capacity, 1), group_spec(count, first_group, capacity, features)],
        [
            jax.ShapeDtypeStruct((groups, capacity, features), jnp.bfloat16),
            jax.ShapeDtypeStruct((groups, capacity, 1), jnp.float32),
        ],
        count, arrays, which, first_group, held,
    )


def expand_kernel(weighted, count, first_group, back_ref, prob_ref, *refs):
    arrays = len(weighted)
    sources, mine_ref, pieces = refs[:arrays], refs[arrays], refs[arrays + 1:arrays + 3]
    loaded, spread, loads, stores = refs[arrays + 3:]
    half = mine_ref.shape[1]
    copies, written = [], []
    for group in range(4 * count):
        for number, source in enumerate(sources):
            place = group * arrays + number
            copies.append(start(source.at[first_group + group], loaded.at[place], loads.at[place]))
    for group in range(4 * count):
        outer, inner = divmod(group, count)
        first, second = divmod(outer, 2)
        for number, by_prob in enumerate(weighted):
            place = group * arrays + number
            copies[place].wait()
            rows = loaded[place]
            if by_prob:
                rows = (rows.astype(jnp.float32) * prob_ref[first_group + group]).astype(jnp.bfloat16)
            spread[place] = jnp.dot(
                back_ref[first_group + group], rows, preferred_element_type=jnp.float32
            ).astype(jnp.bfloat16)
            target = pieces[second].at[(first * count + inner) * arrays + number]
            written += [
                start(spread.at[place, pl.ds(half, half)], target, stores.at[place, 0]),
                start(spread.at[place, pl.ds(0, half)], mine_ref.at[place], stores.at[place, 1]),
            ]
    for copy in written:
        copy.wait()


def expand(back, prob, slots, weighted, count, first_group):
    _, group_rows, capacity = back.shape
    half, features, arrays = group_rows // 2, slots[0].shape[2], len(slots)
    blocks = 4 * count * arrays
    anywhere, whole = pl.BlockSpec(memory_space=pl.ANY), pl.BlockSpec(memory_space=pltpu.VMEM)
    piece = jax.ShapeDtypeStruct((blocks // 2, half, features), jnp.bfloat16)
    return pl.pallas_call(
        functools.partial(expand_kernel, weighted, count, first_group),
        in_specs=[whole, whole] + [anywhere] * arrays,
        out_specs=[anywhere] * 3,
        out_shape=[jax.ShapeDtypeStruct((blocks, half, features), jnp.bfloat16), piece, piece],
        scratch_shapes=[
            pltpu.VMEM((blocks, capacity, features), jnp.bfloat16),
            pltpu.VMEM((blocks, group_rows, features), jnp.bfloat16),
            pltpu.SemaphoreType.DMA((blocks,)),
            pltpu.SemaphoreType.DMA((blocks, 2)),
        ],
        compiler_params=pltpu.CompilerParams(vmem_limit_bytes=VMEM_LIMIT),
        cost_estimate=LITTLE,
    )(back, prob, *slots)


def forward_kernel(rows_ref, gate_up_ref, down_ref, gate_pre_ref, up_pre_ref, hidden_ref, out_ref):
    projected = jnp.dot(rows_ref[...], gate_up_ref[0], preferred_element_type=jnp.float32)
    half_width = hidden_ref.shape[1]
    gate_pre, up_pre = projected[:, :half_width], projected[:, half_width:]
    gate_pre_ref[...] = gate_pre
    up_pre_ref[...] = up_pre
    hidden = (gate_pre * jax.nn.sigmoid(gate_pre) * up_pre).astype(jnp.bfloat16)
    hidden_ref[...] = hidden
    out_ref[...] = jnp.dot(hidden, down_ref[0], preferred_element_type=jnp.float32).astype(jnp.bfloat16)


def forward(rows, gate_up_weight, down_weight):
    slots, features = rows.shape
    width = down_weight.shape[1]
    block = slots // 2

    def row_spec(columns):
        return pl.BlockSpec((block, columns), lambda i: (i, 0))

    return pl.pallas_call(
        forward_kernel,
        grid=(2,),
        in_specs=[
            row_spec(features),
            pl.BlockSpec((1, features, 2 * width), lambda i: (0, 0, 0)),
            pl.BlockSpec((1, width, features), lambda i: (0, 0, 0)),
        ],
        out_specs=[row_spec(width), row_spec(width), row_spec(width), row_spec(features)],
        out_shape=[
            jax.ShapeDtypeStruct((slots, width), jnp.float32),
            jax.ShapeDtypeStruct((slots, width), jnp.float32),
            jax.ShapeDtypeStruct((slots, width), jnp.bfloat16),
            jax.ShapeDtypeStruct((slots, features), jnp.bfloat16),
        ],
        compiler_params=pltpu.CompilerParams(vmem_limit_bytes=VMEM_LIMIT),
        cost_estimate=LITTLE,
    )(rows, gate_up_weight, down_weight)


def inner_kernel(units, grads_ref, gate_pre_ref, up_pre_ref, down_ref, joined_ref):
    step = pl.program_id(0)
    block = gate_pre_ref.shape[1]
    gate_pre, up_pre = gate_pre_ref[...], up_pre_ref[...]
    sigmoid_gate = jax.nn.sigmoid(gate_pre)
    common = times_transposed(grads_ref[...], down_ref[0]) * sigmoid_gate
    gate_grad = common * up_pre * (1.0 + gate_pre * (1.0 - sigmoid_gate))
    start = pl.multiple_of(step * block, block)
    joined_ref[:, pl.ds(start, block)] = gate_grad.astype(jnp.bfloat16)
    joined_ref[:, pl.ds(units * block + start, block)] = (common * gate_pre).astype(jnp.bfloat16)


def backward_hidden(grads, gate_pre, up_pre, down_weight):
    slots, features = grads.shape
    width = down_weight.shape[1]
    block, units = 256, width // 256
    return pl.pallas_call(
        functools.partial(inner_kernel, units),
        grid=(units,),
        in_specs=[
            pl.BlockSpec((slots, features), lambda i: (0, 0)),
            pl.BlockSpec((slots, block), lambda i: (0, i)),
            pl.BlockSpec((slots, block), lambda i: (0, i)),
            pl.BlockSpec((1, block, features), lambda i: (0, i, 0)),
        ],
        out_specs=pl.BlockSpec((slots, 2 * width), lambda i: (0, 0)),
        out_shape=jax.ShapeDtypeStruct((slots, 2 * width), jnp.bfloat16),
        compiler_params=pltpu.CompilerParams(vmem_limit_bytes=VMEM_LIMIT),
        cost_estimate=LITTLE,
    )(grads, gate_pre, up_pre, down_weight)


def input_kernel(joined_ref, gate_up_ref, rows_ref, *refs):
    input_ref, gain_ref = refs[-2:]
    input_grad = times_transposed(joined_ref[...], gate_up_ref[0]).astype(jnp.bfloat16)
    input_ref[...] = input_grad
    terms = input_grad.astype(jnp.float32) * rows_ref[...].astype(jnp.float32)
    gain_ref[...] = jnp.sum(terms, axis=0, keepdims=True)


def backward_input(joined_grad, gate_up_weight, rows, part, held):
    slots, features = rows.shape
    width = joined_grad.shape[1]
    wide = features // 4
    first = 2 * part
    return pl.pallas_call(
        input_kernel,
        grid=(2,),
        in_specs=[
            pl.BlockSpec((slots, width), lambda i: (0, 0)),
            pl.BlockSpec((1, wide, width), lambda i: (0, first + i, 0)),
            pl.BlockSpec((slots, wide), lambda i: (0, first + i)),
        ] + [pl.BlockSpec(memory_space=pl.ANY)] * len(held),
        out_specs=[
            pl.BlockSpec((slots, wide), lambda i: (0, first + i)),
            pl.BlockSpec((1, wide), lambda i: (0, i)),
        ],
        out_shape=[
            jax.ShapeDtypeStruct((slots, features), jnp.bfloat16),
            jax.ShapeDtypeStruct((1, features // 2), jnp.float32),
        ],
        input_output_aliases={3 + n: n for n in range(len(held))},
        compiler_params=pltpu.CompilerParams(vmem_limit_bytes=VMEM_LIMIT),
        cost_estimate=LITTLE,
    )(joined_grad, gate_up_weight, rows, *held)


def pack(columns, gains):
    return jnp.concatenate([columns.reshape(-1, 128), gains])


def unpack_add(columns, gains, got):
    count = gains.shape[0]
    return columns + got[:-count].reshape(columns.shape), gains + got[-count:]


def planes_in_order(gains):
    steps = len(gains)
    order = (lax.axis_index("expert") // 4 - jnp.arange(steps)) % steps
    ordered = jnp.take(jnp.stack(gains), order, axis=0)
    return functools.reduce(jnp.add, [ordered[step] for step in range(steps)]).reshape(-1)


def broadcast_shards(tokens, cotangent, gain, expert_ids, gate_probs, gate_up_weight, down_weight):
    expert_size = lax.axis_size("expert")
    steps = expert_size // 4
    far = 4 * (steps - 1)
    expert, core = lax.axis_index("expert"), lax.axis_index("tensor")
    my_expert = expert * EXP_DEV + core
    group_rows = expert_ids.shape[0]
    half = group_rows // 2
    features = tokens.shape[1]
    capacity = 3 * group_rows * TOP // (2 * EXP_DEV * expert_size)
    near_own = jnp.stack([tokens, cotangent])
    near_pair = jnp.concatenate([near_own, send_second(near_own)])
    near_far_pair = send_first(near_pair)
    tables = plane_tables(
        after(jnp.concatenate([expert_ids.T.astype(jnp.float32), gate_probs.T]), near_pair)
    )
    token_far = after(jnp.stack([send_along(tokens, -step) for step in range(1, steps)]), tables)
    late_tables = after(tables, token_far)
    far_tables = [send_along(late_tables, -step) for step in range(1, steps)]
    late_cot = after(cotangent, token_far)
    cot_steps = [send_along(late_cot, -step) for step in range(1, steps)]
    token_second = after(send_second(token_far), near_far_pair, cot_steps[0], *far_tables)
    token_pair = jnp.concatenate([token_far, token_second])
    tables = far_first(jnp.stack([tables] + far_tables, axis=2))
    tables = jnp.where(core == 0, tables, jnp.roll(tables, half, axis=2))
    matches = tables[:, :TOP] == my_expert.astype(jnp.float32)
    chosen = jnp.any(matches, axis=1)
    weight_of = jnp.sum(jnp.where(matches, tables[:, TOP:], 0.0), axis=1)
    row_ids = jnp.arange(group_rows, dtype=jnp.int32)
    earlier = (row_ids[:, None] < row_ids[None, :]).astype(jnp.bfloat16)
    rank_in = jnp.dot(chosen.astype(jnp.bfloat16), earlier, preferred_element_type=jnp.float32)
    placed = chosen[:, None, :] & (
        rank_in.astype(jnp.int32)[:, None, :] == jnp.arange(capacity, dtype=jnp.int32)[None, :, None]
    )
    pick = placed.astype(jnp.bfloat16)
    back = jnp.swapaxes(pick, 1, 2)
    slot_prob = jnp.sum(jnp.where(placed, weight_of[:, None, :], 0.0), axis=2, keepdims=True)

    gain_row = gain[None, :]
    near_pieces = (near_pair, near_far_pair, send_core(near_pair), send_core(near_far_pair))
    rows, = select_normed(pick, gain_row, near_pieces, 1, 2, far, ())
    cot_steps = together(*cot_steps, rows)
    rows, cot_far = cot_steps[-1], jnp.stack(cot_steps[:-1])
    token_far_pair, cot_far = together(send_first(token_pair), cot_far)
    cot_second = send_second(cot_far)
    token_pieces = (token_pair, token_far_pair, send_core(token_pair), send_core(token_far_pair))
    rows, = select_normed(pick, gain_row, token_pieces, steps - 1, 1, 0, (rows,))
    rows, cot_second = together(rows, cot_second)
    cot_pair = jnp.concatenate([cot_far, cot_second])
    cot_far_pair = send_first(cot_pair)

    rows = rows.reshape(-1, features)
    gate_pre, up_pre, hidden, block_out = forward(rows, gate_up_weight, down_weight)
    out_slots = block_out.reshape(expert_size, capacity, features)
    out_mine, out_low, out_high = expand(back, slot_prob, (out_slots,), (True,), steps - 1, 0)
    out_high, cot_far_pair = together(out_high, cot_far_pair)
    cot_pieces = (cot_pair, cot_far_pair, send_core(cot_pair), send_core(cot_far_pair))

    half_far, one_far = 2 * (steps - 1), steps - 1
    held = select_grads(
        after(pick, out_high), slot_prob, out_slots, near_pieces, 1, 2, 1, far, ()
    )
    out_core_high = after(send_core(out_high), held[1])
    out_core = send_core(out_low)
    out_upper = narrow(add_up(out_mine[half_far:], out_core_high))
    out_first = send_first(out_upper)
    grads, prob_value = select_grads(
        after(pick, out_upper), slot_prob, out_slots, cot_pieces, steps - 1, 1, 0, 0, tuple(held)
    )
    grads = grads.reshape(-1, features)
    joined_grad = backward_hidden(grads, gate_pre, up_pre, down_weight)
    input_grad, gain_low = backward_input(joined_grad, gate_up_weight, rows, 0, ())
    out_first, gain_low = together(out_first, gain_low)
    out_middle = narrow(
        add_up(out_mine[one_far:half_far], out_core[one_far:half_far], out_first[one_far:])
    )
    out_second = send_second(out_middle)
    input_grad, gain_high = backward_input(
        joined_grad, gate_up_weight, after(rows, out_middle), 1, (input_grad,)
    )
    gain_term = jnp.concatenate([gain_low[0], gain_high[0]])
    input_slots = input_grad.reshape(expert_size, capacity, features)
    in_mine, in_low, in_high = expand(back, slot_prob, (input_slots,), (False,), steps - 1, 0)
    in_high, out_second = together(in_high, out_second)
    in_core_high = send_core(in_high)
    in_core = send_core(in_low)

    def own_plane(mine, core_part, first_part, second_part, count):
        return add_up(mine[:count], core_part[:count], first_part[:count], second_part[:count])

    out_planes = narrow(own_plane(out_mine, out_core, out_first, out_second, one_far))
    out_far = [send_along(out_planes[step - 1], step) for step in range(1, steps)]
    in_upper = narrow(add_up(in_mine[half_far:], after(in_core_high, out_planes)))
    in_first = send_first(in_upper)
    near_mine, near_low, near_high = expand(
        back, after(slot_prob, in_upper), (out_slots, input_slots), (True, False), 1, far
    )
    near_core_high = send_core(near_high)
    near_core = send_core(near_low)
    gains = (gain_term / gain).reshape(-1, 128)
    prob_rows = jnp.sum(jnp.where(placed, prob_value, 0.0), axis=1)
    columns = from_far_first(jnp.where(matches, prob_rows[:, None, :], 0.0), steps)
    columns = jnp.where(core == 0, columns, jnp.swapaxes(columns, 0, 1))
    got = send_core(after(pack(columns[..., half:], gains), in_upper))
    down_part = outer_sum(after(hidden, in_upper), grads)

    down_part, got = together(down_part, got)
    columns, gains = unpack_add(columns[..., :half], gains, got)
    got = send_bit(pack(columns[1], gains), 2)
    gate_up_part = outer_sum(after(rows, near_high, down_part), joined_grad)
    gate_up_part, got = together(gate_up_part, got, *out_far[:-1])[:2]
    columns, gains = unpack_add(columns[0], gains, got)
    got = send_bit(pack(columns[1], gains), 1)
    in_first, near_core, near_core_high, got = together(in_first, near_core, near_core_high, got)
    columns, gains = unpack_add(columns[0], gains, got)
    in_middle = narrow(
        add_up(in_mine[one_far:half_far], in_core[one_far:half_far], in_first[one_far:])
    )
    in_second = send_second(in_middle)
    messages = [send_along(pack(columns[step], gains), step) for step in range(1, steps)]
    near_upper = narrow(add_up(near_mine[4:], near_core_high))
    in_second, near_upper, *messages = together(in_second, near_upper, *messages, *out_far[-1:])[:2 + len(messages)]
    in_planes = narrow(own_plane(in_mine, in_core, in_first, in_second, one_far))
    in_far = [send_along(in_planes[step - 1], step) for step in range(1, steps)]
    near_first = send_first(after(near_upper, in_planes))
    near_middle = narrow(add_up(near_mine[2:4], near_core[2:], near_first[2:]))
    near_second = send_second(near_middle)
    near_sum = own_plane(near_mine, near_core, near_first, near_second, 2)
    out_sum = near_sum[0] + add_up(*out_far)
    normed_grad = near_sum[1] + add_up(*in_far)

    prob_sum, all_gains = columns[0], [gains]
    for message in messages:
        prob_sum = prob_sum + message[:-gains.shape[0]].reshape(prob_sum.shape)
        all_gains.append(message[-gains.shape[0]:])
    gain_grad = planes_in_order(all_gains)

    scaled_own, inv_own = normalize(tokens)
    mixed = (tokens.astype(jnp.float32) + out_sum).astype(jnp.bfloat16)
    gain_side = normed_grad * gain[None, :]
    token_grad = (
        cotangent.astype(jnp.float32)
        + inv_own
        * (gain_side - scaled_own * jnp.mean(gain_side * scaled_own, axis=1, keepdims=True))
    ).astype(jnp.bfloat16)
    return (mixed, token_grad, prob_sum.T, gain_grad, gate_up_part[None], down_part[None])


def solution(mesh):
    in_specs = (
        P(("expert", "tensor"), None),
        P(("expert", "tensor"), None),
        P(),
        P("expert", None),
        P("expert", None),
        P(("expert", "tensor"), None, None),
        P(("expert", "tensor"), None, None),
    )
    out_specs = (
        P(("expert", "tensor"), None),
        P(("expert", "tensor"), None),
        P(("expert", "tensor"), None),
        P(),
        P(("expert", "tensor"), None, None),
        P(("expert", "tensor"), None, None),
    )
    expert_size, tensor_size = mesh.shape["expert"], mesh.shape["tensor"]
    few = tensor_size == EXP_DEV and expert_size % 4 == 0 and expert_size <= 4 * TOP
    shards = broadcast_shards if few else routed_shards
    return jax.shard_map(shards, mesh=mesh, in_specs=in_specs, out_specs=out_specs, check_vma=False)
```

```python
import functools

import jax
import jax.numpy as jnp
from jax import lax
from jax.experimental import pallas as pl
from jax.experimental.pallas import tpu as pltpu
from jax.sharding import PartitionSpec as P

TOP = 8
EXP_DEV = 2
VMEM_LIMIT = 63 * 1024 * 1024
LITTLE = pl.CostEstimate(flops=1000000, bytes_accessed=100000, transcendentals=0)


def normalize(rows):
    values = rows.astype(jnp.float32)
    inv_rms = lax.rsqrt(jnp.mean(values * values, axis=1, keepdims=True) + 1e-06)
    return (values * inv_rms, inv_rms)


def expert_forward(rows, gate_up, down_proj):
    projected = jnp.dot(rows, gate_up, preferred_element_type=jnp.float32)
    half_width = down_proj.shape[0]
    gate_pre = projected[:, :half_width]
    up_pre = projected[:, half_width:]
    sigmoid_gate = jax.nn.sigmoid(gate_pre)
    hidden = (gate_pre * sigmoid_gate * up_pre).astype(jnp.bfloat16)
    block_out = jnp.dot(hidden, down_proj, preferred_element_type=jnp.float32).astype(jnp.bfloat16)
    return (gate_pre, up_pre, sigmoid_gate, hidden, block_out)


def times_transposed(left, right):
    return lax.dot_general(left, right, (((1,), (1,)), ((), ())), preferred_element_type=jnp.float32)


def outer_sum(left, right):
    product = lax.dot_general(left, right, (((0,), (0,)), ((), ())), preferred_element_type=jnp.float32)
    return product.astype(jnp.bfloat16)


def backward_inner(slot_grads, down_proj, gate_pre, up_pre, sigmoid_gate):
    hidden_grad = times_transposed(slot_grads, down_proj)
    gate_grad = (
        hidden_grad * up_pre * sigmoid_gate * (1.0 + gate_pre * (1.0 - sigmoid_gate))
    ).astype(jnp.bfloat16)
    up_grad = (hidden_grad * gate_pre * sigmoid_gate).astype(jnp.bfloat16)
    return jnp.concatenate([gate_grad, up_grad], axis=1)


def expert_backward(rows, slot_grads, gate_up, down_proj, gate_pre, up_pre, sigmoid_gate, hidden):
    joined_grad = backward_inner(slot_grads, down_proj, gate_pre, up_pre, sigmoid_gate)
    input_grad = times_transposed(joined_grad, gate_up).astype(jnp.bfloat16)
    return (input_grad, outer_sum(rows, joined_grad), outer_sum(hidden, slot_grads))


def routed_shards(tokens, cotangent, gain, expert_ids, gate_probs, gate_up_weight, down_weight):
    tensor_size = lax.axis_size("tensor")
    expert_size = lax.axis_size("expert")
    my_rank = lax.axis_index("tensor")
    blocks_each = tensor_size // EXP_DEV
    my_type = my_rank // blocks_each
    group_rows = expert_ids.shape[0]
    features = tokens.shape[1]
    capacity = 3 * group_rows * TOP // (2 * EXP_DEV * expert_size)
    highest = lax.Precision.HIGHEST
    scaled_own, inv_own = normalize(tokens)
    carried = (scaled_own * gain[None, :]).astype(jnp.bfloat16)
    group_first, group_grads = (
        lax.all_gather(carried, "tensor", axis=0, tiled=True),
        lax.all_gather(cotangent, "tensor", axis=0, tiled=True),
    )
    targets = jnp.arange(expert_size, dtype=jnp.int32) * EXP_DEV + my_type
    matches = expert_ids[:, :, None] == targets[None, None, :]
    chosen = jnp.any(matches, axis=1)
    weight_of = jnp.sum(jnp.where(matches, gate_probs[:, :, None], 0.0), axis=1)
    slot_of = jnp.sum(
        jnp.where(matches, jnp.arange(TOP, dtype=jnp.int32)[None, :, None], 0), axis=1
    )
    row_ids = jnp.arange(group_rows, dtype=jnp.int32)
    earlier = (row_ids[None, :] < row_ids[:, None]).astype(jnp.bfloat16)
    rank_in = jnp.dot(
        earlier, chosen.astype(jnp.bfloat16), preferred_element_type=jnp.float32
    ).astype(jnp.int32)
    placed = chosen.T[:, None, :] & (
        rank_in.T[:, None, :] == jnp.arange(capacity, dtype=jnp.int32)[None, :, None]
    )
    source = jnp.sum(jnp.where(placed, row_ids[None, None, :], 0), axis=2)
    filled = jnp.any(placed, axis=2)
    slot_prob = jnp.sum(jnp.where(placed, weight_of.T[:, None, :], 0.0), axis=2)
    slot_index = jnp.sum(jnp.where(placed, slot_of.T[:, None, :], 0), axis=2)
    sent_rows = jnp.where(
        filled[:, :, None], jnp.take(group_first, source, axis=0), jnp.zeros((), jnp.bfloat16)
    )
    sent_grads = (
        slot_prob[:, :, None] * jnp.take(group_grads, source, axis=0).astype(jnp.float32)
    ).astype(jnp.bfloat16)
    gate_up = gate_up_weight[0]
    down_proj = down_weight[0]
    arrived_rows, arrived_grads = (
        lax.all_to_all(sent_rows, "expert", split_axis=0, concat_axis=0, tiled=True),
        lax.all_to_all(sent_grads, "expert", split_axis=0, concat_axis=0, tiled=True),
    )
    rows = arrived_rows.reshape(-1, features)
    slot_grads = arrived_grads.reshape(-1, features)
    gate_pre, up_pre, sigmoid_gate, hidden, block_out = expert_forward(rows, gate_up, down_proj)
    out_slots = block_out.reshape(expert_size, capacity, features)
    input_grad, gate_up_part, down_part = expert_backward(
        rows, slot_grads, gate_up, down_proj, gate_pre, up_pre, sigmoid_gate, hidden
    )
    input_slots = input_grad.reshape(expert_size, capacity, features)
    out_back, input_back = (
        lax.all_to_all(out_slots, "expert", split_axis=0, concat_axis=0, tiled=True),
        lax.all_to_all(input_slots, "expert", split_axis=0, concat_axis=0, tiled=True),
    )
    out_flat = out_back.reshape(-1, features)
    input_flat = input_back.reshape(-1, features)
    used_source = source.reshape(-1)
    used_filled = filled.reshape(-1)
    used_prob = slot_prob.reshape(-1)
    used_index = slot_index.reshape(-1)
    cot_slots = jnp.take(group_grads, used_source, axis=0)
    prob_values = jnp.einsum("sd,sd->s", cot_slots, out_flat, preferred_element_type=jnp.float32)
    hit = (row_ids[:, None] == used_source[None, :]) & used_filled[None, :]
    input_part = jnp.dot(hit.astype(jnp.bfloat16), input_flat, preferred_element_type=jnp.float32)
    weighting = jnp.where(hit, used_prob[None, :], 0.0)
    out_part = jnp.dot(
        weighting,
        out_flat.astype(jnp.float32),
        precision=highest,
        preferred_element_type=jnp.float32,
    )
    prob_columns = jnp.where(
        used_index[:, None] == jnp.arange(TOP, dtype=jnp.int32)[None, :], prob_values[:, None], 0.0
    )
    prob_part = jnp.dot(
        hit.astype(jnp.float32), prob_columns, precision=highest, preferred_element_type=jnp.float32
    )
    out_sum, normed_grad, prob_grad = (
        lax.psum_scatter(out_part, "tensor", scatter_dimension=0, tiled=True),
        lax.psum_scatter(input_part, "tensor", scatter_dimension=0, tiled=True),
        lax.psum_scatter(prob_part, "tensor", scatter_dimension=0, tiled=True),
    )
    mixed = (tokens.astype(jnp.float32) + out_sum).astype(jnp.bfloat16)
    gain_side = normed_grad * gain[None, :]
    token_grad = (
        cotangent.astype(jnp.float32)
        + inv_own
        * (gain_side - scaled_own * jnp.mean(gain_side * scaled_own, axis=1, keepdims=True))
    ).astype(jnp.bfloat16)
    gain_grad = lax.psum(jnp.sum(normed_grad * scaled_own, axis=0), ("expert", "tensor"))
    return (mixed, token_grad, prob_grad, gain_grad, gate_up_part[None], down_part[None])


BOTH = ("expert", "tensor")


def flip_first(expert, core):
    return expert ^ (2 if core == 0 else 1)


def flip_second(expert, core):
    return expert ^ (1 if core == 0 else 2)


def send(array, place):
    pairs = []
    for expert in range(lax.axis_size("expert")):
        for core in range(2):
            to_expert, to_core = place(expert, core)
            pairs.append((expert * 2 + core, to_expert * 2 + to_core))
    return lax.ppermute(array, BOTH, pairs)


def send_first(array):
    return send(array, lambda e, c: (flip_first(e, c), c))


def send_second(array):
    return send(array, lambda e, c: (flip_second(e, c), c))


def send_bit(array, bit):
    return send(array, lambda e, c: (e ^ bit, c))


def send_core(array):
    return send(array, lambda e, c: (e, 1 - c))


def send_along(array, step):
    size = lax.axis_size("expert")
    return send(array, lambda e, c: ((e + 4 * step) % size, c))


def after(array, *others):
    return lax.optimization_barrier((array,) + others)[0]


def together(*arrays):
    return lax.optimization_barrier(arrays)


def add_up(*terms):
    return sum(term.astype(jnp.float32) for term in terms)


def narrow(value):
    return value.astype(jnp.bfloat16)


def plane_tables(table):
    pair = jnp.stack([table, send_second(table)])
    return jnp.stack([pair, send_first(pair)])


def far_first(array):
    far = array[:, :, 1:].reshape((-1,) + array.shape[3:])
    return jnp.concatenate([far, array[:, :, 0].reshape((-1,) + array.shape[3:])])


def from_far_first(array, steps):
    far = array[:4 * (steps - 1)].reshape((2, 2, steps - 1) + array.shape[1:])
    return jnp.concatenate([array[4 * (steps - 1):].reshape((2, 2, 1) + array.shape[1:]), far], axis=2)


def start(source, target, semaphore):
    copy = pltpu.make_async_copy(source, target, semaphore)
    copy.start()
    return copy


def chosen_rows(pick, mine, other):
    return jnp.dot(pick, jnp.concatenate([mine, other]), preferred_element_type=jnp.float32)


def norm_kernel(count, pick_ref, *refs):
    pieces, gain_ref, normed_ref = refs[:4], refs[4], refs[-1]

    def work(mine_ref, other_ref):
        for group in range(count):
            rows = chosen_rows(pick_ref[group], mine_ref[group], other_ref[group])
            inv_rms = lax.rsqrt(jnp.mean(rows * rows, axis=1, keepdims=True) + 1e-06)
            normed_ref[group] = (rows * inv_rms * gain_ref[...]).astype(jnp.bfloat16)

    by_place(work, pieces)


def grad_kernel(count, pick_ref, *refs):
    pieces, prob_ref, out_ref, (grad_ref, value_ref) = refs[:4], refs[4], refs[5], refs[-2:]

    def work(mine_ref, other_ref):
        for group in range(count):
            rows = chosen_rows(pick_ref[group], mine_ref[group], other_ref[group])
            grad_ref[group] = (rows * prob_ref[group]).astype(jnp.bfloat16)
            value_ref[group] = jnp.sum(rows * out_ref[group].astype(jnp.float32), axis=1, keepdims=True)

    by_place(work, pieces)


def by_place(work, pieces):
    for first in range(2):
        for second in range(2):
            pl.when(pl.program_id(0) == first * 2 + second)(
                functools.partial(work, pieces[first], pieces[2 + second])
            )


def group_spec(count, first_group, *shape):
    first_block = first_group // count
    return pl.BlockSpec((count,) + shape, lambda i: (first_block + i, 0, 0))


def select(kernel, pick, pieces, extras, extra_specs, out_shapes, count, arrays, which, first_group, held):
    _, capacity, group_rows = pick.shape
    half, features = pieces[0].shape[1:]

    def piece_spec(place):
        return pl.BlockSpec((count, half, features), lambda i: (place(i) * arrays + which, 0, 0))

    return pl.pallas_call(
        functools.partial(kernel, count),
        grid=(4,),
        in_specs=[
            group_spec(count, first_group, capacity, group_rows),
            piece_spec(lambda i: jnp.minimum(i, 1)),
            piece_spec(lambda i: jnp.maximum(i - 2, 0)),
            piece_spec(lambda i: i // 2),
            piece_spec(lambda i: jnp.maximum(i - 2, 0)),
        ] + extra_specs + [pl.BlockSpec(memory_space=pl.ANY)] * len(held),
        out_specs=[group_spec(count, first_group, *out.shape[1:]) for out in out_shapes],
        out_shape=out_shapes,
        input_output_aliases={5 + len(extras) + n: n for n in range(len(held))},
        compiler_params=pltpu.CompilerParams(vmem_limit_bytes=VMEM_LIMIT),
        cost_estimate=LITTLE,
    )(pick, *pieces, *extras, *held)


def select_normed(pick, gain, pieces, count, arrays, first_group, held):
    groups, capacity, _ = pick.shape
    features = pieces[0].shape[2]
    return select(
        norm_kernel, pick, pieces, [gain], [pl.BlockSpec((1, features), lambda i: (0, 0))],
        [jax.ShapeDtypeStruct((groups, capacity, features), jnp.bfloat16)],
        count, arrays, 0, first_group, held,
    )


def select_grads(pick, prob, out_slots, pieces, count, arrays, which, first_group, held):
    groups, capacity, _ = pick.shape
    features = pieces[0].shape[2]
    return select(
        grad_kernel, pick, pieces, [prob, out_slots],
        [group_spec(count, first_group, capacity, 1), group_spec(count, first_group, capacity, features)],
        [
            jax.ShapeDtypeStruct((groups, capacity, features), jnp.bfloat16),
            jax.ShapeDtypeStruct((groups, capacity, 1), jnp.float32),
        ],
        count, arrays, which, first_group, held,
    )


def expand_kernel(weighted, count, first_group, back_ref, prob_ref, *refs):
    arrays = len(weighted)
    sources, mine_ref, pieces = refs[:arrays], refs[arrays], refs[arrays + 1:arrays + 3]
    loaded, spread, loads, stores = refs[arrays + 3:]
    half = mine_ref.shape[1]
    copies, written = [], []
    for group in range(4 * count):
        for number, source in enumerate(sources):
            place = group * arrays + number
            copies.append(start(source.at[first_group + group], loaded.at[place], loads.at[place]))
    for group in range(4 * count):
        outer, inner = divmod(group, count)
        first, second = divmod(outer, 2)
        for number, by_prob in enumerate(weighted):
            place = group * arrays + number
            copies[place].wait()
            rows = loaded[place]
            if by_prob:
                rows = (rows.astype(jnp.float32) * prob_ref[first_group + group]).astype(jnp.bfloat16)
            spread[place] = jnp.dot(
                back_ref[first_group + group], rows, preferred_element_type=jnp.float32
            ).astype(jnp.bfloat16)
            target = pieces[second].at[(first * count + inner) * arrays + number]
            written += [
                start(spread.at[place, pl.ds(half, half)], target, stores.at[place, 0]),
                start(spread.at[place, pl.ds(0, half)], mine_ref.at[place], stores.at[place, 1]),
            ]
    for copy in written:
        copy.wait()


def expand(back, prob, slots, weighted, count, first_group):
    _, group_rows, capacity = back.shape
    half, features, arrays = group_rows // 2, slots[0].shape[2], len(slots)
    blocks = 4 * count * arrays
    anywhere, whole = pl.BlockSpec(memory_space=pl.ANY), pl.BlockSpec(memory_space=pltpu.VMEM)
    piece = jax.ShapeDtypeStruct((blocks // 2, half, features), jnp.bfloat16)
    return pl.pallas_call(
        functools.partial(expand_kernel, weighted, count, first_group),
        in_specs=[whole, whole] + [anywhere] * arrays,
        out_specs=[anywhere] * 3,
        out_shape=[jax.ShapeDtypeStruct((blocks, half, features), jnp.bfloat16), piece, piece],
        scratch_shapes=[
            pltpu.VMEM((blocks, capacity, features), jnp.bfloat16),
            pltpu.VMEM((blocks, group_rows, features), jnp.bfloat16),
            pltpu.SemaphoreType.DMA((blocks,)),
            pltpu.SemaphoreType.DMA((blocks, 2)),
        ],
        compiler_params=pltpu.CompilerParams(vmem_limit_bytes=VMEM_LIMIT),
        cost_estimate=LITTLE,
    )(back, prob, *slots)


def forward_kernel(rows_ref, gate_up_ref, down_ref, gate_pre_ref, up_pre_ref, hidden_ref, out_ref):
    projected = jnp.dot(rows_ref[...], gate_up_ref[0], preferred_element_type=jnp.float32)
    half_width = hidden_ref.shape[1]
    gate_pre, up_pre = projected[:, :half_width], projected[:, half_width:]
    gate_pre_ref[...] = gate_pre
    up_pre_ref[...] = up_pre
    hidden = (gate_pre * jax.nn.sigmoid(gate_pre) * up_pre).astype(jnp.bfloat16)
    hidden_ref[...] = hidden
    out_ref[...] = jnp.dot(hidden, down_ref[0], preferred_element_type=jnp.float32).astype(jnp.bfloat16)


def forward(rows, gate_up_weight, down_weight):
    slots, features = rows.shape
    width = down_weight.shape[1]
    block = slots // 2

    def row_spec(columns):
        return pl.BlockSpec((block, columns), lambda i: (i, 0))

    return pl.pallas_call(
        forward_kernel,
        grid=(2,),
        in_specs=[
            row_spec(features),
            pl.BlockSpec((1, features, 2 * width), lambda i: (0, 0, 0)),
            pl.BlockSpec((1, width, features), lambda i: (0, 0, 0)),
        ],
        out_specs=[row_spec(width), row_spec(width), row_spec(width), row_spec(features)],
        out_shape=[
            jax.ShapeDtypeStruct((slots, width), jnp.float32),
            jax.ShapeDtypeStruct((slots, width), jnp.float32),
            jax.ShapeDtypeStruct((slots, width), jnp.bfloat16),
            jax.ShapeDtypeStruct((slots, features), jnp.bfloat16),
        ],
        compiler_params=pltpu.CompilerParams(vmem_limit_bytes=VMEM_LIMIT),
        cost_estimate=LITTLE,
    )(rows, gate_up_weight, down_weight)


def inner_kernel(units, grads_ref, gate_pre_ref, up_pre_ref, down_ref, joined_ref):
    step = pl.program_id(0)
    block = gate_pre_ref.shape[1]
    gate_pre, up_pre = gate_pre_ref[...], up_pre_ref[...]
    sigmoid_gate = jax.nn.sigmoid(gate_pre)
    common = times_transposed(grads_ref[...], down_ref[0]) * sigmoid_gate
    gate_grad = common * up_pre * (1.0 + gate_pre * (1.0 - sigmoid_gate))
    start = pl.multiple_of(step * block, block)
    joined_ref[:, pl.ds(start, block)] = gate_grad.astype(jnp.bfloat16)
    joined_ref[:, pl.ds(units * block + start, block)] = (common * gate_pre).astype(jnp.bfloat16)


def backward_hidden(grads, gate_pre, up_pre, down_weight):
    slots, features = grads.shape
    width = down_weight.shape[1]
    block, units = 256, width // 256
    return pl.pallas_call(
        functools.partial(inner_kernel, units),
        grid=(units,),
        in_specs=[
            pl.BlockSpec((slots, features), lambda i: (0, 0)),
            pl.BlockSpec((slots, block), lambda i: (0, i)),
            pl.BlockSpec((slots, block), lambda i: (0, i)),
            pl.BlockSpec((1, block, features), lambda i: (0, i, 0)),
        ],
        out_specs=pl.BlockSpec((slots, 2 * width), lambda i: (0, 0)),
        out_shape=jax.ShapeDtypeStruct((slots, 2 * width), jnp.bfloat16),
        compiler_params=pltpu.CompilerParams(vmem_limit_bytes=VMEM_LIMIT),
        cost_estimate=LITTLE,
    )(grads, gate_pre, up_pre, down_weight)


def input_kernel(joined_ref, gate_up_ref, rows_ref, *refs):
    input_ref, gain_ref = refs[-2:]
    input_grad = times_transposed(joined_ref[...], gate_up_ref[0]).astype(jnp.bfloat16)
    input_ref[...] = input_grad
    terms = input_grad.astype(jnp.float32) * rows_ref[...].astype(jnp.float32)
    gain_ref[...] = jnp.sum(terms, axis=0, keepdims=True)


def backward_input(joined_grad, gate_up_weight, rows, part, held):
    slots, features = rows.shape
    width = joined_grad.shape[1]
    wide = features // 4
    first = 2 * part
    return pl.pallas_call(
        input_kernel,
        grid=(2,),
        in_specs=[
            pl.BlockSpec((slots, width), lambda i: (0, 0)),
            pl.BlockSpec((1, wide, width), lambda i: (0, first + i, 0)),
            pl.BlockSpec((slots, wide), lambda i: (0, first + i)),
        ] + [pl.BlockSpec(memory_space=pl.ANY)] * len(held),
        out_specs=[
            pl.BlockSpec((slots, wide), lambda i: (0, first + i)),
            pl.BlockSpec((1, wide), lambda i: (0, i)),
        ],
        out_shape=[
            jax.ShapeDtypeStruct((slots, features), jnp.bfloat16),
            jax.ShapeDtypeStruct((1, features // 2), jnp.float32),
        ],
        input_output_aliases={3 + n: n for n in range(len(held))},
        compiler_params=pltpu.CompilerParams(vmem_limit_bytes=VMEM_LIMIT),
        cost_estimate=LITTLE,
    )(joined_grad, gate_up_weight, rows, *held)


def pack(columns, gains):
    return jnp.concatenate([columns.reshape(-1, 128), gains])


def unpack_add(columns, gains, got):
    count = gains.shape[0]
    return columns + got[:-count].reshape(columns.shape), gains + got[-count:]


def planes_in_order(gains):
    steps = len(gains)
    order = (lax.axis_index("expert") // 4 - jnp.arange(steps)) % steps
    ordered = jnp.take(jnp.stack(gains), order, axis=0)
    return functools.reduce(jnp.add, [ordered[step] for step in range(steps)]).reshape(-1)


def broadcast_shards(tokens, cotangent, gain, expert_ids, gate_probs, gate_up_weight, down_weight):
    expert_size = lax.axis_size("expert")
    steps = expert_size // 4
    far = 4 * (steps - 1)
    expert, core = lax.axis_index("expert"), lax.axis_index("tensor")
    my_expert = expert * EXP_DEV + core
    group_rows = expert_ids.shape[0]
    half = group_rows // 2
    features = tokens.shape[1]
    capacity = 3 * group_rows * TOP // (2 * EXP_DEV * expert_size)
    near_own = jnp.stack([tokens, cotangent])
    near_pair = jnp.concatenate([near_own, send_second(near_own)])
    near_far_pair = send_first(near_pair)
    tables = plane_tables(
        after(jnp.concatenate([expert_ids.T.astype(jnp.float32), gate_probs.T]), near_pair)
    )
    token_far = after(jnp.stack([send_along(tokens, -step) for step in range(1, steps)]), tables)
    late_tables = after(tables, token_far)
    far_tables = [send_along(late_tables, -step) for step in range(1, steps)]
    late_cot = after(cotangent, token_far)
    cot_steps = [send_along(late_cot, -step) for step in range(1, steps)]
    token_second = after(send_second(token_far), near_far_pair, cot_steps[0], *far_tables)
    token_pair = jnp.concatenate([token_far, token_second])
    tables = far_first(jnp.stack([tables] + far_tables, axis=2))
    tables = jnp.where(core == 0, tables, jnp.roll(tables, half, axis=2))
    matches = tables[:, :TOP] == my_expert.astype(jnp.float32)
    chosen = jnp.any(matches, axis=1)
    weight_of = jnp.sum(jnp.where(matches, tables[:, TOP:], 0.0), axis=1)
    row_ids = jnp.arange(group_rows, dtype=jnp.int32)
    earlier = (row_ids[:, None] < row_ids[None, :]).astype(jnp.bfloat16)
    rank_in = jnp.dot(chosen.astype(jnp.bfloat16), earlier, preferred_element_type=jnp.float32)
    placed = chosen[:, None, :] & (
        rank_in.astype(jnp.int32)[:, None, :] == jnp.arange(capacity, dtype=jnp.int32)[None, :, None]
    )
    pick = placed.astype(jnp.bfloat16)
    back = jnp.swapaxes(pick, 1, 2)
    slot_prob = jnp.sum(jnp.where(placed, weight_of[:, None, :], 0.0), axis=2, keepdims=True)

    gain_row = gain[None, :]
    near_pieces = (near_pair, near_far_pair, send_core(near_pair), send_core(near_far_pair))
    rows, = select_normed(pick, gain_row, near_pieces, 1, 2, far, ())
    cot_steps = together(*cot_steps, rows)
    rows, cot_far = cot_steps[-1], jnp.stack(cot_steps[:-1])
    token_far_pair, cot_far = together(send_first(token_pair), cot_far)
    cot_second = send_second(cot_far)
    token_pieces = (token_pair, token_far_pair, send_core(token_pair), send_core(token_far_pair))
    rows, = select_normed(pick, gain_row, token_pieces, steps - 1, 1, 0, (rows,))
    rows, cot_second = together(rows, cot_second)
    cot_pair = jnp.concatenate([cot_far, cot_second])
    cot_far_pair = send_first(cot_pair)

    rows = rows.reshape(-1, features)
    gate_pre, up_pre, hidden, block_out = forward(rows, gate_up_weight, down_weight)
    out_slots = block_out.reshape(expert_size, capacity, features)
    out_mine, out_low, out_high = expand(back, slot_prob, (out_slots,), (True,), steps - 1, 0)
    out_high, cot_far_pair = together(out_high, cot_far_pair)
    cot_pieces = (cot_pair, cot_far_pair, send_core(cot_pair), send_core(cot_far_pair))

    half_far, one_far = 2 * (steps - 1), steps - 1
    held = select_grads(
        after(pick, out_high), slot_prob, out_slots, near_pieces, 1, 2, 1, far, ()
    )
    out_core_high = after(send_core(out_high), held[1])
    out_core = send_core(out_low)
    out_upper = narrow(add_up(out_mine[half_far:], out_core_high))
    out_first = send_first(out_upper)
    grads, prob_value = select_grads(
        after(pick, out_upper), slot_prob, out_slots, cot_pieces, steps - 1, 1, 0, 0, tuple(held)
    )
    grads = grads.reshape(-1, features)
    joined_grad = backward_hidden(grads, gate_pre, up_pre, down_weight)
    input_grad, gain_low = backward_input(joined_grad, gate_up_weight, rows, 0, ())
    out_first, gain_low = together(out_first, gain_low)
    out_middle = narrow(
        add_up(out_mine[one_far:half_far], out_core[one_far:half_far], out_first[one_far:])
    )
    out_second = send_second(out_middle)
    input_grad, gain_high = backward_input(
        joined_grad, gate_up_weight, after(rows, out_middle), 1, (input_grad,)
    )
    gain_term = jnp.concatenate([gain_low[0], gain_high[0]])
    input_slots = input_grad.reshape(expert_size, capacity, features)
    in_mine, in_low, in_high = expand(back, slot_prob, (input_slots,), (False,), steps - 1, 0)
    in_high, out_second = together(in_high, out_second)
    in_core_high = send_core(in_high)
    in_core = send_core(in_low)

    def own_plane(mine, core_part, first_part, second_part, count):
        return add_up(mine[:count], core_part[:count], first_part[:count], second_part[:count])

    out_planes = narrow(own_plane(out_mine, out_core, out_first, out_second, one_far))
    out_far = [send_along(out_planes[step - 1], step) for step in range(1, steps)]
    in_upper = narrow(add_up(in_mine[half_far:], after(in_core_high, out_planes)))
    in_first = send_first(in_upper)
    gains = (gain_term / gain).reshape(-1, 128)
    prob_rows = jnp.sum(jnp.where(placed, prob_value, 0.0), axis=1)
    columns = from_far_first(jnp.where(matches, prob_rows[:, None, :], 0.0), steps)
    columns = jnp.where(core == 0, columns, jnp.swapaxes(columns, 0, 1))
    got = send_core(after(pack(columns[..., half:], gains), in_upper))
    gate_up_part = outer_sum(after(rows, in_upper), joined_grad)
    gate_up_part, got = together(gate_up_part, got)
    columns, gains = unpack_add(columns[..., :half], gains, got)
    got = send_bit(pack(columns[1], gains), 2)
    near_mine, near_low, near_high = expand(
        back, after(slot_prob, got), (out_slots, input_slots), (True, False), 1, far
    )
    near_high, got = together(near_high, got, *out_far[:-1])[:2]
    columns, gains = unpack_add(columns[0], gains, got)
    got = send_bit(pack(columns[1], gains), 1)
    near_core_high = send_core(near_high)
    near_core = send_core(near_low)
    down_part = outer_sum(after(hidden, near_high), grads)
    down_part, in_first, near_core, near_core_high, got = together(
        down_part, in_first, near_core, near_core_high, got
    )
    columns, gains = unpack_add(columns[0], gains, got)
    in_middle = narrow(
        add_up(in_mine[one_far:half_far], in_core[one_far:half_far], in_first[one_far:])
    )
    in_second = send_second(in_middle)
    messages = [send_along(pack(columns[step], gains), step) for step in range(1, steps)]
    near_upper = narrow(add_up(near_mine[4:], near_core_high))
    in_second, near_upper, *messages = together(in_second, near_upper, *messages, *out_far[-1:])[:2 + len(messages)]
    in_planes = narrow(own_plane(in_mine, in_core, in_first, in_second, one_far))
    in_far = [send_along(in_planes[step - 1], step) for step in range(1, steps)]
    near_first = send_first(after(near_upper, in_planes))
    near_middle = narrow(add_up(near_mine[2:4], near_core[2:], near_first[2:]))
    near_second = send_second(near_middle)
    near_sum = own_plane(near_mine, near_core, near_first, near_second, 2)
    out_sum = near_sum[0] + add_up(*out_far)
    normed_grad = near_sum[1] + add_up(*in_far)

    prob_sum, all_gains = columns[0], [gains]
    for message in messages:
        prob_sum = prob_sum + message[:-gains.shape[0]].reshape(prob_sum.shape)
        all_gains.append(message[-gains.shape[0]:])
    gain_grad = planes_in_order(all_gains)

    scaled_own, inv_own = normalize(tokens)
    mixed = (tokens.astype(jnp.float32) + out_sum).astype(jnp.bfloat16)
    gain_side = normed_grad * gain[None, :]
    token_grad = (
        cotangent.astype(jnp.float32)
        + inv_own
        * (gain_side - scaled_own * jnp.mean(gain_side * scaled_own, axis=1, keepdims=True))
    ).astype(jnp.bfloat16)
    return (mixed, token_grad, prob_sum.T, gain_grad, gate_up_part[None], down_part[None])


def solution(mesh):
    in_specs = (
        P(("expert", "tensor"), None),
        P(("expert", "tensor"), None),
        P(),
        P("expert", None),
        P("expert", None),
        P(("expert", "tensor"), None, None),
        P(("expert", "tensor"), None, None),
    )
    out_specs = (
        P(("expert", "tensor"), None),
        P(("expert", "tensor"), None),
        P(("expert", "tensor"), None),
        P(),
        P(("expert", "tensor"), None, None),
        P(("expert", "tensor"), None, None),
    )
    expert_size, tensor_size = mesh.shape["expert"], mesh.shape["tensor"]
    few = tensor_size == EXP_DEV and expert_size % 4 == 0 and expert_size <= 4 * TOP
    shards = broadcast_shards if few else routed_shards
    return jax.shard_map(shards, mesh=mesh, in_specs=in_specs, out_specs=out_specs, check_vma=False)
```

```python
import functools

import jax
import jax.numpy as jnp
from jax import lax
from jax.experimental import pallas as pl
from jax.experimental.pallas import tpu as pltpu
from jax.sharding import PartitionSpec as P

TOP = 8
EXP_DEV = 2
VMEM_LIMIT = 63 * 1024 * 1024
LITTLE = pl.CostEstimate(flops=1000000, bytes_accessed=100000, transcendentals=0)


def normalize(rows):
    values = rows.astype(jnp.float32)
    inv_rms = lax.rsqrt(jnp.mean(values * values, axis=1, keepdims=True) + 1e-06)
    return (values * inv_rms, inv_rms)


def expert_forward(rows, gate_up, down_proj):
    projected = jnp.dot(rows, gate_up, preferred_element_type=jnp.float32)
    half_width = down_proj.shape[0]
    gate_pre = projected[:, :half_width]
    up_pre = projected[:, half_width:]
    sigmoid_gate = jax.nn.sigmoid(gate_pre)
    hidden = (gate_pre * sigmoid_gate * up_pre).astype(jnp.bfloat16)
    block_out = jnp.dot(hidden, down_proj, preferred_element_type=jnp.float32).astype(jnp.bfloat16)
    return (gate_pre, up_pre, sigmoid_gate, hidden, block_out)


def times_transposed(left, right):
    return lax.dot_general(left, right, (((1,), (1,)), ((), ())), preferred_element_type=jnp.float32)


def outer_sum(left, right):
    product = lax.dot_general(left, right, (((0,), (0,)), ((), ())), preferred_element_type=jnp.float32)
    return product.astype(jnp.bfloat16)


def backward_inner(slot_grads, down_proj, gate_pre, up_pre, sigmoid_gate):
    hidden_grad = times_transposed(slot_grads, down_proj)
    gate_grad = (
        hidden_grad * up_pre * sigmoid_gate * (1.0 + gate_pre * (1.0 - sigmoid_gate))
    ).astype(jnp.bfloat16)
    up_grad = (hidden_grad * gate_pre * sigmoid_gate).astype(jnp.bfloat16)
    return jnp.concatenate([gate_grad, up_grad], axis=1)


def expert_backward(rows, slot_grads, gate_up, down_proj, gate_pre, up_pre, sigmoid_gate, hidden):
    joined_grad = backward_inner(slot_grads, down_proj, gate_pre, up_pre, sigmoid_gate)
    input_grad = times_transposed(joined_grad, gate_up).astype(jnp.bfloat16)
    return (input_grad, outer_sum(rows, joined_grad), outer_sum(hidden, slot_grads))


def routed_shards(tokens, cotangent, gain, expert_ids, gate_probs, gate_up_weight, down_weight):
    tensor_size = lax.axis_size("tensor")
    expert_size = lax.axis_size("expert")
    my_rank = lax.axis_index("tensor")
    blocks_each = tensor_size // EXP_DEV
    my_type = my_rank // blocks_each
    group_rows = expert_ids.shape[0]
    features = tokens.shape[1]
    capacity = 3 * group_rows * TOP // (2 * EXP_DEV * expert_size)
    highest = lax.Precision.HIGHEST
    scaled_own, inv_own = normalize(tokens)
    carried = (scaled_own * gain[None, :]).astype(jnp.bfloat16)
    group_first, group_grads = (
        lax.all_gather(carried, "tensor", axis=0, tiled=True),
        lax.all_gather(cotangent, "tensor", axis=0, tiled=True),
    )
    targets = jnp.arange(expert_size, dtype=jnp.int32) * EXP_DEV + my_type
    matches = expert_ids[:, :, None] == targets[None, None, :]
    chosen = jnp.any(matches, axis=1)
    weight_of = jnp.sum(jnp.where(matches, gate_probs[:, :, None], 0.0), axis=1)
    slot_of = jnp.sum(
        jnp.where(matches, jnp.arange(TOP, dtype=jnp.int32)[None, :, None], 0), axis=1
    )
    row_ids = jnp.arange(group_rows, dtype=jnp.int32)
    earlier = (row_ids[None, :] < row_ids[:, None]).astype(jnp.bfloat16)
    rank_in = jnp.dot(
        earlier, chosen.astype(jnp.bfloat16), preferred_element_type=jnp.float32
    ).astype(jnp.int32)
    placed = chosen.T[:, None, :] & (
        rank_in.T[:, None, :] == jnp.arange(capacity, dtype=jnp.int32)[None, :, None]
    )
    source = jnp.sum(jnp.where(placed, row_ids[None, None, :], 0), axis=2)
    filled = jnp.any(placed, axis=2)
    slot_prob = jnp.sum(jnp.where(placed, weight_of.T[:, None, :], 0.0), axis=2)
    slot_index = jnp.sum(jnp.where(placed, slot_of.T[:, None, :], 0), axis=2)
    sent_rows = jnp.where(
        filled[:, :, None], jnp.take(group_first, source, axis=0), jnp.zeros((), jnp.bfloat16)
    )
    sent_grads = (
        slot_prob[:, :, None] * jnp.take(group_grads, source, axis=0).astype(jnp.float32)
    ).astype(jnp.bfloat16)
    gate_up = gate_up_weight[0]
    down_proj = down_weight[0]
    arrived_rows, arrived_grads = (
        lax.all_to_all(sent_rows, "expert", split_axis=0, concat_axis=0, tiled=True),
        lax.all_to_all(sent_grads, "expert", split_axis=0, concat_axis=0, tiled=True),
    )
    rows = arrived_rows.reshape(-1, features)
    slot_grads = arrived_grads.reshape(-1, features)
    gate_pre, up_pre, sigmoid_gate, hidden, block_out = expert_forward(rows, gate_up, down_proj)
    out_slots = block_out.reshape(expert_size, capacity, features)
    input_grad, gate_up_part, down_part = expert_backward(
        rows, slot_grads, gate_up, down_proj, gate_pre, up_pre, sigmoid_gate, hidden
    )
    input_slots = input_grad.reshape(expert_size, capacity, features)
    out_back, input_back = (
        lax.all_to_all(out_slots, "expert", split_axis=0, concat_axis=0, tiled=True),
        lax.all_to_all(input_slots, "expert", split_axis=0, concat_axis=0, tiled=True),
    )
    out_flat = out_back.reshape(-1, features)
    input_flat = input_back.reshape(-1, features)
    used_source = source.reshape(-1)
    used_filled = filled.reshape(-1)
    used_prob = slot_prob.reshape(-1)
    used_index = slot_index.reshape(-1)
    cot_slots = jnp.take(group_grads, used_source, axis=0)
    prob_values = jnp.einsum("sd,sd->s", cot_slots, out_flat, preferred_element_type=jnp.float32)
    hit = (row_ids[:, None] == used_source[None, :]) & used_filled[None, :]
    input_part = jnp.dot(hit.astype(jnp.bfloat16), input_flat, preferred_element_type=jnp.float32)
    weighting = jnp.where(hit, used_prob[None, :], 0.0)
    out_part = jnp.dot(
        weighting,
        out_flat.astype(jnp.float32),
        precision=highest,
        preferred_element_type=jnp.float32,
    )
    prob_columns = jnp.where(
        used_index[:, None] == jnp.arange(TOP, dtype=jnp.int32)[None, :], prob_values[:, None], 0.0
    )
    prob_part = jnp.dot(
        hit.astype(jnp.float32), prob_columns, precision=highest, preferred_element_type=jnp.float32
    )
    out_sum, normed_grad, prob_grad = (
        lax.psum_scatter(out_part, "tensor", scatter_dimension=0, tiled=True),
        lax.psum_scatter(input_part, "tensor", scatter_dimension=0, tiled=True),
        lax.psum_scatter(prob_part, "tensor", scatter_dimension=0, tiled=True),
    )
    mixed = (tokens.astype(jnp.float32) + out_sum).astype(jnp.bfloat16)
    gain_side = normed_grad * gain[None, :]
    token_grad = (
        cotangent.astype(jnp.float32)
        + inv_own
        * (gain_side - scaled_own * jnp.mean(gain_side * scaled_own, axis=1, keepdims=True))
    ).astype(jnp.bfloat16)
    gain_grad = lax.psum(jnp.sum(normed_grad * scaled_own, axis=0), ("expert", "tensor"))
    return (mixed, token_grad, prob_grad, gain_grad, gate_up_part[None], down_part[None])


BOTH = ("expert", "tensor")


def flip_first(expert, core):
    return expert ^ (2 if core == 0 else 1)


def flip_second(expert, core):
    return expert ^ (1 if core == 0 else 2)


def send(array, place):
    pairs = []
    for expert in range(lax.axis_size("expert")):
        for core in range(2):
            to_expert, to_core = place(expert, core)
            pairs.append((expert * 2 + core, to_expert * 2 + to_core))
    return lax.ppermute(array, BOTH, pairs)


def send_first(array):
    return send(array, lambda e, c: (flip_first(e, c), c))


def send_second(array):
    return send(array, lambda e, c: (flip_second(e, c), c))


def send_bit(array, bit):
    return send(array, lambda e, c: (e ^ bit, c))


def send_core(array):
    return send(array, lambda e, c: (e, 1 - c))


def send_along(array, step):
    size = lax.axis_size("expert")
    return send(array, lambda e, c: ((e + 4 * step) % size, c))


def after(array, *others):
    return lax.optimization_barrier((array,) + others)[0]


def together(*arrays):
    return lax.optimization_barrier(arrays)


def add_up(*terms):
    return sum(term.astype(jnp.float32) for term in terms)


def narrow(value):
    return value.astype(jnp.bfloat16)


def plane_tables(table):
    pair = jnp.stack([table, send_second(table)])
    return jnp.stack([pair, send_first(pair)])


def far_first(array):
    far = array[:, :, 1:].reshape((-1,) + array.shape[3:])
    return jnp.concatenate([far, array[:, :, 0].reshape((-1,) + array.shape[3:])])


def from_far_first(array, steps):
    far = array[:4 * (steps - 1)].reshape((2, 2, steps - 1) + array.shape[1:])
    return jnp.concatenate([array[4 * (steps - 1):].reshape((2, 2, 1) + array.shape[1:]), far], axis=2)


def start(source, target, semaphore):
    copy = pltpu.make_async_copy(source, target, semaphore)
    copy.start()
    return copy


def chosen_rows(pick, mine, other):
    return jnp.dot(pick, jnp.concatenate([mine, other]), preferred_element_type=jnp.float32)


def norm_kernel(count, pick_ref, *refs):
    pieces, gain_ref, normed_ref = refs[:4], refs[4], refs[-1]

    def work(mine_ref, other_ref):
        for group in range(count):
            rows = chosen_rows(pick_ref[group], mine_ref[group], other_ref[group])
            inv_rms = lax.rsqrt(jnp.mean(rows * rows, axis=1, keepdims=True) + 1e-06)
            normed_ref[group] = (rows * inv_rms * gain_ref[...]).astype(jnp.bfloat16)

    by_place(work, pieces)


def grad_kernel(count, pick_ref, *refs):
    pieces, prob_ref, out_ref, (grad_ref, value_ref) = refs[:4], refs[4], refs[5], refs[-2:]

    def work(mine_ref, other_ref):
        for group in range(count):
            rows = chosen_rows(pick_ref[group], mine_ref[group], other_ref[group])
            grad_ref[group] = (rows * prob_ref[group]).astype(jnp.bfloat16)
            value_ref[group] = jnp.sum(rows * out_ref[group].astype(jnp.float32), axis=1, keepdims=True)

    by_place(work, pieces)


def by_place(work, pieces):
    for first in range(2):
        for second in range(2):
            pl.when(pl.program_id(0) == first * 2 + second)(
                functools.partial(work, pieces[first], pieces[2 + second])
            )


def group_spec(count, first_group, *shape):
    first_block = first_group // count
    return pl.BlockSpec((count,) + shape, lambda i: (first_block + i, 0, 0))


def select(kernel, pick, pieces, extras, extra_specs, out_shapes, count, arrays, which, first_group, held):
    _, capacity, group_rows = pick.shape
    half, features = pieces[0].shape[1:]

    def piece_spec(place):
        return pl.BlockSpec((count, half, features), lambda i: (place(i) * arrays + which, 0, 0))

    return pl.pallas_call(
        functools.partial(kernel, count),
        grid=(4,),
        in_specs=[
            group_spec(count, first_group, capacity, group_rows),
            piece_spec(lambda i: jnp.minimum(i, 1)),
            piece_spec(lambda i: jnp.maximum(i - 2, 0)),
            piece_spec(lambda i: i // 2),
            piece_spec(lambda i: jnp.maximum(i - 2, 0)),
        ] + extra_specs + [pl.BlockSpec(memory_space=pl.ANY)] * len(held),
        out_specs=[group_spec(count, first_group, *out.shape[1:]) for out in out_shapes],
        out_shape=out_shapes,
        input_output_aliases={5 + len(extras) + n: n for n in range(len(held))},
        compiler_params=pltpu.CompilerParams(vmem_limit_bytes=VMEM_LIMIT),
        cost_estimate=LITTLE,
    )(pick, *pieces, *extras, *held)


def select_normed(pick, gain, pieces, count, arrays, first_group, held):
    groups, capacity, _ = pick.shape
    features = pieces[0].shape[2]
    return select(
        norm_kernel, pick, pieces, [gain], [pl.BlockSpec((1, features), lambda i: (0, 0))],
        [jax.ShapeDtypeStruct((groups, capacity, features), jnp.bfloat16)],
        count, arrays, 0, first_group, held,
    )


def select_grads(pick, prob, out_slots, pieces, count, arrays, which, first_group, held):
    groups, capacity, _ = pick.shape
    features = pieces[0].shape[2]
    return select(
        grad_kernel, pick, pieces, [prob, out_slots],
        [group_spec(count, first_group, capacity, 1), group_spec(count, first_group, capacity, features)],
        [
            jax.ShapeDtypeStruct((groups, capacity, features), jnp.bfloat16),
            jax.ShapeDtypeStruct((groups, capacity, 1), jnp.float32),
        ],
        count, arrays, which, first_group, held,
    )


def expand_kernel(weighted, count, first_group, back_ref, prob_ref, *refs):
    arrays = len(weighted)
    sources, mine_ref, pieces = refs[:arrays], refs[arrays], refs[arrays + 1:arrays + 3]
    loaded, spread, loads, stores = refs[arrays + 3:]
    half = mine_ref.shape[1]
    copies, written = [], []
    for group in range(4 * count):
        for number, source in enumerate(sources):
            place = group * arrays + number
            copies.append(start(source.at[first_group + group], loaded.at[place], loads.at[place]))
    for group in range(4 * count):
        outer, inner = divmod(group, count)
        first, second = divmod(outer, 2)
        for number, by_prob in enumerate(weighted):
            place = group * arrays + number
            copies[place].wait()
            rows = loaded[place]
            if by_prob:
                rows = (rows.astype(jnp.float32) * prob_ref[first_group + group]).astype(jnp.bfloat16)
            spread[place] = jnp.dot(
                back_ref[first_group + group], rows, preferred_element_type=jnp.float32
            ).astype(jnp.bfloat16)
            target = pieces[second].at[(first * count + inner) * arrays + number]
            written += [
                start(spread.at[place, pl.ds(half, half)], target, stores.at[place, 0]),
                start(spread.at[place, pl.ds(0, half)], mine_ref.at[place], stores.at[place, 1]),
            ]
    for copy in written:
        copy.wait()


def expand(back, prob, slots, weighted, count, first_group):
    _, group_rows, capacity = back.shape
    half, features, arrays = group_rows // 2, slots[0].shape[2], len(slots)
    blocks = 4 * count * arrays
    anywhere, whole = pl.BlockSpec(memory_space=pl.ANY), pl.BlockSpec(memory_space=pltpu.VMEM)
    piece = jax.ShapeDtypeStruct((blocks // 2, half, features), jnp.bfloat16)
    return pl.pallas_call(
        functools.partial(expand_kernel, weighted, count, first_group),
        in_specs=[whole, whole] + [anywhere] * arrays,
        out_specs=[anywhere] * 3,
        out_shape=[jax.ShapeDtypeStruct((blocks, half, features), jnp.bfloat16), piece, piece],
        scratch_shapes=[
            pltpu.VMEM((blocks, capacity, features), jnp.bfloat16),
            pltpu.VMEM((blocks, group_rows, features), jnp.bfloat16),
            pltpu.SemaphoreType.DMA((blocks,)),
            pltpu.SemaphoreType.DMA((blocks, 2)),
        ],
        compiler_params=pltpu.CompilerParams(vmem_limit_bytes=VMEM_LIMIT),
        cost_estimate=LITTLE,
    )(back, prob, *slots)


def forward_kernel(rows_ref, gate_up_ref, down_ref, gate_pre_ref, up_pre_ref, hidden_ref, out_ref):
    projected = jnp.dot(rows_ref[...], gate_up_ref[0], preferred_element_type=jnp.float32)
    half_width = hidden_ref.shape[1]
    gate_pre, up_pre = projected[:, :half_width], projected[:, half_width:]
    gate_pre_ref[...] = gate_pre.astype(jnp.bfloat16)
    up_pre_ref[...] = up_pre.astype(jnp.bfloat16)
    hidden = (gate_pre * jax.nn.sigmoid(gate_pre) * up_pre).astype(jnp.bfloat16)
    hidden_ref[...] = hidden
    out_ref[...] = jnp.dot(hidden, down_ref[0], preferred_element_type=jnp.float32).astype(jnp.bfloat16)


def forward(rows, gate_up_weight, down_weight):
    slots, features = rows.shape
    width = down_weight.shape[1]
    block = slots // 2

    def row_spec(columns):
        return pl.BlockSpec((block, columns), lambda i: (i, 0))

    return pl.pallas_call(
        forward_kernel,
        grid=(2,),
        in_specs=[
            row_spec(features),
            pl.BlockSpec((1, features, 2 * width), lambda i: (0, 0, 0)),
            pl.BlockSpec((1, width, features), lambda i: (0, 0, 0)),
        ],
        out_specs=[row_spec(width), row_spec(width), row_spec(width), row_spec(features)],
        out_shape=[
            jax.ShapeDtypeStruct((slots, width), jnp.bfloat16),
            jax.ShapeDtypeStruct((slots, width), jnp.bfloat16),
            jax.ShapeDtypeStruct((slots, width), jnp.bfloat16),
            jax.ShapeDtypeStruct((slots, features), jnp.bfloat16),
        ],
        compiler_params=pltpu.CompilerParams(vmem_limit_bytes=VMEM_LIMIT),
        cost_estimate=LITTLE,
    )(rows, gate_up_weight, down_weight)


def inner_kernel(units, grads_ref, gate_pre_ref, up_pre_ref, down_ref, joined_ref):
    step = pl.program_id(0)
    block = gate_pre_ref.shape[1]
    gate_pre, up_pre = gate_pre_ref[...].astype(jnp.float32), up_pre_ref[...].astype(jnp.float32)
    sigmoid_gate = jax.nn.sigmoid(gate_pre)
    common = times_transposed(grads_ref[...], down_ref[0]) * sigmoid_gate
    gate_grad = common * up_pre * (1.0 + gate_pre * (1.0 - sigmoid_gate))
    start = pl.multiple_of(step * block, block)
    joined_ref[:, pl.ds(start, block)] = gate_grad.astype(jnp.bfloat16)
    joined_ref[:, pl.ds(units * block + start, block)] = (common * gate_pre).astype(jnp.bfloat16)


def backward_hidden(grads, gate_pre, up_pre, down_weight):
    slots, features = grads.shape
    width = down_weight.shape[1]
    block, units = 256, width // 256
    return pl.pallas_call(
        functools.partial(inner_kernel, units),
        grid=(units,),
        in_specs=[
            pl.BlockSpec((slots, features), lambda i: (0, 0)),
            pl.BlockSpec((slots, block), lambda i: (0, i)),
            pl.BlockSpec((slots, block), lambda i: (0, i)),
            pl.BlockSpec((1, block, features), lambda i: (0, i, 0)),
        ],
        out_specs=pl.BlockSpec((slots, 2 * width), lambda i: (0, 0)),
        out_shape=jax.ShapeDtypeStruct((slots, 2 * width), jnp.bfloat16),
        compiler_params=pltpu.CompilerParams(vmem_limit_bytes=VMEM_LIMIT),
        cost_estimate=LITTLE,
    )(grads, gate_pre, up_pre, down_weight)


def input_kernel(joined_ref, gate_up_ref, rows_ref, *refs):
    input_ref, gain_ref = refs[-2:]
    input_grad = times_transposed(joined_ref[...], gate_up_ref[0]).astype(jnp.bfloat16)
    input_ref[...] = input_grad
    terms = input_grad.astype(jnp.float32) * rows_ref[...].astype(jnp.float32)
    gain_ref[...] = jnp.sum(terms, axis=0, keepdims=True)


def backward_input(joined_grad, gate_up_weight, rows, part, held):
    slots, features = rows.shape
    width = joined_grad.shape[1]
    wide = features // 4
    first = 2 * part
    return pl.pallas_call(
        input_kernel,
        grid=(2,),
        in_specs=[
            pl.BlockSpec((slots, width), lambda i: (0, 0)),
            pl.BlockSpec((1, wide, width), lambda i: (0, first + i, 0)),
            pl.BlockSpec((slots, wide), lambda i: (0, first + i)),
        ] + [pl.BlockSpec(memory_space=pl.ANY)] * len(held),
        out_specs=[
            pl.BlockSpec((slots, wide), lambda i: (0, first + i)),
            pl.BlockSpec((1, wide), lambda i: (0, i)),
        ],
        out_shape=[
            jax.ShapeDtypeStruct((slots, features), jnp.bfloat16),
            jax.ShapeDtypeStruct((1, features // 2), jnp.float32),
        ],
        input_output_aliases={3 + n: n for n in range(len(held))},
        compiler_params=pltpu.CompilerParams(vmem_limit_bytes=VMEM_LIMIT),
        cost_estimate=LITTLE,
    )(joined_grad, gate_up_weight, rows, *held)


def pack(columns, gains):
    return jnp.concatenate([columns.reshape(-1, 128), gains])


def unpack_add(columns, gains, got):
    count = gains.shape[0]
    return columns + got[:-count].reshape(columns.shape), gains + got[-count:]


def planes_in_order(gains):
    steps = len(gains)
    order = (lax.axis_index("expert") // 4 - jnp.arange(steps)) % steps
    ordered = jnp.take(jnp.stack(gains), order, axis=0)
    return functools.reduce(jnp.add, [ordered[step] for step in range(steps)]).reshape(-1)


def broadcast_shards(tokens, cotangent, gain, expert_ids, gate_probs, gate_up_weight, down_weight):
    expert_size = lax.axis_size("expert")
    steps = expert_size // 4
    far = 4 * (steps - 1)
    expert, core = lax.axis_index("expert"), lax.axis_index("tensor")
    my_expert = expert * EXP_DEV + core
    group_rows = expert_ids.shape[0]
    half = group_rows // 2
    features = tokens.shape[1]
    capacity = 3 * group_rows * TOP // (2 * EXP_DEV * expert_size)
    near_own = jnp.stack([tokens, cotangent])
    near_pair = jnp.concatenate([near_own, send_second(near_own)])
    near_far_pair = send_first(near_pair)
    tables = plane_tables(
        after(jnp.concatenate([expert_ids.T.astype(jnp.float32), gate_probs.T]), near_pair)
    )
    token_far = after(jnp.stack([send_along(tokens, -step) for step in range(1, steps)]), tables)
    late_tables = after(tables, token_far)
    far_tables = [send_along(late_tables, -step) for step in range(1, steps)]
    late_cot = after(cotangent, token_far)
    cot_steps = [send_along(late_cot, -step) for step in range(1, steps)]
    token_second = after(send_second(token_far), near_far_pair, cot_steps[0], *far_tables)
    token_pair = jnp.concatenate([token_far, token_second])
    tables = far_first(jnp.stack([tables] + far_tables, axis=2))
    tables = jnp.where(core == 0, tables, jnp.roll(tables, half, axis=2))
    matches = tables[:, :TOP] == my_expert.astype(jnp.float32)
    chosen = jnp.any(matches, axis=1)
    weight_of = jnp.sum(jnp.where(matches, tables[:, TOP:], 0.0), axis=1)
    row_ids = jnp.arange(group_rows, dtype=jnp.int32)
    earlier = (row_ids[:, None] < row_ids[None, :]).astype(jnp.bfloat16)
    rank_in = jnp.dot(chosen.astype(jnp.bfloat16), earlier, preferred_element_type=jnp.float32)
    placed = chosen[:, None, :] & (
        rank_in.astype(jnp.int32)[:, None, :] == jnp.arange(capacity, dtype=jnp.int32)[None, :, None]
    )
    pick = placed.astype(jnp.bfloat16)
    back = jnp.swapaxes(pick, 1, 2)
    slot_prob = jnp.sum(jnp.where(placed, weight_of[:, None, :], 0.0), axis=2, keepdims=True)

    gain_row = gain[None, :]
    near_pieces = (near_pair, near_far_pair, send_core(near_pair), send_core(near_far_pair))
    rows, = select_normed(pick, gain_row, near_pieces, 1, 2, far, ())
    cot_steps = together(*cot_steps, rows)
    rows, cot_far = cot_steps[-1], jnp.stack(cot_steps[:-1])
    token_far_pair, cot_far = together(send_first(token_pair), cot_far)
    cot_second = send_second(cot_far)
    token_pieces = (token_pair, token_far_pair, send_core(token_pair), send_core(token_far_pair))
    rows, = select_normed(pick, gain_row, token_pieces, steps - 1, 1, 0, (rows,))
    rows, cot_second = together(rows, cot_second)
    cot_pair = jnp.concatenate([cot_far, cot_second])
    cot_far_pair = send_first(cot_pair)

    rows = rows.reshape(-1, features)
    gate_pre, up_pre, hidden, block_out = forward(rows, gate_up_weight, down_weight)
    out_slots = block_out.reshape(expert_size, capacity, features)
    out_mine, out_low, out_high = expand(back, slot_prob, (out_slots,), (True,), steps - 1, 0)
    out_high, cot_far_pair = together(out_high, cot_far_pair)
    cot_pieces = (cot_pair, cot_far_pair, send_core(cot_pair), send_core(cot_far_pair))

    half_far, one_far = 2 * (steps - 1), steps - 1
    held = select_grads(
        after(pick, out_high), slot_prob, out_slots, near_pieces, 1, 2, 1, far, ()
    )
    out_core_high = after(send_core(out_high), held[1])
    out_core = send_core(out_low)
    out_upper = narrow(add_up(out_mine[half_far:], out_core_high))
    out_first = send_first(out_upper)
    grads, prob_value = select_grads(
        after(pick, out_upper), slot_prob, out_slots, cot_pieces, steps - 1, 1, 0, 0, tuple(held)
    )
    grads = grads.reshape(-1, features)
    joined_grad = backward_hidden(grads, gate_pre, up_pre, down_weight)
    input_grad, gain_low = backward_input(joined_grad, gate_up_weight, rows, 0, ())
    out_first, gain_low = together(out_first, gain_low)
    out_middle = narrow(
        add_up(out_mine[one_far:half_far], out_core[one_far:half_far], out_first[one_far:])
    )
    out_second = send_second(out_middle)
    input_grad, gain_high = backward_input(
        joined_grad, gate_up_weight, after(rows, out_middle), 1, (input_grad,)
    )
    gain_term = jnp.concatenate([gain_low[0], gain_high[0]])
    input_slots = input_grad.reshape(expert_size, capacity, features)
    in_mine, in_low, in_high = expand(back, slot_prob, (input_slots,), (False,), steps - 1, 0)
    in_high, out_second = together(in_high, out_second)
    in_core_high = send_core(in_high)
    in_core = send_core(in_low)

    def own_plane(mine, core_part, first_part, second_part, count):
        return add_up(mine[:count], core_part[:count], first_part[:count], second_part[:count])

    out_planes = narrow(own_plane(out_mine, out_core, out_first, out_second, one_far))
    out_far = [send_along(out_planes[step - 1], step) for step in range(1, steps)]
    in_upper = narrow(add_up(in_mine[half_far:], after(in_core_high, out_planes)))
    in_first = send_first(in_upper)
    gains = (gain_term / gain).reshape(-1, 128)
    prob_rows = jnp.sum(jnp.where(placed, prob_value, 0.0), axis=1)
    columns = from_far_first(jnp.where(matches, prob_rows[:, None, :], 0.0), steps)
    columns = jnp.where(core == 0, columns, jnp.swapaxes(columns, 0, 1))
    got = send_core(after(pack(columns[..., half:], gains), in_upper))
    gate_up_part = outer_sum(after(rows, in_upper), joined_grad)
    gate_up_part, got = together(gate_up_part, got)
    columns, gains = unpack_add(columns[..., :half], gains, got)
    got = send_bit(pack(columns[1], gains), 2)
    near_mine, near_low, near_high = expand(
        back, after(slot_prob, gate_up_part), (out_slots, input_slots), (True, False), 1, far
    )
    near_high = after(near_high, *out_far[:-1])
    near_core_high = send_core(near_high)
    near_core = send_core(near_low)
    down_part = outer_sum(after(hidden, near_high), grads)
    down_part, in_first, near_core, near_core_high, got = together(
        down_part, in_first, near_core, near_core_high, got
    )
    columns, gains = unpack_add(columns[0], gains, got)
    in_middle = narrow(
        add_up(in_mine[one_far:half_far], in_core[one_far:half_far], in_first[one_far:])
    )
    in_second = send_second(in_middle)
    got = send_bit(pack(columns[1], gains), 1)
    near_upper = narrow(add_up(near_mine[4:], near_core_high))
    in_second, near_upper, got = together(in_second, near_upper, got, *out_far[-1:])[:3]
    columns, gains = unpack_add(columns[0], gains, got)
    in_planes = narrow(own_plane(in_mine, in_core, in_first, in_second, one_far))
    in_far = [send_along(in_planes[step - 1], step) for step in range(1, steps)]
    near_first = send_first(after(near_upper, in_planes))
    near_first, *in_far[:-1] = together(near_first, *in_far[:-1])
    near_middle = narrow(add_up(near_mine[2:4], near_core[2:], near_first[2:]))
    near_second = send_second(near_middle)
    messages = [
        send_along(after(pack(columns[step], gains), near_middle), step) for step in range(1, steps)
    ]
    near_sum = own_plane(near_mine, near_core, near_first, near_second, 2)
    out_sum = near_sum[0] + add_up(*out_far)
    normed_grad = near_sum[1] + add_up(*in_far)

    prob_sum, all_gains = columns[0], [gains]
    for message in messages:
        prob_sum = prob_sum + message[:-gains.shape[0]].reshape(prob_sum.shape)
        all_gains.append(message[-gains.shape[0]:])
    gain_grad = planes_in_order(all_gains)

    scaled_own, inv_own = normalize(tokens)
    mixed = (tokens.astype(jnp.float32) + out_sum).astype(jnp.bfloat16)
    gain_side = normed_grad * gain[None, :]
    token_grad = (
        cotangent.astype(jnp.float32)
        + inv_own
        * (gain_side - scaled_own * jnp.mean(gain_side * scaled_own, axis=1, keepdims=True))
    ).astype(jnp.bfloat16)
    return (mixed, token_grad, prob_sum.T, gain_grad, gate_up_part[None], down_part[None])


def solution(mesh):
    in_specs = (
        P(("expert", "tensor"), None),
        P(("expert", "tensor"), None),
        P(),
        P("expert", None),
        P("expert", None),
        P(("expert", "tensor"), None, None),
        P(("expert", "tensor"), None, None),
    )
    out_specs = (
        P(("expert", "tensor"), None),
        P(("expert", "tensor"), None),
        P(("expert", "tensor"), None),
        P(),
        P(("expert", "tensor"), None, None),
        P(("expert", "tensor"), None, None),
    )
    expert_size, tensor_size = mesh.shape["expert"], mesh.shape["tensor"]
    few = tensor_size == EXP_DEV and expert_size % 4 == 0 and expert_size <= 4 * TOP
    shards = broadcast_shards if few else routed_shards
    return jax.shard_map(shards, mesh=mesh, in_specs=in_specs, out_specs=out_specs, check_vma=False)
```

```python
import functools

import jax
import jax.numpy as jnp
from jax import lax
from jax.experimental import pallas as pl
from jax.experimental.pallas import tpu as pltpu
from jax.sharding import PartitionSpec as P

TOP = 8
EXP_DEV = 2
VMEM_LIMIT = 63 * 1024 * 1024
LITTLE = pl.CostEstimate(flops=1000000, bytes_accessed=100000, transcendentals=0)


def normalize(rows):
    values = rows.astype(jnp.float32)
    inv_rms = lax.rsqrt(jnp.mean(values * values, axis=1, keepdims=True) + 1e-06)
    return (values * inv_rms, inv_rms)


def expert_forward(rows, gate_up, down_proj):
    projected = jnp.dot(rows, gate_up, preferred_element_type=jnp.float32)
    half_width = down_proj.shape[0]
    gate_pre = projected[:, :half_width]
    up_pre = projected[:, half_width:]
    sigmoid_gate = jax.nn.sigmoid(gate_pre)
    hidden = (gate_pre * sigmoid_gate * up_pre).astype(jnp.bfloat16)
    block_out = jnp.dot(hidden, down_proj, preferred_element_type=jnp.float32).astype(jnp.bfloat16)
    return (gate_pre, up_pre, sigmoid_gate, hidden, block_out)


def times_transposed(left, right):
    return lax.dot_general(left, right, (((1,), (1,)), ((), ())), preferred_element_type=jnp.float32)


def outer_sum(left, right):
    product = lax.dot_general(left, right, (((0,), (0,)), ((), ())), preferred_element_type=jnp.float32)
    return product.astype(jnp.bfloat16)


def backward_inner(slot_grads, down_proj, gate_pre, up_pre, sigmoid_gate):
    hidden_grad = times_transposed(slot_grads, down_proj)
    gate_grad = (
        hidden_grad * up_pre * sigmoid_gate * (1.0 + gate_pre * (1.0 - sigmoid_gate))
    ).astype(jnp.bfloat16)
    up_grad = (hidden_grad * gate_pre * sigmoid_gate).astype(jnp.bfloat16)
    return jnp.concatenate([gate_grad, up_grad], axis=1)


def expert_backward(rows, slot_grads, gate_up, down_proj, gate_pre, up_pre, sigmoid_gate, hidden):
    joined_grad = backward_inner(slot_grads, down_proj, gate_pre, up_pre, sigmoid_gate)
    input_grad = times_transposed(joined_grad, gate_up).astype(jnp.bfloat16)
    return (input_grad, outer_sum(rows, joined_grad), outer_sum(hidden, slot_grads))


def routed_shards(tokens, cotangent, gain, expert_ids, gate_probs, gate_up_weight, down_weight):
    tensor_size = lax.axis_size("tensor")
    expert_size = lax.axis_size("expert")
    my_rank = lax.axis_index("tensor")
    blocks_each = tensor_size // EXP_DEV
    my_type = my_rank // blocks_each
    group_rows = expert_ids.shape[0]
    features = tokens.shape[1]
    capacity = 3 * group_rows * TOP // (2 * EXP_DEV * expert_size)
    highest = lax.Precision.HIGHEST
    scaled_own, inv_own = normalize(tokens)
    carried = (scaled_own * gain[None, :]).astype(jnp.bfloat16)
    group_first, group_grads = (
        lax.all_gather(carried, "tensor", axis=0, tiled=True),
        lax.all_gather(cotangent, "tensor", axis=0, tiled=True),
    )
    targets = jnp.arange(expert_size, dtype=jnp.int32) * EXP_DEV + my_type
    matches = expert_ids[:, :, None] == targets[None, None, :]
    chosen = jnp.any(matches, axis=1)
    weight_of = jnp.sum(jnp.where(matches, gate_probs[:, :, None], 0.0), axis=1)
    slot_of = jnp.sum(
        jnp.where(matches, jnp.arange(TOP, dtype=jnp.int32)[None, :, None], 0), axis=1
    )
    row_ids = jnp.arange(group_rows, dtype=jnp.int32)
    earlier = (row_ids[None, :] < row_ids[:, None]).astype(jnp.bfloat16)
    rank_in = jnp.dot(
        earlier, chosen.astype(jnp.bfloat16), preferred_element_type=jnp.float32
    ).astype(jnp.int32)
    placed = chosen.T[:, None, :] & (
        rank_in.T[:, None, :] == jnp.arange(capacity, dtype=jnp.int32)[None, :, None]
    )
    source = jnp.sum(jnp.where(placed, row_ids[None, None, :], 0), axis=2)
    filled = jnp.any(placed, axis=2)
    slot_prob = jnp.sum(jnp.where(placed, weight_of.T[:, None, :], 0.0), axis=2)
    slot_index = jnp.sum(jnp.where(placed, slot_of.T[:, None, :], 0), axis=2)
    sent_rows = jnp.where(
        filled[:, :, None], jnp.take(group_first, source, axis=0), jnp.zeros((), jnp.bfloat16)
    )
    sent_grads = (
        slot_prob[:, :, None] * jnp.take(group_grads, source, axis=0).astype(jnp.float32)
    ).astype(jnp.bfloat16)
    gate_up = gate_up_weight[0]
    down_proj = down_weight[0]
    arrived_rows, arrived_grads = (
        lax.all_to_all(sent_rows, "expert", split_axis=0, concat_axis=0, tiled=True),
        lax.all_to_all(sent_grads, "expert", split_axis=0, concat_axis=0, tiled=True),
    )
    rows = arrived_rows.reshape(-1, features)
    slot_grads = arrived_grads.reshape(-1, features)
    gate_pre, up_pre, sigmoid_gate, hidden, block_out = expert_forward(rows, gate_up, down_proj)
    out_slots = block_out.reshape(expert_size, capacity, features)
    input_grad, gate_up_part, down_part = expert_backward(
        rows, slot_grads, gate_up, down_proj, gate_pre, up_pre, sigmoid_gate, hidden
    )
    input_slots = input_grad.reshape(expert_size, capacity, features)
    out_back, input_back = (
        lax.all_to_all(out_slots, "expert", split_axis=0, concat_axis=0, tiled=True),
        lax.all_to_all(input_slots, "expert", split_axis=0, concat_axis=0, tiled=True),
    )
    out_flat = out_back.reshape(-1, features)
    input_flat = input_back.reshape(-1, features)
    used_source = source.reshape(-1)
    used_filled = filled.reshape(-1)
    used_prob = slot_prob.reshape(-1)
    used_index = slot_index.reshape(-1)
    cot_slots = jnp.take(group_grads, used_source, axis=0)
    prob_values = jnp.einsum("sd,sd->s", cot_slots, out_flat, preferred_element_type=jnp.float32)
    hit = (row_ids[:, None] == used_source[None, :]) & used_filled[None, :]
    input_part = jnp.dot(hit.astype(jnp.bfloat16), input_flat, preferred_element_type=jnp.float32)
    weighting = jnp.where(hit, used_prob[None, :], 0.0)
    out_part = jnp.dot(
        weighting,
        out_flat.astype(jnp.float32),
        precision=highest,
        preferred_element_type=jnp.float32,
    )
    prob_columns = jnp.where(
        used_index[:, None] == jnp.arange(TOP, dtype=jnp.int32)[None, :], prob_values[:, None], 0.0
    )
    prob_part = jnp.dot(
        hit.astype(jnp.float32), prob_columns, precision=highest, preferred_element_type=jnp.float32
    )
    out_sum, normed_grad, prob_grad = (
        lax.psum_scatter(out_part, "tensor", scatter_dimension=0, tiled=True),
        lax.psum_scatter(input_part, "tensor", scatter_dimension=0, tiled=True),
        lax.psum_scatter(prob_part, "tensor", scatter_dimension=0, tiled=True),
    )
    mixed = (tokens.astype(jnp.float32) + out_sum).astype(jnp.bfloat16)
    gain_side = normed_grad * gain[None, :]
    token_grad = (
        cotangent.astype(jnp.float32)
        + inv_own
        * (gain_side - scaled_own * jnp.mean(gain_side * scaled_own, axis=1, keepdims=True))
    ).astype(jnp.bfloat16)
    gain_grad = lax.psum(jnp.sum(normed_grad * scaled_own, axis=0), ("expert", "tensor"))
    return (mixed, token_grad, prob_grad, gain_grad, gate_up_part[None], down_part[None])


BOTH = ("expert", "tensor")


def flip_first(expert, core):
    return expert ^ (2 if core == 0 else 1)


def flip_second(expert, core):
    return expert ^ (1 if core == 0 else 2)


def send(array, place):
    pairs = []
    for expert in range(lax.axis_size("expert")):
        for core in range(2):
            to_expert, to_core = place(expert, core)
            pairs.append((expert * 2 + core, to_expert * 2 + to_core))
    return lax.ppermute(array, BOTH, pairs)


def send_first(array):
    return send(array, lambda e, c: (flip_first(e, c), c))


def send_second(array):
    return send(array, lambda e, c: (flip_second(e, c), c))


def send_bit(array, bit):
    return send(array, lambda e, c: (e ^ bit, c))


def send_core(array):
    return send(array, lambda e, c: (e, 1 - c))


def send_along(array, step):
    size = lax.axis_size("expert")
    return send(array, lambda e, c: ((e + 4 * step) % size, c))


def after(array, *others):
    return lax.optimization_barrier((array,) + others)[0]


def together(*arrays):
    return lax.optimization_barrier(arrays)


def add_up(*terms):
    return sum(term.astype(jnp.float32) for term in terms)


def narrow(value):
    return value.astype(jnp.bfloat16)


def plane_tables(table):
    pair = jnp.stack([table, send_second(table)])
    return jnp.stack([pair, send_first(pair)])


def far_first(array):
    far = array[:, :, 1:].reshape((-1,) + array.shape[3:])
    return jnp.concatenate([far, array[:, :, 0].reshape((-1,) + array.shape[3:])])


def from_far_first(array, steps):
    far = array[:4 * (steps - 1)].reshape((2, 2, steps - 1) + array.shape[1:])
    return jnp.concatenate([array[4 * (steps - 1):].reshape((2, 2, 1) + array.shape[1:]), far], axis=2)


def start(source, target, semaphore):
    copy = pltpu.make_async_copy(source, target, semaphore)
    copy.start()
    return copy


def chosen_rows(pick, mine, other):
    return jnp.dot(pick, jnp.concatenate([mine, other]), preferred_element_type=jnp.float32)


def norm_kernel(count, pick_ref, *refs):
    pieces, gain_ref, normed_ref = refs[:4], refs[4], refs[-1]

    def work(mine_ref, other_ref):
        for group in range(count):
            rows = chosen_rows(pick_ref[group], mine_ref[group], other_ref[group])
            inv_rms = lax.rsqrt(jnp.mean(rows * rows, axis=1, keepdims=True) + 1e-06)
            normed_ref[group] = (rows * inv_rms * gain_ref[...]).astype(jnp.bfloat16)

    by_place(work, pieces)


def grad_kernel(count, pick_ref, *refs):
    pieces, prob_ref, out_ref, (grad_ref, value_ref) = refs[:4], refs[4], refs[5], refs[-2:]

    def work(mine_ref, other_ref):
        for group in range(count):
            rows = chosen_rows(pick_ref[group], mine_ref[group], other_ref[group])
            grad_ref[group] = (rows * prob_ref[group]).astype(jnp.bfloat16)
            value_ref[group] = jnp.sum(rows * out_ref[group].astype(jnp.float32), axis=1, keepdims=True)

    by_place(work, pieces)


def by_place(work, pieces):
    for first in range(2):
        for second in range(2):
            pl.when(pl.program_id(0) == first * 2 + second)(
                functools.partial(work, pieces[first], pieces[2 + second])
            )


def group_spec(count, first_group, *shape):
    first_block = first_group // count
    return pl.BlockSpec((count,) + shape, lambda i: (first_block + i, 0, 0))


def select(kernel, pick, pieces, extras, extra_specs, out_shapes, count, arrays, which, first_group, held):
    _, capacity, group_rows = pick.shape
    half, features = pieces[0].shape[1:]

    def piece_spec(place):
        return pl.BlockSpec((count, half, features), lambda i: (place(i) * arrays + which, 0, 0))

    return pl.pallas_call(
        functools.partial(kernel, count),
        grid=(4,),
        in_specs=[
            group_spec(count, first_group, capacity, group_rows),
            piece_spec(lambda i: jnp.minimum(i, 1)),
            piece_spec(lambda i: jnp.maximum(i - 2, 0)),
            piece_spec(lambda i: i // 2),
            piece_spec(lambda i: jnp.maximum(i - 2, 0)),
        ] + extra_specs + [pl.BlockSpec(memory_space=pl.ANY)] * len(held),
        out_specs=[group_spec(count, first_group, *out.shape[1:]) for out in out_shapes],
        out_shape=out_shapes,
        input_output_aliases={5 + len(extras) + n: n for n in range(len(held))},
        compiler_params=pltpu.CompilerParams(vmem_limit_bytes=VMEM_LIMIT),
        cost_estimate=LITTLE,
    )(pick, *pieces, *extras, *held)


def select_normed(pick, gain, pieces, count, arrays, first_group, held):
    groups, capacity, _ = pick.shape
    features = pieces[0].shape[2]
    return select(
        norm_kernel, pick, pieces, [gain], [pl.BlockSpec((1, features), lambda i: (0, 0))],
        [jax.ShapeDtypeStruct((groups, capacity, features), jnp.bfloat16)],
        count, arrays, 0, first_group, held,
    )


def select_grads(pick, prob, out_slots, pieces, count, arrays, which, first_group, held):
    groups, capacity, _ = pick.shape
    features = pieces[0].shape[2]
    return select(
        grad_kernel, pick, pieces, [prob, out_slots],
        [group_spec(count, first_group, capacity, 1), group_spec(count, first_group, capacity, features)],
        [
            jax.ShapeDtypeStruct((groups, capacity, features), jnp.bfloat16),
            jax.ShapeDtypeStruct((groups, capacity, 1), jnp.float32),
        ],
        count, arrays, which, first_group, held,
    )


def expand_kernel(weighted, count, first_group, back_ref, prob_ref, *refs):
    arrays = len(weighted)
    sources, mine_ref, pieces = refs[:arrays], refs[arrays], refs[arrays + 1:arrays + 3]
    loaded, spread, loads, stores = refs[arrays + 3:]
    half = mine_ref.shape[1]
    copies, written = [], []
    for group in range(4 * count):
        for number, source in enumerate(sources):
            place = group * arrays + number
            copies.append(start(source.at[first_group + group], loaded.at[place], loads.at[place]))
    for group in range(4 * count):
        outer, inner = divmod(group, count)
        first, second = divmod(outer, 2)
        for number, by_prob in enumerate(weighted):
            place = group * arrays + number
            copies[place].wait()
            rows = loaded[place]
            if by_prob:
                rows = (rows.astype(jnp.float32) * prob_ref[first_group + group]).astype(jnp.bfloat16)
            spread[place] = jnp.dot(
                back_ref[first_group + group], rows, preferred_element_type=jnp.float32
            ).astype(jnp.bfloat16)
            target = pieces[second].at[(first * count + inner) * arrays + number]
            written += [
                start(spread.at[place, pl.ds(half, half)], target, stores.at[place, 0]),
                start(spread.at[place, pl.ds(0, half)], mine_ref.at[place], stores.at[place, 1]),
            ]
    for copy in written:
        copy.wait()


def expand(back, prob, slots, weighted, count, first_group):
    _, group_rows, capacity = back.shape
    half, features, arrays = group_rows // 2, slots[0].shape[2], len(slots)
    blocks = 4 * count * arrays
    anywhere, whole = pl.BlockSpec(memory_space=pl.ANY), pl.BlockSpec(memory_space=pltpu.VMEM)
    piece = jax.ShapeDtypeStruct((blocks // 2, half, features), jnp.bfloat16)
    return pl.pallas_call(
        functools.partial(expand_kernel, weighted, count, first_group),
        in_specs=[whole, whole] + [anywhere] * arrays,
        out_specs=[anywhere] * 3,
        out_shape=[jax.ShapeDtypeStruct((blocks, half, features), jnp.bfloat16), piece, piece],
        scratch_shapes=[
            pltpu.VMEM((blocks, capacity, features), jnp.bfloat16),
            pltpu.VMEM((blocks, group_rows, features), jnp.bfloat16),
            pltpu.SemaphoreType.DMA((blocks,)),
            pltpu.SemaphoreType.DMA((blocks, 2)),
        ],
        compiler_params=pltpu.CompilerParams(vmem_limit_bytes=VMEM_LIMIT),
        cost_estimate=LITTLE,
    )(back, prob, *slots)


def forward_kernel(rows_ref, gate_up_ref, down_ref, gate_pre_ref, up_pre_ref, hidden_ref, out_ref):
    projected = jnp.dot(rows_ref[...], gate_up_ref[0], preferred_element_type=jnp.float32)
    half_width = hidden_ref.shape[1]
    gate_pre, up_pre = projected[:, :half_width], projected[:, half_width:]
    gate_pre_ref[...] = gate_pre
    up_pre_ref[...] = up_pre
    hidden = (gate_pre * jax.nn.sigmoid(gate_pre) * up_pre).astype(jnp.bfloat16)
    hidden_ref[...] = hidden
    out_ref[...] = jnp.dot(hidden, down_ref[0], preferred_element_type=jnp.float32).astype(jnp.bfloat16)


def forward(rows, gate_up_weight, down_weight):
    slots, features = rows.shape
    width = down_weight.shape[1]
    block = slots // 2

    def row_spec(columns):
        return pl.BlockSpec((block, columns), lambda i: (i, 0))

    return pl.pallas_call(
        forward_kernel,
        grid=(2,),
        in_specs=[
            row_spec(features),
            pl.BlockSpec((1, features, 2 * width), lambda i: (0, 0, 0)),
            pl.BlockSpec((1, width, features), lambda i: (0, 0, 0)),
        ],
        out_specs=[row_spec(width), row_spec(width), row_spec(width), row_spec(features)],
        out_shape=[
            jax.ShapeDtypeStruct((slots, width), jnp.float32),
            jax.ShapeDtypeStruct((slots, width), jnp.float32),
            jax.ShapeDtypeStruct((slots, width), jnp.bfloat16),
            jax.ShapeDtypeStruct((slots, features), jnp.bfloat16),
        ],
        compiler_params=pltpu.CompilerParams(vmem_limit_bytes=VMEM_LIMIT),
        cost_estimate=LITTLE,
    )(rows, gate_up_weight, down_weight)


def inner_kernel(units, grads_ref, gate_pre_ref, up_pre_ref, down_ref, joined_ref):
    step = pl.program_id(0)
    block = gate_pre_ref.shape[1]
    gate_pre, up_pre = gate_pre_ref[...], up_pre_ref[...]
    sigmoid_gate = jax.nn.sigmoid(gate_pre)
    common = times_transposed(grads_ref[...], down_ref[0]) * sigmoid_gate
    gate_grad = common * up_pre * (1.0 + gate_pre * (1.0 - sigmoid_gate))
    start = pl.multiple_of(step * block, block)
    joined_ref[:, pl.ds(start, block)] = gate_grad.astype(jnp.bfloat16)
    joined_ref[:, pl.ds(units * block + start, block)] = (common * gate_pre).astype(jnp.bfloat16)


def backward_hidden(grads, gate_pre, up_pre, down_weight):
    slots, features = grads.shape
    width = down_weight.shape[1]
    block, units = 256, width // 256
    return pl.pallas_call(
        functools.partial(inner_kernel, units),
        grid=(units,),
        in_specs=[
            pl.BlockSpec((slots, features), lambda i: (0, 0)),
            pl.BlockSpec((slots, block), lambda i: (0, i)),
            pl.BlockSpec((slots, block), lambda i: (0, i)),
            pl.BlockSpec((1, block, features), lambda i: (0, i, 0)),
        ],
        out_specs=pl.BlockSpec((slots, 2 * width), lambda i: (0, 0)),
        out_shape=jax.ShapeDtypeStruct((slots, 2 * width), jnp.bfloat16),
        compiler_params=pltpu.CompilerParams(vmem_limit_bytes=VMEM_LIMIT),
        cost_estimate=LITTLE,
    )(grads, gate_pre, up_pre, down_weight)


def input_kernel(joined_ref, gate_up_ref, rows_ref, *refs):
    input_ref, gain_ref = refs[-2:]
    input_grad = times_transposed(joined_ref[...], gate_up_ref[0]).astype(jnp.bfloat16)
    input_ref[...] = input_grad
    terms = input_grad.astype(jnp.float32) * rows_ref[...].astype(jnp.float32)
    gain_ref[...] = jnp.sum(terms, axis=0, keepdims=True)


def backward_input(joined_grad, gate_up_weight, rows, part, held):
    slots, features = rows.shape
    width = joined_grad.shape[1]
    wide = features // 4
    first = 2 * part
    return pl.pallas_call(
        input_kernel,
        grid=(2,),
        in_specs=[
            pl.BlockSpec((slots, width), lambda i: (0, 0)),
            pl.BlockSpec((1, wide, width), lambda i: (0, first + i, 0)),
            pl.BlockSpec((slots, wide), lambda i: (0, first + i)),
        ] + [pl.BlockSpec(memory_space=pl.ANY)] * len(held),
        out_specs=[
            pl.BlockSpec((slots, wide), lambda i: (0, first + i)),
            pl.BlockSpec((1, wide), lambda i: (0, i)),
        ],
        out_shape=[
            jax.ShapeDtypeStruct((slots, features), jnp.bfloat16),
            jax.ShapeDtypeStruct((1, features // 2), jnp.float32),
        ],
        input_output_aliases={3 + n: n for n in range(len(held))},
        compiler_params=pltpu.CompilerParams(vmem_limit_bytes=VMEM_LIMIT),
        cost_estimate=LITTLE,
    )(joined_grad, gate_up_weight, rows, *held)


def pack(columns, gains):
    return jnp.concatenate([columns.reshape(-1, 128), gains])


def unpack_add(columns, gains, got):
    count = gains.shape[0]
    return columns + got[:-count].reshape(columns.shape), gains + got[-count:]


def planes_in_order(gains):
    steps = len(gains)
    order = (lax.axis_index("expert") // 4 - jnp.arange(steps)) % steps
    ordered = jnp.take(jnp.stack(gains), order, axis=0)
    return functools.reduce(jnp.add, [ordered[step] for step in range(steps)])


def broadcast_shards(tokens, cotangent, gain, expert_ids, gate_probs, gate_up_weight, down_weight):
    expert_size = lax.axis_size("expert")
    steps = expert_size // 4
    far = 4 * (steps - 1)
    expert, core = lax.axis_index("expert"), lax.axis_index("tensor")
    my_expert = expert * EXP_DEV + core
    group_rows = expert_ids.shape[0]
    half = group_rows // 2
    features = tokens.shape[1]
    capacity = 3 * group_rows * TOP // (2 * EXP_DEV * expert_size)
    near_own = jnp.stack([tokens, cotangent])
    near_pair = jnp.concatenate([near_own, send_second(near_own)])
    near_far_pair = send_first(near_pair)
    tables = plane_tables(
        after(jnp.concatenate([expert_ids.T.astype(jnp.float32), gate_probs.T]), near_pair)
    )
    token_far = after(jnp.stack([send_along(tokens, -step) for step in range(1, steps)]), tables)
    late_tables = after(tables, token_far)
    far_tables = [send_along(late_tables, -step) for step in range(1, steps)]
    late_cot = after(cotangent, token_far)
    cot_steps = [send_along(late_cot, -step) for step in range(1, steps)]
    token_second = after(send_second(token_far), near_far_pair, cot_steps[0], *far_tables)
    token_pair = jnp.concatenate([token_far, token_second])
    tables = far_first(jnp.stack([tables] + far_tables, axis=2))
    tables = jnp.where(core == 0, tables, jnp.roll(tables, half, axis=2))
    matches = tables[:, :TOP] == my_expert.astype(jnp.float32)
    chosen = jnp.any(matches, axis=1)
    weight_of = jnp.sum(jnp.where(matches, tables[:, TOP:], 0.0), axis=1)
    row_ids = jnp.arange(group_rows, dtype=jnp.int32)
    earlier = (row_ids[:, None] < row_ids[None, :]).astype(jnp.bfloat16)
    rank_in = jnp.dot(chosen.astype(jnp.bfloat16), earlier, preferred_element_type=jnp.float32)
    placed = chosen[:, None, :] & (
        rank_in.astype(jnp.int32)[:, None, :] == jnp.arange(capacity, dtype=jnp.int32)[None, :, None]
    )
    pick = placed.astype(jnp.bfloat16)
    back = jnp.swapaxes(pick, 1, 2)
    slot_prob = jnp.sum(jnp.where(placed, weight_of[:, None, :], 0.0), axis=2, keepdims=True)

    gain_row = gain[None, :]
    near_pieces = (near_pair, near_far_pair, send_core(near_pair), send_core(near_far_pair))
    rows, = select_normed(pick, gain_row, near_pieces, 1, 2, far, ())
    cot_steps = together(*cot_steps, rows)
    rows, cot_far = cot_steps[-1], jnp.stack(cot_steps[:-1])
    token_far_pair, cot_far = together(send_first(token_pair), cot_far)
    cot_second = send_second(cot_far)
    token_pieces = (token_pair, token_far_pair, send_core(token_pair), send_core(token_far_pair))
    rows, = select_normed(pick, gain_row, token_pieces, steps - 1, 1, 0, (rows,))
    rows, cot_second = together(rows, cot_second)
    cot_pair = jnp.concatenate([cot_far, cot_second])
    cot_far_pair = send_first(cot_pair)

    rows = rows.reshape(-1, features)
    gate_pre, up_pre, hidden, block_out = forward(rows, gate_up_weight, down_weight)
    out_slots = block_out.reshape(expert_size, capacity, features)
    out_mine, out_low, out_high = expand(back, slot_prob, (out_slots,), (True,), steps - 1, 0)
    out_high, cot_far_pair = together(out_high, cot_far_pair)
    cot_pieces = (cot_pair, cot_far_pair, send_core(cot_pair), send_core(cot_far_pair))

    half_far, one_far = 2 * (steps - 1), steps - 1
    held = select_grads(
        after(pick, out_high), slot_prob, out_slots, near_pieces, 1, 2, 1, far, ()
    )
    out_core_high = after(send_core(out_high), held[1])
    out_core = send_core(out_low)
    out_upper = narrow(add_up(out_mine[half_far:], out_core_high))
    out_first = send_first(out_upper)
    grads, prob_value = select_grads(
        after(pick, out_upper), slot_prob, out_slots, cot_pieces, steps - 1, 1, 0, 0, tuple(held)
    )
    grads = grads.reshape(-1, features)
    joined_grad = backward_hidden(grads, gate_pre, up_pre, down_weight)
    input_grad, gain_low = backward_input(joined_grad, gate_up_weight, rows, 0, ())
    out_first, gain_low = together(out_first, gain_low)
    out_middle = narrow(
        add_up(out_mine[one_far:half_far], out_core[one_far:half_far], out_first[one_far:])
    )
    out_second = send_second(out_middle)
    input_grad, gain_high = backward_input(
        joined_grad, gate_up_weight, after(rows, out_middle), 1, (input_grad,)
    )
    gain_term = jnp.concatenate([gain_low[0], gain_high[0]])
    input_slots = input_grad.reshape(expert_size, capacity, features)
    in_mine, in_low, in_high = expand(back, slot_prob, (input_slots,), (False,), steps - 1, 0)
    in_high, out_second = together(in_high, out_second)
    in_core_high = send_core(in_high)
    in_core = send_core(in_low)

    def own_plane(mine, core_part, first_part, second_part, count):
        return add_up(mine[:count], core_part[:count], first_part[:count], second_part[:count])

    out_planes = narrow(own_plane(out_mine, out_core, out_first, out_second, one_far))
    out_far = [send_along(out_planes[step - 1], step) for step in range(1, steps)]
    in_upper = narrow(add_up(in_mine[half_far:], after(in_core_high, out_planes)))
    in_first = send_first(in_upper)
    gains = (gain_term / gain).reshape(-1, 128)
    prob_rows = jnp.sum(jnp.where(placed, prob_value, 0.0), axis=1)
    columns = from_far_first(jnp.where(matches, prob_rows[:, None, :], 0.0), steps)
    columns = jnp.where(core == 0, columns, jnp.swapaxes(columns, 0, 1))
    got = send_core(after(pack(columns[..., half:], gains), in_upper))
    gate_up_part = outer_sum(after(rows, in_upper), joined_grad)
    gate_up_part, got = together(gate_up_part, got)
    columns, gains = unpack_add(columns[..., :half], gains, got)
    messages = [send_along(pack(columns[:, :, step], gains), step) for step in range(1, steps)]
    near_mine, near_low, near_high = expand(
        back, after(slot_prob, gate_up_part), (out_slots, input_slots), (True, False), 1, far
    )
    near_high = after(near_high, *out_far[:-1])
    near_core_high = send_core(near_high)
    near_core = send_core(near_low)
    down_part = outer_sum(after(hidden, near_high), grads)
    down_part, in_first, near_core, near_core_high, *messages = together(
        down_part, in_first, near_core, near_core_high, *messages
    )
    columns, all_gains = columns[:, :, 0], [gains]
    for message in messages:
        columns = columns + message[:-gains.shape[0]].reshape(columns.shape)
        all_gains.append(message[-gains.shape[0]:])
    gains = planes_in_order(all_gains)
    got = send_bit(pack(columns[1], gains), 2)
    in_middle = narrow(
        add_up(in_mine[one_far:half_far], in_core[one_far:half_far], in_first[one_far:])
    )
    in_second = send_second(in_middle)
    near_upper = narrow(add_up(near_mine[4:], after(near_core_high, in_middle)))
    near_first = send_first(near_upper)
    in_second, got = together(in_second, got, *out_far[-1:])[:2]
    columns, gains = unpack_add(columns[0], gains, got)
    in_planes = narrow(own_plane(in_mine, in_core, in_first, in_second, one_far))
    in_far = [send_along(in_planes[step - 1], step) for step in range(1, steps)]
    middle = len(in_far) // 2
    near_first, in_far[middle] = together(near_first, in_far[middle])
    near_middle = narrow(add_up(near_mine[2:4], near_core[2:], near_first[2:]))
    near_second = send_second(near_middle)
    got = send_bit(after(pack(columns[1], gains), near_middle), 1)
    prob_sum, gains = unpack_add(columns[0], gains, got)
    near_sum = own_plane(near_mine, near_core, near_first, near_second, 2)
    out_sum = near_sum[0] + add_up(*out_far)
    normed_grad = near_sum[1] + add_up(*in_far)

    scaled_own, inv_own = normalize(tokens)
    mixed = (tokens.astype(jnp.float32) + out_sum).astype(jnp.bfloat16)
    gain_side = normed_grad * gain[None, :]
    token_grad = (
        cotangent.astype(jnp.float32)
        + inv_own
        * (gain_side - scaled_own * jnp.mean(gain_side * scaled_own, axis=1, keepdims=True))
    ).astype(jnp.bfloat16)
    return (mixed, token_grad, prob_sum.T, gains.reshape(-1), gate_up_part[None], down_part[None])


def solution(mesh):
    in_specs = (
        P(("expert", "tensor"), None),
        P(("expert", "tensor"), None),
        P(),
        P("expert", None),
        P("expert", None),
        P(("expert", "tensor"), None, None),
        P(("expert", "tensor"), None, None),
    )
    out_specs = (
        P(("expert", "tensor"), None),
        P(("expert", "tensor"), None),
        P(("expert", "tensor"), None),
        P(),
        P(("expert", "tensor"), None, None),
        P(("expert", "tensor"), None, None),
    )
    expert_size, tensor_size = mesh.shape["expert"], mesh.shape["tensor"]
    few = tensor_size == EXP_DEV and expert_size % 4 == 0 and expert_size <= 4 * TOP
    shards = broadcast_shards if few else routed_shards
    return jax.shard_map(shards, mesh=mesh, in_specs=in_specs, out_specs=out_specs, check_vma=False)
```

```python
import functools

import jax
import jax.numpy as jnp
from jax import lax
from jax.experimental import pallas as pl
from jax.experimental.pallas import tpu as pltpu
from jax.sharding import PartitionSpec as P

TOP = 8
EXP_DEV = 2
VMEM_LIMIT = 63 * 1024 * 1024
LITTLE = pl.CostEstimate(flops=1000000, bytes_accessed=100000, transcendentals=0)


def normalize(rows):
    values = rows.astype(jnp.float32)
    inv_rms = lax.rsqrt(jnp.mean(values * values, axis=1, keepdims=True) + 1e-06)
    return (values * inv_rms, inv_rms)


def expert_forward(rows, gate_up, down_proj):
    projected = jnp.dot(rows, gate_up, preferred_element_type=jnp.float32)
    half_width = down_proj.shape[0]
    gate_pre = projected[:, :half_width]
    up_pre = projected[:, half_width:]
    sigmoid_gate = jax.nn.sigmoid(gate_pre)
    hidden = (gate_pre * sigmoid_gate * up_pre).astype(jnp.bfloat16)
    block_out = jnp.dot(hidden, down_proj, preferred_element_type=jnp.float32).astype(jnp.bfloat16)
    return (gate_pre, up_pre, sigmoid_gate, hidden, block_out)


def times_transposed(left, right):
    return lax.dot_general(left, right, (((1,), (1,)), ((), ())), preferred_element_type=jnp.float32)


def outer_sum(left, right):
    product = lax.dot_general(left, right, (((0,), (0,)), ((), ())), preferred_element_type=jnp.float32)
    return product.astype(jnp.bfloat16)


def backward_inner(slot_grads, down_proj, gate_pre, up_pre, sigmoid_gate):
    hidden_grad = times_transposed(slot_grads, down_proj)
    gate_grad = (
        hidden_grad * up_pre * sigmoid_gate * (1.0 + gate_pre * (1.0 - sigmoid_gate))
    ).astype(jnp.bfloat16)
    up_grad = (hidden_grad * gate_pre * sigmoid_gate).astype(jnp.bfloat16)
    return jnp.concatenate([gate_grad, up_grad], axis=1)


def expert_backward(rows, slot_grads, gate_up, down_proj, gate_pre, up_pre, sigmoid_gate, hidden):
    joined_grad = backward_inner(slot_grads, down_proj, gate_pre, up_pre, sigmoid_gate)
    input_grad = times_transposed(joined_grad, gate_up).astype(jnp.bfloat16)
    return (input_grad, outer_sum(rows, joined_grad), outer_sum(hidden, slot_grads))


def routed_shards(tokens, cotangent, gain, expert_ids, gate_probs, gate_up_weight, down_weight):
    tensor_size = lax.axis_size("tensor")
    expert_size = lax.axis_size("expert")
    my_rank = lax.axis_index("tensor")
    blocks_each = tensor_size // EXP_DEV
    my_type = my_rank // blocks_each
    group_rows = expert_ids.shape[0]
    features = tokens.shape[1]
    capacity = 3 * group_rows * TOP // (2 * EXP_DEV * expert_size)
    highest = lax.Precision.HIGHEST
    scaled_own, inv_own = normalize(tokens)
    carried = (scaled_own * gain[None, :]).astype(jnp.bfloat16)
    group_first, group_grads = (
        lax.all_gather(carried, "tensor", axis=0, tiled=True),
        lax.all_gather(cotangent, "tensor", axis=0, tiled=True),
    )
    targets = jnp.arange(expert_size, dtype=jnp.int32) * EXP_DEV + my_type
    matches = expert_ids[:, :, None] == targets[None, None, :]
    chosen = jnp.any(matches, axis=1)
    weight_of = jnp.sum(jnp.where(matches, gate_probs[:, :, None], 0.0), axis=1)
    slot_of = jnp.sum(
        jnp.where(matches, jnp.arange(TOP, dtype=jnp.int32)[None, :, None], 0), axis=1
    )
    row_ids = jnp.arange(group_rows, dtype=jnp.int32)
    earlier = (row_ids[None, :] < row_ids[:, None]).astype(jnp.bfloat16)
    rank_in = jnp.dot(
        earlier, chosen.astype(jnp.bfloat16), preferred_element_type=jnp.float32
    ).astype(jnp.int32)
    placed = chosen.T[:, None, :] & (
        rank_in.T[:, None, :] == jnp.arange(capacity, dtype=jnp.int32)[None, :, None]
    )
    source = jnp.sum(jnp.where(placed, row_ids[None, None, :], 0), axis=2)
    filled = jnp.any(placed, axis=2)
    slot_prob = jnp.sum(jnp.where(placed, weight_of.T[:, None, :], 0.0), axis=2)
    slot_index = jnp.sum(jnp.where(placed, slot_of.T[:, None, :], 0), axis=2)
    sent_rows = jnp.where(
        filled[:, :, None], jnp.take(group_first, source, axis=0), jnp.zeros((), jnp.bfloat16)
    )
    sent_grads = (
        slot_prob[:, :, None] * jnp.take(group_grads, source, axis=0).astype(jnp.float32)
    ).astype(jnp.bfloat16)
    gate_up = gate_up_weight[0]
    down_proj = down_weight[0]
    arrived_rows, arrived_grads = (
        lax.all_to_all(sent_rows, "expert", split_axis=0, concat_axis=0, tiled=True),
        lax.all_to_all(sent_grads, "expert", split_axis=0, concat_axis=0, tiled=True),
    )
    rows = arrived_rows.reshape(-1, features)
    slot_grads = arrived_grads.reshape(-1, features)
    gate_pre, up_pre, sigmoid_gate, hidden, block_out = expert_forward(rows, gate_up, down_proj)
    out_slots = block_out.reshape(expert_size, capacity, features)
    input_grad, gate_up_part, down_part = expert_backward(
        rows, slot_grads, gate_up, down_proj, gate_pre, up_pre, sigmoid_gate, hidden
    )
    input_slots = input_grad.reshape(expert_size, capacity, features)
    out_back, input_back = (
        lax.all_to_all(out_slots, "expert", split_axis=0, concat_axis=0, tiled=True),
        lax.all_to_all(input_slots, "expert", split_axis=0, concat_axis=0, tiled=True),
    )
    out_flat = out_back.reshape(-1, features)
    input_flat = input_back.reshape(-1, features)
    used_source = source.reshape(-1)
    used_filled = filled.reshape(-1)
    used_prob = slot_prob.reshape(-1)
    used_index = slot_index.reshape(-1)
    cot_slots = jnp.take(group_grads, used_source, axis=0)
    prob_values = jnp.einsum("sd,sd->s", cot_slots, out_flat, preferred_element_type=jnp.float32)
    hit = (row_ids[:, None] == used_source[None, :]) & used_filled[None, :]
    input_part = jnp.dot(hit.astype(jnp.bfloat16), input_flat, preferred_element_type=jnp.float32)
    weighting = jnp.where(hit, used_prob[None, :], 0.0)
    out_part = jnp.dot(
        weighting,
        out_flat.astype(jnp.float32),
        precision=highest,
        preferred_element_type=jnp.float32,
    )
    prob_columns = jnp.where(
        used_index[:, None] == jnp.arange(TOP, dtype=jnp.int32)[None, :], prob_values[:, None], 0.0
    )
    prob_part = jnp.dot(
        hit.astype(jnp.float32), prob_columns, precision=highest, preferred_element_type=jnp.float32
    )
    out_sum, normed_grad, prob_grad = (
        lax.psum_scatter(out_part, "tensor", scatter_dimension=0, tiled=True),
        lax.psum_scatter(input_part, "tensor", scatter_dimension=0, tiled=True),
        lax.psum_scatter(prob_part, "tensor", scatter_dimension=0, tiled=True),
    )
    mixed = (tokens.astype(jnp.float32) + out_sum).astype(jnp.bfloat16)
    gain_side = normed_grad * gain[None, :]
    token_grad = (
        cotangent.astype(jnp.float32)
        + inv_own
        * (gain_side - scaled_own * jnp.mean(gain_side * scaled_own, axis=1, keepdims=True))
    ).astype(jnp.bfloat16)
    gain_grad = lax.psum(jnp.sum(normed_grad * scaled_own, axis=0), ("expert", "tensor"))
    return (mixed, token_grad, prob_grad, gain_grad, gate_up_part[None], down_part[None])


BOTH = ("expert", "tensor")


def flip_first(expert, core):
    return expert ^ (2 if core == 0 else 1)


def flip_second(expert, core):
    return expert ^ (1 if core == 0 else 2)


def send(array, place):
    pairs = []
    for expert in range(lax.axis_size("expert")):
        for core in range(2):
            to_expert, to_core = place(expert, core)
            pairs.append((expert * 2 + core, to_expert * 2 + to_core))
    return lax.ppermute(array, BOTH, pairs)


def send_first(array):
    return send(array, lambda e, c: (flip_first(e, c), c))


def send_second(array):
    return send(array, lambda e, c: (flip_second(e, c), c))


def send_both(array):
    return send(array, lambda e, c: (e ^ 3, c))


def send_bit(array, bit):
    return send(array, lambda e, c: (e ^ bit, c))


def send_core(array):
    return send(array, lambda e, c: (e, 1 - c))


def send_along(array, step):
    size = lax.axis_size("expert")
    return send(array, lambda e, c: ((e + 4 * step) % size, c))


def after(array, *others):
    return lax.optimization_barrier((array,) + others)[0]


def together(*arrays):
    return lax.optimization_barrier(arrays)


def add_up(*terms):
    return sum(term.astype(jnp.float32) for term in terms)


def narrow(value):
    return value.astype(jnp.bfloat16)


def plane_tables(table):
    pair = jnp.stack([table, send_second(table)])
    return jnp.stack([pair, send_first(pair)])


def far_first(array):
    far = array[:, :, 1:].reshape((-1,) + array.shape[3:])
    return jnp.concatenate([far, array[:, :, 0].reshape((-1,) + array.shape[3:])])


def from_far_first(array, steps):
    far = array[:4 * (steps - 1)].reshape((2, 2, steps - 1) + array.shape[1:])
    return jnp.concatenate([array[4 * (steps - 1):].reshape((2, 2, 1) + array.shape[1:]), far], axis=2)


def start(source, target, semaphore):
    copy = pltpu.make_async_copy(source, target, semaphore)
    copy.start()
    return copy


def chosen_rows(pick, mine, other):
    return jnp.dot(pick, jnp.concatenate([mine, other]), preferred_element_type=jnp.float32)


def norm_kernel(count, pick_ref, *refs):
    pieces, gain_ref, normed_ref = refs[:4], refs[4], refs[-1]

    def work(mine_ref, other_ref):
        for group in range(count):
            rows = chosen_rows(pick_ref[group], mine_ref[group], other_ref[group])
            inv_rms = lax.rsqrt(jnp.mean(rows * rows, axis=1, keepdims=True) + 1e-06)
            normed_ref[group] = (rows * inv_rms * gain_ref[...]).astype(jnp.bfloat16)

    by_place(work, pieces)


def grad_kernel(count, pick_ref, *refs):
    pieces, prob_ref, out_ref, (grad_ref, value_ref) = refs[:4], refs[4], refs[5], refs[-2:]

    def work(mine_ref, other_ref):
        for group in range(count):
            rows = chosen_rows(pick_ref[group], mine_ref[group], other_ref[group])
            grad_ref[group] = (rows * prob_ref[group]).astype(jnp.bfloat16)
            value_ref[group] = jnp.sum(rows * out_ref[group].astype(jnp.float32), axis=1, keepdims=True)

    by_place(work, pieces)


def by_place(work, pieces):
    for first in range(2):
        for second in range(2):
            pl.when(pl.program_id(0) == first * 2 + second)(
                functools.partial(work, pieces[first], pieces[2 + second])
            )


def group_spec(count, first_group, *shape):
    first_block = first_group // count
    return pl.BlockSpec((count,) + shape, lambda i: (first_block + i, 0, 0))


def select(kernel, pick, pieces, extras, extra_specs, out_shapes, count, arrays, which, first_group, held):
    _, capacity, group_rows = pick.shape
    half, features = pieces[0].shape[1:]

    def piece_spec(place):
        return pl.BlockSpec((count, half, features), lambda i: (place(i) * arrays + which, 0, 0))

    return pl.pallas_call(
        functools.partial(kernel, count),
        grid=(4,),
        in_specs=[
            group_spec(count, first_group, capacity, group_rows),
            piece_spec(lambda i: jnp.minimum(i, 1)),
            piece_spec(lambda i: jnp.maximum(i - 2, 0)),
            piece_spec(lambda i: i // 2),
            piece_spec(lambda i: jnp.maximum(i - 2, 0)),
        ] + extra_specs + [pl.BlockSpec(memory_space=pl.ANY)] * len(held),
        out_specs=[group_spec(count, first_group, *out.shape[1:]) for out in out_shapes],
        out_shape=out_shapes,
        input_output_aliases={5 + len(extras) + n: n for n in range(len(held))},
        compiler_params=pltpu.CompilerParams(vmem_limit_bytes=VMEM_LIMIT),
        cost_estimate=LITTLE,
    )(pick, *pieces, *extras, *held)


def select_normed(pick, gain, pieces, count, arrays, first_group, held):
    groups, capacity, _ = pick.shape
    features = pieces[0].shape[2]
    return select(
        norm_kernel, pick, pieces, [gain], [pl.BlockSpec((1, features), lambda i: (0, 0))],
        [jax.ShapeDtypeStruct((groups, capacity, features), jnp.bfloat16)],
        count, arrays, 0, first_group, held,
    )


def select_grads(pick, prob, out_slots, pieces, count, arrays, which, first_group, held):
    groups, capacity, _ = pick.shape
    features = pieces[0].shape[2]
    return select(
        grad_kernel, pick, pieces, [prob, out_slots],
        [group_spec(count, first_group, capacity, 1), group_spec(count, first_group, capacity, features)],
        [
            jax.ShapeDtypeStruct((groups, capacity, features), jnp.bfloat16),
            jax.ShapeDtypeStruct((groups, capacity, 1), jnp.float32),
        ],
        count, arrays, which, first_group, held,
    )


def expand_kernel(weighted, count, first_group, back_ref, prob_ref, *refs):
    arrays = len(weighted)
    sources, mine_ref, pieces = refs[:arrays], refs[arrays], refs[arrays + 1:arrays + 3]
    loaded, spread, loads, stores = refs[arrays + 3:]
    half = mine_ref.shape[1]
    copies, written = [], []
    for group in range(4 * count):
        for number, source in enumerate(sources):
            place = group * arrays + number
            copies.append(start(source.at[first_group + group], loaded.at[place], loads.at[place]))
    for group in range(4 * count):
        outer, inner = divmod(group, count)
        first, second = divmod(outer, 2)
        for number, by_prob in enumerate(weighted):
            place = group * arrays + number
            copies[place].wait()
            rows = loaded[place]
            if by_prob:
                rows = (rows.astype(jnp.float32) * prob_ref[first_group + group]).astype(jnp.bfloat16)
            spread[place] = jnp.dot(
                back_ref[first_group + group], rows, preferred_element_type=jnp.float32
            ).astype(jnp.bfloat16)
            target = pieces[second].at[(first * count + inner) * arrays + number]
            written += [
                start(spread.at[place, pl.ds(half, half)], target, stores.at[place, 0]),
                start(spread.at[place, pl.ds(0, half)], mine_ref.at[place], stores.at[place, 1]),
            ]
    for copy in written:
        copy.wait()


def expand(back, prob, slots, weighted, count, first_group):
    _, group_rows, capacity = back.shape
    half, features, arrays = group_rows // 2, slots[0].shape[2], len(slots)
    blocks = 4 * count * arrays
    anywhere, whole = pl.BlockSpec(memory_space=pl.ANY), pl.BlockSpec(memory_space=pltpu.VMEM)
    piece = jax.ShapeDtypeStruct((blocks // 2, half, features), jnp.bfloat16)
    return pl.pallas_call(
        functools.partial(expand_kernel, weighted, count, first_group),
        in_specs=[whole, whole] + [anywhere] * arrays,
        out_specs=[anywhere] * 3,
        out_shape=[jax.ShapeDtypeStruct((blocks, half, features), jnp.bfloat16), piece, piece],
        scratch_shapes=[
            pltpu.VMEM((blocks, capacity, features), jnp.bfloat16),
            pltpu.VMEM((blocks, group_rows, features), jnp.bfloat16),
            pltpu.SemaphoreType.DMA((blocks,)),
            pltpu.SemaphoreType.DMA((blocks, 2)),
        ],
        compiler_params=pltpu.CompilerParams(vmem_limit_bytes=VMEM_LIMIT),
        cost_estimate=LITTLE,
    )(back, prob, *slots)


def forward_kernel(rows_ref, gate_up_ref, down_ref, gate_pre_ref, up_pre_ref, hidden_ref, out_ref):
    projected = jnp.dot(rows_ref[...], gate_up_ref[0], preferred_element_type=jnp.float32)
    half_width = hidden_ref.shape[1]
    gate_pre, up_pre = projected[:, :half_width], projected[:, half_width:]
    gate_pre_ref[...] = gate_pre
    up_pre_ref[...] = up_pre
    hidden = (gate_pre * jax.nn.sigmoid(gate_pre) * up_pre).astype(jnp.bfloat16)
    hidden_ref[...] = hidden
    out_ref[...] = jnp.dot(hidden, down_ref[0], preferred_element_type=jnp.float32).astype(jnp.bfloat16)


def forward(rows, gate_up_weight, down_weight):
    slots, features = rows.shape
    width = down_weight.shape[1]
    block = slots // 2

    def row_spec(columns):
        return pl.BlockSpec((block, columns), lambda i: (i, 0))

    return pl.pallas_call(
        forward_kernel,
        grid=(2,),
        in_specs=[
            row_spec(features),
            pl.BlockSpec((1, features, 2 * width), lambda i: (0, 0, 0)),
            pl.BlockSpec((1, width, features), lambda i: (0, 0, 0)),
        ],
        out_specs=[row_spec(width), row_spec(width), row_spec(width), row_spec(features)],
        out_shape=[
            jax.ShapeDtypeStruct((slots, width), jnp.float32),
            jax.ShapeDtypeStruct((slots, width), jnp.float32),
            jax.ShapeDtypeStruct((slots, width), jnp.bfloat16),
            jax.ShapeDtypeStruct((slots, features), jnp.bfloat16),
        ],
        compiler_params=pltpu.CompilerParams(vmem_limit_bytes=VMEM_LIMIT),
        cost_estimate=LITTLE,
    )(rows, gate_up_weight, down_weight)


def inner_kernel(units, grads_ref, gate_pre_ref, up_pre_ref, down_ref, joined_ref):
    step = pl.program_id(0)
    block = gate_pre_ref.shape[1]
    gate_pre, up_pre = gate_pre_ref[...], up_pre_ref[...]
    sigmoid_gate = jax.nn.sigmoid(gate_pre)
    common = times_transposed(grads_ref[...], down_ref[0]) * sigmoid_gate
    gate_grad = common * up_pre * (1.0 + gate_pre * (1.0 - sigmoid_gate))
    start = pl.multiple_of(step * block, block)
    joined_ref[:, pl.ds(start, block)] = gate_grad.astype(jnp.bfloat16)
    joined_ref[:, pl.ds(units * block + start, block)] = (common * gate_pre).astype(jnp.bfloat16)


def backward_hidden(grads, gate_pre, up_pre, down_weight):
    slots, features = grads.shape
    width = down_weight.shape[1]
    block, units = 256, width // 256
    return pl.pallas_call(
        functools.partial(inner_kernel, units),
        grid=(units,),
        in_specs=[
            pl.BlockSpec((slots, features), lambda i: (0, 0)),
            pl.BlockSpec((slots, block), lambda i: (0, i)),
            pl.BlockSpec((slots, block), lambda i: (0, i)),
            pl.BlockSpec((1, block, features), lambda i: (0, i, 0)),
        ],
        out_specs=pl.BlockSpec((slots, 2 * width), lambda i: (0, 0)),
        out_shape=jax.ShapeDtypeStruct((slots, 2 * width), jnp.bfloat16),
        compiler_params=pltpu.CompilerParams(vmem_limit_bytes=VMEM_LIMIT),
        cost_estimate=LITTLE,
    )(grads, gate_pre, up_pre, down_weight)


def input_kernel(joined_ref, gate_up_ref, rows_ref, *refs):
    input_ref, gain_ref = refs[-2:]
    input_grad = times_transposed(joined_ref[...], gate_up_ref[0]).astype(jnp.bfloat16)
    input_ref[...] = input_grad
    terms = input_grad.astype(jnp.float32) * rows_ref[...].astype(jnp.float32)
    gain_ref[...] = jnp.sum(terms, axis=0, keepdims=True)


def backward_input(joined_grad, gate_up_weight, rows, part, held):
    slots, features = rows.shape
    width = joined_grad.shape[1]
    wide = features // 4
    first = 2 * part
    return pl.pallas_call(
        input_kernel,
        grid=(2,),
        in_specs=[
            pl.BlockSpec((slots, width), lambda i: (0, 0)),
            pl.BlockSpec((1, wide, width), lambda i: (0, first + i, 0)),
            pl.BlockSpec((slots, wide), lambda i: (0, first + i)),
        ] + [pl.BlockSpec(memory_space=pl.ANY)] * len(held),
        out_specs=[
            pl.BlockSpec((slots, wide), lambda i: (0, first + i)),
            pl.BlockSpec((1, wide), lambda i: (0, i)),
        ],
        out_shape=[
            jax.ShapeDtypeStruct((slots, features), jnp.bfloat16),
            jax.ShapeDtypeStruct((1, features // 2), jnp.float32),
        ],
        input_output_aliases={3 + n: n for n in range(len(held))},
        compiler_params=pltpu.CompilerParams(vmem_limit_bytes=VMEM_LIMIT),
        cost_estimate=LITTLE,
    )(joined_grad, gate_up_weight, rows, *held)


def pack(columns, gains):
    return jnp.concatenate([columns.reshape(-1, 128), gains])


def unpack_add(columns, gains, got):
    count = gains.shape[0]
    return columns + got[:-count].reshape(columns.shape), gains + got[-count:]


def planes_in_order(gains):
    steps = len(gains)
    order = (lax.axis_index("expert") // 4 - jnp.arange(steps)) % steps
    ordered = jnp.take(jnp.stack(gains), order, axis=0)
    return functools.reduce(jnp.add, [ordered[step] for step in range(steps)]).reshape(-1)


def broadcast_shards(tokens, cotangent, gain, expert_ids, gate_probs, gate_up_weight, down_weight):
    expert_size = lax.axis_size("expert")
    steps = expert_size // 4
    far = 4 * (steps - 1)
    expert, core = lax.axis_index("expert"), lax.axis_index("tensor")
    my_expert = expert * EXP_DEV + core
    group_rows = expert_ids.shape[0]
    half = group_rows // 2
    features = tokens.shape[1]
    capacity = 3 * group_rows * TOP // (2 * EXP_DEV * expert_size)
    near_own = jnp.stack([tokens, cotangent])
    near_pair = jnp.concatenate([near_own, send_second(near_own)])
    near_far_pair = send_first(near_pair)
    tables = plane_tables(
        after(jnp.concatenate([expert_ids.T.astype(jnp.float32), gate_probs.T]), near_pair)
    )
    token_far = after(jnp.stack([send_along(tokens, -step) for step in range(1, steps)]), tables)
    late_tables = after(tables, token_far)
    far_tables = [send_along(late_tables, -step) for step in range(1, steps)]
    late_cot = after(cotangent, token_far)
    cot_steps = [send_along(late_cot, -step) for step in range(1, steps)]
    token_second = after(send_second(token_far), near_far_pair, cot_steps[0], *far_tables)
    token_pair = jnp.concatenate([token_far, token_second])
    tables = far_first(jnp.stack([tables] + far_tables, axis=2))
    tables = jnp.where(core == 0, tables, jnp.roll(tables, half, axis=2))
    matches = tables[:, :TOP] == my_expert.astype(jnp.float32)
    chosen = jnp.any(matches, axis=1)
    weight_of = jnp.sum(jnp.where(matches, tables[:, TOP:], 0.0), axis=1)
    row_ids = jnp.arange(group_rows, dtype=jnp.int32)
    earlier = (row_ids[:, None] < row_ids[None, :]).astype(jnp.bfloat16)
    rank_in = jnp.dot(chosen.astype(jnp.bfloat16), earlier, preferred_element_type=jnp.float32)
    placed = chosen[:, None, :] & (
        rank_in.astype(jnp.int32)[:, None, :] == jnp.arange(capacity, dtype=jnp.int32)[None, :, None]
    )
    pick = placed.astype(jnp.bfloat16)
    back = jnp.swapaxes(pick, 1, 2)
    slot_prob = jnp.sum(jnp.where(placed, weight_of[:, None, :], 0.0), axis=2, keepdims=True)

    gain_row = gain[None, :]
    near_pieces = (near_pair, near_far_pair, send_core(near_pair), send_core(near_far_pair))
    rows, = select_normed(pick, gain_row, near_pieces, 1, 2, far, ())
    cot_steps = together(*cot_steps, rows)
    rows, cot_far = cot_steps[-1], jnp.stack(cot_steps[:-1])
    token_far_pair, cot_far = together(send_first(token_pair), cot_far)
    cot_second = send_second(cot_far)
    token_pieces = (token_pair, token_far_pair, send_core(token_pair), send_core(token_far_pair))
    rows, = select_normed(pick, gain_row, token_pieces, steps - 1, 1, 0, (rows,))
    rows, cot_second = together(rows, cot_second)
    cot_pair = jnp.concatenate([cot_far, cot_second])
    cot_far_pair = send_first(cot_pair)

    rows = rows.reshape(-1, features)
    gate_pre, up_pre, hidden, block_out = forward(rows, gate_up_weight, down_weight)
    out_slots = block_out.reshape(expert_size, capacity, features)
    out_mine, out_low, out_high = expand(back, slot_prob, (out_slots,), (True,), steps - 1, 0)
    out_high, cot_far_pair = together(out_high, cot_far_pair)
    cot_pieces = (cot_pair, cot_far_pair, send_core(cot_pair), send_core(cot_far_pair))

    half_far, one_far = 2 * (steps - 1), steps - 1
    held = select_grads(
        after(pick, out_high), slot_prob, out_slots, near_pieces, 1, 2, 1, far, ()
    )
    out_core_high = after(send_core(out_high), held[1])
    out_core = send_core(out_low)
    out_upper = narrow(add_up(out_mine[half_far:], out_core_high))
    out_first = send_first(out_upper)
    grads, prob_value = select_grads(
        after(pick, out_upper), slot_prob, out_slots, cot_pieces, steps - 1, 1, 0, 0, tuple(held)
    )
    grads = grads.reshape(-1, features)
    joined_grad = backward_hidden(grads, gate_pre, up_pre, down_weight)
    input_grad, gain_low = backward_input(joined_grad, gate_up_weight, rows, 0, ())
    out_first, gain_low = together(out_first, gain_low)
    out_middle = narrow(
        add_up(out_mine[one_far:half_far], out_core[one_far:half_far], out_first[one_far:])
    )
    out_second = send_second(out_middle)
    input_grad, gain_high = backward_input(
        joined_grad, gate_up_weight, after(rows, out_middle), 1, (input_grad,)
    )
    gain_term = jnp.concatenate([gain_low[0], gain_high[0]])
    input_slots = input_grad.reshape(expert_size, capacity, features)
    in_mine, in_low, in_high = expand(back, slot_prob, (input_slots,), (False,), steps - 1, 0)
    in_high, out_second = together(in_high, out_second)
    in_core_high = send_core(in_high)
    in_core = send_core(in_low)

    def own_plane(mine, core_part, first_part, second_part, count):
        return add_up(mine[:count], core_part[:count], first_part[:count], second_part[:count])

    out_planes = narrow(own_plane(out_mine, out_core, out_first, out_second, one_far))
    out_far = [send_along(out_planes[step - 1], step) for step in range(1, steps)]
    in_upper = narrow(add_up(in_mine[half_far:], after(in_core_high, out_planes)))
    in_first = send_first(in_upper)
    gains = (gain_term / gain).reshape(-1, 128)
    prob_rows = jnp.sum(jnp.where(placed, prob_value, 0.0), axis=1)
    columns = from_far_first(jnp.where(matches, prob_rows[:, None, :], 0.0), steps)
    columns = jnp.where(core == 0, columns, jnp.swapaxes(columns, 0, 1))
    got = send_core(after(pack(columns[..., half:], gains), in_upper))
    gate_up_part = outer_sum(after(rows, in_upper), joined_grad)
    gate_up_part, got = together(gate_up_part, got)
    columns, gains = unpack_add(columns[..., :half], gains, got)
    got = send_bit(pack(columns[1], gains), 2)
    near_mine, near_low, near_high = expand(
        back, after(slot_prob, gate_up_part), (out_slots, input_slots), (True, False), 1, far
    )
    near_high = after(near_high, *out_far[:-1])
    near_core_high = send_core(near_high)
    near_core = send_core(near_low)
    down_part = outer_sum(after(hidden, near_high), grads)
    down_part, in_first, near_core, near_core_high, got = together(
        down_part, in_first, near_core, near_core_high, got
    )
    columns, gains = unpack_add(columns[0], gains, got)
    in_middle = narrow(
        add_up(in_mine[one_far:half_far], in_core[one_far:half_far], in_first[one_far:])
    )
    in_second = send_second(in_middle)
    got = send_bit(pack(columns[1], gains), 1)
    near_core, near_core_high = after(near_core, in_middle), after(near_core_high, in_middle)
    near_parts = [
        narrow(add_up(near_mine[2:4], near_core[2:])),
        narrow(add_up(near_mine[4:6], near_core_high[:2])),
        narrow(add_up(near_mine[6:], near_core_high[2:])),
    ]
    in_second, got, *near_parts = together(in_second, got, *near_parts, *out_far[-1:])[:5]
    columns, gains = unpack_add(columns[0], gains, got)
    in_planes = narrow(own_plane(in_mine, in_core, in_first, in_second, one_far))
    in_far = [send_along(in_planes[step - 1], step) for step in range(1, steps)]
    messages = [send_along(pack(columns[step], gains), step) for step in range(1, steps)]
    near_parts = [after(part, in_planes) for part in near_parts]
    arrived = [send_second(near_parts[0]), send_first(near_parts[1]), send_both(near_parts[2])]
    near_terms = [near_mine[:2], near_core[:2]] + arrived
    out_sum = add_up(*out_far, *[term[0] for term in near_terms])
    normed_grad = add_up(*in_far, *[term[1] for term in near_terms])

    prob_sum, all_gains = columns[0], [gains]
    for message in messages:
        prob_sum = prob_sum + message[:-gains.shape[0]].reshape(prob_sum.shape)
        all_gains.append(message[-gains.shape[0]:])
    gain_grad = planes_in_order(all_gains)

    scaled_own, inv_own = normalize(tokens)
    mixed = (tokens.astype(jnp.float32) + out_sum).astype(jnp.bfloat16)
    gain_side = normed_grad * gain[None, :]
    token_grad = (
        cotangent.astype(jnp.float32)
        + inv_own
        * (gain_side - scaled_own * jnp.mean(gain_side * scaled_own, axis=1, keepdims=True))
    ).astype(jnp.bfloat16)
    return (mixed, token_grad, prob_sum.T, gain_grad, gate_up_part[None], down_part[None])


def solution(mesh):
    in_specs = (
        P(("expert", "tensor"), None),
        P(("expert", "tensor"), None),
        P(),
        P("expert", None),
        P("expert", None),
        P(("expert", "tensor"), None, None),
        P(("expert", "tensor"), None, None),
    )
    out_specs = (
        P(("expert", "tensor"), None),
        P(("expert", "tensor"), None),
        P(("expert", "tensor"), None),
        P(),
        P(("expert", "tensor"), None, None),
        P(("expert", "tensor"), None, None),
    )
    expert_size, tensor_size = mesh.shape["expert"], mesh.shape["tensor"]
    few = tensor_size == EXP_DEV and expert_size % 4 == 0 and expert_size <= 4 * TOP
    shards = broadcast_shards if few else routed_shards
    return jax.shard_map(shards, mesh=mesh, in_specs=in_specs, out_specs=out_specs, check_vma=False)
```

```python
import functools

import jax
import jax.numpy as jnp
from jax import lax
from jax.experimental import pallas as pl
from jax.experimental.pallas import tpu as pltpu
from jax.sharding import PartitionSpec as P

TOP = 8
EXP_DEV = 2
VMEM_LIMIT = 63 * 1024 * 1024
LITTLE = pl.CostEstimate(flops=1000000, bytes_accessed=100000, transcendentals=0)


def normalize(rows):
    values = rows.astype(jnp.float32)
    inv_rms = lax.rsqrt(jnp.mean(values * values, axis=1, keepdims=True) + 1e-06)
    return (values * inv_rms, inv_rms)


def expert_forward(rows, gate_up, down_proj):
    projected = jnp.dot(rows, gate_up, preferred_element_type=jnp.float32)
    half_width = down_proj.shape[0]
    gate_pre = projected[:, :half_width]
    up_pre = projected[:, half_width:]
    sigmoid_gate = jax.nn.sigmoid(gate_pre)
    hidden = (gate_pre * sigmoid_gate * up_pre).astype(jnp.bfloat16)
    block_out = jnp.dot(hidden, down_proj, preferred_element_type=jnp.float32).astype(jnp.bfloat16)
    return (gate_pre, up_pre, sigmoid_gate, hidden, block_out)


def times_transposed(left, right):
    return lax.dot_general(left, right, (((1,), (1,)), ((), ())), preferred_element_type=jnp.float32)


def outer_sum(left, right):
    product = lax.dot_general(left, right, (((0,), (0,)), ((), ())), preferred_element_type=jnp.float32)
    return product.astype(jnp.bfloat16)


def backward_inner(slot_grads, down_proj, gate_pre, up_pre, sigmoid_gate):
    hidden_grad = times_transposed(slot_grads, down_proj)
    gate_grad = (
        hidden_grad * up_pre * sigmoid_gate * (1.0 + gate_pre * (1.0 - sigmoid_gate))
    ).astype(jnp.bfloat16)
    up_grad = (hidden_grad * gate_pre * sigmoid_gate).astype(jnp.bfloat16)
    return jnp.concatenate([gate_grad, up_grad], axis=1)


def expert_backward(rows, slot_grads, gate_up, down_proj, gate_pre, up_pre, sigmoid_gate, hidden):
    joined_grad = backward_inner(slot_grads, down_proj, gate_pre, up_pre, sigmoid_gate)
    input_grad = times_transposed(joined_grad, gate_up).astype(jnp.bfloat16)
    return (input_grad, outer_sum(rows, joined_grad), outer_sum(hidden, slot_grads))


def routed_shards(tokens, cotangent, gain, expert_ids, gate_probs, gate_up_weight, down_weight):
    tensor_size = lax.axis_size("tensor")
    expert_size = lax.axis_size("expert")
    my_rank = lax.axis_index("tensor")
    blocks_each = tensor_size // EXP_DEV
    my_type = my_rank // blocks_each
    group_rows = expert_ids.shape[0]
    features = tokens.shape[1]
    capacity = 3 * group_rows * TOP // (2 * EXP_DEV * expert_size)
    highest = lax.Precision.HIGHEST
    scaled_own, inv_own = normalize(tokens)
    carried = (scaled_own * gain[None, :]).astype(jnp.bfloat16)
    group_first, group_grads = (
        lax.all_gather(carried, "tensor", axis=0, tiled=True),
        lax.all_gather(cotangent, "tensor", axis=0, tiled=True),
    )
    targets = jnp.arange(expert_size, dtype=jnp.int32) * EXP_DEV + my_type
    matches = expert_ids[:, :, None] == targets[None, None, :]
    chosen = jnp.any(matches, axis=1)
    weight_of = jnp.sum(jnp.where(matches, gate_probs[:, :, None], 0.0), axis=1)
    slot_of = jnp.sum(
        jnp.where(matches, jnp.arange(TOP, dtype=jnp.int32)[None, :, None], 0), axis=1
    )
    row_ids = jnp.arange(group_rows, dtype=jnp.int32)
    earlier = (row_ids[None, :] < row_ids[:, None]).astype(jnp.bfloat16)
    rank_in = jnp.dot(
        earlier, chosen.astype(jnp.bfloat16), preferred_element_type=jnp.float32
    ).astype(jnp.int32)
    placed = chosen.T[:, None, :] & (
        rank_in.T[:, None, :] == jnp.arange(capacity, dtype=jnp.int32)[None, :, None]
    )
    source = jnp.sum(jnp.where(placed, row_ids[None, None, :], 0), axis=2)
    filled = jnp.any(placed, axis=2)
    slot_prob = jnp.sum(jnp.where(placed, weight_of.T[:, None, :], 0.0), axis=2)
    slot_index = jnp.sum(jnp.where(placed, slot_of.T[:, None, :], 0), axis=2)
    sent_rows = jnp.where(
        filled[:, :, None], jnp.take(group_first, source, axis=0), jnp.zeros((), jnp.bfloat16)
    )
    sent_grads = (
        slot_prob[:, :, None] * jnp.take(group_grads, source, axis=0).astype(jnp.float32)
    ).astype(jnp.bfloat16)
    gate_up = gate_up_weight[0]
    down_proj = down_weight[0]
    arrived_rows, arrived_grads = (
        lax.all_to_all(sent_rows, "expert", split_axis=0, concat_axis=0, tiled=True),
        lax.all_to_all(sent_grads, "expert", split_axis=0, concat_axis=0, tiled=True),
    )
    rows = arrived_rows.reshape(-1, features)
    slot_grads = arrived_grads.reshape(-1, features)
    gate_pre, up_pre, sigmoid_gate, hidden, block_out = expert_forward(rows, gate_up, down_proj)
    out_slots = block_out.reshape(expert_size, capacity, features)
    input_grad, gate_up_part, down_part = expert_backward(
        rows, slot_grads, gate_up, down_proj, gate_pre, up_pre, sigmoid_gate, hidden
    )
    input_slots = input_grad.reshape(expert_size, capacity, features)
    out_back, input_back = (
        lax.all_to_all(out_slots, "expert", split_axis=0, concat_axis=0, tiled=True),
        lax.all_to_all(input_slots, "expert", split_axis=0, concat_axis=0, tiled=True),
    )
    out_flat = out_back.reshape(-1, features)
    input_flat = input_back.reshape(-1, features)
    used_source = source.reshape(-1)
    used_filled = filled.reshape(-1)
    used_prob = slot_prob.reshape(-1)
    used_index = slot_index.reshape(-1)
    cot_slots = jnp.take(group_grads, used_source, axis=0)
    prob_values = jnp.einsum("sd,sd->s", cot_slots, out_flat, preferred_element_type=jnp.float32)
    hit = (row_ids[:, None] == used_source[None, :]) & used_filled[None, :]
    input_part = jnp.dot(hit.astype(jnp.bfloat16), input_flat, preferred_element_type=jnp.float32)
    weighting = jnp.where(hit, used_prob[None, :], 0.0)
    out_part = jnp.dot(
        weighting,
        out_flat.astype(jnp.float32),
        precision=highest,
        preferred_element_type=jnp.float32,
    )
    prob_columns = jnp.where(
        used_index[:, None] == jnp.arange(TOP, dtype=jnp.int32)[None, :], prob_values[:, None], 0.0
    )
    prob_part = jnp.dot(
        hit.astype(jnp.float32), prob_columns, precision=highest, preferred_element_type=jnp.float32
    )
    out_sum, normed_grad, prob_grad = (
        lax.psum_scatter(out_part, "tensor", scatter_dimension=0, tiled=True),
        lax.psum_scatter(input_part, "tensor", scatter_dimension=0, tiled=True),
        lax.psum_scatter(prob_part, "tensor", scatter_dimension=0, tiled=True),
    )
    mixed = (tokens.astype(jnp.float32) + out_sum).astype(jnp.bfloat16)
    gain_side = normed_grad * gain[None, :]
    token_grad = (
        cotangent.astype(jnp.float32)
        + inv_own
        * (gain_side - scaled_own * jnp.mean(gain_side * scaled_own, axis=1, keepdims=True))
    ).astype(jnp.bfloat16)
    gain_grad = lax.psum(jnp.sum(normed_grad * scaled_own, axis=0), ("expert", "tensor"))
    return (mixed, token_grad, prob_grad, gain_grad, gate_up_part[None], down_part[None])


BOTH = ("expert", "tensor")


def flip_first(expert, core):
    return expert ^ (2 if core == 0 else 1)


def flip_second(expert, core):
    return expert ^ (1 if core == 0 else 2)


def send(array, place):
    pairs = []
    for expert in range(lax.axis_size("expert")):
        for core in range(2):
            to_expert, to_core = place(expert, core)
            pairs.append((expert * 2 + core, to_expert * 2 + to_core))
    return lax.ppermute(array, BOTH, pairs)


def send_first(array):
    return send(array, lambda e, c: (flip_first(e, c), c))


def send_second(array):
    return send(array, lambda e, c: (flip_second(e, c), c))


def send_both(array):
    return send(array, lambda e, c: (e ^ 3, c))


def send_bit(array, bit):
    return send(array, lambda e, c: (e ^ bit, c))


def send_core(array):
    return send(array, lambda e, c: (e, 1 - c))


def send_along(array, step):
    size = lax.axis_size("expert")
    return send(array, lambda e, c: ((e + 4 * step) % size, c))


def after(array, *others):
    return lax.optimization_barrier((array,) + others)[0]


def together(*arrays):
    return lax.optimization_barrier(arrays)


def add_up(*terms):
    return sum(term.astype(jnp.float32) for term in terms)


def narrow(value):
    return value.astype(jnp.bfloat16)


def plane_tables(table):
    pair = jnp.stack([table, send_second(table)])
    return jnp.stack([pair, send_first(pair)])


def far_first(array):
    far = array[:, :, 1:].reshape((-1,) + array.shape[3:])
    return jnp.concatenate([far, array[:, :, 0].reshape((-1,) + array.shape[3:])])


def from_far_first(array, steps):
    far = array[:4 * (steps - 1)].reshape((2, 2, steps - 1) + array.shape[1:])
    return jnp.concatenate([array[4 * (steps - 1):].reshape((2, 2, 1) + array.shape[1:]), far], axis=2)


def start(source, target, semaphore):
    copy = pltpu.make_async_copy(source, target, semaphore)
    copy.start()
    return copy


def chosen_rows(pick, mine, other):
    return jnp.dot(pick, jnp.concatenate([mine, other]), preferred_element_type=jnp.float32)


def norm_kernel(count, pick_ref, *refs):
    pieces, gain_ref, normed_ref = refs[:4], refs[4], refs[-1]

    def work(mine_ref, other_ref):
        for group in range(count):
            rows = chosen_rows(pick_ref[group], mine_ref[group], other_ref[group])
            inv_rms = lax.rsqrt(jnp.mean(rows * rows, axis=1, keepdims=True) + 1e-06)
            normed_ref[group] = (rows * inv_rms * gain_ref[...]).astype(jnp.bfloat16)

    by_place(work, pieces)


def grad_kernel(count, pick_ref, *refs):
    pieces, prob_ref, out_ref, (grad_ref, value_ref) = refs[:4], refs[4], refs[5], refs[-2:]

    def work(mine_ref, other_ref):
        for group in range(count):
            rows = chosen_rows(pick_ref[group], mine_ref[group], other_ref[group])
            grad_ref[group] = (rows * prob_ref[group]).astype(jnp.bfloat16)
            value_ref[group] = jnp.sum(rows * out_ref[group].astype(jnp.float32), axis=1, keepdims=True)

    by_place(work, pieces)


def by_place(work, pieces):
    for first in range(2):
        for second in range(2):
            pl.when(pl.program_id(0) == first * 2 + second)(
                functools.partial(work, pieces[first], pieces[2 + second])
            )


def group_spec(count, first_group, *shape):
    first_block = first_group // count
    return pl.BlockSpec((count,) + shape, lambda i: (first_block + i, 0, 0))


def select(kernel, pick, pieces, extras, extra_specs, out_shapes, count, arrays, which, first_group, held):
    _, capacity, group_rows = pick.shape
    half, features = pieces[0].shape[1:]

    def piece_spec(place):
        return pl.BlockSpec((count, half, features), lambda i: (place(i) * arrays + which, 0, 0))

    return pl.pallas_call(
        functools.partial(kernel, count),
        grid=(4,),
        in_specs=[
            group_spec(count, first_group, capacity, group_rows),
            piece_spec(lambda i: jnp.minimum(i, 1)),
            piece_spec(lambda i: jnp.maximum(i - 2, 0)),
            piece_spec(lambda i: i // 2),
            piece_spec(lambda i: jnp.maximum(i - 2, 0)),
        ] + extra_specs + [pl.BlockSpec(memory_space=pl.ANY)] * len(held),
        out_specs=[group_spec(count, first_group, *out.shape[1:]) for out in out_shapes],
        out_shape=out_shapes,
        input_output_aliases={5 + len(extras) + n: n for n in range(len(held))},
        compiler_params=pltpu.CompilerParams(vmem_limit_bytes=VMEM_LIMIT),
        cost_estimate=LITTLE,
    )(pick, *pieces, *extras, *held)


def select_normed(pick, gain, pieces, count, arrays, first_group, held):
    groups, capacity, _ = pick.shape
    features = pieces[0].shape[2]
    return select(
        norm_kernel, pick, pieces, [gain], [pl.BlockSpec((1, features), lambda i: (0, 0))],
        [jax.ShapeDtypeStruct((groups, capacity, features), jnp.bfloat16)],
        count, arrays, 0, first_group, held,
    )


def select_grads(pick, prob, out_slots, pieces, count, arrays, which, first_group, held):
    groups, capacity, _ = pick.shape
    features = pieces[0].shape[2]
    return select(
        grad_kernel, pick, pieces, [prob, out_slots],
        [group_spec(count, first_group, capacity, 1), group_spec(count, first_group, capacity, features)],
        [
            jax.ShapeDtypeStruct((groups, capacity, features), jnp.bfloat16),
            jax.ShapeDtypeStruct((groups, capacity, 1), jnp.float32),
        ],
        count, arrays, which, first_group, held,
    )


def expand_kernel(weighted, count, first_group, back_ref, prob_ref, *refs):
    arrays = len(weighted)
    sources, mine_ref, pieces = refs[:arrays], refs[arrays], refs[arrays + 1:arrays + 3]
    loaded, spread, loads, stores = refs[arrays + 3:]
    half = mine_ref.shape[1]
    copies, written = [], []
    for group in range(4 * count):
        for number, source in enumerate(sources):
            place = group * arrays + number
            copies.append(start(source.at[first_group + group], loaded.at[place], loads.at[place]))
    for group in range(4 * count):
        outer, inner = divmod(group, count)
        first, second = divmod(outer, 2)
        for number, by_prob in enumerate(weighted):
            place = group * arrays + number
            copies[place].wait()
            rows = loaded[place]
            if by_prob:
                rows = (rows.astype(jnp.float32) * prob_ref[first_group + group]).astype(jnp.bfloat16)
            spread[place] = jnp.dot(
                back_ref[first_group + group], rows, preferred_element_type=jnp.float32
            ).astype(jnp.bfloat16)
            target = pieces[second].at[(first * count + inner) * arrays + number]
            written += [
                start(spread.at[place, pl.ds(half, half)], target, stores.at[place, 0]),
                start(spread.at[place, pl.ds(0, half)], mine_ref.at[place], stores.at[place, 1]),
            ]
    for copy in written:
        copy.wait()


def expand(back, prob, slots, weighted, count, first_group):
    _, group_rows, capacity = back.shape
    half, features, arrays = group_rows // 2, slots[0].shape[2], len(slots)
    blocks = 4 * count * arrays
    anywhere, whole = pl.BlockSpec(memory_space=pl.ANY), pl.BlockSpec(memory_space=pltpu.VMEM)
    piece = jax.ShapeDtypeStruct((blocks // 2, half, features), jnp.bfloat16)
    return pl.pallas_call(
        functools.partial(expand_kernel, weighted, count, first_group),
        in_specs=[whole, whole] + [anywhere] * arrays,
        out_specs=[anywhere] * 3,
        out_shape=[jax.ShapeDtypeStruct((blocks, half, features), jnp.bfloat16), piece, piece],
        scratch_shapes=[
            pltpu.VMEM((blocks, capacity, features), jnp.bfloat16),
            pltpu.VMEM((blocks, group_rows, features), jnp.bfloat16),
            pltpu.SemaphoreType.DMA((blocks,)),
            pltpu.SemaphoreType.DMA((blocks, 2)),
        ],
        compiler_params=pltpu.CompilerParams(vmem_limit_bytes=VMEM_LIMIT),
        cost_estimate=LITTLE,
    )(back, prob, *slots)


def forward_kernel(rows_ref, gate_up_ref, down_ref, gate_pre_ref, up_pre_ref, hidden_ref, out_ref):
    projected = jnp.dot(rows_ref[...], gate_up_ref[0], preferred_element_type=jnp.float32)
    half_width = hidden_ref.shape[1]
    gate_pre, up_pre = projected[:, :half_width], projected[:, half_width:]
    gate_pre_ref[...] = gate_pre
    up_pre_ref[...] = up_pre
    hidden = (gate_pre * jax.nn.sigmoid(gate_pre) * up_pre).astype(jnp.bfloat16)
    hidden_ref[...] = hidden
    out_ref[...] = jnp.dot(hidden, down_ref[0], preferred_element_type=jnp.float32).astype(jnp.bfloat16)


def forward(rows, gate_up_weight, down_weight):
    slots, features = rows.shape
    width = down_weight.shape[1]
    block = slots // 2

    def row_spec(columns):
        return pl.BlockSpec((block, columns), lambda i: (i, 0))

    return pl.pallas_call(
        forward_kernel,
        grid=(2,),
        in_specs=[
            row_spec(features),
            pl.BlockSpec((1, features, 2 * width), lambda i: (0, 0, 0)),
            pl.BlockSpec((1, width, features), lambda i: (0, 0, 0)),
        ],
        out_specs=[row_spec(width), row_spec(width), row_spec(width), row_spec(features)],
        out_shape=[
            jax.ShapeDtypeStruct((slots, width), jnp.float32),
            jax.ShapeDtypeStruct((slots, width), jnp.float32),
            jax.ShapeDtypeStruct((slots, width), jnp.bfloat16),
            jax.ShapeDtypeStruct((slots, features), jnp.bfloat16),
        ],
        compiler_params=pltpu.CompilerParams(vmem_limit_bytes=VMEM_LIMIT),
        cost_estimate=LITTLE,
    )(rows, gate_up_weight, down_weight)


def inner_kernel(units, grads_ref, gate_pre_ref, up_pre_ref, down_ref, joined_ref):
    step = pl.program_id(0)
    block = gate_pre_ref.shape[1]
    gate_pre, up_pre = gate_pre_ref[...], up_pre_ref[...]
    sigmoid_gate = jax.nn.sigmoid(gate_pre)
    common = times_transposed(grads_ref[...], down_ref[0]) * sigmoid_gate
    gate_grad = common * up_pre * (1.0 + gate_pre * (1.0 - sigmoid_gate))
    start = pl.multiple_of(step * block, block)
    joined_ref[:, pl.ds(start, block)] = gate_grad.astype(jnp.bfloat16)
    joined_ref[:, pl.ds(units * block + start, block)] = (common * gate_pre).astype(jnp.bfloat16)


def backward_hidden(grads, gate_pre, up_pre, down_weight):
    slots, features = grads.shape
    width = down_weight.shape[1]
    block, units = 256, width // 256
    return pl.pallas_call(
        functools.partial(inner_kernel, units),
        grid=(units,),
        in_specs=[
            pl.BlockSpec((slots, features), lambda i: (0, 0)),
            pl.BlockSpec((slots, block), lambda i: (0, i)),
            pl.BlockSpec((slots, block), lambda i: (0, i)),
            pl.BlockSpec((1, block, features), lambda i: (0, i, 0)),
        ],
        out_specs=pl.BlockSpec((slots, 2 * width), lambda i: (0, 0)),
        out_shape=jax.ShapeDtypeStruct((slots, 2 * width), jnp.bfloat16),
        compiler_params=pltpu.CompilerParams(vmem_limit_bytes=VMEM_LIMIT),
        cost_estimate=LITTLE,
    )(grads, gate_pre, up_pre, down_weight)


def input_kernel(joined_ref, gate_up_ref, rows_ref, *refs):
    input_ref, gain_ref = refs[-2:]
    input_grad = times_transposed(joined_ref[...], gate_up_ref[0]).astype(jnp.bfloat16)
    input_ref[...] = input_grad
    terms = input_grad.astype(jnp.float32) * rows_ref[...].astype(jnp.float32)
    gain_ref[...] = jnp.sum(terms, axis=0, keepdims=True)


def backward_input(joined_grad, gate_up_weight, rows, part, held):
    slots, features = rows.shape
    width = joined_grad.shape[1]
    wide = features // 4
    first = 2 * part
    return pl.pallas_call(
        input_kernel,
        grid=(2,),
        in_specs=[
            pl.BlockSpec((slots, width), lambda i: (0, 0)),
            pl.BlockSpec((1, wide, width), lambda i: (0, first + i, 0)),
            pl.BlockSpec((slots, wide), lambda i: (0, first + i)),
        ] + [pl.BlockSpec(memory_space=pl.ANY)] * len(held),
        out_specs=[
            pl.BlockSpec((slots, wide), lambda i: (0, first + i)),
            pl.BlockSpec((1, wide), lambda i: (0, i)),
        ],
        out_shape=[
            jax.ShapeDtypeStruct((slots, features), jnp.bfloat16),
            jax.ShapeDtypeStruct((1, features // 2), jnp.float32),
        ],
        input_output_aliases={3 + n: n for n in range(len(held))},
        compiler_params=pltpu.CompilerParams(vmem_limit_bytes=VMEM_LIMIT),
        cost_estimate=LITTLE,
    )(joined_grad, gate_up_weight, rows, *held)


def pack(columns, gains):
    return jnp.concatenate([columns.reshape(-1, 128), gains])


def unpack_add(columns, gains, got):
    count = gains.shape[0]
    return columns + got[:-count].reshape(columns.shape), gains + got[-count:]


def planes_in_order(gains):
    steps = len(gains)
    order = (lax.axis_index("expert") // 4 - jnp.arange(steps)) % steps
    ordered = jnp.take(jnp.stack(gains), order, axis=0)
    return functools.reduce(jnp.add, [ordered[step] for step in range(steps)]).reshape(-1)


def broadcast_shards(tokens, cotangent, gain, expert_ids, gate_probs, gate_up_weight, down_weight):
    expert_size = lax.axis_size("expert")
    steps = expert_size // 4
    far = 4 * (steps - 1)
    expert, core = lax.axis_index("expert"), lax.axis_index("tensor")
    my_expert = expert * EXP_DEV + core
    group_rows = expert_ids.shape[0]
    half = group_rows // 2
    features = tokens.shape[1]
    capacity = 3 * group_rows * TOP // (2 * EXP_DEV * expert_size)
    near_own = jnp.stack([tokens, cotangent])
    near_pair = jnp.concatenate([near_own, send_second(near_own)])
    near_far_pair = send_first(near_pair)
    tables = plane_tables(
        after(jnp.concatenate([expert_ids.T.astype(jnp.float32), gate_probs.T]), near_pair)
    )
    token_far = after(jnp.stack([send_along(tokens, -step) for step in range(1, steps)]), tables)
    late_tables = after(tables, token_far)
    far_tables = [send_along(late_tables, -step) for step in range(1, steps)]
    late_cot = after(cotangent, token_far)
    cot_steps = [send_along(late_cot, -step) for step in range(1, steps)]
    token_second = after(send_second(token_far), near_far_pair, cot_steps[0], *far_tables)
    token_pair = jnp.concatenate([token_far, token_second])
    tables = far_first(jnp.stack([tables] + far_tables, axis=2))
    tables = jnp.where(core == 0, tables, jnp.roll(tables, half, axis=2))
    matches = tables[:, :TOP] == my_expert.astype(jnp.float32)
    chosen = jnp.any(matches, axis=1)
    weight_of = jnp.sum(jnp.where(matches, tables[:, TOP:], 0.0), axis=1)
    row_ids = jnp.arange(group_rows, dtype=jnp.int32)
    earlier = (row_ids[:, None] < row_ids[None, :]).astype(jnp.bfloat16)
    rank_in = jnp.dot(chosen.astype(jnp.bfloat16), earlier, preferred_element_type=jnp.float32)
    placed = chosen[:, None, :] & (
        rank_in.astype(jnp.int32)[:, None, :] == jnp.arange(capacity, dtype=jnp.int32)[None, :, None]
    )
    pick = placed.astype(jnp.bfloat16)
    back = jnp.swapaxes(pick, 1, 2)
    slot_prob = jnp.sum(jnp.where(placed, weight_of[:, None, :], 0.0), axis=2, keepdims=True)

    gain_row = gain[None, :]
    near_pieces = (near_pair, near_far_pair, send_core(near_pair), send_core(near_far_pair))
    rows, = select_normed(pick, gain_row, near_pieces, 1, 2, far, ())
    cot_steps = together(*cot_steps, rows)
    rows, cot_far = cot_steps[-1], jnp.stack(cot_steps[:-1])
    token_far_pair, cot_far = together(send_first(token_pair), cot_far)
    cot_second = send_second(cot_far)
    token_pieces = (token_pair, token_far_pair, send_core(token_pair), send_core(token_far_pair))
    rows, = select_normed(pick, gain_row, token_pieces, steps - 1, 1, 0, (rows,))
    rows, cot_second = together(rows, cot_second)
    cot_pair = jnp.concatenate([cot_far, cot_second])
    cot_far_pair = send_first(cot_pair)

    rows = rows.reshape(-1, features)
    gate_pre, up_pre, hidden, block_out = forward(rows, gate_up_weight, down_weight)
    out_slots = block_out.reshape(expert_size, capacity, features)
    out_mine, out_low, out_high = expand(back, slot_prob, (out_slots,), (True,), steps - 1, 0)
    out_high, cot_far_pair = together(out_high, cot_far_pair)
    cot_pieces = (cot_pair, cot_far_pair, send_core(cot_pair), send_core(cot_far_pair))

    half_far, one_far = 2 * (steps - 1), steps - 1
    held = select_grads(
        after(pick, out_high), slot_prob, out_slots, near_pieces, 1, 2, 1, far, ()
    )
    out_core_high = after(send_core(out_high), held[1])
    out_core = send_core(out_low)
    out_upper = narrow(add_up(out_mine[half_far:], out_core_high))
    out_first = send_first(out_upper)
    grads, prob_value = select_grads(
        after(pick, out_upper), slot_prob, out_slots, cot_pieces, steps - 1, 1, 0, 0, tuple(held)
    )
    grads = grads.reshape(-1, features)
    joined_grad = backward_hidden(grads, gate_pre, up_pre, down_weight)
    input_grad, gain_low = backward_input(joined_grad, gate_up_weight, rows, 0, ())
    out_first, gain_low = together(out_first, gain_low)
    out_middle = narrow(
        add_up(out_mine[one_far:half_far], out_core[one_far:half_far], out_first[one_far:])
    )
    out_second = send_second(out_middle)
    input_grad, gain_high = backward_input(
        joined_grad, gate_up_weight, after(rows, out_middle), 1, (input_grad,)
    )
    gain_term = jnp.concatenate([gain_low[0], gain_high[0]])
    input_slots = input_grad.reshape(expert_size, capacity, features)
    in_mine, in_low, in_high = expand(back, slot_prob, (input_slots,), (False,), steps - 1, 0)
    in_high, out_second = together(in_high, out_second)
    in_core_high = send_core(in_high)
    in_core = send_core(in_low)

    def own_plane(mine, core_part, first_part, second_part, count):
        return add_up(mine[:count], core_part[:count], first_part[:count], second_part[:count])

    out_planes = narrow(own_plane(out_mine, out_core, out_first, out_second, one_far))
    out_far = [send_along(out_planes[step - 1], step) for step in range(1, steps)]
    in_upper = narrow(add_up(in_mine[half_far:], after(in_core_high, out_planes)))
    in_first = send_first(in_upper)
    gains = (gain_term / gain).reshape(-1, 128)
    prob_rows = jnp.sum(jnp.where(placed, prob_value, 0.0), axis=1)
    columns = from_far_first(jnp.where(matches, prob_rows[:, None, :], 0.0), steps)
    columns = jnp.where(core == 0, columns, jnp.swapaxes(columns, 0, 1))
    got = send_core(after(pack(columns[..., half:], gains), in_upper))
    gate_up_part = outer_sum(after(rows, in_upper), joined_grad)
    gate_up_part, got = together(gate_up_part, got)
    columns, gains = unpack_add(columns[..., :half], gains, got)
    got = send_bit(pack(columns[1], gains), 2)
    near_mine, near_low, near_high = expand(
        after(back, gate_up_part), slot_prob, (out_slots, input_slots), (True, False), 1, far
    )
    near_high = after(near_high, *out_far[:-1])
    near_core_high = send_core(near_high)
    near_core = send_core(near_low)
    in_first, near_core, near_core_high, got = together(in_first, near_core, near_core_high, got)
    columns, gains = unpack_add(columns[0], gains, got)
    in_middle = narrow(
        add_up(in_mine[one_far:half_far], in_core[one_far:half_far], in_first[one_far:])
    )
    in_second = send_second(in_middle)
    got = send_bit(pack(columns[1], gains), 1)
    near_core, near_core_high = after(near_core, in_middle), after(near_core_high, in_middle)
    near_parts = [
        narrow(add_up(near_mine[2:4], near_core[2:])),
        narrow(add_up(near_mine[4:6], near_core_high[:2])),
        narrow(add_up(near_mine[6:], near_core_high[2:])),
    ]
    down_part = outer_sum(after(hidden, in_middle), grads)
    in_second, got, down_part, *near_parts = together(
        in_second, got, down_part, *near_parts, *out_far[-1:]
    )[:6]
    columns, gains = unpack_add(columns[0], gains, got)
    in_planes = narrow(own_plane(in_mine, in_core, in_first, in_second, one_far))
    in_far = [send_along(in_planes[step - 1], step) for step in range(1, steps)]
    messages = [send_along(pack(columns[step], gains), step) for step in range(1, steps)]
    near_parts = [after(part, in_planes) for part in near_parts]
    arrived = [send_second(near_parts[0]), send_first(near_parts[1]), send_both(near_parts[2])]
    near_terms = [near_mine[:2], near_core[:2]] + arrived
    out_sum = add_up(*out_far, *[term[0] for term in near_terms])
    normed_grad = add_up(*in_far, *[term[1] for term in near_terms])

    prob_sum, all_gains = columns[0], [gains]
    for message in messages:
        prob_sum = prob_sum + message[:-gains.shape[0]].reshape(prob_sum.shape)
        all_gains.append(message[-gains.shape[0]:])
    gain_grad = planes_in_order(all_gains)

    scaled_own, inv_own = normalize(tokens)
    mixed = (tokens.astype(jnp.float32) + out_sum).astype(jnp.bfloat16)
    gain_side = normed_grad * gain[None, :]
    token_grad = (
        cotangent.astype(jnp.float32)
        + inv_own
        * (gain_side - scaled_own * jnp.mean(gain_side * scaled_own, axis=1, keepdims=True))
    ).astype(jnp.bfloat16)
    return (mixed, token_grad, prob_sum.T, gain_grad, gate_up_part[None], down_part[None])


def solution(mesh):
    in_specs = (
        P(("expert", "tensor"), None),
        P(("expert", "tensor"), None),
        P(),
        P("expert", None),
        P("expert", None),
        P(("expert", "tensor"), None, None),
        P(("expert", "tensor"), None, None),
    )
    out_specs = (
        P(("expert", "tensor"), None),
        P(("expert", "tensor"), None),
        P(("expert", "tensor"), None),
        P(),
        P(("expert", "tensor"), None, None),
        P(("expert", "tensor"), None, None),
    )
    expert_size, tensor_size = mesh.shape["expert"], mesh.shape["tensor"]
    few = tensor_size == EXP_DEV and expert_size % 4 == 0 and expert_size <= 4 * TOP
    shards = broadcast_shards if few else routed_shards
    return jax.shard_map(shards, mesh=mesh, in_specs=in_specs, out_specs=out_specs, check_vma=False)
```

```python
import functools

import jax
import jax.numpy as jnp
from jax import lax
from jax.experimental import pallas as pl
from jax.experimental.pallas import tpu as pltpu
from jax.sharding import PartitionSpec as P

TOP = 8
EXP_DEV = 2
VMEM_LIMIT = 63 * 1024 * 1024
LITTLE = pl.CostEstimate(flops=1000000, bytes_accessed=100000, transcendentals=0)


def normalize(rows):
    values = rows.astype(jnp.float32)
    inv_rms = lax.rsqrt(jnp.mean(values * values, axis=1, keepdims=True) + 1e-06)
    return (values * inv_rms, inv_rms)


def expert_forward(rows, gate_up, down_proj):
    projected = jnp.dot(rows, gate_up, preferred_element_type=jnp.float32)
    half_width = down_proj.shape[0]
    gate_pre = projected[:, :half_width]
    up_pre = projected[:, half_width:]
    sigmoid_gate = jax.nn.sigmoid(gate_pre)
    hidden = (gate_pre * sigmoid_gate * up_pre).astype(jnp.bfloat16)
    block_out = jnp.dot(hidden, down_proj, preferred_element_type=jnp.float32).astype(jnp.bfloat16)
    return (gate_pre, up_pre, sigmoid_gate, hidden, block_out)


def times_transposed(left, right):
    return lax.dot_general(left, right, (((1,), (1,)), ((), ())), preferred_element_type=jnp.float32)


def outer_sum(left, right):
    product = lax.dot_general(left, right, (((0,), (0,)), ((), ())), preferred_element_type=jnp.float32)
    return product.astype(jnp.bfloat16)


def backward_inner(slot_grads, down_proj, gate_pre, up_pre, sigmoid_gate):
    hidden_grad = times_transposed(slot_grads, down_proj)
    gate_grad = (
        hidden_grad * up_pre * sigmoid_gate * (1.0 + gate_pre * (1.0 - sigmoid_gate))
    ).astype(jnp.bfloat16)
    up_grad = (hidden_grad * gate_pre * sigmoid_gate).astype(jnp.bfloat16)
    return jnp.concatenate([gate_grad, up_grad], axis=1)


def expert_backward(rows, slot_grads, gate_up, down_proj, gate_pre, up_pre, sigmoid_gate, hidden):
    joined_grad = backward_inner(slot_grads, down_proj, gate_pre, up_pre, sigmoid_gate)
    input_grad = times_transposed(joined_grad, gate_up).astype(jnp.bfloat16)
    return (input_grad, outer_sum(rows, joined_grad), outer_sum(hidden, slot_grads))


def routed_shards(tokens, cotangent, gain, expert_ids, gate_probs, gate_up_weight, down_weight):
    tensor_size = lax.axis_size("tensor")
    expert_size = lax.axis_size("expert")
    my_rank = lax.axis_index("tensor")
    blocks_each = tensor_size // EXP_DEV
    my_type = my_rank // blocks_each
    group_rows = expert_ids.shape[0]
    features = tokens.shape[1]
    capacity = 3 * group_rows * TOP // (2 * EXP_DEV * expert_size)
    highest = lax.Precision.HIGHEST
    scaled_own, inv_own = normalize(tokens)
    carried = (scaled_own * gain[None, :]).astype(jnp.bfloat16)
    group_first, group_grads = (
        lax.all_gather(carried, "tensor", axis=0, tiled=True),
        lax.all_gather(cotangent, "tensor", axis=0, tiled=True),
    )
    targets = jnp.arange(expert_size, dtype=jnp.int32) * EXP_DEV + my_type
    matches = expert_ids[:, :, None] == targets[None, None, :]
    chosen = jnp.any(matches, axis=1)
    weight_of = jnp.sum(jnp.where(matches, gate_probs[:, :, None], 0.0), axis=1)
    slot_of = jnp.sum(
        jnp.where(matches, jnp.arange(TOP, dtype=jnp.int32)[None, :, None], 0), axis=1
    )
    row_ids = jnp.arange(group_rows, dtype=jnp.int32)
    earlier = (row_ids[None, :] < row_ids[:, None]).astype(jnp.bfloat16)
    rank_in = jnp.dot(
        earlier, chosen.astype(jnp.bfloat16), preferred_element_type=jnp.float32
    ).astype(jnp.int32)
    placed = chosen.T[:, None, :] & (
        rank_in.T[:, None, :] == jnp.arange(capacity, dtype=jnp.int32)[None, :, None]
    )
    source = jnp.sum(jnp.where(placed, row_ids[None, None, :], 0), axis=2)
    filled = jnp.any(placed, axis=2)
    slot_prob = jnp.sum(jnp.where(placed, weight_of.T[:, None, :], 0.0), axis=2)
    slot_index = jnp.sum(jnp.where(placed, slot_of.T[:, None, :], 0), axis=2)
    sent_rows = jnp.where(
        filled[:, :, None], jnp.take(group_first, source, axis=0), jnp.zeros((), jnp.bfloat16)
    )
    sent_grads = (
        slot_prob[:, :, None] * jnp.take(group_grads, source, axis=0).astype(jnp.float32)
    ).astype(jnp.bfloat16)
    gate_up = gate_up_weight[0]
    down_proj = down_weight[0]
    arrived_rows, arrived_grads = (
        lax.all_to_all(sent_rows, "expert", split_axis=0, concat_axis=0, tiled=True),
        lax.all_to_all(sent_grads, "expert", split_axis=0, concat_axis=0, tiled=True),
    )
    rows = arrived_rows.reshape(-1, features)
    slot_grads = arrived_grads.reshape(-1, features)
    gate_pre, up_pre, sigmoid_gate, hidden, block_out = expert_forward(rows, gate_up, down_proj)
    out_slots = block_out.reshape(expert_size, capacity, features)
    input_grad, gate_up_part, down_part = expert_backward(
        rows, slot_grads, gate_up, down_proj, gate_pre, up_pre, sigmoid_gate, hidden
    )
    input_slots = input_grad.reshape(expert_size, capacity, features)
    out_back, input_back = (
        lax.all_to_all(out_slots, "expert", split_axis=0, concat_axis=0, tiled=True),
        lax.all_to_all(input_slots, "expert", split_axis=0, concat_axis=0, tiled=True),
    )
    out_flat = out_back.reshape(-1, features)
    input_flat = input_back.reshape(-1, features)
    used_source = source.reshape(-1)
    used_filled = filled.reshape(-1)
    used_prob = slot_prob.reshape(-1)
    used_index = slot_index.reshape(-1)
    cot_slots = jnp.take(group_grads, used_source, axis=0)
    prob_values = jnp.einsum("sd,sd->s", cot_slots, out_flat, preferred_element_type=jnp.float32)
    hit = (row_ids[:, None] == used_source[None, :]) & used_filled[None, :]
    input_part = jnp.dot(hit.astype(jnp.bfloat16), input_flat, preferred_element_type=jnp.float32)
    weighting = jnp.where(hit, used_prob[None, :], 0.0)
    out_part = jnp.dot(
        weighting,
        out_flat.astype(jnp.float32),
        precision=highest,
        preferred_element_type=jnp.float32,
    )
    prob_columns = jnp.where(
        used_index[:, None] == jnp.arange(TOP, dtype=jnp.int32)[None, :], prob_values[:, None], 0.0
    )
    prob_part = jnp.dot(
        hit.astype(jnp.float32), prob_columns, precision=highest, preferred_element_type=jnp.float32
    )
    out_sum, normed_grad, prob_grad = (
        lax.psum_scatter(out_part, "tensor", scatter_dimension=0, tiled=True),
        lax.psum_scatter(input_part, "tensor", scatter_dimension=0, tiled=True),
        lax.psum_scatter(prob_part, "tensor", scatter_dimension=0, tiled=True),
    )
    mixed = (tokens.astype(jnp.float32) + out_sum).astype(jnp.bfloat16)
    gain_side = normed_grad * gain[None, :]
    token_grad = (
        cotangent.astype(jnp.float32)
        + inv_own
        * (gain_side - scaled_own * jnp.mean(gain_side * scaled_own, axis=1, keepdims=True))
    ).astype(jnp.bfloat16)
    gain_grad = lax.psum(jnp.sum(normed_grad * scaled_own, axis=0), ("expert", "tensor"))
    return (mixed, token_grad, prob_grad, gain_grad, gate_up_part[None], down_part[None])


BOTH = ("expert", "tensor")


def flip_first(expert, core):
    return expert ^ (2 if core == 0 else 1)


def flip_second(expert, core):
    return expert ^ (1 if core == 0 else 2)


def send(array, place):
    pairs = []
    for expert in range(lax.axis_size("expert")):
        for core in range(2):
            to_expert, to_core = place(expert, core)
            pairs.append((expert * 2 + core, to_expert * 2 + to_core))
    return lax.ppermute(array, BOTH, pairs)


def send_first(array):
    return send(array, lambda e, c: (flip_first(e, c), c))


def send_second(array):
    return send(array, lambda e, c: (flip_second(e, c), c))


def send_both(array):
    return send(array, lambda e, c: (e ^ 3, c))


def send_bit(array, bit):
    return send(array, lambda e, c: (e ^ bit, c))


def send_core(array):
    return send(array, lambda e, c: (e, 1 - c))


def send_along(array, step):
    size = lax.axis_size("expert")
    return send(array, lambda e, c: ((e + 4 * step) % size, c))


def after(array, *others):
    return lax.optimization_barrier((array,) + others)[0]


def together(*arrays):
    return lax.optimization_barrier(arrays)


def add_up(*terms):
    return sum(term.astype(jnp.float32) for term in terms)


def narrow(value):
    return value.astype(jnp.bfloat16)


def plane_tables(table):
    pair = jnp.stack([table, send_second(table)])
    return jnp.stack([pair, send_first(pair)])


def far_first(array):
    far = array[:, :, 1:].reshape((-1,) + array.shape[3:])
    return jnp.concatenate([far, array[:, :, 0].reshape((-1,) + array.shape[3:])])


def from_far_first(array, steps):
    far = array[:4 * (steps - 1)].reshape((2, 2, steps - 1) + array.shape[1:])
    return jnp.concatenate([array[4 * (steps - 1):].reshape((2, 2, 1) + array.shape[1:]), far], axis=2)


def start(source, target, semaphore):
    copy = pltpu.make_async_copy(source, target, semaphore)
    copy.start()
    return copy


def chosen_rows(pick, mine, other):
    return jnp.dot(pick, jnp.concatenate([mine, other]), preferred_element_type=jnp.float32)


def norm_kernel(count, pick_ref, *refs):
    pieces, gain_ref, normed_ref = refs[:4], refs[4], refs[-1]

    def work(mine_ref, other_ref):
        for group in range(count):
            rows = chosen_rows(pick_ref[group], mine_ref[group], other_ref[group])
            inv_rms = lax.rsqrt(jnp.mean(rows * rows, axis=1, keepdims=True) + 1e-06)
            normed_ref[group] = (rows * inv_rms * gain_ref[...]).astype(jnp.bfloat16)

    by_place(work, pieces)


def grad_kernel(count, pick_ref, *refs):
    pieces, prob_ref, out_ref, (grad_ref, value_ref) = refs[:4], refs[4], refs[5], refs[-2:]

    def work(mine_ref, other_ref):
        for group in range(count):
            rows = chosen_rows(pick_ref[group], mine_ref[group], other_ref[group])
            grad_ref[group] = (rows * prob_ref[group]).astype(jnp.bfloat16)
            value_ref[group] = jnp.sum(rows * out_ref[group].astype(jnp.float32), axis=1, keepdims=True)

    by_place(work, pieces)


def by_place(work, pieces):
    for first in range(2):
        for second in range(2):
            pl.when(pl.program_id(0) == first * 2 + second)(
                functools.partial(work, pieces[first], pieces[2 + second])
            )


def group_spec(count, first_group, *shape):
    first_block = first_group // count
    return pl.BlockSpec((count,) + shape, lambda i: (first_block + i, 0, 0))


def select(kernel, pick, pieces, extras, extra_specs, out_shapes, count, arrays, which, first_group, held):
    _, capacity, group_rows = pick.shape
    half, features = pieces[0].shape[1:]

    def piece_spec(place):
        return pl.BlockSpec((count, half, features), lambda i: (place(i) * arrays + which, 0, 0))

    return pl.pallas_call(
        functools.partial(kernel, count),
        grid=(4,),
        in_specs=[
            group_spec(count, first_group, capacity, group_rows),
            piece_spec(lambda i: jnp.minimum(i, 1)),
            piece_spec(lambda i: jnp.maximum(i - 2, 0)),
            piece_spec(lambda i: i // 2),
            piece_spec(lambda i: jnp.maximum(i - 2, 0)),
        ] + extra_specs + [pl.BlockSpec(memory_space=pl.ANY)] * len(held),
        out_specs=[group_spec(count, first_group, *out.shape[1:]) for out in out_shapes],
        out_shape=out_shapes,
        input_output_aliases={5 + len(extras) + n: n for n in range(len(held))},
        compiler_params=pltpu.CompilerParams(vmem_limit_bytes=VMEM_LIMIT),
        cost_estimate=LITTLE,
    )(pick, *pieces, *extras, *held)


def select_normed(pick, gain, pieces, count, arrays, first_group, held):
    groups, capacity, _ = pick.shape
    features = pieces[0].shape[2]
    return select(
        norm_kernel, pick, pieces, [gain], [pl.BlockSpec((1, features), lambda i: (0, 0))],
        [jax.ShapeDtypeStruct((groups, capacity, features), jnp.bfloat16)],
        count, arrays, 0, first_group, held,
    )


def select_grads(pick, prob, out_slots, pieces, count, arrays, which, first_group, held):
    groups, capacity, _ = pick.shape
    features = pieces[0].shape[2]
    return select(
        grad_kernel, pick, pieces, [prob, out_slots],
        [group_spec(count, first_group, capacity, 1), group_spec(count, first_group, capacity, features)],
        [
            jax.ShapeDtypeStruct((groups, capacity, features), jnp.bfloat16),
            jax.ShapeDtypeStruct((groups, capacity, 1), jnp.float32),
        ],
        count, arrays, which, first_group, held,
    )


def expand_kernel(weighted, count, first_group, back_ref, prob_ref, *refs):
    arrays = len(weighted)
    sources, mine_ref, pieces = refs[:arrays], refs[arrays], refs[arrays + 1:arrays + 3]
    loaded, spread, loads, stores = refs[arrays + 3:]
    half = mine_ref.shape[1]
    copies, written = [], []
    for group in range(4 * count):
        for number, source in enumerate(sources):
            place = group * arrays + number
            copies.append(start(source.at[first_group + group], loaded.at[place], loads.at[place]))
    for group in range(4 * count):
        outer, inner = divmod(group, count)
        first, second = divmod(outer, 2)
        for number, by_prob in enumerate(weighted):
            place = group * arrays + number
            copies[place].wait()
            rows = loaded[place]
            if by_prob:
                rows = (rows.astype(jnp.float32) * prob_ref[first_group + group]).astype(jnp.bfloat16)
            spread[place] = jnp.dot(
                back_ref[first_group + group], rows, preferred_element_type=jnp.float32
            ).astype(jnp.bfloat16)
            target = pieces[second].at[(first * count + inner) * arrays + number]
            written += [
                start(spread.at[place, pl.ds(half, half)], target, stores.at[place, 0]),
                start(spread.at[place, pl.ds(0, half)], mine_ref.at[place], stores.at[place, 1]),
            ]
    for copy in written:
        copy.wait()


def expand(back, prob, slots, weighted, count, first_group):
    _, group_rows, capacity = back.shape
    half, features, arrays = group_rows // 2, slots[0].shape[2], len(slots)
    blocks = 4 * count * arrays
    anywhere, whole = pl.BlockSpec(memory_space=pl.ANY), pl.BlockSpec(memory_space=pltpu.VMEM)
    piece = jax.ShapeDtypeStruct((blocks // 2, half, features), jnp.bfloat16)
    return pl.pallas_call(
        functools.partial(expand_kernel, weighted, count, first_group),
        in_specs=[whole, whole] + [anywhere] * arrays,
        out_specs=[anywhere] * 3,
        out_shape=[jax.ShapeDtypeStruct((blocks, half, features), jnp.bfloat16), piece, piece],
        scratch_shapes=[
            pltpu.VMEM((blocks, capacity, features), jnp.bfloat16),
            pltpu.VMEM((blocks, group_rows, features), jnp.bfloat16),
            pltpu.SemaphoreType.DMA((blocks,)),
            pltpu.SemaphoreType.DMA((blocks, 2)),
        ],
        compiler_params=pltpu.CompilerParams(vmem_limit_bytes=VMEM_LIMIT),
        cost_estimate=LITTLE,
    )(back, prob, *slots)


def forward_kernel(rows_ref, gate_up_ref, down_ref, gate_pre_ref, up_pre_ref, hidden_ref, out_ref):
    projected = jnp.dot(rows_ref[...], gate_up_ref[0], preferred_element_type=jnp.float32)
    half_width = hidden_ref.shape[1]
    gate_pre, up_pre = projected[:, :half_width], projected[:, half_width:]
    gate_pre_ref[...] = gate_pre
    up_pre_ref[...] = up_pre
    hidden = (gate_pre * jax.nn.sigmoid(gate_pre) * up_pre).astype(jnp.bfloat16)
    hidden_ref[...] = hidden
    out_ref[...] = jnp.dot(hidden, down_ref[0], preferred_element_type=jnp.float32).astype(jnp.bfloat16)


def forward(rows, gate_up_weight, down_weight):
    slots, features = rows.shape
    width = down_weight.shape[1]
    block = slots // 2

    def row_spec(columns):
        return pl.BlockSpec((block, columns), lambda i: (i, 0))

    return pl.pallas_call(
        forward_kernel,
        grid=(2,),
        in_specs=[
            row_spec(features),
            pl.BlockSpec((1, features, 2 * width), lambda i: (0, 0, 0)),
            pl.BlockSpec((1, width, features), lambda i: (0, 0, 0)),
        ],
        out_specs=[row_spec(width), row_spec(width), row_spec(width), row_spec(features)],
        out_shape=[
            jax.ShapeDtypeStruct((slots, width), jnp.float32),
            jax.ShapeDtypeStruct((slots, width), jnp.float32),
            jax.ShapeDtypeStruct((slots, width), jnp.bfloat16),
            jax.ShapeDtypeStruct((slots, features), jnp.bfloat16),
        ],
        compiler_params=pltpu.CompilerParams(vmem_limit_bytes=VMEM_LIMIT),
        cost_estimate=LITTLE,
    )(rows, gate_up_weight, down_weight)


def inner_kernel(units, grads_ref, gate_pre_ref, up_pre_ref, down_ref, joined_ref):
    step = pl.program_id(0)
    block = gate_pre_ref.shape[1]
    gate_pre, up_pre = gate_pre_ref[...], up_pre_ref[...]
    sigmoid_gate = jax.nn.sigmoid(gate_pre)
    common = times_transposed(grads_ref[...], down_ref[0]) * sigmoid_gate
    gate_grad = common * up_pre * (1.0 + gate_pre * (1.0 - sigmoid_gate))
    start = pl.multiple_of(step * block, block)
    joined_ref[:, pl.ds(start, block)] = gate_grad.astype(jnp.bfloat16)
    joined_ref[:, pl.ds(units * block + start, block)] = (common * gate_pre).astype(jnp.bfloat16)


def backward_hidden(grads, gate_pre, up_pre, down_weight):
    slots, features = grads.shape
    width = down_weight.shape[1]
    block, units = 256, width // 256
    return pl.pallas_call(
        functools.partial(inner_kernel, units),
        grid=(units,),
        in_specs=[
            pl.BlockSpec((slots, features), lambda i: (0, 0)),
            pl.BlockSpec((slots, block), lambda i: (0, i)),
            pl.BlockSpec((slots, block), lambda i: (0, i)),
            pl.BlockSpec((1, block, features), lambda i: (0, i, 0)),
        ],
        out_specs=pl.BlockSpec((slots, 2 * width), lambda i: (0, 0)),
        out_shape=jax.ShapeDtypeStruct((slots, 2 * width), jnp.bfloat16),
        compiler_params=pltpu.CompilerParams(vmem_limit_bytes=VMEM_LIMIT),
        cost_estimate=LITTLE,
    )(grads, gate_pre, up_pre, down_weight)


def input_kernel(joined_ref, gate_up_ref, rows_ref, *refs):
    input_ref, gain_ref = refs[-2:]
    input_grad = times_transposed(joined_ref[...], gate_up_ref[0]).astype(jnp.bfloat16)
    input_ref[...] = input_grad
    terms = input_grad.astype(jnp.float32) * rows_ref[...].astype(jnp.float32)
    gain_ref[...] = jnp.sum(terms, axis=0, keepdims=True)


def backward_input(joined_grad, gate_up_weight, rows, part, held):
    slots, features = rows.shape
    width = joined_grad.shape[1]
    wide = features // 4
    first = 2 * part
    return pl.pallas_call(
        input_kernel,
        grid=(2,),
        in_specs=[
            pl.BlockSpec((slots, width), lambda i: (0, 0)),
            pl.BlockSpec((1, wide, width), lambda i: (0, first + i, 0)),
            pl.BlockSpec((slots, wide), lambda i: (0, first + i)),
        ] + [pl.BlockSpec(memory_space=pl.ANY)] * len(held),
        out_specs=[
            pl.BlockSpec((slots, wide), lambda i: (0, first + i)),
            pl.BlockSpec((1, wide), lambda i: (0, i)),
        ],
        out_shape=[
            jax.ShapeDtypeStruct((slots, features), jnp.bfloat16),
            jax.ShapeDtypeStruct((1, features // 2), jnp.float32),
        ],
        input_output_aliases={3 + n: n for n in range(len(held))},
        compiler_params=pltpu.CompilerParams(vmem_limit_bytes=VMEM_LIMIT),
        cost_estimate=LITTLE,
    )(joined_grad, gate_up_weight, rows, *held)


def pack(columns, gains):
    return jnp.concatenate([columns.reshape(-1, 128), gains])


def unpack_add(columns, gains, got):
    count = gains.shape[0]
    return columns + got[:-count].reshape(columns.shape), gains + got[-count:]


def planes_in_order(gains):
    steps = len(gains)
    order = (lax.axis_index("expert") // 4 - jnp.arange(steps)) % steps
    ordered = jnp.take(jnp.stack(gains), order, axis=0)
    return functools.reduce(jnp.add, [ordered[step] for step in range(steps)]).reshape(-1)


def broadcast_shards(tokens, cotangent, gain, expert_ids, gate_probs, gate_up_weight, down_weight):
    expert_size = lax.axis_size("expert")
    steps = expert_size // 4
    far = 4 * (steps - 1)
    expert, core = lax.axis_index("expert"), lax.axis_index("tensor")
    my_expert = expert * EXP_DEV + core
    group_rows = expert_ids.shape[0]
    half = group_rows // 2
    features = tokens.shape[1]
    capacity = 3 * group_rows * TOP // (2 * EXP_DEV * expert_size)
    near_own = jnp.stack([tokens, cotangent])
    near_pair = jnp.concatenate([near_own, send_second(near_own)])
    near_far_pair = send_first(near_pair)
    tables = plane_tables(
        after(jnp.concatenate([expert_ids.T.astype(jnp.float32), gate_probs.T]), near_pair)
    )
    token_far = after(jnp.stack([send_along(tokens, -step) for step in range(1, steps)]), tables)
    late_tables = after(tables, token_far)
    far_tables = [send_along(late_tables, -step) for step in range(1, steps)]
    late_cot = after(cotangent, token_far)
    cot_steps = [send_along(late_cot, -step) for step in range(1, steps)]
    token_second = after(send_second(token_far), near_far_pair, cot_steps[0], *far_tables)
    token_pair = jnp.concatenate([token_far, token_second])
    tables = far_first(jnp.stack([tables] + far_tables, axis=2))
    tables = jnp.where(core == 0, tables, jnp.roll(tables, half, axis=2))
    matches = tables[:, :TOP] == my_expert.astype(jnp.float32)
    chosen = jnp.any(matches, axis=1)
    weight_of = jnp.sum(jnp.where(matches, tables[:, TOP:], 0.0), axis=1)
    row_ids = jnp.arange(group_rows, dtype=jnp.int32)
    earlier = (row_ids[:, None] < row_ids[None, :]).astype(jnp.bfloat16)
    rank_in = jnp.dot(chosen.astype(jnp.bfloat16), earlier, preferred_element_type=jnp.float32)
    placed = chosen[:, None, :] & (
        rank_in.astype(jnp.int32)[:, None, :] == jnp.arange(capacity, dtype=jnp.int32)[None, :, None]
    )
    pick = placed.astype(jnp.bfloat16)
    back = jnp.swapaxes(pick, 1, 2)
    slot_prob = jnp.sum(jnp.where(placed, weight_of[:, None, :], 0.0), axis=2, keepdims=True)

    gain_row = gain[None, :]
    near_pieces = (near_pair, near_far_pair, send_core(near_pair), send_core(near_far_pair))
    rows, = select_normed(pick, gain_row, near_pieces, 1, 2, far, ())
    cot_steps = together(*cot_steps, rows)
    rows, cot_far = cot_steps[-1], jnp.stack(cot_steps[:-1])
    token_far_pair, cot_far = together(send_first(token_pair), cot_far)
    cot_second = send_second(cot_far)
    token_pieces = (token_pair, token_far_pair, send_core(token_pair), send_core(token_far_pair))
    rows, = select_normed(pick, gain_row, token_pieces, steps - 1, 1, 0, (rows,))
    rows, cot_second = together(rows, cot_second)
    cot_pair = jnp.concatenate([cot_far, cot_second])
    cot_far_pair = send_first(cot_pair)

    rows = rows.reshape(-1, features)
    gate_pre, up_pre, hidden, block_out = forward(rows, gate_up_weight, down_weight)
    block_out, cot_core_pair = together(block_out, send_core(cot_pair))
    out_slots = block_out.reshape(expert_size, capacity, features)
    out_mine, out_low, out_high = expand(back, slot_prob, (out_slots,), (True,), steps - 1, 0)
    out_high, cot_far_pair = together(out_high, cot_far_pair)
    cot_pieces = (cot_pair, cot_far_pair, cot_core_pair, send_core(cot_far_pair))

    half_far, one_far = 2 * (steps - 1), steps - 1
    held = select_grads(
        after(pick, out_high), slot_prob, out_slots, near_pieces, 1, 2, 1, far, ()
    )
    out_core_high = after(send_core(out_high), held[1])
    out_upper = narrow(add_up(out_mine[half_far:], out_core_high))
    out_core = send_core(after(out_low, out_upper))
    out_first = send_first(out_upper)
    grads, prob_value = select_grads(
        after(pick, out_upper), slot_prob, out_slots, cot_pieces, steps - 1, 1, 0, 0, tuple(held)
    )
    grads = grads.reshape(-1, features)
    joined_grad = backward_hidden(grads, gate_pre, up_pre, down_weight)
    input_grad, gain_low = backward_input(joined_grad, gate_up_weight, rows, 0, ())
    out_first, gain_low = together(out_first, gain_low)
    out_middle = narrow(
        add_up(out_mine[one_far:half_far], out_core[one_far:half_far], out_first[one_far:])
    )
    out_second = send_second(out_middle)
    input_grad, gain_high = backward_input(
        joined_grad, gate_up_weight, after(rows, out_middle), 1, (input_grad,)
    )
    gain_term = jnp.concatenate([gain_low[0], gain_high[0]])
    input_slots = input_grad.reshape(expert_size, capacity, features)
    in_mine, in_low, in_high = expand(back, slot_prob, (input_slots,), (False,), steps - 1, 0)
    in_high, out_second = together(in_high, out_second)
    in_core_high = send_core(in_high)
    in_core = send_core(in_low)

    def own_plane(mine, core_part, first_part, second_part, count):
        return add_up(mine[:count], core_part[:count], first_part[:count], second_part[:count])

    out_planes = narrow(own_plane(out_mine, out_core, out_first, out_second, one_far))
    out_far = [send_along(out_planes[step - 1], step) for step in range(1, steps)]
    in_upper = narrow(add_up(in_mine[half_far:], after(in_core_high, out_planes)))
    in_first = send_first(in_upper)
    gains = (gain_term / gain).reshape(-1, 128)
    prob_rows = jnp.sum(jnp.where(placed, prob_value, 0.0), axis=1)
    columns = from_far_first(jnp.where(matches, prob_rows[:, None, :], 0.0), steps)
    columns = jnp.where(core == 0, columns, jnp.swapaxes(columns, 0, 1))
    got = send_core(after(pack(columns[..., half:], gains), in_upper))
    gate_up_part = outer_sum(after(rows, in_upper), joined_grad)
    gate_up_part, got = together(gate_up_part, got)
    columns, gains = unpack_add(columns[..., :half], gains, got)
    got = send_bit(pack(columns[1], gains), 2)
    near_mine, near_low, near_high = expand(
        after(back, gate_up_part), slot_prob, (out_slots, input_slots), (True, False), 1, far
    )
    near_high = after(near_high, *out_far[:-1])
    near_core_high = send_core(near_high)
    near_core = send_core(near_low)
    in_first, near_core, near_core_high, got = together(in_first, near_core, near_core_high, got)
    columns, gains = unpack_add(columns[0], gains, got)
    in_middle = narrow(
        add_up(in_mine[one_far:half_far], in_core[one_far:half_far], in_first[one_far:])
    )
    in_second = send_second(in_middle)
    got = send_bit(pack(columns[1], gains), 1)
    near_core, near_core_high = after(near_core, in_middle), after(near_core_high, in_middle)
    near_parts = [
        narrow(add_up(near_mine[2:4], near_core[2:])),
        narrow(add_up(near_mine[4:6], near_core_high[:2])),
        narrow(add_up(near_mine[6:], near_core_high[2:])),
    ]
    down_part = outer_sum(after(hidden, in_middle), grads)
    in_second, got, down_part, *near_parts = together(
        in_second, got, down_part, *near_parts, *out_far[-1:]
    )[:6]
    columns, gains = unpack_add(columns[0], gains, got)
    in_planes = narrow(own_plane(in_mine, in_core, in_first, in_second, one_far))
    in_far = [send_along(in_planes[step - 1], step) for step in range(1, steps)]
    messages = [
        send_along(after(pack(columns[step], gains), in_planes), step) for step in range(1, steps)
    ]
    near_parts = [after(part, in_planes) for part in near_parts]
    arrived = [send_second(near_parts[0]), send_first(near_parts[1]), send_both(near_parts[2])]
    near_terms = [near_mine[:2], near_core[:2]] + arrived
    out_sum = add_up(*out_far, *[term[0] for term in near_terms])
    normed_grad = add_up(*in_far, *[term[1] for term in near_terms])

    prob_sum, all_gains = columns[0], [gains]
    for message in messages:
        prob_sum = prob_sum + message[:-gains.shape[0]].reshape(prob_sum.shape)
        all_gains.append(message[-gains.shape[0]:])
    gain_grad = planes_in_order(all_gains)

    scaled_own, inv_own = normalize(tokens)
    mixed = (tokens.astype(jnp.float32) + out_sum).astype(jnp.bfloat16)
    gain_side = normed_grad * gain[None, :]
    token_grad = (
        cotangent.astype(jnp.float32)
        + inv_own
        * (gain_side - scaled_own * jnp.mean(gain_side * scaled_own, axis=1, keepdims=True))
    ).astype(jnp.bfloat16)
    return (mixed, token_grad, prob_sum.T, gain_grad, gate_up_part[None], down_part[None])


def solution(mesh):
    in_specs = (
        P(("expert", "tensor"), None),
        P(("expert", "tensor"), None),
        P(),
        P("expert", None),
        P("expert", None),
        P(("expert", "tensor"), None, None),
        P(("expert", "tensor"), None, None),
    )
    out_specs = (
        P(("expert", "tensor"), None),
        P(("expert", "tensor"), None),
        P(("expert", "tensor"), None),
        P(),
        P(("expert", "tensor"), None, None),
        P(("expert", "tensor"), None, None),
    )
    expert_size, tensor_size = mesh.shape["expert"], mesh.shape["tensor"]
    few = tensor_size == EXP_DEV and expert_size % 4 == 0 and expert_size <= 4 * TOP
    shards = broadcast_shards if few else routed_shards
    return jax.shard_map(shards, mesh=mesh, in_specs=in_specs, out_specs=out_specs, check_vma=False)
```

```python
import functools

import jax
import jax.numpy as jnp
from jax import lax
from jax.experimental import pallas as pl
from jax.experimental.pallas import tpu as pltpu
from jax.sharding import PartitionSpec as P

TOP = 8
EXP_DEV = 2
VMEM_LIMIT = 63 * 1024 * 1024
LITTLE = pl.CostEstimate(flops=1000000, bytes_accessed=100000, transcendentals=0)


def normalize(rows):
    values = rows.astype(jnp.float32)
    inv_rms = lax.rsqrt(jnp.mean(values * values, axis=1, keepdims=True) + 1e-06)
    return (values * inv_rms, inv_rms)


def expert_forward(rows, gate_up, down_proj):
    projected = jnp.dot(rows, gate_up, preferred_element_type=jnp.float32)
    half_width = down_proj.shape[0]
    gate_pre = projected[:, :half_width]
    up_pre = projected[:, half_width:]
    sigmoid_gate = jax.nn.sigmoid(gate_pre)
    hidden = (gate_pre * sigmoid_gate * up_pre).astype(jnp.bfloat16)
    block_out = jnp.dot(hidden, down_proj, preferred_element_type=jnp.float32).astype(jnp.bfloat16)
    return (gate_pre, up_pre, sigmoid_gate, hidden, block_out)


def times_transposed(left, right):
    return lax.dot_general(left, right, (((1,), (1,)), ((), ())), preferred_element_type=jnp.float32)


def outer_sum(left, right):
    product = lax.dot_general(left, right, (((0,), (0,)), ((), ())), preferred_element_type=jnp.float32)
    return product.astype(jnp.bfloat16)


def backward_inner(slot_grads, down_proj, gate_pre, up_pre, sigmoid_gate):
    hidden_grad = times_transposed(slot_grads, down_proj)
    gate_grad = (
        hidden_grad * up_pre * sigmoid_gate * (1.0 + gate_pre * (1.0 - sigmoid_gate))
    ).astype(jnp.bfloat16)
    up_grad = (hidden_grad * gate_pre * sigmoid_gate).astype(jnp.bfloat16)
    return jnp.concatenate([gate_grad, up_grad], axis=1)


def expert_backward(rows, slot_grads, gate_up, down_proj, gate_pre, up_pre, sigmoid_gate, hidden):
    joined_grad = backward_inner(slot_grads, down_proj, gate_pre, up_pre, sigmoid_gate)
    input_grad = times_transposed(joined_grad, gate_up).astype(jnp.bfloat16)
    return (input_grad, outer_sum(rows, joined_grad), outer_sum(hidden, slot_grads))


def routed_shards(tokens, cotangent, gain, expert_ids, gate_probs, gate_up_weight, down_weight):
    tensor_size = lax.axis_size("tensor")
    expert_size = lax.axis_size("expert")
    my_rank = lax.axis_index("tensor")
    blocks_each = tensor_size // EXP_DEV
    my_type = my_rank // blocks_each
    group_rows = expert_ids.shape[0]
    features = tokens.shape[1]
    capacity = 3 * group_rows * TOP // (2 * EXP_DEV * expert_size)
    highest = lax.Precision.HIGHEST
    scaled_own, inv_own = normalize(tokens)
    carried = (scaled_own * gain[None, :]).astype(jnp.bfloat16)
    group_first, group_grads = (
        lax.all_gather(carried, "tensor", axis=0, tiled=True),
        lax.all_gather(cotangent, "tensor", axis=0, tiled=True),
    )
    targets = jnp.arange(expert_size, dtype=jnp.int32) * EXP_DEV + my_type
    matches = expert_ids[:, :, None] == targets[None, None, :]
    chosen = jnp.any(matches, axis=1)
    weight_of = jnp.sum(jnp.where(matches, gate_probs[:, :, None], 0.0), axis=1)
    slot_of = jnp.sum(
        jnp.where(matches, jnp.arange(TOP, dtype=jnp.int32)[None, :, None], 0), axis=1
    )
    row_ids = jnp.arange(group_rows, dtype=jnp.int32)
    earlier = (row_ids[None, :] < row_ids[:, None]).astype(jnp.bfloat16)
    rank_in = jnp.dot(
        earlier, chosen.astype(jnp.bfloat16), preferred_element_type=jnp.float32
    ).astype(jnp.int32)
    placed = chosen.T[:, None, :] & (
        rank_in.T[:, None, :] == jnp.arange(capacity, dtype=jnp.int32)[None, :, None]
    )
    source = jnp.sum(jnp.where(placed, row_ids[None, None, :], 0), axis=2)
    filled = jnp.any(placed, axis=2)
    slot_prob = jnp.sum(jnp.where(placed, weight_of.T[:, None, :], 0.0), axis=2)
    slot_index = jnp.sum(jnp.where(placed, slot_of.T[:, None, :], 0), axis=2)
    sent_rows = jnp.where(
        filled[:, :, None], jnp.take(group_first, source, axis=0), jnp.zeros((), jnp.bfloat16)
    )
    sent_grads = (
        slot_prob[:, :, None] * jnp.take(group_grads, source, axis=0).astype(jnp.float32)
    ).astype(jnp.bfloat16)
    gate_up = gate_up_weight[0]
    down_proj = down_weight[0]
    arrived_rows, arrived_grads = (
        lax.all_to_all(sent_rows, "expert", split_axis=0, concat_axis=0, tiled=True),
        lax.all_to_all(sent_grads, "expert", split_axis=0, concat_axis=0, tiled=True),
    )
    rows = arrived_rows.reshape(-1, features)
    slot_grads = arrived_grads.reshape(-1, features)
    gate_pre, up_pre, sigmoid_gate, hidden, block_out = expert_forward(rows, gate_up, down_proj)
    out_slots = block_out.reshape(expert_size, capacity, features)
    input_grad, gate_up_part, down_part = expert_backward(
        rows, slot_grads, gate_up, down_proj, gate_pre, up_pre, sigmoid_gate, hidden
    )
    input_slots = input_grad.reshape(expert_size, capacity, features)
    out_back, input_back = (
        lax.all_to_all(out_slots, "expert", split_axis=0, concat_axis=0, tiled=True),
        lax.all_to_all(input_slots, "expert", split_axis=0, concat_axis=0, tiled=True),
    )
    out_flat = out_back.reshape(-1, features)
    input_flat = input_back.reshape(-1, features)
    used_source = source.reshape(-1)
    used_filled = filled.reshape(-1)
    used_prob = slot_prob.reshape(-1)
    used_index = slot_index.reshape(-1)
    cot_slots = jnp.take(group_grads, used_source, axis=0)
    prob_values = jnp.einsum("sd,sd->s", cot_slots, out_flat, preferred_element_type=jnp.float32)
    hit = (row_ids[:, None] == used_source[None, :]) & used_filled[None, :]
    input_part = jnp.dot(hit.astype(jnp.bfloat16), input_flat, preferred_element_type=jnp.float32)
    weighting = jnp.where(hit, used_prob[None, :], 0.0)
    out_part = jnp.dot(
        weighting,
        out_flat.astype(jnp.float32),
        precision=highest,
        preferred_element_type=jnp.float32,
    )
    prob_columns = jnp.where(
        used_index[:, None] == jnp.arange(TOP, dtype=jnp.int32)[None, :], prob_values[:, None], 0.0
    )
    prob_part = jnp.dot(
        hit.astype(jnp.float32), prob_columns, precision=highest, preferred_element_type=jnp.float32
    )
    out_sum, normed_grad, prob_grad = (
        lax.psum_scatter(out_part, "tensor", scatter_dimension=0, tiled=True),
        lax.psum_scatter(input_part, "tensor", scatter_dimension=0, tiled=True),
        lax.psum_scatter(prob_part, "tensor", scatter_dimension=0, tiled=True),
    )
    mixed = (tokens.astype(jnp.float32) + out_sum).astype(jnp.bfloat16)
    gain_side = normed_grad * gain[None, :]
    token_grad = (
        cotangent.astype(jnp.float32)
        + inv_own
        * (gain_side - scaled_own * jnp.mean(gain_side * scaled_own, axis=1, keepdims=True))
    ).astype(jnp.bfloat16)
    gain_grad = lax.psum(jnp.sum(normed_grad * scaled_own, axis=0), ("expert", "tensor"))
    return (mixed, token_grad, prob_grad, gain_grad, gate_up_part[None], down_part[None])


BOTH = ("expert", "tensor")


def flip_first(expert, core):
    return expert ^ (2 if core == 0 else 1)


def flip_second(expert, core):
    return expert ^ (1 if core == 0 else 2)


def send(array, place):
    pairs = []
    for expert in range(lax.axis_size("expert")):
        for core in range(2):
            to_expert, to_core = place(expert, core)
            pairs.append((expert * 2 + core, to_expert * 2 + to_core))
    return lax.ppermute(array, BOTH, pairs)


def send_first(array):
    return send(array, lambda e, c: (flip_first(e, c), c))


def send_second(array):
    return send(array, lambda e, c: (flip_second(e, c), c))


def send_both(array):
    return send(array, lambda e, c: (e ^ 3, c))


def send_bit(array, bit):
    return send(array, lambda e, c: (e ^ bit, c))


def send_core(array):
    return send(array, lambda e, c: (e, 1 - c))


def send_along(array, step):
    size = lax.axis_size("expert")
    return send(array, lambda e, c: ((e + 4 * step) % size, c))


def after(array, *others):
    return lax.optimization_barrier((array,) + others)[0]


def together(*arrays):
    return lax.optimization_barrier(arrays)


def add_up(*terms):
    return sum(term.astype(jnp.float32) for term in terms)


def narrow(value):
    return value.astype(jnp.bfloat16)


def plane_tables(table):
    pair = jnp.stack([table, send_second(table)])
    return jnp.stack([pair, send_first(pair)])


def far_first(array):
    far = array[:, :, 1:].reshape((-1,) + array.shape[3:])
    return jnp.concatenate([far, array[:, :, 0].reshape((-1,) + array.shape[3:])])


def from_far_first(array, steps):
    far = array[:4 * (steps - 1)].reshape((2, 2, steps - 1) + array.shape[1:])
    return jnp.concatenate([array[4 * (steps - 1):].reshape((2, 2, 1) + array.shape[1:]), far], axis=2)


def start(source, target, semaphore):
    copy = pltpu.make_async_copy(source, target, semaphore)
    copy.start()
    return copy


def chosen_rows(pick, mine, other):
    return jnp.dot(pick, jnp.concatenate([mine, other]), preferred_element_type=jnp.float32)


def norm_kernel(count, pick_ref, *refs):
    pieces, gain_ref, normed_ref = refs[:4], refs[4], refs[-1]

    def work(mine_ref, other_ref):
        for group in range(count):
            rows = chosen_rows(pick_ref[group], mine_ref[group], other_ref[group])
            inv_rms = lax.rsqrt(jnp.mean(rows * rows, axis=1, keepdims=True) + 1e-06)
            normed_ref[group] = (rows * inv_rms * gain_ref[...]).astype(jnp.bfloat16)

    by_place(work, pieces)


def grad_kernel(count, pick_ref, *refs):
    pieces, prob_ref, out_ref, (grad_ref, value_ref) = refs[:4], refs[4], refs[5], refs[-2:]

    def work(mine_ref, other_ref):
        for group in range(count):
            rows = chosen_rows(pick_ref[group], mine_ref[group], other_ref[group])
            grad_ref[group] = (rows * prob_ref[group]).astype(jnp.bfloat16)
            value_ref[group] = jnp.sum(rows * out_ref[group].astype(jnp.float32), axis=1, keepdims=True)

    by_place(work, pieces)


def by_place(work, pieces):
    for first in range(2):
        for second in range(2):
            pl.when(pl.program_id(0) == first * 2 + second)(
                functools.partial(work, pieces[first], pieces[2 + second])
            )


def group_spec(count, first_group, *shape):
    first_block = first_group // count
    return pl.BlockSpec((count,) + shape, lambda i: (first_block + i, 0, 0))


def select(kernel, pick, pieces, extras, extra_specs, out_shapes, count, arrays, which, first_group, held):
    _, capacity, group_rows = pick.shape
    half, features = pieces[0].shape[1:]

    def piece_spec(place):
        return pl.BlockSpec((count, half, features), lambda i: (place(i) * arrays + which, 0, 0))

    return pl.pallas_call(
        functools.partial(kernel, count),
        grid=(4,),
        in_specs=[
            group_spec(count, first_group, capacity, group_rows),
            piece_spec(lambda i: jnp.minimum(i, 1)),
            piece_spec(lambda i: jnp.maximum(i - 2, 0)),
            piece_spec(lambda i: i // 2),
            piece_spec(lambda i: jnp.maximum(i - 2, 0)),
        ] + extra_specs + [pl.BlockSpec(memory_space=pl.ANY)] * len(held),
        out_specs=[group_spec(count, first_group, *out.shape[1:]) for out in out_shapes],
        out_shape=out_shapes,
        input_output_aliases={5 + len(extras) + n: n for n in range(len(held))},
        compiler_params=pltpu.CompilerParams(vmem_limit_bytes=VMEM_LIMIT),
        cost_estimate=LITTLE,
    )(pick, *pieces, *extras, *held)


def select_normed(pick, gain, pieces, count, arrays, first_group, held):
    groups, capacity, _ = pick.shape
    features = pieces[0].shape[2]
    return select(
        norm_kernel, pick, pieces, [gain], [pl.BlockSpec((1, features), lambda i: (0, 0))],
        [jax.ShapeDtypeStruct((groups, capacity, features), jnp.bfloat16)],
        count, arrays, 0, first_group, held,
    )


def select_grads(pick, prob, out_slots, pieces, count, arrays, which, first_group, held):
    groups, capacity, _ = pick.shape
    features = pieces[0].shape[2]
    return select(
        grad_kernel, pick, pieces, [prob, out_slots],
        [group_spec(count, first_group, capacity, 1), group_spec(count, first_group, capacity, features)],
        [
            jax.ShapeDtypeStruct((groups, capacity, features), jnp.bfloat16),
            jax.ShapeDtypeStruct((groups, capacity, 1), jnp.float32),
        ],
        count, arrays, which, first_group, held,
    )


def expand_kernel(weighted, count, first_group, back_ref, prob_ref, *refs):
    arrays = len(weighted)
    sources, mine_ref, pieces = refs[:arrays], refs[arrays], refs[arrays + 1:arrays + 3]
    loaded, spread, loads, stores = refs[arrays + 3:]
    half = mine_ref.shape[1]
    copies, written = [], []
    for group in range(4 * count):
        for number, source in enumerate(sources):
            place = group * arrays + number
            copies.append(start(source.at[first_group + group], loaded.at[place], loads.at[place]))
    for group in range(4 * count):
        outer, inner = divmod(group, count)
        first, second = divmod(outer, 2)
        for number, by_prob in enumerate(weighted):
            place = group * arrays + number
            copies[place].wait()
            rows = loaded[place]
            if by_prob:
                rows = (rows.astype(jnp.float32) * prob_ref[first_group + group]).astype(jnp.bfloat16)
            spread[place] = jnp.dot(
                back_ref[first_group + group], rows, preferred_element_type=jnp.float32
            ).astype(jnp.bfloat16)
            target = pieces[second].at[(first * count + inner) * arrays + number]
            written += [
                start(spread.at[place, pl.ds(half, half)], target, stores.at[place, 0]),
                start(spread.at[place, pl.ds(0, half)], mine_ref.at[place], stores.at[place, 1]),
            ]
    for copy in written:
        copy.wait()


def expand(back, prob, slots, weighted, count, first_group):
    _, group_rows, capacity = back.shape
    half, features, arrays = group_rows // 2, slots[0].shape[2], len(slots)
    blocks = 4 * count * arrays
    anywhere, whole = pl.BlockSpec(memory_space=pl.ANY), pl.BlockSpec(memory_space=pltpu.VMEM)
    piece = jax.ShapeDtypeStruct((blocks // 2, half, features), jnp.bfloat16)
    return pl.pallas_call(
        functools.partial(expand_kernel, weighted, count, first_group),
        in_specs=[whole, whole] + [anywhere] * arrays,
        out_specs=[anywhere] * 3,
        out_shape=[jax.ShapeDtypeStruct((blocks, half, features), jnp.bfloat16), piece, piece],
        scratch_shapes=[
            pltpu.VMEM((blocks, capacity, features), jnp.bfloat16),
            pltpu.VMEM((blocks, group_rows, features), jnp.bfloat16),
            pltpu.SemaphoreType.DMA((blocks,)),
            pltpu.SemaphoreType.DMA((blocks, 2)),
        ],
        compiler_params=pltpu.CompilerParams(vmem_limit_bytes=VMEM_LIMIT),
        cost_estimate=LITTLE,
    )(back, prob, *slots)


def forward_kernel(rows_ref, gate_up_ref, down_ref, *refs):
    gate_pre_ref, up_pre_ref, hidden_ref, out_ref = refs[-4:]
    projected = jnp.dot(rows_ref[...], gate_up_ref[0], preferred_element_type=jnp.float32)
    half_width = hidden_ref.shape[1]
    gate_pre, up_pre = projected[:, :half_width], projected[:, half_width:]
    gate_pre_ref[...] = gate_pre
    up_pre_ref[...] = up_pre
    hidden = (gate_pre * jax.nn.sigmoid(gate_pre) * up_pre).astype(jnp.bfloat16)
    hidden_ref[...] = hidden
    out_ref[...] = jnp.dot(hidden, down_ref[0], preferred_element_type=jnp.float32).astype(jnp.bfloat16)


def forward(rows, gate_up_weight, down_weight, block, first, steps, held):
    slots, features = rows.shape
    width = down_weight.shape[1]
    def row_spec(columns):
        return pl.BlockSpec((block, columns), lambda i: (first + i, 0))

    return pl.pallas_call(
        forward_kernel,
        grid=(steps,),
        in_specs=[
            row_spec(features),
            pl.BlockSpec((1, features, 2 * width), lambda i: (0, 0, 0)),
            pl.BlockSpec((1, width, features), lambda i: (0, 0, 0)),
        ] + [pl.BlockSpec(memory_space=pl.ANY)] * len(held),
        out_specs=[row_spec(width), row_spec(width), row_spec(width), row_spec(features)],
        out_shape=[
            jax.ShapeDtypeStruct((slots, width), jnp.float32),
            jax.ShapeDtypeStruct((slots, width), jnp.float32),
            jax.ShapeDtypeStruct((slots, width), jnp.bfloat16),
            jax.ShapeDtypeStruct((slots, features), jnp.bfloat16),
        ],
        input_output_aliases={3 + n: n for n in range(len(held))},
        compiler_params=pltpu.CompilerParams(vmem_limit_bytes=VMEM_LIMIT),
        cost_estimate=LITTLE,
    )(rows, gate_up_weight, down_weight, *held)


def inner_kernel(units, grads_ref, gate_pre_ref, up_pre_ref, down_ref, joined_ref):
    step = pl.program_id(0)
    block = gate_pre_ref.shape[1]
    gate_pre, up_pre = gate_pre_ref[...], up_pre_ref[...]
    sigmoid_gate = jax.nn.sigmoid(gate_pre)
    common = times_transposed(grads_ref[...], down_ref[0]) * sigmoid_gate
    gate_grad = common * up_pre * (1.0 + gate_pre * (1.0 - sigmoid_gate))
    start = pl.multiple_of(step * block, block)
    joined_ref[:, pl.ds(start, block)] = gate_grad.astype(jnp.bfloat16)
    joined_ref[:, pl.ds(units * block + start, block)] = (common * gate_pre).astype(jnp.bfloat16)


def backward_hidden(grads, gate_pre, up_pre, down_weight):
    slots, features = grads.shape
    width = down_weight.shape[1]
    block, units = 256, width // 256
    return pl.pallas_call(
        functools.partial(inner_kernel, units),
        grid=(units,),
        in_specs=[
            pl.BlockSpec((slots, features), lambda i: (0, 0)),
            pl.BlockSpec((slots, block), lambda i: (0, i)),
            pl.BlockSpec((slots, block), lambda i: (0, i)),
            pl.BlockSpec((1, block, features), lambda i: (0, i, 0)),
        ],
        out_specs=pl.BlockSpec((slots, 2 * width), lambda i: (0, 0)),
        out_shape=jax.ShapeDtypeStruct((slots, 2 * width), jnp.bfloat16),
        compiler_params=pltpu.CompilerParams(vmem_limit_bytes=VMEM_LIMIT),
        cost_estimate=LITTLE,
    )(grads, gate_pre, up_pre, down_weight)


def input_kernel(joined_ref, gate_up_ref, rows_ref, *refs):
    input_ref, gain_ref = refs[-2:]
    input_grad = times_transposed(joined_ref[...], gate_up_ref[0]).astype(jnp.bfloat16)
    input_ref[...] = input_grad
    terms = input_grad.astype(jnp.float32) * rows_ref[...].astype(jnp.float32)
    gain_ref[...] = jnp.sum(terms, axis=0, keepdims=True)


def backward_input(joined_grad, gate_up_weight, rows, part, held):
    slots, features = rows.shape
    width = joined_grad.shape[1]
    wide = features // 4
    first = 2 * part
    return pl.pallas_call(
        input_kernel,
        grid=(2,),
        in_specs=[
            pl.BlockSpec((slots, width), lambda i: (0, 0)),
            pl.BlockSpec((1, wide, width), lambda i: (0, first + i, 0)),
            pl.BlockSpec((slots, wide), lambda i: (0, first + i)),
        ] + [pl.BlockSpec(memory_space=pl.ANY)] * len(held),
        out_specs=[
            pl.BlockSpec((slots, wide), lambda i: (0, first + i)),
            pl.BlockSpec((1, wide), lambda i: (0, i)),
        ],
        out_shape=[
            jax.ShapeDtypeStruct((slots, features), jnp.bfloat16),
            jax.ShapeDtypeStruct((1, features // 2), jnp.float32),
        ],
        input_output_aliases={3 + n: n for n in range(len(held))},
        compiler_params=pltpu.CompilerParams(vmem_limit_bytes=VMEM_LIMIT),
        cost_estimate=LITTLE,
    )(joined_grad, gate_up_weight, rows, *held)


def pack(columns, gains):
    return jnp.concatenate([columns.reshape(-1, 128), gains])


def unpack_add(columns, gains, got):
    count = gains.shape[0]
    return columns + got[:-count].reshape(columns.shape), gains + got[-count:]


def planes_in_order(gains):
    steps = len(gains)
    order = (lax.axis_index("expert") // 4 - jnp.arange(steps)) % steps
    ordered = jnp.take(jnp.stack(gains), order, axis=0)
    return functools.reduce(jnp.add, [ordered[step] for step in range(steps)]).reshape(-1)


def broadcast_shards(tokens, cotangent, gain, expert_ids, gate_probs, gate_up_weight, down_weight):
    expert_size = lax.axis_size("expert")
    steps = expert_size // 4
    far = 4 * (steps - 1)
    expert, core = lax.axis_index("expert"), lax.axis_index("tensor")
    my_expert = expert * EXP_DEV + core
    group_rows = expert_ids.shape[0]
    half = group_rows // 2
    features = tokens.shape[1]
    capacity = 3 * group_rows * TOP // (2 * EXP_DEV * expert_size)
    near_own = jnp.stack([tokens, cotangent])
    near_pair = jnp.concatenate([near_own, send_second(near_own)])
    near_far_pair = send_first(near_pair)
    tables = plane_tables(
        after(jnp.concatenate([expert_ids.T.astype(jnp.float32), gate_probs.T]), near_pair)
    )
    token_far = after(jnp.stack([send_along(tokens, -step) for step in range(1, steps)]), tables)
    late_tables = after(tables, token_far)
    far_tables = [send_along(late_tables, -step) for step in range(1, steps)]
    late_cot = after(cotangent, token_far)
    cot_steps = [send_along(late_cot, -step) for step in range(1, steps)]
    token_second = after(send_second(token_far), near_far_pair, cot_steps[0], *far_tables)
    token_pair = jnp.concatenate([token_far, token_second])
    tables = far_first(jnp.stack([tables] + far_tables, axis=2))
    tables = jnp.where(core == 0, tables, jnp.roll(tables, half, axis=2))
    matches = tables[:, :TOP] == my_expert.astype(jnp.float32)
    chosen = jnp.any(matches, axis=1)
    weight_of = jnp.sum(jnp.where(matches, tables[:, TOP:], 0.0), axis=1)
    row_ids = jnp.arange(group_rows, dtype=jnp.int32)
    earlier = (row_ids[:, None] < row_ids[None, :]).astype(jnp.bfloat16)
    rank_in = jnp.dot(chosen.astype(jnp.bfloat16), earlier, preferred_element_type=jnp.float32)
    placed = chosen[:, None, :] & (
        rank_in.astype(jnp.int32)[:, None, :] == jnp.arange(capacity, dtype=jnp.int32)[None, :, None]
    )
    pick = placed.astype(jnp.bfloat16)
    back = jnp.swapaxes(pick, 1, 2)
    slot_prob = jnp.sum(jnp.where(placed, weight_of[:, None, :], 0.0), axis=2, keepdims=True)

    gain_row = gain[None, :]
    near_pieces = (near_pair, near_far_pair, send_core(near_pair), send_core(near_far_pair))
    rows, = select_normed(pick, gain_row, near_pieces, 1, 2, far, ())
    near_slots = 4 * capacity
    made = list(forward(
        rows.reshape(-1, features), gate_up_weight, down_weight, near_slots, far // 4, 1, ()
    ))
    *cot_steps, made[2] = together(*cot_steps, made[2])
    cot_far = jnp.stack(cot_steps)
    token_far_pair, cot_far = together(send_first(token_pair), cot_far)
    cot_second = send_second(cot_far)
    token_pieces = (token_pair, token_far_pair, send_core(token_pair), send_core(token_far_pair))
    rows, = select_normed(pick, gain_row, token_pieces, steps - 1, 1, 0, (rows,))
    rows, cot_second = together(rows, cot_second)
    cot_pair = jnp.concatenate([cot_far, cot_second])
    cot_far_pair = send_first(cot_pair)

    rows = rows.reshape(-1, features)
    gate_pre, up_pre, hidden, block_out = forward(
        rows, gate_up_weight, down_weight, far * capacity // 2, 0, 2, tuple(made)
    )
    out_slots = block_out.reshape(expert_size, capacity, features)
    out_mine, out_low, out_high = expand(back, slot_prob, (out_slots,), (True,), steps - 1, 0)
    out_high, cot_far_pair = together(out_high, cot_far_pair)
    cot_pieces = (cot_pair, cot_far_pair, send_core(cot_pair), send_core(cot_far_pair))

    half_far, one_far = 2 * (steps - 1), steps - 1
    held = select_grads(
        after(pick, out_high), slot_prob, out_slots, near_pieces, 1, 2, 1, far, ()
    )
    out_core_high = after(send_core(out_high), held[1])
    out_core = send_core(out_low)
    out_upper = narrow(add_up(out_mine[half_far:], out_core_high))
    out_first = send_first(out_upper)
    grads, prob_value = select_grads(
        after(pick, out_upper), slot_prob, out_slots, cot_pieces, steps - 1, 1, 0, 0, tuple(held)
    )
    grads = grads.reshape(-1, features)
    joined_grad = backward_hidden(grads, gate_pre, up_pre, down_weight)
    input_grad, gain_low = backward_input(joined_grad, gate_up_weight, rows, 0, ())
    out_first, gain_low = together(out_first, gain_low)
    out_middle = narrow(
        add_up(out_mine[one_far:half_far], out_core[one_far:half_far], out_first[one_far:])
    )
    out_second = send_second(out_middle)
    input_grad, gain_high = backward_input(
        joined_grad, gate_up_weight, after(rows, out_middle), 1, (input_grad,)
    )
    gain_term = jnp.concatenate([gain_low[0], gain_high[0]])
    input_slots = input_grad.reshape(expert_size, capacity, features)
    in_mine, in_low, in_high = expand(back, slot_prob, (input_slots,), (False,), steps - 1, 0)
    in_high, out_second = together(in_high, out_second)
    in_core_high = send_core(in_high)
    in_core = send_core(in_low)

    def own_plane(mine, core_part, first_part, second_part, count):
        return add_up(mine[:count], core_part[:count], first_part[:count], second_part[:count])

    out_planes = narrow(own_plane(out_mine, out_core, out_first, out_second, one_far))
    out_far = [send_along(out_planes[step - 1], step) for step in range(1, steps)]
    in_upper = narrow(add_up(in_mine[half_far:], after(in_core_high, out_planes)))
    in_first = send_first(in_upper)
    gains = (gain_term / gain).reshape(-1, 128)
    prob_rows = jnp.sum(jnp.where(placed, prob_value, 0.0), axis=1)
    columns = from_far_first(jnp.where(matches, prob_rows[:, None, :], 0.0), steps)
    columns = jnp.where(core == 0, columns, jnp.swapaxes(columns, 0, 1))
    got = send_core(after(pack(columns[..., half:], gains), in_upper))
    gate_up_part = outer_sum(after(rows, in_upper), joined_grad)
    gate_up_part, got = together(gate_up_part, got)
    columns, gains = unpack_add(columns[..., :half], gains, got)
    got = send_bit(pack(columns[1], gains), 2)
    near_mine, near_low, near_high = expand(
        after(back, gate_up_part), slot_prob, (out_slots, input_slots), (True, False), 1, far
    )
    near_high = after(near_high, *out_far[:-1])
    near_core_high = send_core(near_high)
    near_core = send_core(near_low)
    in_first, near_core, near_core_high, got = together(in_first, near_core, near_core_high, got)
    columns, gains = unpack_add(columns[0], gains, got)
    in_middle = narrow(
        add_up(in_mine[one_far:half_far], in_core[one_far:half_far], in_first[one_far:])
    )
    in_second = send_second(in_middle)
    got = send_bit(pack(columns[1], gains), 1)
    near_core, near_core_high = after(near_core, in_middle), after(near_core_high, in_middle)
    near_parts = [
        narrow(add_up(near_mine[2:4], near_core[2:])),
        narrow(add_up(near_mine[4:6], near_core_high[:2])),
        narrow(add_up(near_mine[6:], near_core_high[2:])),
    ]
    down_part = outer_sum(after(hidden, in_middle), grads)
    in_second, got, down_part, *near_parts = together(
        in_second, got, down_part, *near_parts, *out_far[-1:]
    )[:6]
    columns, gains = unpack_add(columns[0], gains, got)
    in_planes = narrow(own_plane(in_mine, in_core, in_first, in_second, one_far))
    in_far = [send_along(in_planes[step - 1], step) for step in range(1, steps)]
    messages = [send_along(pack(columns[step], gains), step) for step in range(1, steps)]
    near_parts = [after(part, in_planes) for part in near_parts]
    arrived = [send_second(near_parts[0]), send_first(near_parts[1]), send_both(near_parts[2])]
    near_terms = [near_mine[:2], near_core[:2]] + arrived
    out_sum = add_up(*out_far, *[term[0] for term in near_terms])
    normed_grad = add_up(*in_far, *[term[1] for term in near_terms])

    prob_sum, all_gains = columns[0], [gains]
    for message in messages:
        prob_sum = prob_sum + message[:-gains.shape[0]].reshape(prob_sum.shape)
        all_gains.append(message[-gains.shape[0]:])
    gain_grad = planes_in_order(all_gains)

    scaled_own, inv_own = normalize(tokens)
    mixed = (tokens.astype(jnp.float32) + out_sum).astype(jnp.bfloat16)
    gain_side = normed_grad * gain[None, :]
    token_grad = (
        cotangent.astype(jnp.float32)
        + inv_own
        * (gain_side - scaled_own * jnp.mean(gain_side * scaled_own, axis=1, keepdims=True))
    ).astype(jnp.bfloat16)
    return (mixed, token_grad, prob_sum.T, gain_grad, gate_up_part[None], down_part[None])


def solution(mesh):
    in_specs = (
        P(("expert", "tensor"), None),
        P(("expert", "tensor"), None),
        P(),
        P("expert", None),
        P("expert", None),
        P(("expert", "tensor"), None, None),
        P(("expert", "tensor"), None, None),
    )
    out_specs = (
        P(("expert", "tensor"), None),
        P(("expert", "tensor"), None),
        P(("expert", "tensor"), None),
        P(),
        P(("expert", "tensor"), None, None),
        P(("expert", "tensor"), None, None),
    )
    expert_size, tensor_size = mesh.shape["expert"], mesh.shape["tensor"]
    few = tensor_size == EXP_DEV and expert_size % 4 == 0 and expert_size <= 4 * TOP
    shards = broadcast_shards if few else routed_shards
    return jax.shard_map(shards, mesh=mesh, in_specs=in_specs, out_specs=out_specs, check_vma=False)
```

```python
import functools

import jax
import jax.numpy as jnp
from jax import lax
from jax.experimental import pallas as pl
from jax.experimental.pallas import tpu as pltpu
from jax.sharding import PartitionSpec as P

TOP = 8
EXP_DEV = 2
VMEM_LIMIT = 63 * 1024 * 1024
LITTLE = pl.CostEstimate(flops=1000000, bytes_accessed=100000, transcendentals=0)


def normalize(rows):
    values = rows.astype(jnp.float32)
    inv_rms = lax.rsqrt(jnp.mean(values * values, axis=1, keepdims=True) + 1e-06)
    return (values * inv_rms, inv_rms)


def expert_forward(rows, gate_up, down_proj):
    projected = jnp.dot(rows, gate_up, preferred_element_type=jnp.float32)
    half_width = down_proj.shape[0]
    gate_pre = projected[:, :half_width]
    up_pre = projected[:, half_width:]
    sigmoid_gate = jax.nn.sigmoid(gate_pre)
    hidden = (gate_pre * sigmoid_gate * up_pre).astype(jnp.bfloat16)
    block_out = jnp.dot(hidden, down_proj, preferred_element_type=jnp.float32).astype(jnp.bfloat16)
    return (gate_pre, up_pre, sigmoid_gate, hidden, block_out)


def times_transposed(left, right):
    return lax.dot_general(left, right, (((1,), (1,)), ((), ())), preferred_element_type=jnp.float32)


def outer_sum(left, right):
    product = lax.dot_general(left, right, (((0,), (0,)), ((), ())), preferred_element_type=jnp.float32)
    return product.astype(jnp.bfloat16)


def backward_inner(slot_grads, down_proj, gate_pre, up_pre, sigmoid_gate):
    hidden_grad = times_transposed(slot_grads, down_proj)
    gate_grad = (
        hidden_grad * up_pre * sigmoid_gate * (1.0 + gate_pre * (1.0 - sigmoid_gate))
    ).astype(jnp.bfloat16)
    up_grad = (hidden_grad * gate_pre * sigmoid_gate).astype(jnp.bfloat16)
    return jnp.concatenate([gate_grad, up_grad], axis=1)


def expert_backward(rows, slot_grads, gate_up, down_proj, gate_pre, up_pre, sigmoid_gate, hidden):
    joined_grad = backward_inner(slot_grads, down_proj, gate_pre, up_pre, sigmoid_gate)
    input_grad = times_transposed(joined_grad, gate_up).astype(jnp.bfloat16)
    return (input_grad, outer_sum(rows, joined_grad), outer_sum(hidden, slot_grads))


def routed_shards(tokens, cotangent, gain, expert_ids, gate_probs, gate_up_weight, down_weight):
    tensor_size = lax.axis_size("tensor")
    expert_size = lax.axis_size("expert")
    my_rank = lax.axis_index("tensor")
    blocks_each = tensor_size // EXP_DEV
    my_type = my_rank // blocks_each
    group_rows = expert_ids.shape[0]
    features = tokens.shape[1]
    capacity = 3 * group_rows * TOP // (2 * EXP_DEV * expert_size)
    highest = lax.Precision.HIGHEST
    scaled_own, inv_own = normalize(tokens)
    carried = (scaled_own * gain[None, :]).astype(jnp.bfloat16)
    group_first, group_grads = (
        lax.all_gather(carried, "tensor", axis=0, tiled=True),
        lax.all_gather(cotangent, "tensor", axis=0, tiled=True),
    )
    targets = jnp.arange(expert_size, dtype=jnp.int32) * EXP_DEV + my_type
    matches = expert_ids[:, :, None] == targets[None, None, :]
    chosen = jnp.any(matches, axis=1)
    weight_of = jnp.sum(jnp.where(matches, gate_probs[:, :, None], 0.0), axis=1)
    slot_of = jnp.sum(
        jnp.where(matches, jnp.arange(TOP, dtype=jnp.int32)[None, :, None], 0), axis=1
    )
    row_ids = jnp.arange(group_rows, dtype=jnp.int32)
    earlier = (row_ids[None, :] < row_ids[:, None]).astype(jnp.bfloat16)
    rank_in = jnp.dot(
        earlier, chosen.astype(jnp.bfloat16), preferred_element_type=jnp.float32
    ).astype(jnp.int32)
    placed = chosen.T[:, None, :] & (
        rank_in.T[:, None, :] == jnp.arange(capacity, dtype=jnp.int32)[None, :, None]
    )
    source = jnp.sum(jnp.where(placed, row_ids[None, None, :], 0), axis=2)
    filled = jnp.any(placed, axis=2)
    slot_prob = jnp.sum(jnp.where(placed, weight_of.T[:, None, :], 0.0), axis=2)
    slot_index = jnp.sum(jnp.where(placed, slot_of.T[:, None, :], 0), axis=2)
    sent_rows = jnp.where(
        filled[:, :, None], jnp.take(group_first, source, axis=0), jnp.zeros((), jnp.bfloat16)
    )
    sent_grads = (
        slot_prob[:, :, None] * jnp.take(group_grads, source, axis=0).astype(jnp.float32)
    ).astype(jnp.bfloat16)
    gate_up = gate_up_weight[0]
    down_proj = down_weight[0]
    arrived_rows, arrived_grads = (
        lax.all_to_all(sent_rows, "expert", split_axis=0, concat_axis=0, tiled=True),
        lax.all_to_all(sent_grads, "expert", split_axis=0, concat_axis=0, tiled=True),
    )
    rows = arrived_rows.reshape(-1, features)
    slot_grads = arrived_grads.reshape(-1, features)
    gate_pre, up_pre, sigmoid_gate, hidden, block_out = expert_forward(rows, gate_up, down_proj)
    out_slots = block_out.reshape(expert_size, capacity, features)
    input_grad, gate_up_part, down_part = expert_backward(
        rows, slot_grads, gate_up, down_proj, gate_pre, up_pre, sigmoid_gate, hidden
    )
    input_slots = input_grad.reshape(expert_size, capacity, features)
    out_back, input_back = (
        lax.all_to_all(out_slots, "expert", split_axis=0, concat_axis=0, tiled=True),
        lax.all_to_all(input_slots, "expert", split_axis=0, concat_axis=0, tiled=True),
    )
    out_flat = out_back.reshape(-1, features)
    input_flat = input_back.reshape(-1, features)
    used_source = source.reshape(-1)
    used_filled = filled.reshape(-1)
    used_prob = slot_prob.reshape(-1)
    used_index = slot_index.reshape(-1)
    cot_slots = jnp.take(group_grads, used_source, axis=0)
    prob_values = jnp.einsum("sd,sd->s", cot_slots, out_flat, preferred_element_type=jnp.float32)
    hit = (row_ids[:, None] == used_source[None, :]) & used_filled[None, :]
    input_part = jnp.dot(hit.astype(jnp.bfloat16), input_flat, preferred_element_type=jnp.float32)
    weighting = jnp.where(hit, used_prob[None, :], 0.0)
    out_part = jnp.dot(
        weighting,
        out_flat.astype(jnp.float32),
        precision=highest,
        preferred_element_type=jnp.float32,
    )
    prob_columns = jnp.where(
        used_index[:, None] == jnp.arange(TOP, dtype=jnp.int32)[None, :], prob_values[:, None], 0.0
    )
    prob_part = jnp.dot(
        hit.astype(jnp.float32), prob_columns, precision=highest, preferred_element_type=jnp.float32
    )
    out_sum, normed_grad, prob_grad = (
        lax.psum_scatter(out_part, "tensor", scatter_dimension=0, tiled=True),
        lax.psum_scatter(input_part, "tensor", scatter_dimension=0, tiled=True),
        lax.psum_scatter(prob_part, "tensor", scatter_dimension=0, tiled=True),
    )
    mixed = (tokens.astype(jnp.float32) + out_sum).astype(jnp.bfloat16)
    gain_side = normed_grad * gain[None, :]
    token_grad = (
        cotangent.astype(jnp.float32)
        + inv_own
        * (gain_side - scaled_own * jnp.mean(gain_side * scaled_own, axis=1, keepdims=True))
    ).astype(jnp.bfloat16)
    gain_grad = lax.psum(jnp.sum(normed_grad * scaled_own, axis=0), ("expert", "tensor"))
    return (mixed, token_grad, prob_grad, gain_grad, gate_up_part[None], down_part[None])


BOTH = ("expert", "tensor")


def flip_first(expert, core):
    return expert ^ (2 if core == 0 else 1)


def flip_second(expert, core):
    return expert ^ (1 if core == 0 else 2)


def send(array, place):
    pairs = []
    for expert in range(lax.axis_size("expert")):
        for core in range(2):
            to_expert, to_core = place(expert, core)
            pairs.append((expert * 2 + core, to_expert * 2 + to_core))
    return lax.ppermute(array, BOTH, pairs)


def send_first(array):
    return send(array, lambda e, c: (flip_first(e, c), c))


def send_second(array):
    return send(array, lambda e, c: (flip_second(e, c), c))


def send_both(array):
    return send(array, lambda e, c: (e ^ 3, c))


def send_bit(array, bit):
    return send(array, lambda e, c: (e ^ bit, c))


def send_core(array):
    return send(array, lambda e, c: (e, 1 - c))


def send_along(array, step):
    size = lax.axis_size("expert")
    return send(array, lambda e, c: ((e + 4 * step) % size, c))


def after(array, *others):
    return lax.optimization_barrier((array,) + others)[0]


def together(*arrays):
    return lax.optimization_barrier(arrays)


def add_up(*terms):
    return sum(term.astype(jnp.float32) for term in terms)


def narrow(value):
    return value.astype(jnp.bfloat16)


def plane_tables(table):
    pair = jnp.stack([table, send_second(table)])
    return jnp.stack([pair, send_first(pair)])


def far_first(array):
    far = array[:, :, 1:].reshape((-1,) + array.shape[3:])
    return jnp.concatenate([far, array[:, :, 0].reshape((-1,) + array.shape[3:])])


def from_far_first(array, steps):
    far = array[:4 * (steps - 1)].reshape((2, 2, steps - 1) + array.shape[1:])
    return jnp.concatenate([array[4 * (steps - 1):].reshape((2, 2, 1) + array.shape[1:]), far], axis=2)


def start(source, target, semaphore):
    copy = pltpu.make_async_copy(source, target, semaphore)
    copy.start()
    return copy


def chosen_rows(pick, mine, other):
    return jnp.dot(pick, jnp.concatenate([mine, other]), preferred_element_type=jnp.float32)


def norm_kernel(count, pick_ref, *refs):
    pieces, gain_ref, normed_ref = refs[:4], refs[4], refs[-1]

    def work(mine_ref, other_ref):
        for group in range(count):
            rows = chosen_rows(pick_ref[group], mine_ref[group], other_ref[group])
            inv_rms = lax.rsqrt(jnp.mean(rows * rows, axis=1, keepdims=True) + 1e-06)
            normed_ref[group] = (rows * inv_rms * gain_ref[...]).astype(jnp.bfloat16)

    by_place(work, pieces)


def grad_kernel(count, pick_ref, *refs):
    pieces, prob_ref, out_ref, (grad_ref, value_ref) = refs[:4], refs[4], refs[5], refs[-2:]

    def work(mine_ref, other_ref):
        for group in range(count):
            rows = chosen_rows(pick_ref[group], mine_ref[group], other_ref[group])
            grad_ref[group] = (rows * prob_ref[group]).astype(jnp.bfloat16)
            value_ref[group] = jnp.sum(rows * out_ref[group].astype(jnp.float32), axis=1, keepdims=True)

    by_place(work, pieces)


def by_place(work, pieces):
    for first in range(2):
        for second in range(2):
            pl.when(pl.program_id(0) == first * 2 + second)(
                functools.partial(work, pieces[first], pieces[2 + second])
            )


def group_spec(count, first_group, *shape):
    first_block = first_group // count
    return pl.BlockSpec((count,) + shape, lambda i: (first_block + i, 0, 0))


def select(kernel, pick, pieces, extras, extra_specs, out_shapes, count, arrays, which, first_group, held):
    _, capacity, group_rows = pick.shape
    half, features = pieces[0].shape[1:]

    def piece_spec(place):
        return pl.BlockSpec((count, half, features), lambda i: (place(i) * arrays + which, 0, 0))

    return pl.pallas_call(
        functools.partial(kernel, count),
        grid=(4,),
        in_specs=[
            group_spec(count, first_group, capacity, group_rows),
            piece_spec(lambda i: jnp.minimum(i, 1)),
            piece_spec(lambda i: jnp.maximum(i - 2, 0)),
            piece_spec(lambda i: i // 2),
            piece_spec(lambda i: jnp.maximum(i - 2, 0)),
        ] + extra_specs + [pl.BlockSpec(memory_space=pl.ANY)] * len(held),
        out_specs=[group_spec(count, first_group, *out.shape[1:]) for out in out_shapes],
        out_shape=out_shapes,
        input_output_aliases={5 + len(extras) + n: n for n in range(len(held))},
        compiler_params=pltpu.CompilerParams(vmem_limit_bytes=VMEM_LIMIT),
        cost_estimate=LITTLE,
    )(pick, *pieces, *extras, *held)


def select_normed(pick, gain, pieces, count, arrays, first_group, held):
    groups, capacity, _ = pick.shape
    features = pieces[0].shape[2]
    return select(
        norm_kernel, pick, pieces, [gain], [pl.BlockSpec((1, features), lambda i: (0, 0))],
        [jax.ShapeDtypeStruct((groups, capacity, features), jnp.bfloat16)],
        count, arrays, 0, first_group, held,
    )


def select_grads(pick, prob, out_slots, pieces, count, arrays, which, first_group, held):
    groups, capacity, _ = pick.shape
    features = pieces[0].shape[2]
    return select(
        grad_kernel, pick, pieces, [prob, out_slots],
        [group_spec(count, first_group, capacity, 1), group_spec(count, first_group, capacity, features)],
        [
            jax.ShapeDtypeStruct((groups, capacity, features), jnp.bfloat16),
            jax.ShapeDtypeStruct((groups, capacity, 1), jnp.float32),
        ],
        count, arrays, which, first_group, held,
    )


def expand_kernel(weighted, count, first_group, back_ref, prob_ref, *refs):
    arrays = len(weighted)
    sources, mine_ref, pieces = refs[:arrays], refs[arrays], refs[arrays + 1:arrays + 3]
    loaded, spread, loads, stores = refs[arrays + 3:]
    half = mine_ref.shape[1]
    copies, written = [], []
    for group in range(4 * count):
        for number, source in enumerate(sources):
            place = group * arrays + number
            copies.append(start(source.at[first_group + group], loaded.at[place], loads.at[place]))
    for group in range(4 * count):
        outer, inner = divmod(group, count)
        first, second = divmod(outer, 2)
        for number, by_prob in enumerate(weighted):
            place = group * arrays + number
            copies[place].wait()
            rows = loaded[place]
            if by_prob:
                rows = (rows.astype(jnp.float32) * prob_ref[first_group + group]).astype(jnp.bfloat16)
            spread[place] = jnp.dot(
                back_ref[first_group + group], rows, preferred_element_type=jnp.float32
            ).astype(jnp.bfloat16)
            target = pieces[second].at[(first * count + inner) * arrays + number]
            written += [
                start(spread.at[place, pl.ds(half, half)], target, stores.at[place, 0]),
                start(spread.at[place, pl.ds(0, half)], mine_ref.at[place], stores.at[place, 1]),
            ]
    for copy in written:
        copy.wait()


def expand(back, prob, slots, weighted, count, first_group):
    _, group_rows, capacity = back.shape
    half, features, arrays = group_rows // 2, slots[0].shape[2], len(slots)
    blocks = 4 * count * arrays
    anywhere, whole = pl.BlockSpec(memory_space=pl.ANY), pl.BlockSpec(memory_space=pltpu.VMEM)
    piece = jax.ShapeDtypeStruct((blocks // 2, half, features), jnp.bfloat16)
    return pl.pallas_call(
        functools.partial(expand_kernel, weighted, count, first_group),
        in_specs=[whole, whole] + [anywhere] * arrays,
        out_specs=[anywhere] * 3,
        out_shape=[jax.ShapeDtypeStruct((blocks, half, features), jnp.bfloat16), piece, piece],
        scratch_shapes=[
            pltpu.VMEM((blocks, capacity, features), jnp.bfloat16),
            pltpu.VMEM((blocks, group_rows, features), jnp.bfloat16),
            pltpu.SemaphoreType.DMA((blocks,)),
            pltpu.SemaphoreType.DMA((blocks, 2)),
        ],
        compiler_params=pltpu.CompilerParams(vmem_limit_bytes=VMEM_LIMIT),
        cost_estimate=LITTLE,
    )(back, prob, *slots)


def forward_kernel(rows_ref, gate_up_ref, down_ref, *refs):
    gate_pre_ref, up_pre_ref, hidden_ref, out_ref = refs[-4:]
    projected = jnp.dot(rows_ref[...], gate_up_ref[0], preferred_element_type=jnp.float32)
    half_width = hidden_ref.shape[1]
    gate_pre, up_pre = projected[:, :half_width], projected[:, half_width:]
    gate_pre_ref[...] = gate_pre
    up_pre_ref[...] = up_pre
    hidden = (gate_pre * jax.nn.sigmoid(gate_pre) * up_pre).astype(jnp.bfloat16)
    hidden_ref[...] = hidden
    out_ref[...] = jnp.dot(hidden, down_ref[0], preferred_element_type=jnp.float32).astype(jnp.bfloat16)


def forward(rows, gate_up_weight, down_weight, block, first, steps, held):
    slots, features = rows.shape
    width = down_weight.shape[1]
    def row_spec(columns):
        return pl.BlockSpec((block, columns), lambda i: (first + i, 0))

    return pl.pallas_call(
        forward_kernel,
        grid=(steps,),
        in_specs=[
            row_spec(features),
            pl.BlockSpec((1, features, 2 * width), lambda i: (0, 0, 0)),
            pl.BlockSpec((1, width, features), lambda i: (0, 0, 0)),
        ] + [pl.BlockSpec(memory_space=pl.ANY)] * len(held),
        out_specs=[row_spec(width), row_spec(width), row_spec(width), row_spec(features)],
        out_shape=[
            jax.ShapeDtypeStruct((slots, width), jnp.float32),
            jax.ShapeDtypeStruct((slots, width), jnp.float32),
            jax.ShapeDtypeStruct((slots, width), jnp.bfloat16),
            jax.ShapeDtypeStruct((slots, features), jnp.bfloat16),
        ],
        input_output_aliases={3 + n: n for n in range(len(held))},
        compiler_params=pltpu.CompilerParams(vmem_limit_bytes=VMEM_LIMIT),
        cost_estimate=LITTLE,
    )(rows, gate_up_weight, down_weight, *held)


def inner_kernel(units, grads_ref, gate_pre_ref, up_pre_ref, down_ref, joined_ref):
    step = pl.program_id(0)
    block = gate_pre_ref.shape[1]
    gate_pre, up_pre = gate_pre_ref[...], up_pre_ref[...]
    sigmoid_gate = jax.nn.sigmoid(gate_pre)
    common = times_transposed(grads_ref[...], down_ref[0]) * sigmoid_gate
    gate_grad = common * up_pre * (1.0 + gate_pre * (1.0 - sigmoid_gate))
    start = pl.multiple_of(step * block, block)
    joined_ref[:, pl.ds(start, block)] = gate_grad.astype(jnp.bfloat16)
    joined_ref[:, pl.ds(units * block + start, block)] = (common * gate_pre).astype(jnp.bfloat16)


def backward_hidden(grads, gate_pre, up_pre, down_weight):
    slots, features = grads.shape
    width = down_weight.shape[1]
    block, units = 256, width // 256
    return pl.pallas_call(
        functools.partial(inner_kernel, units),
        grid=(units,),
        in_specs=[
            pl.BlockSpec((slots, features), lambda i: (0, 0)),
            pl.BlockSpec((slots, block), lambda i: (0, i)),
            pl.BlockSpec((slots, block), lambda i: (0, i)),
            pl.BlockSpec((1, block, features), lambda i: (0, i, 0)),
        ],
        out_specs=pl.BlockSpec((slots, 2 * width), lambda i: (0, 0)),
        out_shape=jax.ShapeDtypeStruct((slots, 2 * width), jnp.bfloat16),
        compiler_params=pltpu.CompilerParams(vmem_limit_bytes=VMEM_LIMIT),
        cost_estimate=LITTLE,
    )(grads, gate_pre, up_pre, down_weight)


def input_kernel(joined_ref, gate_up_ref, rows_ref, *refs):
    input_ref, gain_ref = refs[-2:]
    input_grad = times_transposed(joined_ref[...], gate_up_ref[0]).astype(jnp.bfloat16)
    input_ref[...] = input_grad
    terms = input_grad.astype(jnp.float32) * rows_ref[...].astype(jnp.float32)
    gain_ref[...] = jnp.sum(terms, axis=0, keepdims=True)


def backward_input(joined_grad, gate_up_weight, rows, part, held):
    slots, features = rows.shape
    width = joined_grad.shape[1]
    wide = features // 4
    first = 2 * part
    return pl.pallas_call(
        input_kernel,
        grid=(2,),
        in_specs=[
            pl.BlockSpec((slots, width), lambda i: (0, 0)),
            pl.BlockSpec((1, wide, width), lambda i: (0, first + i, 0)),
            pl.BlockSpec((slots, wide), lambda i: (0, first + i)),
        ] + [pl.BlockSpec(memory_space=pl.ANY)] * len(held),
        out_specs=[
            pl.BlockSpec((slots, wide), lambda i: (0, first + i)),
            pl.BlockSpec((1, wide), lambda i: (0, i)),
        ],
        out_shape=[
            jax.ShapeDtypeStruct((slots, features), jnp.bfloat16),
            jax.ShapeDtypeStruct((1, features // 2), jnp.float32),
        ],
        input_output_aliases={3 + n: n for n in range(len(held))},
        compiler_params=pltpu.CompilerParams(vmem_limit_bytes=VMEM_LIMIT),
        cost_estimate=LITTLE,
    )(joined_grad, gate_up_weight, rows, *held)


def pack(columns, gains):
    return jnp.concatenate([columns.reshape(-1, 128), gains])


def unpack_add(columns, gains, got):
    count = gains.shape[0]
    return columns + got[:-count].reshape(columns.shape), gains + got[-count:]


def planes_in_order(gains):
    steps = len(gains)
    order = (lax.axis_index("expert") // 4 - jnp.arange(steps)) % steps
    ordered = jnp.take(jnp.stack(gains), order, axis=0)
    return functools.reduce(jnp.add, [ordered[step] for step in range(steps)]).reshape(-1)


def broadcast_shards(tokens, cotangent, gain, expert_ids, gate_probs, gate_up_weight, down_weight):
    expert_size = lax.axis_size("expert")
    steps = expert_size // 4
    far = 4 * (steps - 1)
    expert, core = lax.axis_index("expert"), lax.axis_index("tensor")
    my_expert = expert * EXP_DEV + core
    group_rows = expert_ids.shape[0]
    half = group_rows // 2
    features = tokens.shape[1]
    capacity = 3 * group_rows * TOP // (2 * EXP_DEV * expert_size)
    near_own = jnp.stack([tokens, cotangent])
    near_pair = jnp.concatenate([near_own, send_second(near_own)])
    near_far_pair = send_first(near_pair)
    tables = plane_tables(
        after(jnp.concatenate([expert_ids.T.astype(jnp.float32), gate_probs.T]), near_pair)
    )
    token_far = after(jnp.stack([send_along(tokens, -step) for step in range(1, steps)]), tables)
    late_tables = after(tables, token_far)
    far_tables = [send_along(late_tables, -step) for step in range(1, steps)]
    late_cot = after(cotangent, token_far)
    cot_steps = [send_along(late_cot, -step) for step in range(1, steps)]
    token_second = after(send_second(token_far), near_far_pair, cot_steps[0], *far_tables)
    token_pair = jnp.concatenate([token_far, token_second])
    tables = far_first(jnp.stack([tables] + far_tables, axis=2))
    tables = jnp.where(core == 0, tables, jnp.roll(tables, half, axis=2))
    matches = tables[:, :TOP] == my_expert.astype(jnp.float32)
    chosen = jnp.any(matches, axis=1)
    weight_of = jnp.sum(jnp.where(matches, tables[:, TOP:], 0.0), axis=1)
    row_ids = jnp.arange(group_rows, dtype=jnp.int32)
    earlier = (row_ids[:, None] < row_ids[None, :]).astype(jnp.bfloat16)
    rank_in = jnp.dot(chosen.astype(jnp.bfloat16), earlier, preferred_element_type=jnp.float32)
    placed = chosen[:, None, :] & (
        rank_in.astype(jnp.int32)[:, None, :] == jnp.arange(capacity, dtype=jnp.int32)[None, :, None]
    )
    pick = placed.astype(jnp.bfloat16)
    back = jnp.swapaxes(pick, 1, 2)
    slot_prob = jnp.sum(jnp.where(placed, weight_of[:, None, :], 0.0), axis=2, keepdims=True)

    gain_row = gain[None, :]
    near_pieces = (near_pair, near_far_pair, send_core(near_pair), send_core(near_far_pair))
    rows, = select_normed(pick, gain_row, near_pieces, 1, 2, far, ())
    near_slots = 4 * capacity
    made = list(forward(
        rows.reshape(-1, features), gate_up_weight, down_weight, near_slots, far // 4, 1, ()
    ))
    *cot_steps, made[2] = together(*cot_steps, made[2])
    cot_far = jnp.stack(cot_steps)
    token_far_pair, cot_far = together(send_first(token_pair), cot_far)
    cot_second = send_second(cot_far)
    token_pieces = (token_pair, token_far_pair, send_core(token_pair), send_core(token_far_pair))
    rows, = select_normed(pick, gain_row, token_pieces, steps - 1, 1, 0, (rows,))
    rows, cot_second = together(rows, cot_second)
    cot_pair = jnp.concatenate([cot_far, cot_second])
    cot_far_pair = send_first(cot_pair)

    rows = rows.reshape(-1, features)
    gate_pre, up_pre, hidden, block_out = forward(
        rows, gate_up_weight, down_weight, far * capacity, 0, 1, tuple(made)
    )
    out_slots = block_out.reshape(expert_size, capacity, features)
    out_mine, out_low, out_high = expand(back, slot_prob, (out_slots,), (True,), steps - 1, 0)
    out_high, cot_far_pair = together(out_high, cot_far_pair)
    cot_pieces = (cot_pair, cot_far_pair, send_core(cot_pair), send_core(cot_far_pair))

    half_far, one_far = 2 * (steps - 1), steps - 1
    held = select_grads(
        after(pick, out_high), slot_prob, out_slots, near_pieces, 1, 2, 1, far, ()
    )
    out_core_high = after(send_core(out_high), held[1])
    out_core = send_core(out_low)
    out_upper = narrow(add_up(out_mine[half_far:], out_core_high))
    out_first = send_first(out_upper)
    grads, prob_value = select_grads(
        after(pick, out_upper), slot_prob, out_slots, cot_pieces, steps - 1, 1, 0, 0, tuple(held)
    )
    grads = grads.reshape(-1, features)
    joined_grad = backward_hidden(grads, gate_pre, up_pre, down_weight)
    input_grad, gain_low = backward_input(joined_grad, gate_up_weight, rows, 0, ())
    out_first, gain_low = together(out_first, gain_low)
    out_middle = narrow(
        add_up(out_mine[one_far:half_far], out_core[one_far:half_far], out_first[one_far:])
    )
    out_second = send_second(out_middle)
    input_grad, gain_high = backward_input(
        joined_grad, gate_up_weight, after(rows, out_middle), 1, (input_grad,)
    )
    gain_term = jnp.concatenate([gain_low[0], gain_high[0]])
    input_slots = input_grad.reshape(expert_size, capacity, features)
    in_mine, in_low, in_high = expand(back, slot_prob, (input_slots,), (False,), steps - 1, 0)
    in_high, out_second = together(in_high, out_second)
    in_core_high = send_core(in_high)
    in_core = send_core(in_low)

    def own_plane(mine, core_part, first_part, second_part, count):
        return add_up(mine[:count], core_part[:count], first_part[:count], second_part[:count])

    out_planes = narrow(own_plane(out_mine, out_core, out_first, out_second, one_far))
    out_far = [send_along(out_planes[step - 1], step) for step in range(1, steps)]
    in_upper = narrow(add_up(in_mine[half_far:], after(in_core_high, out_planes)))
    in_first = send_first(in_upper)
    gains = (gain_term / gain).reshape(-1, 128)
    prob_rows = jnp.sum(jnp.where(placed, prob_value, 0.0), axis=1)
    columns = from_far_first(jnp.where(matches, prob_rows[:, None, :], 0.0), steps)
    columns = jnp.where(core == 0, columns, jnp.swapaxes(columns, 0, 1))
    got = send_core(after(pack(columns[..., half:], gains), in_upper))
    gate_up_part = outer_sum(after(rows, in_upper), joined_grad)
    gate_up_part, got = together(gate_up_part, got)
    columns, gains = unpack_add(columns[..., :half], gains, got)
    got = send_bit(pack(columns[1], gains), 2)
    near_mine, near_low, near_high = expand(
        after(back, gate_up_part), slot_prob, (out_slots, input_slots), (True, False), 1, far
    )
    near_high = after(near_high, *out_far[:-1])
    near_core_high = send_core(near_high)
    near_core = send_core(near_low)
    in_first, near_core, near_core_high, got = together(in_first, near_core, near_core_high, got)
    columns, gains = unpack_add(columns[0], gains, got)
    in_middle = narrow(
        add_up(in_mine[one_far:half_far], in_core[one_far:half_far], in_first[one_far:])
    )
    in_second = send_second(in_middle)
    got = send_bit(pack(columns[1], gains), 1)
    near_core, near_core_high = after(near_core, in_middle), after(near_core_high, in_middle)
    near_parts = [
        narrow(add_up(near_mine[2:4], near_core[2:])),
        narrow(add_up(near_mine[4:6], near_core_high[:2])),
        narrow(add_up(near_mine[6:], near_core_high[2:])),
    ]
    down_part = outer_sum(after(hidden, in_middle), grads)
    in_second, got, down_part, *near_parts = together(
        in_second, got, down_part, *near_parts, *out_far[-1:]
    )[:6]
    columns, gains = unpack_add(columns[0], gains, got)
    in_planes = narrow(own_plane(in_mine, in_core, in_first, in_second, one_far))
    in_far = [send_along(in_planes[step - 1], step) for step in range(1, steps)]
    messages = [send_along(pack(columns[step], gains), step) for step in range(1, steps)]
    near_parts = [after(part, in_planes) for part in near_parts]
    arrived = [send_second(near_parts[0]), send_first(near_parts[1]), send_both(near_parts[2])]
    near_terms = [near_mine[:2], near_core[:2]] + arrived
    out_sum = add_up(*out_far, *[term[0] for term in near_terms])
    normed_grad = add_up(*in_far, *[term[1] for term in near_terms])

    prob_sum, all_gains = columns[0], [gains]
    for message in messages:
        prob_sum = prob_sum + message[:-gains.shape[0]].reshape(prob_sum.shape)
        all_gains.append(message[-gains.shape[0]:])
    gain_grad = planes_in_order(all_gains)

    scaled_own, inv_own = normalize(tokens)
    mixed = (tokens.astype(jnp.float32) + out_sum).astype(jnp.bfloat16)
    gain_side = normed_grad * gain[None, :]
    token_grad = (
        cotangent.astype(jnp.float32)
        + inv_own
        * (gain_side - scaled_own * jnp.mean(gain_side * scaled_own, axis=1, keepdims=True))
    ).astype(jnp.bfloat16)
    return (mixed, token_grad, prob_sum.T, gain_grad, gate_up_part[None], down_part[None])


def solution(mesh):
    in_specs = (
        P(("expert", "tensor"), None),
        P(("expert", "tensor"), None),
        P(),
        P("expert", None),
        P("expert", None),
        P(("expert", "tensor"), None, None),
        P(("expert", "tensor"), None, None),
    )
    out_specs = (
        P(("expert", "tensor"), None),
        P(("expert", "tensor"), None),
        P(("expert", "tensor"), None),
        P(),
        P(("expert", "tensor"), None, None),
        P(("expert", "tensor"), None, None),
    )
    expert_size, tensor_size = mesh.shape["expert"], mesh.shape["tensor"]
    few = tensor_size == EXP_DEV and expert_size % 4 == 0 and expert_size <= 4 * TOP
    shards = broadcast_shards if few else routed_shards
    return jax.shard_map(shards, mesh=mesh, in_specs=in_specs, out_specs=out_specs, check_vma=False)
```
